32 devices in a mesh: dp: 16 (over z, y, x), mp: 2 (over core).
Axes of the slice: x: 2, y: 2, z: 4, core: 2. Of those that a mesh axis runs over, the one named last changes fastest.
Arguments:
- pixels: bfloat16 [32768, 768], P('dp'), may hold values from -6 to 6
- target: bfloat16 [32768, 768], P('dp'), may hold values from -6 to 6
- band_ids: int32 [32768, 768], P('dp'), may hold values from 0 to 2, as said below
- kept_index: int32 [128, 64], P('dp'), may hold values from 0 to 255, as said below
- intersection: int32 [128, 256], P('dp'), may hold values 0 or 1
- gsd_scale: int32 [128], P('dp'), may hold values from 1 to 8
- enc_attn: float32 [4, 1024, 1024], P(None, 'dp', 'mp')
- enc_mlp: float32 [2, 1024, 4096], P(None, 'dp', 'mp'), may hold values from -0.1875 to 0.1875
- dec_attn: float32 [4, 512, 512], P(None, 'dp', 'mp')
- dec_mlp: float32 [2, 512, 2048], P(None, 'dp', 'mp'), may hold values from -0.25 to 0.25
- patch_embed: float32 [768, 1024], P(None, 'dp'), may hold values from -0.21875 to 0.21875
- bridge: float32 [1024, 512], P('dp'), may hold values from -0.1875 to 0.1875
- predict: float32 [512, 768], P('dp'), may hold values from -0.25 to 0.25
- vectors: float32 [11520], P('dp')
- first_enc_attn: float32 [4, 1024, 1024], P(None, 'dp', 'mp'), may hold values from -7.4505806e-08 to 7.4505806e-08
- first_enc_mlp: float32 [2, 1024, 4096], P(None, 'dp', 'mp'), may hold values from -7.4505806e-08 to 7.4505806e-08
- first_dec_attn: float32 [4, 512, 512], P(None, 'dp', 'mp'), may hold values from -7.4505806e-08 to 7.4505806e-08
- first_dec_mlp: float32 [2, 512, 2048], P(None, 'dp', 'mp'), may hold values from -7.4505806e-08 to 7.4505806e-08
- first_patch_embed: float32 [768, 1024], P(None, 'dp'), may hold values from -7.4505806e-08 to 7.4505806e-08
- first_bridge: float32 [1024, 512], P('dp'), may hold values from -7.4505806e-08 to 7.4505806e-08
- first_predict: float32 [512, 768], P('dp'), may hold values from -7.4505806e-08 to 7.4505806e-08
- first_vectors: float32 [11520], P('dp'), may hold values from -2.3841858e-07 to 2.3841858e-07
- second_enc_attn: float32 [4, 1024, 1024], P(None, 'dp', 'mp'), may hold values from 2.2930394e-18 to 9.1721575e-18
- second_enc_mlp: float32 [2, 1024, 4096], P(None, 'dp', 'mp'), may hold values from 2.2930394e-18 to 9.1721575e-18
- second_dec_attn: float32 [4, 512, 512], P(None, 'dp', 'mp'), may hold values from 2.2930394e-18 to 9.1721575e-18
- second_dec_mlp: float32 [2, 512, 2048], P(None, 'dp', 'mp'), may hold values from 2.2930394e-18 to 9.1721575e-18
- second_patch_embed: float32 [768, 1024], P(None, 'dp'), may hold values from 2.2930394e-18 to 9.1721575e-18
- second_bridge: float32 [1024, 512], P('dp'), may hold values from 2.2930394e-18 to 9.1721575e-18
- second_predict: float32 [512, 768], P('dp'), may hold values from 2.2930394e-18 to 9.1721575e-18
- second_vectors: float32 [11520], P('dp'), may hold values from 2.2930395e-17 to 9.172158e-17
- ema_enc_attn: float32 [4, 1024, 1024], P(None, 'dp', 'mp'), may hold values from -0.1875 to 0.1875
- ema_enc_mlp: float32 [2, 1024, 4096], P(None, 'dp', 'mp'), may hold values from -0.1875 to 0.1875
- ema_patch_embed: float32 [768, 1024], P(None, 'dp'), may hold values from -0.21875 to 0.21875
Outputs:
- loss: float32 [], replicated
- band_weight: float32 [3], replicated
- grad_norm: float32 [], replicated
- next_enc_attn: float32 [4, 1024, 1024], P(None, 'dp', 'mp')
- next_enc_mlp: float32 [2, 1024, 4096], P(None, 'dp', 'mp')
- next_dec_attn: float32 [4, 512, 512], P(None, 'dp', 'mp')
- next_dec_mlp: float32 [2, 512, 2048], P(None, 'dp', 'mp')
- next_patch_embed: float32 [768, 1024], P(None, 'dp')
- next_bridge: float32 [1024, 512], P('dp')
- next_predict: float32 [512, 768], P('dp')
- next_vectors: float32 [11520], P('dp')
- next_first_enc_attn: float32 [4, 1024, 1024], P(None, 'dp', 'mp')
- next_first_enc_mlp: float32 [2, 1024, 4096], P(None, 'dp', 'mp')
- next_first_dec_attn: float32 [4, 512, 512], P(None, 'dp', 'mp')
- next_first_dec_mlp: float32 [2, 512, 2048], P(None, 'dp', 'mp')
- next_first_patch_embed: float32 [768, 1024], P(None, 'dp')
- next_first_bridge: float32 [1024, 512], P('dp')
- next_first_predict: float32 [512, 768], P('dp')
- next_first_vectors: float32 [11520], P('dp')
- next_second_enc_attn: float32 [4, 1024, 1024], P(None, 'dp', 'mp')
- next_second_enc_mlp: float32 [2, 1024, 4096], P(None, 'dp', 'mp')
- next_second_dec_attn: float32 [4, 512, 512], P(None, 'dp', 'mp')
- next_second_dec_mlp: float32 [2, 512, 2048], P(None, 'dp', 'mp')
- next_second_patch_embed: float32 [768, 1024], P(None, 'dp')
- next_second_bridge: float32 [1024, 512], P('dp')
- next_second_predict: float32 [512, 768], P('dp')
- next_second_vectors: float32 [11520], P('dp')
- next_ema_enc_attn: float32 [4, 1024, 1024], P(None, 'dp', 'mp')
- next_ema_enc_mlp: float32 [2, 1024, 4096], P(None, 'dp', 'mp')
- next_ema_patch_embed: float32 [768, 1024], P(None, 'dp')
The draws below stay inside these ranges and needn't reach their ends.
Inputs may be any that keep to these rules, and one draw needn't show every extreme that they name: `kept_index`: each row names 64 different patches of its image. `band_ids`: the first 3 pixels of every patch are of bands 0, 1, 2 in that order.
All inputs are finite; a program needn't handle non-finite values. No bound on the sum of `intersection` on one device may be relied on, other than what follows from the above.
Results may differ from the reference program's by a relative error of at most 0.0082.
Values may be sent and summed in bfloat16 or wider, within the bound.
A program may use at most 256 MiB of HBM per device.

```python
import math
import jax
import jax.numpy as jnp
from jax import lax

D = 1024
HEADS = 16
FF = 4096
E = 512
DHEADS = 16
FF2 = 2048
P_SIZE = 768
GRID = 16
NB = 3
STEP = 10
IMG_DEV = 8
PATCHES = 256
KEEP = 64
IMAGES = 128
NVEC = 11520
NPARAM = 17444096
N_DP = 16


def draw_band_ids(key, part):
    key = jax.random.fold_in(key, 11)
    first_key, second_key = jax.random.split(key)
    row_count = IMAGES * PATCHES
    drawn = jax.random.randint(first_key, (row_count, P_SIZE), 0, 4 * IMAGES)
    image_of = (jnp.arange(row_count, dtype=jnp.int32) // PATCHES)[:, None]
    alternate = jax.random.randint(second_key, (row_count, P_SIZE), 0, 2)
    chosen = jnp.where(drawn < IMAGES + 2 * image_of, 2, alternate)
    column = jnp.arange(P_SIZE, dtype=jnp.int32)[None, :]
    return jnp.where(column < NB, column, chosen).astype(jnp.int32)


def first_patches(one_key):
    return jax.random.permutation(one_key, PATCHES)[:KEEP]


def draw_kept_index(key, part):
    key = jax.random.fold_in(key, 12)
    image_keys = jax.random.split(key, IMAGES)
    return jax.vmap(first_patches)(image_keys).astype(jnp.int32)


def rising(one_key, length, bottom):
    ramp = bottom + jnp.arange(length).astype(jnp.float32) / (length - 1)
    return ramp * jax.random.uniform(one_key, (length,), jnp.float32, 0.85, 1.15)


def draw_vectors(key, part):
    key = jax.random.fold_in(key, 13)
    keys = jax.random.split(key, 15)
    bottom = 0.5
    pieces = [0.3 * jax.random.normal(keys[0], (D,), jnp.float32)]
    for pair_index in range(3):
        pieces.append(rising(keys[1 + 2 * pair_index], D, bottom))
        pieces.append(0.2 * jax.random.normal(keys[2 + 2 * pair_index], (D,), jnp.float32))
    pieces.append(jax.random.normal(keys[7], (E,), jnp.float32))
    for pair_index in range(3):
        pieces.append(rising(keys[8 + 2 * pair_index], E, bottom))
        pieces.append(0.2 * jax.random.normal(keys[9 + 2 * pair_index], (E,), jnp.float32))
    pieces.append(0.3 * jax.random.normal(keys[14], (P_SIZE,), jnp.float32))
    return jnp.concatenate(pieces)


def attention_stack(one_key, feature_width, key_count):
    base = jax.random.normal(one_key, (4, feature_width, feature_width), jnp.float32) * feature_width ** (-0.5)
    boost = jnp.where(jnp.arange(4)[:, None, None] == 3, 0.5 * key_count ** 0.5, 1.0)
    return base * boost


def draw_enc_attn(key, part):
    key = jax.random.fold_in(key, 14)
    return attention_stack(key, D, KEEP)


def draw_dec_attn(key, part):
    key = jax.random.fold_in(key, 15)
    return attention_stack(key, E, PATCHES)


def set_ends(values, rng, low, top_value):
    longest = values.shape.index(max(values.shape))
    spots = []
    for shift in (0, 1):
        where = [jax.random.randint(jax.random.fold_in(rng, axis), (), 0, length) for axis, length in enumerate(values.shape)]
        where[longest] = (where[longest] + shift) % values.shape[longest]
        spots.append(tuple(where))
    return values.at[spots[0]].set(low).at[spots[1]].set(top_value)


def level_of(stream_key, dims, cuts, low, largest):
    def one(dim, parts):
        steps = jax.random.uniform(jax.random.fold_in(jax.random.fold_in(stream_key, 6), dim), (parts,), jnp.float32, low / len(cuts), largest / len(cuts))
        return jnp.repeat(jnp.exp(steps), dims[dim] // parts).reshape((-1,) + (1,) * (len(dims) - dim - 1))

    loudness = one(*cuts[0])
    for cut in cuts[1:]:
        loudness = loudness * one(*cut)
    return loudness


def noise(key, shape, deviation, most, shards=(), kind=jnp.bfloat16):
    result = jax.random.normal(key, shape, jnp.float32) * deviation
    if len(shards) > 0:
        result = level_of(key, shape, shards, -0.22, 0.18) * result
    return jnp.clip(result, min=-most, max=most).astype(kind)


def setup_inputs(seed: int = 0) -> dict:
    key_of = jax.random.split(jax.random.key(seed), 34)
    pixels = noise(key_of[0], (IMAGES * PATCHES, P_SIZE), 1.0, 6.0, ((0, 16),))
    target = noise(key_of[1], (IMAGES * PATCHES, P_SIZE), 1.0, 6.0, ((0, 16),))
    band_ids = draw_band_ids(jax.random.fold_in(key_of[33], 71), 0)
    kept_index = draw_kept_index(jax.random.fold_in(key_of[33], 71), 0)
    intersection = set_ends((jax.random.randint(key_of[4], (IMAGES, PATCHES), 0, 4) < 1).astype(jnp.int32), jax.random.fold_in(key_of[4], 1), 0, 1)
    gsd_scale = set_ends(jax.random.randint(key_of[5], (IMAGES,), 1, 9), jax.random.fold_in(key_of[5], 1), 1, 8).astype(jnp.int32)
    enc_attn = draw_enc_attn(jax.random.fold_in(key_of[33], 71), 0)
    enc_mlp = noise(key_of[7], (2, D, FF), D ** -0.5, 0.1875, ((1, 16), (2, 2)), jnp.float32)
    dec_attn = draw_dec_attn(jax.random.fold_in(key_of[33], 71), 0)
    dec_mlp = noise(key_of[9], (2, E, FF2), E ** -0.5, 0.25, ((1, 16), (2, 2)), jnp.float32)
    patch_embed = noise(key_of[10], (P_SIZE, D), P_SIZE ** -0.5, 0.21875, ((1, 16),), jnp.float32)
    bridge = noise(key_of[11], (D, E), D ** -0.5, 0.1875, ((0, 16),), jnp.float32)
    predict = noise(key_of[12], (E, P_SIZE), E ** -0.5, 0.25, ((0, 16),), jnp.float32)
    vectors = draw_vectors(jax.random.fold_in(key_of[33], 71), 0)
    first_enc_attn = noise(key_of[14], (4, D, D), (0.0000222 / NPARAM ** 0.5), 7.450580596923828e-08, ((1, 16), (2, 2)), jnp.float32)
    first_enc_mlp = noise(key_of[15], (2, D, FF), (0.0000222 / NPARAM ** 0.5), 7.450580596923828e-08, ((1, 16), (2, 2)), jnp.float32)
    first_dec_attn = noise(key_of[16], (4, E, E), (0.0000222 / NPARAM ** 0.5), 7.450580596923828e-08, ((1, 16), (2, 2)), jnp.float32)
    first_dec_mlp = noise(key_of[17], (2, E, FF2), (0.0000222 / NPARAM ** 0.5), 7.450580596923828e-08, ((1, 16), (2, 2)), jnp.float32)
    first_patch_embed = noise(key_of[18], (P_SIZE, D), (0.0000222 / NPARAM ** 0.5), 7.450580596923828e-08, ((1, 16),), jnp.float32)
    first_bridge = noise(key_of[19], (D, E), (0.0000222 / NPARAM ** 0.5), 7.450580596923828e-08, ((0, 16),), jnp.float32)
    first_predict = noise(key_of[20], (E, P_SIZE), (0.0000222 / NPARAM ** 0.5), 7.450580596923828e-08, ((0, 16),), jnp.float32)
    first_vectors = noise(key_of[21], (NVEC,), (0.0000666 / NPARAM ** 0.5), 2.384185791015625e-07, ((0, 16),), jnp.float32)
    second_enc_attn = jnp.clip(jnp.exp(math.log(9.17215748070852e-18) - 1.3862944 * jax.random.uniform(key_of[22], (4, D, D), jnp.float32) ** level_of(key_of[22], (4, D, D), ((1, 16), (2, 2)), -0.2, 0.2)), 2.29303937017713e-18, 9.17215748070852e-18)
    second_enc_mlp = jnp.clip(jnp.exp(math.log(9.17215748070852e-18) - 1.3862944 * jax.random.uniform(key_of[23], (2, D, FF), jnp.float32) ** level_of(key_of[23], (2, D, FF), ((1, 16), (2, 2)), -0.2, 0.2)), 2.29303937017713e-18, 9.17215748070852e-18)
    second_dec_attn = jnp.clip(jnp.exp(math.log(9.17215748070852e-18) - 1.3862944 * jax.random.uniform(key_of[24], (4, E, E), jnp.float32) ** level_of(key_of[24], (4, E, E), ((1, 16), (2, 2)), -0.2, 0.2)), 2.29303937017713e-18, 9.17215748070852e-18)
    second_dec_mlp = jnp.clip(jnp.exp(math.log(9.17215748070852e-18) - 1.3862944 * jax.random.uniform(key_of[25], (2, E, FF2), jnp.float32) ** level_of(key_of[25], (2, E, FF2), ((1, 16), (2, 2)), -0.2, 0.2)), 2.29303937017713e-18, 9.17215748070852e-18)
    second_patch_embed = jnp.clip(jnp.exp(math.log(9.17215748070852e-18) - 1.3862944 * jax.random.uniform(key_of[26], (P_SIZE, D), jnp.float32) ** level_of(key_of[26], (P_SIZE, D), ((1, 16),), -0.2, 0.2)), 2.29303937017713e-18, 9.17215748070852e-18)
    second_bridge = jnp.clip(jnp.exp(math.log(9.17215748070852e-18) - 1.3862944 * jax.random.uniform(key_of[27], (D, E), jnp.float32) ** level_of(key_of[27], (D, E), ((0, 16),), -0.2, 0.2)), 2.29303937017713e-18, 9.17215748070852e-18)
    second_predict = jnp.clip(jnp.exp(math.log(9.17215748070852e-18) - 1.3862944 * jax.random.uniform(key_of[28], (E, P_SIZE), jnp.float32) ** level_of(key_of[28], (E, P_SIZE), ((0, 16),), -0.2, 0.2)), 2.29303937017713e-18, 9.17215748070852e-18)
    second_vectors = jnp.clip(jnp.exp(math.log(9.172157811580765e-17) - 1.3862944 * jax.random.uniform(key_of[29], (NVEC,), jnp.float32) ** level_of(key_of[29], (NVEC,), ((0, 16),), -0.2, 0.2)), 2.2930394528951913e-17, 9.172157811580765e-17)
    ema_enc_attn = noise(key_of[30], (4, D, D), D ** -0.5, 0.1875, ((1, 16), (2, 2)), jnp.float32)
    ema_enc_mlp = noise(key_of[31], (2, D, FF), D ** -0.5, 0.1875, ((1, 16), (2, 2)), jnp.float32)
    ema_patch_embed = noise(key_of[32], (P_SIZE, D), P_SIZE ** -0.5, 0.21875, ((1, 16),), jnp.float32)
    return {"pixels": pixels, "target": target, "band_ids": band_ids, "kept_index": kept_index, "intersection": intersection, "gsd_scale": gsd_scale, "enc_attn": enc_attn, "enc_mlp": enc_mlp, "dec_attn": dec_attn, "dec_mlp": dec_mlp, "patch_embed": patch_embed, "bridge": bridge, "predict": predict, "vectors": vectors, "first_enc_attn": first_enc_attn, "first_enc_mlp": first_enc_mlp, "first_dec_attn": first_dec_attn, "first_dec_mlp": first_dec_mlp, "first_patch_embed": first_patch_embed, "first_bridge": first_bridge, "first_predict": first_predict, "first_vectors": first_vectors, "second_enc_attn": second_enc_attn, "second_enc_mlp": second_enc_mlp, "second_dec_attn": second_dec_attn, "second_dec_mlp": second_dec_mlp, "second_patch_embed": second_patch_embed, "second_bridge": second_bridge, "second_predict": second_predict, "second_vectors": second_vectors, "ema_enc_attn": ema_enc_attn, "ema_enc_mlp": ema_enc_mlp, "ema_patch_embed": ema_patch_embed}


@jax.custom_vjp
def low(v):
    return lax.optimization_barrier(v.astype(jnp.bfloat16)).astype(jnp.float32)

@jax.custom_vjp
def low_back(v):
    return v

def low_keep(v):
    return (low(v), None)

def low_pass(kept, grad):
    return (grad,)

def back_keep(v):
    return (v, None)

def back_low(kept, grad):
    return (low(grad),)
low.defvjp(low_keep, low_pass)
low_back.defvjp(back_keep, back_low)
HIGH = lax.Precision.HIGHEST
EPS_LN = 1e-06
EPS_C = 0.01
CLIP = 0.0002
BETA_ONE = 0.9
BETA_TWO = 0.999
ADAM_EPS = 1e-12
RATE_MAT = 0.06
RATE_VEC = 0.5
DECAY_MAT = 0.05
EMA_KEEP = 0.9
REF_GSD = 4.0

def round_both(value):
    return low(low_back(value))

def matmul(left, right):
    return jnp.dot(left, right, precision=HIGH, preferred_element_type=jnp.float32)

def layer_norm(token_rows, gain_vec, bias_vec):
    centred = token_rows - lax.optimization_barrier(jnp.mean(token_rows, axis=-1, keepdims=True))
    spread = lax.optimization_barrier(jnp.mean(centred * centred, axis=-1, keepdims=True))
    return centred * lax.rsqrt(spread + EPS_LN) * gain_vec + bias_vec

def position_table(gsd_values, feature_width, grid_side):
    positions = jnp.arange(grid_side * grid_side, dtype=jnp.int32)
    row_pos = (positions // grid_side).astype(jnp.float32)
    col_pos = (positions % grid_side).astype(jnp.float32)
    quarter = feature_width // 4
    frequency = jnp.exp(-jnp.log(10000.0) * jnp.arange(quarter).astype(jnp.float32) / quarter)
    gsd_ratio = gsd_values.astype(jnp.float32)[:, None, None] / REF_GSD
    row_arg = row_pos[None, :, None] * gsd_ratio * frequency
    col_arg = col_pos[None, :, None] * gsd_ratio * frequency
    return jnp.concatenate([jnp.sin(row_arg), jnp.cos(row_arg), jnp.sin(col_arg), jnp.cos(col_arg)], axis=-1)

def split_vectors(flat_vec, enc_width, dec_width):
    lengths = [enc_width] * 7 + [dec_width] * 7
    pieces = []
    offset = 0
    for length in lengths:
        pieces.append(flat_vec[offset:offset + length])
        offset = offset + length
    pieces.append(flat_vec[offset:])
    return pieces

def attention(normed, stack, head_count, sequences):
    row_count, feature_width = normed.shape
    head_dim = feature_width // head_count
    queries = round_both(matmul(normed, stack[0])).reshape(sequences, -1, head_count, head_dim)
    key_rows = round_both(matmul(normed, stack[1])).reshape(sequences, -1, head_count, head_dim)
    values = round_both(matmul(normed, stack[2])).reshape(sequences, -1, head_count, head_dim)
    scores = low_back(jnp.einsum('bqhd,bkhd->bhqk', queries, key_rows, precision=HIGH) * head_dim ** (-0.5))
    row_top = lax.optimization_barrier(jnp.max(scores, axis=-1, keepdims=True))
    exponent = jnp.exp(scores - row_top)
    weights_soft = low(exponent / lax.optimization_barrier(jnp.sum(exponent, axis=-1, keepdims=True)))
    mixed = jnp.einsum('bhqk,bkhd->bqhd', weights_soft, values, precision=HIGH)
    mixed = round_both(mixed.reshape(row_count, feature_width))
    return low_back(matmul(mixed, stack[3].T))

def feed_forward(normed, stack):
    hidden = low(jax.nn.gelu(low_back(matmul(normed, stack[0]))))
    return low_back(matmul(hidden, stack[1].T))

def layer_block(token_rows, attn_stack, mlp_stack, norms, head_count, sequences):
    gain_a, bias_a, gain_b, bias_b = norms
    after_attn = token_rows + attention(low(layer_norm(token_rows, gain_a, bias_a)), attn_stack, head_count, sequences)
    return after_attn + feed_forward(low(layer_norm(after_attn, gain_b, bias_b)), mlp_stack)

def group_loss(weights, batch_data):
    enc_attn, enc_mlp, dec_attn, dec_mlp, patch_embed, bridge, predict, vectors = weights
    pixels, target, kept_index, gsd_scale, pixel_weight = batch_data
    images, keep_count = kept_index.shape
    pieces = split_vectors(vectors, D, E)
    image_rows = jnp.arange(images, dtype=jnp.int32)[:, None]
    flat_index = (kept_index + PATCHES * image_rows).reshape(-1)
    kept_pixels = pixels[flat_index]
    enc_pos = jnp.take_along_axis(position_table(gsd_scale, D, GRID), kept_index[:, :, None], axis=1).reshape(-1, D)
    token_rows = low_back(matmul(kept_pixels, patch_embed)) + pieces[0] + enc_pos
    token_rows = layer_block(token_rows, enc_attn, enc_mlp, pieces[1:5], HEADS, images)
    latent = low_back(matmul(low(layer_norm(token_rows, pieces[5], pieces[6])), bridge))
    canvas = jnp.broadcast_to(pieces[7], (images, PATCHES, E))
    canvas = canvas.at[image_rows, kept_index].set(latent.reshape(images, keep_count, E))
    dec_rows = (canvas + position_table(gsd_scale, E, GRID)).reshape(-1, E)
    dec_rows = layer_block(dec_rows, dec_attn, dec_mlp, pieces[8:12], DHEADS, images)
    predicted = low_back(matmul(low(layer_norm(dec_rows, pieces[12], pieces[13])), predict)) + pieces[14]
    mismatch = predicted - target
    return jnp.sum(pixel_weight * jnp.sqrt(mismatch * mismatch + EPS_C))

def adam_update(master, gradient, first_old, second_old, step_rate, decay_rate):
    first_new = BETA_ONE * first_old + (1.0 - BETA_ONE) * gradient
    second_new = BETA_TWO * second_old + (1.0 - BETA_TWO) * gradient * gradient
    first_hat = first_new / (1.0 - BETA_ONE ** STEP)
    second_hat = second_new / (1.0 - BETA_TWO ** STEP)
    updated = master - step_rate * (first_hat / (jnp.sqrt(second_hat) + ADAM_EPS) + decay_rate * master)
    return (updated, first_new, second_new)

def reference(pixels, target, band_ids, kept_index, intersection, gsd_scale, enc_attn, enc_mlp, dec_attn, dec_mlp, patch_embed, bridge, predict, vectors, first_enc_attn, first_enc_mlp, first_dec_attn, first_dec_mlp, first_patch_embed, first_bridge, first_predict, first_vectors, second_enc_attn, second_enc_mlp, second_dec_attn, second_dec_mlp, second_patch_embed, second_bridge, second_predict, second_vectors, ema_enc_attn, ema_enc_mlp, ema_patch_embed):
    masters = (enc_attn, enc_mlp, dec_attn, dec_mlp, patch_embed, bridge, predict, vectors)
    firsts = (first_enc_attn, first_enc_mlp, first_dec_attn, first_dec_mlp, first_patch_embed, first_bridge, first_predict, first_vectors)
    seconds = (second_enc_attn, second_enc_mlp, second_dec_attn, second_dec_mlp, second_patch_embed, second_bridge, second_predict, second_vectors)
    patch_index = jnp.arange(PATCHES, dtype=jnp.int32)
    kept_flags = jnp.any(kept_index[:, :, None] == patch_index[None, None, :], axis=1).astype(jnp.float32)
    patch_weight = ((1.0 - kept_flags) * (1.0 - 0.5 * intersection.astype(jnp.float32))).reshape(-1, 1)
    band_weight = jnp.stack([jnp.sum(patch_weight * (band_ids == band_level).astype(jnp.float32)) for band_level in range(NB)])
    inverse = 1.0 / band_weight
    pixel_weight = patch_weight * inverse[band_ids]
    batches = (pixels.astype(jnp.float32).reshape(N_DP, -1, P_SIZE), target.astype(jnp.float32).reshape(N_DP, -1, P_SIZE), kept_index.reshape(N_DP, IMG_DEV, KEEP), gsd_scale.reshape(N_DP, IMG_DEV), pixel_weight.reshape(N_DP, -1, P_SIZE))
    checked = jax.checkpoint(group_loss)

    def loss_of(weights):
        lowered = tuple((low(master) for master in weights))

        def add_group(running, batch_data):
            return (running + checked(lowered, batch_data), None)
        total_loss, _ = lax.scan(add_group, jnp.zeros((), jnp.float32), batches)
        return total_loss
    loss, pullback = jax.vjp(loss_of, masters)
    gradients = pullback(jnp.ones((), jnp.float32))[0]
    squares = jnp.zeros((), jnp.float32)
    for gradient in gradients:
        squares = squares + jnp.sum(gradient * gradient)
    grad_norm = jnp.sqrt(squares)
    factor = CLIP / jnp.maximum(grad_norm, CLIP)
    news, new_firsts, new_seconds = ([], [], [])
    for position, master in enumerate(masters):
        is_vec = position == 7
        updated, first_new, second_new = adam_update(master, gradients[position] * factor, firsts[position], seconds[position], RATE_VEC if is_vec else RATE_MAT, 0.0 if is_vec else DECAY_MAT)
        news.append(updated)
        new_firsts.append(first_new)
        new_seconds.append(second_new)
    ema_attn = EMA_KEEP * ema_enc_attn + (1.0 - EMA_KEEP) * news[0]
    ema_mlp = EMA_KEEP * ema_enc_mlp + (1.0 - EMA_KEEP) * news[1]
    ema_embed = EMA_KEEP * ema_patch_embed + (1.0 - EMA_KEEP) * news[4]
    return (loss, band_weight, grad_norm, news[0], news[1], news[2], news[3], news[4], news[5], news[6], news[7], new_firsts[0], new_firsts[1], new_firsts[2], new_firsts[3], new_firsts[4], new_firsts[5], new_firsts[6], new_firsts[7], new_seconds[0], new_seconds[1], new_seconds[2], new_seconds[3], new_seconds[4], new_seconds[5], new_seconds[6], new_seconds[7], ema_attn, ema_mlp, ema_embed)
```

```python
import jax
import jax.numpy as jnp
from jax import lax
from jax.sharding import PartitionSpec as P

D = 1024
DH = 64
E = 512
DDH = 32
GRID = 16
NB = 3
STEP = 10


EPS_LN = 1e-06
EPS_C = 0.01
CLIP = 0.0002
BETA_ONE = 0.9
BETA_TWO = 0.999
ADAM_EPS = 1e-12
RATE_MAT = 0.06
RATE_VEC = 0.5
DECAY_MAT = 0.05
EMA_KEEP = 0.9
REF_GSD = 4.0


def layer_norm(token_rows, gain_vec, bias_vec):
    centred = token_rows - jnp.mean(token_rows, axis=-1, keepdims=True)
    spread = jnp.mean(centred * centred, axis=-1, keepdims=True)
    return centred * lax.rsqrt(spread + EPS_LN) * gain_vec + bias_vec


def position_table(gsd_values, feature_width, grid_side):
    positions = jnp.arange(grid_side * grid_side, dtype=jnp.int32)
    row_pos = (positions // grid_side).astype(jnp.float32)
    col_pos = (positions % grid_side).astype(jnp.float32)
    quarter = feature_width // 4
    frequency = jnp.exp(-jnp.log(10000.0) * jnp.arange(quarter).astype(jnp.float32) / quarter)
    gsd_ratio = gsd_values.astype(jnp.float32)[:, None, None] / REF_GSD
    row_arg = row_pos[None, :, None] * gsd_ratio * frequency
    col_arg = col_pos[None, :, None] * gsd_ratio * frequency
    return jnp.concatenate(
        [jnp.sin(row_arg), jnp.cos(row_arg), jnp.sin(col_arg), jnp.cos(col_arg)], axis=-1
    )


def split_vectors(flat_vec, enc_width, dec_width):
    lengths = [enc_width] * 7 + [dec_width] * 7
    pieces = []
    offset = 0
    for length in lengths:
        pieces.append(flat_vec[offset : offset + length])
        offset = offset + length
    pieces.append(flat_vec[offset:])
    return pieces


def plain_dot(left, right):
    return jnp.dot(left, right, preferred_element_type=jnp.float32)


def contract_rows(left, right):
    return lax.dot_general(
        left, right, (((0,), (0,)), ((), ())), preferred_element_type=jnp.float32
    )


def contract_cols(left, right):
    return lax.dot_general(
        left, right, (((1,), (1,)), ((), ())), preferred_element_type=jnp.float32
    )


def mp_total(partial_rows):
    low = partial_rows.astype(jnp.bfloat16)
    other = lax.ppermute(low, "mp", [(0, 1), (1, 0)])
    return low.astype(jnp.float32) + other.astype(jnp.float32)


mp_back = mp_total


def dp_bits():
    return lax.axis_size("dp").bit_length() - 1


def orders():
    bits = dp_bits()
    high = list(range(bits - 1, 1, -1))
    return (high + [0, 1], high + [1, 0])


def swap(block, bit):
    size = lax.axis_size("dp")
    return lax.ppermute(block, "dp", [(i, i ^ (1 << bit)) for i in range(size)])


def my_bit(bit):
    return (lax.axis_index("dp") >> bit) & 1


def gather_dp(block, axis, order):
    lead, rest = (block.shape[:axis], block.shape[axis:])
    done = []
    cur = block
    for bit in order:
        other = swap(cur, bit)
        mine = my_bit(bit) == 1
        place = axis + sum(1 for b in done if b > bit)
        cur = jnp.stack([jnp.where(mine, other, cur), jnp.where(mine, cur, other)], axis=place)
        done.append(bit)
    return cur.reshape(lead + (rest[0] * lax.axis_size("dp"),) + rest[1:])


def reduce_dp(block, axis, order, wire):
    bits = dp_bits()
    lead, rest = (block.shape[:axis], block.shape[axis:])
    shard = rest[0] // lax.axis_size("dp")
    cur = block.reshape(lead + (2,) * bits + (shard,) + rest[1:])
    left = list(range(bits - 1, -1, -1))
    for bit in reversed(order):
        place = axis + left.index(bit)
        mine = my_bit(bit)
        keep = lax.dynamic_index_in_dim(cur, mine, place, keepdims=False)
        give = lax.dynamic_index_in_dim(cur, 1 - mine, place, keepdims=False)
        other = swap(give.astype(wire), bit)
        cur = keep + other.astype(jnp.float32)
        left.remove(bit)
    return cur


def total_dp(value):
    for bit in range(dp_bits()):
        value = value + swap(value, bit)
    return value


def block_forward(token_rows, attn_stack, mlp_stack, norms, sequences, head_dim):
    gain_a, bias_a, gain_b, bias_b = norms
    row_count = token_rows.shape[0]
    local_width = attn_stack.shape[2]
    heads_here = local_width // head_dim
    normed_a = layer_norm(token_rows, gain_a, bias_a).astype(jnp.bfloat16)
    queries = (
        plain_dot(normed_a, attn_stack[0])
        .astype(jnp.bfloat16)
        .reshape(sequences, -1, heads_here, head_dim)
    )
    key_rows = (
        plain_dot(normed_a, attn_stack[1])
        .astype(jnp.bfloat16)
        .reshape(sequences, -1, heads_here, head_dim)
    )
    values = (
        plain_dot(normed_a, attn_stack[2])
        .astype(jnp.bfloat16)
        .reshape(sequences, -1, heads_here, head_dim)
    )
    scores = jnp.einsum(
        "bqhd,bkhd->bhqk", queries, key_rows, preferred_element_type=jnp.float32
    ) * head_dim ** (-0.5)
    row_top = jnp.max(scores, axis=-1, keepdims=True)
    log_total = row_top + jnp.log(jnp.sum(jnp.exp(scores - row_top), axis=-1, keepdims=True))
    weights_soft = jnp.exp(scores - log_total).astype(jnp.bfloat16)
    mixed = jnp.einsum("bhqk,bkhd->bqhd", weights_soft, values, preferred_element_type=jnp.float32)
    mixed = mixed.astype(jnp.bfloat16).reshape(row_count, local_width)
    after_attn = token_rows + mp_total(contract_cols(mixed, attn_stack[3]))
    normed_b = layer_norm(after_attn, gain_b, bias_b).astype(jnp.bfloat16)
    upward = plain_dot(normed_b, mlp_stack[0])
    hidden = jax.nn.gelu(upward).astype(jnp.bfloat16)
    result = after_attn + mp_total(contract_cols(hidden, mlp_stack[1]))
    saved = (
        token_rows,
        normed_a,
        queries,
        key_rows,
        values,
        log_total,
        mixed,
        after_attn,
        normed_b,
        upward,
        hidden,
    )
    return (result, saved)


def block_backward(grad_out, saved, attn_stack, mlp_stack, norms, sequences, head_dim):
    (
        token_rows,
        normed_a,
        queries,
        key_rows,
        values,
        log_total,
        mixed,
        after_attn,
        normed_b,
        upward,
        hidden,
    ) = saved
    gain_a, bias_a, gain_b, bias_b = norms
    row_count, local_width = mixed.shape
    heads_here = local_width // head_dim
    score_scale = head_dim ** (-0.5)
    grad_low = grad_out.astype(jnp.bfloat16)
    grad_down = contract_rows(grad_low, hidden)
    grad_hidden = plain_dot(grad_low, mlp_stack[1])
    _, gelu_back = jax.vjp(jax.nn.gelu, upward)
    grad_upward = gelu_back(grad_hidden)[0].astype(jnp.bfloat16)
    grad_up = contract_rows(normed_b, grad_upward)
    grad_normed_b = mp_back(contract_cols(grad_upward, mlp_stack[0]))
    _, norm_back_b = jax.vjp(layer_norm, after_attn, gain_b, bias_b)
    grad_after, grad_gain_b, grad_bias_b = norm_back_b(grad_normed_b)
    grad_after = grad_after + grad_out
    grad_attn_low = grad_after.astype(jnp.bfloat16)
    grad_out_proj = contract_rows(grad_attn_low, mixed)
    grad_mixed = plain_dot(grad_attn_low, attn_stack[3]).astype(jnp.bfloat16)
    grad_mixed = grad_mixed.reshape(sequences, -1, heads_here, head_dim)
    scores = (
        jnp.einsum("bqhd,bkhd->bhqk", queries, key_rows, preferred_element_type=jnp.float32)
        * score_scale
    )
    weights_soft = jnp.exp(scores - log_total)
    grad_values = (
        jnp.einsum(
            "bhqk,bqhd->bkhd",
            weights_soft.astype(jnp.bfloat16),
            grad_mixed,
            preferred_element_type=jnp.float32,
        )
        .astype(jnp.bfloat16)
        .reshape(row_count, local_width)
    )
    grad_soft = jnp.einsum(
        "bqhd,bkhd->bhqk", grad_mixed, values, preferred_element_type=jnp.float32
    )
    grad_scores = weights_soft * (
        grad_soft - jnp.sum(weights_soft * grad_soft, axis=-1, keepdims=True)
    )
    grad_scores = grad_scores.astype(jnp.bfloat16)
    grad_queries = (
        (
            jnp.einsum("bhqk,bkhd->bqhd", grad_scores, key_rows, preferred_element_type=jnp.float32)
            * score_scale
        )
        .astype(jnp.bfloat16)
        .reshape(row_count, local_width)
    )
    grad_keys = (
        (
            jnp.einsum("bhqk,bqhd->bkhd", grad_scores, queries, preferred_element_type=jnp.float32)
            * score_scale
        )
        .astype(jnp.bfloat16)
        .reshape(row_count, local_width)
    )
    grad_attn = jnp.stack(
        [
            contract_rows(normed_a, grad_queries),
            contract_rows(normed_a, grad_keys),
            contract_rows(normed_a, grad_values),
            grad_out_proj,
        ]
    )
    grad_normed_a = mp_back(
        contract_cols(grad_queries, attn_stack[0])
        + contract_cols(grad_keys, attn_stack[1])
        + contract_cols(grad_values, attn_stack[2])
    )
    _, norm_back_a = jax.vjp(layer_norm, token_rows, gain_a, bias_a)
    grad_rows, grad_gain_a, grad_bias_a = norm_back_a(grad_normed_a)
    return (
        grad_rows + grad_after,
        grad_attn,
        [grad_up, grad_down],
        [grad_gain_a, grad_bias_a, grad_gain_b, grad_bias_b],
    )


def adam_update(master, gradient, first_old, second_old, step_rate, decay_rate):
    first_new = BETA_ONE * first_old + (1.0 - BETA_ONE) * gradient
    second_new = BETA_TWO * second_old + (1.0 - BETA_TWO) * gradient * gradient
    first_hat = first_new / (1.0 - BETA_ONE**STEP)
    second_hat = second_new / (1.0 - BETA_TWO**STEP)
    updated = master - step_rate * (
        first_hat / (jnp.sqrt(second_hat) + ADAM_EPS) + decay_rate * master
    )
    return (updated, first_new, second_new)


def per_device(
    pixels,
    target,
    band_ids,
    kept_index,
    intersection,
    gsd_scale,
    enc_attn,
    enc_mlp,
    dec_attn,
    dec_mlp,
    patch_embed,
    bridge,
    predict,
    vectors,
    first_enc_attn,
    first_enc_mlp,
    first_dec_attn,
    first_dec_mlp,
    first_patch_embed,
    first_bridge,
    first_predict,
    first_vectors,
    second_enc_attn,
    second_enc_mlp,
    second_dec_attn,
    second_dec_mlp,
    second_patch_embed,
    second_bridge,
    second_predict,
    second_vectors,
    ema_enc_attn,
    ema_enc_mlp,
    ema_patch_embed,
):
    masters = (enc_attn, enc_mlp, dec_attn, dec_mlp, patch_embed, bridge, predict, vectors)
    firsts = (
        first_enc_attn,
        first_enc_mlp,
        first_dec_attn,
        first_dec_mlp,
        first_patch_embed,
        first_bridge,
        first_predict,
        first_vectors,
    )
    seconds = (
        second_enc_attn,
        second_enc_mlp,
        second_dec_attn,
        second_dec_mlp,
        second_patch_embed,
        second_bridge,
        second_predict,
        second_vectors,
    )
    order_a, order_b = orders()
    low = jnp.bfloat16
    embed_w = gather_dp(patch_embed.astype(low).T, 0, order_a).T
    vector_low = gather_dp(vectors.astype(low).reshape(1, -1), 0, order_b).reshape(-1)
    enc_attn_w = jnp.concatenate([
        gather_dp(enc_attn[:2].astype(low), 1, order_a),
        gather_dp(enc_attn[2:].astype(low), 1, order_b)])
    enc_mlp_w = [
        gather_dp(enc_mlp[0].astype(low), 0, order_a),
        gather_dp(enc_mlp[1].astype(low), 0, order_b)]
    bridge_w = gather_dp(bridge.astype(low), 0, order_a)
    dec_attn_w = jnp.concatenate([
        gather_dp(dec_attn[:2].astype(low), 1, order_a),
        gather_dp(dec_attn[2:].astype(low), 1, order_b)])
    dec_mlp_w = [
        gather_dp(dec_mlp[0].astype(low), 0, order_a),
        gather_dp(dec_mlp[1].astype(low), 0, order_b)]
    predict_w = gather_dp(predict.astype(low), 0, order_b)
    pieces = split_vectors(vector_low.astype(jnp.float32), D, E)
    images, keep_count = kept_index.shape
    patch_count = intersection.shape[1]
    patch_index = jnp.arange(patch_count, dtype=jnp.int32)
    kept_flags = jnp.any(kept_index[:, :, None] == patch_index[None, None, :], axis=1).astype(
        jnp.float32
    )
    patch_weight = ((1.0 - kept_flags) * (1.0 - 0.5 * intersection.astype(jnp.float32))).reshape(
        -1, 1
    )
    local_counts = jnp.stack(
        [
            jnp.sum(patch_weight * (band_ids == band_level).astype(jnp.float32))
            for band_level in range(NB)
        ]
    )
    band_weight = total_dp(local_counts)
    inverse = 1.0 / band_weight
    band_scale = jnp.zeros(band_ids.shape, jnp.float32)
    for band_level in range(NB):
        band_scale = band_scale + jnp.where(band_ids == band_level, inverse[band_level], 0.0)
    pixel_weight = patch_weight * band_scale
    image_rows = jnp.arange(images, dtype=jnp.int32)[:, None]
    flat_index = (kept_index + patch_count * image_rows).reshape(-1)
    kept_pixels = pixels[flat_index]
    enc_pos = jnp.take_along_axis(
        position_table(gsd_scale, D, GRID), kept_index[:, :, None], axis=1
    ).reshape(-1, D)
    token_rows = plain_dot(kept_pixels, embed_w) + pieces[0] + enc_pos
    enc_out, enc_saved = block_forward(token_rows, enc_attn_w, enc_mlp_w, pieces[1:5], images, DH)
    final_enc = layer_norm(enc_out, pieces[5], pieces[6]).astype(jnp.bfloat16)
    latent = plain_dot(final_enc, bridge_w)
    canvas = jnp.broadcast_to(pieces[7], (images, patch_count, E))
    place = jnp.argmax(kept_index[:, :, None] == patch_index[None, None, :], axis=1)
    spread_rows = jnp.take_along_axis(
        latent.reshape(images, keep_count, E), place[:, :, None], axis=1)
    canvas = jnp.where(kept_flags[:, :, None] > 0.5, spread_rows, canvas)
    dec_rows = (canvas + position_table(gsd_scale, E, GRID)).reshape(-1, E)
    dec_out, dec_saved = block_forward(dec_rows, dec_attn_w, dec_mlp_w, pieces[8:12], images, DDH)
    final_dec = layer_norm(dec_out, pieces[12], pieces[13]).astype(jnp.bfloat16)
    predicted = plain_dot(final_dec, predict_w) + pieces[14]
    mismatch = predicted - target.astype(jnp.float32)
    smooth = jnp.sqrt(mismatch * mismatch + EPS_C)
    loss_local = jnp.sum(pixel_weight * smooth)
    loss = total_dp(loss_local)
    grad_pred = pixel_weight * mismatch / smooth
    grad_pred_low = grad_pred.astype(jnp.bfloat16)
    grad_pbias = jnp.sum(grad_pred, axis=0)
    grad_predict = contract_rows(final_dec, grad_pred_low)
    grad_final_dec = contract_cols(grad_pred_low, predict_w)
    _, dec_norm_back = jax.vjp(layer_norm, dec_out, pieces[12], pieces[13])
    grad_dec_out, grad_dec_fg, grad_dec_fb = dec_norm_back(grad_final_dec)
    grad_dec_rows, grad_dec_attn, grad_dec_mlp, dec_norm_grads = block_backward(
        grad_dec_out, dec_saved, dec_attn_w, dec_mlp_w, pieces[8:12], images, DDH
    )
    grad_canvas = grad_dec_rows.reshape(images, patch_count, E)
    grad_mask = jnp.sum(grad_canvas * (1.0 - kept_flags)[:, :, None], axis=(0, 1))
    grad_latent = grad_canvas[image_rows, kept_index].reshape(-1, E).astype(jnp.bfloat16)
    grad_bridge = contract_rows(final_enc, grad_latent)
    grad_final_enc = contract_cols(grad_latent, bridge_w)
    _, enc_norm_back = jax.vjp(layer_norm, enc_out, pieces[5], pieces[6])
    grad_enc_out, grad_enc_fg, grad_enc_fb = enc_norm_back(grad_final_enc)
    grad_tokens, grad_enc_attn, grad_enc_mlp, enc_norm_grads = block_backward(
        grad_enc_out, enc_saved, enc_attn_w, enc_mlp_w, pieces[1:5], images, DH
    )
    grad_ebias = jnp.sum(grad_tokens, axis=0)
    grad_embed = contract_rows(kept_pixels, grad_tokens.astype(jnp.bfloat16))
    grad_vectors = jnp.concatenate(
        [grad_ebias]
        + enc_norm_grads
        + [grad_enc_fg, grad_enc_fb, grad_mask]
        + dec_norm_grads
        + [grad_dec_fg, grad_dec_fb, grad_pbias]
    )
    reduced = (
        jnp.concatenate([
            reduce_dp(grad_enc_attn[:2], 1, order_a, low),
            reduce_dp(grad_enc_attn[2:], 1, order_b, low)]),
        jnp.stack([
            reduce_dp(grad_enc_mlp[0], 0, order_a, low),
            reduce_dp(grad_enc_mlp[1], 0, order_b, low)]),
        jnp.concatenate([
            reduce_dp(grad_dec_attn[:2], 1, order_a, low),
            reduce_dp(grad_dec_attn[2:], 1, order_b, low)]),
        jnp.stack([
            reduce_dp(grad_dec_mlp[0], 0, order_a, low),
            reduce_dp(grad_dec_mlp[1], 0, order_b, low)]),
        reduce_dp(grad_embed.T, 0, order_a, low).T,
        reduce_dp(grad_bridge, 0, order_a, low),
        reduce_dp(grad_predict, 0, order_b, low),
        reduce_dp(grad_vectors, 0, order_b, jnp.float32),
    )
    shares = (1.0, 1.0, 1.0, 1.0, 0.5, 0.5, 0.5, 0.5)
    squares = jnp.zeros((), jnp.float32)
    for position, gradient in enumerate(reduced):
        squares = squares + shares[position] * jnp.sum(gradient * gradient)
    total_squares = total_dp(squares)
    total_squares = total_squares + lax.ppermute(total_squares, "mp", [(0, 1), (1, 0)])
    grad_norm = jnp.sqrt(total_squares)
    factor = CLIP / jnp.maximum(grad_norm, CLIP)
    news, new_firsts, new_seconds = ([], [], [])
    for position, master in enumerate(masters):
        is_vec = position == 7
        updated, first_new, second_new = adam_update(
            master,
            reduced[position] * factor,
            firsts[position],
            seconds[position],
            RATE_VEC if is_vec else RATE_MAT,
            0.0 if is_vec else DECAY_MAT,
        )
        news.append(updated)
        new_firsts.append(first_new)
        new_seconds.append(second_new)
    ema_attn = EMA_KEEP * ema_enc_attn + (1.0 - EMA_KEEP) * news[0]
    ema_mlp = EMA_KEEP * ema_enc_mlp + (1.0 - EMA_KEEP) * news[1]
    ema_embed = EMA_KEEP * ema_patch_embed + (1.0 - EMA_KEEP) * news[4]
    return (
        loss,
        band_weight,
        grad_norm,
        news[0],
        news[1],
        news[2],
        news[3],
        news[4],
        news[5],
        news[6],
        news[7],
        new_firsts[0],
        new_firsts[1],
        new_firsts[2],
        new_firsts[3],
        new_firsts[4],
        new_firsts[5],
        new_firsts[6],
        new_firsts[7],
        new_seconds[0],
        new_seconds[1],
        new_seconds[2],
        new_seconds[3],
        new_seconds[4],
        new_seconds[5],
        new_seconds[6],
        new_seconds[7],
        ema_attn,
        ema_mlp,
        ema_embed,
    )


def solution(mesh):
    return jax.shard_map(
        per_device,
        mesh=mesh,
        in_specs=(
            P("dp", None),
            P("dp", None),
            P("dp", None),
            P("dp", None),
            P("dp", None),
            P("dp"),
            P(None, "dp", "mp"),
            P(None, "dp", "mp"),
            P(None, "dp", "mp"),
            P(None, "dp", "mp"),
            P(None, "dp"),
            P("dp", None),
            P("dp", None),
            P("dp"),
            P(None, "dp", "mp"),
            P(None, "dp", "mp"),
            P(None, "dp", "mp"),
            P(None, "dp", "mp"),
            P(None, "dp"),
            P("dp", None),
            P("dp", None),
            P("dp"),
            P(None, "dp", "mp"),
            P(None, "dp", "mp"),
            P(None, "dp", "mp"),
            P(None, "dp", "mp"),
            P(None, "dp"),
            P("dp", None),
            P("dp", None),
            P("dp"),
            P(None, "dp", "mp"),
            P(None, "dp", "mp"),
            P(None, "dp"),
        ),
        out_specs=(
            P(),
            P(),
            P(),
            P(None, "dp", "mp"),
            P(None, "dp", "mp"),
            P(None, "dp", "mp"),
            P(None, "dp", "mp"),
            P(None, "dp"),
            P("dp", None),
            P("dp", None),
            P("dp"),
            P(None, "dp", "mp"),
            P(None, "dp", "mp"),
            P(None, "dp", "mp"),
            P(None, "dp", "mp"),
            P(None, "dp"),
            P("dp", None),
            P("dp", None),
            P("dp"),
            P(None, "dp", "mp"),
            P(None, "dp", "mp"),
            P(None, "dp", "mp"),
            P(None, "dp", "mp"),
            P(None, "dp"),
            P("dp", None),
            P("dp", None),
            P("dp"),
            P(None, "dp", "mp"),
            P(None, "dp", "mp"),
            P(None, "dp"),
        ),
        check_vma=False,
    )
```

```python
import functools
import math

import jax
import jax.numpy as jnp
from jax import lax
from jax.experimental import pallas as pl
from jax.experimental.pallas import tpu as pltpu
from jax.sharding import PartitionSpec as P

D = 1024
DH = 64
E = 512
DDH = 32
GRID = 16
NB = 3
STEP = 10


EPS_LN = 1e-06
EPS_C = 0.01
CLIP = 0.0002
BETA_ONE = 0.9
BETA_TWO = 0.999
ADAM_EPS = 1e-12
RATE_MAT = 0.06
RATE_VEC = 0.5
DECAY_MAT = 0.05
EMA_KEEP = 0.9
REF_GSD = 4.0


def split_vectors(flat_vec, enc_width, dec_width):
    lengths = [enc_width] * 7 + [dec_width] * 7
    pieces = []
    offset = 0
    for length in lengths:
        pieces.append(flat_vec[offset : offset + length])
        offset = offset + length
    pieces.append(flat_vec[offset:])
    return pieces


F32 = jnp.float32
BF16 = jnp.bfloat16
VMEM_LIMIT = 58 * 2**20
GELU_C = math.sqrt(2.0 / math.pi)


def dot_nn(left, right):
    return jnp.dot(left, right, preferred_element_type=F32)


def dot_nt(left, right):
    return lax.dot_general(left, right, (((1,), (1,)), ((), ())), preferred_element_type=F32)


def dot_tn(left, right):
    return lax.dot_general(left, right, (((0,), (0,)), ((), ())), preferred_element_type=F32)


def dot_exact(left, right):
    return jnp.dot(left, right, preferred_element_type=F32, precision=lax.Precision.HIGHEST)


def normalize(rows):
    centred = rows - jnp.mean(rows, axis=-1, keepdims=True)
    rstd = lax.rsqrt(jnp.mean(centred * centred, axis=-1, keepdims=True) + EPS_LN)
    return centred * rstd, rstd


def norm_back(grad, gain, unit, rstd):
    scaled = grad * gain
    mean_one = jnp.mean(scaled, axis=-1, keepdims=True)
    mean_two = jnp.mean(scaled * unit, axis=-1, keepdims=True)
    grad_in = rstd * (scaled - mean_one - unit * mean_two)
    return (
        grad_in,
        jnp.sum(grad * unit, axis=0, keepdims=True),
        jnp.sum(grad, axis=0, keepdims=True),
    )


def both(mine_ref, other_ref, rows):
    return mine_ref[rows, :].astype(F32) + other_ref[rows, :].astype(F32)


def gelu_parts(up):
    square = up * up
    bent = jnp.tanh(GELU_C * up * (1.0 + 0.044715 * square))
    half = 0.5 * (1.0 + bent)
    return square, bent, half


def group_mask(group, length):
    if group == length:
        return None
    row_image = lax.broadcasted_iota(jnp.int32, (group, group), 0) // length
    col_image = lax.broadcasted_iota(jnp.int32, (group, group), 1) // length
    return row_image == col_image


def attend(qkv_ref, mixed_ref, lse_ref, cols, width, head_dim, mask):
    scale = head_dim ** (-0.5)
    for head in range(width // head_dim):
        at = pl.ds(head * head_dim, head_dim)
        queries = qkv_ref[at, cols]
        keys = qkv_ref[pl.ds(width + head * head_dim, head_dim), cols]
        values = qkv_ref[pl.ds(2 * width + head * head_dim, head_dim), cols]
        scores = dot_tn(keys, queries) * scale
        if mask is not None:
            scores = jnp.where(mask, scores, -1e30)
        top = jnp.max(scores, axis=0, keepdims=True)
        weights = jnp.exp(scores - top)
        total = jnp.sum(weights, axis=0, keepdims=True)
        lse_ref[pl.ds(head, 1), cols] = top + jnp.log(total)
        soft = (weights * (1.0 / total)).astype(BF16)
        mixed_ref[at, cols] = dot_nn(values, soft).astype(BF16)


def attend_back(qkv_ref, grad_ref, lse_ref, out_ref, cols, width, head_dim, mask):
    scale = head_dim ** (-0.5)
    for head in range(width // head_dim):
        at = pl.ds(head * head_dim, head_dim)
        at_k = pl.ds(width + head * head_dim, head_dim)
        at_v = pl.ds(2 * width + head * head_dim, head_dim)
        queries, keys, values = qkv_ref[at, cols], qkv_ref[at_k, cols], qkv_ref[at_v, cols]
        grad = grad_ref[at, :]
        scores = dot_tn(keys, queries) * scale
        if mask is not None:
            scores = jnp.where(mask, scores, -1e30)
        soft = jnp.exp(scores - lse_ref[pl.ds(head, 1), cols])
        out_ref[at_v, cols] = dot_nt(grad, soft.astype(BF16)).astype(BF16)
        grad_soft = dot_tn(values, grad)
        inner = jnp.sum(soft * grad_soft, axis=0, keepdims=True)
        grad_scores = (soft * (grad_soft - inner)).astype(BF16)
        out_ref[at, cols] = (dot_nn(keys, grad_scores) * scale).astype(BF16)
        out_ref[at_k, cols] = (dot_nt(queries, grad_scores) * scale).astype(BF16)


def transposed_weights(attn_ref, flat_ref):
    width = attn_ref.shape[2]
    for part in range(4):
        flat_ref[pl.ds(part * width, width), :] = attn_ref[part].T


def attention_rows(unit, vec_ref, flat_ref, qkv_ref, mixed_ref, lse_ref, part_ref, rows, head_dim, mask, attn_ref):
    width = mixed_ref.shape[0]
    low = (unit * vec_ref[1:2, :] + vec_ref[2:3, :]).astype(BF16)
    qkv_ref[:, rows] = dot_nt(flat_ref[: 3 * width, :], low).astype(BF16)
    attend(qkv_ref, mixed_ref, lse_ref, rows, width, head_dim, mask)
    part_ref[rows, :] = dot_nt(mixed_ref[:, rows].T, attn_ref[3]).astype(BF16)


def enc_in_kernel(length, group, head_dim, pix_ref, kept_ref, table_ref, embed_ref, vec_ref, attn_ref,
                  x_ref, qkv_ref, mixed_ref, lse_ref, part_ref, pixk_ref, flat_ref):
    images, patches = table_ref.shape[0], pix_ref.shape[0] // table_ref.shape[0]
    side = table_ref.shape[1]
    transposed_weights(attn_ref, flat_ref)

    def pick(image, carry):
        rows = pl.ds(image * length, length)
        index = kept_ref[rows, :]
        hot = lax.broadcasted_iota(jnp.int32, (length, patches), 1) == index
        pixels = pix_ref[pl.ds(image * patches, patches), :]
        pixk_ref[rows, :] = dot_nn(hot.astype(BF16), pixels).astype(BF16)
        grid_at = lax.broadcasted_iota(jnp.int32, (length, side), 1)
        table = table_ref[image]
        half = table.shape[1]
        x_ref[rows, :half] = dot_exact((grid_at == index // side).astype(F32), table)
        x_ref[rows, half:] = dot_exact((grid_at == index % side).astype(F32), table)
        return carry

    lax.fori_loop(0, images, pick, 0)
    mask = group_mask(group, length)

    def step(number, carry):
        rows = pl.ds(pl.multiple_of(number * group, group), group)
        rows_x = dot_nt(pixk_ref[rows, :], embed_ref[...]) + vec_ref[0:1, :] + x_ref[rows, :]
        x_ref[rows, :] = rows_x
        unit, _ = normalize(rows_x)
        attention_rows(unit, vec_ref, flat_ref, qkv_ref, mixed_ref, lse_ref, part_ref, rows, head_dim, mask, attn_ref)
        return carry

    lax.fori_loop(0, x_ref.shape[0] // group, step, 0)


def dec_in_kernel(length, head_dim, x1_ref, mine_ref, other_ref, evec_ref, bridge_ref, kept_ref, hidden_ref,
                  table_ref, vec_ref, attn_ref,
                  x2_ref, final_ref, x_ref, qkv_ref, mixed_ref, lse_ref, part_ref, flat_ref, latent_ref):
    images, side, half = table_ref.shape
    patches = side * side
    transposed_weights(attn_ref, flat_ref)
    every = pl.ds(0, x1_ref.shape[0])
    out = x1_ref[...] + both(mine_ref, other_ref, every)
    x2_ref[...] = out
    unit, _ = normalize(out)
    final = (unit * evec_ref[5:6, :] + evec_ref[6:7, :]).astype(BF16)
    final_ref[...] = final
    latent_ref[...] = dot_nn(final, bridge_ref[...])

    def step(image, carry):
        rows = pl.ds(pl.multiple_of(image * patches, patches), patches)
        hot = lax.broadcasted_iota(jnp.int32, (patches, length), 0) == kept_ref[pl.ds(image, 1), :]
        latent = latent_ref[pl.ds(image * length, length), :]
        table = table_ref[image]
        by_row = jnp.broadcast_to(table[:, None, :], (side, side, half)).reshape(patches, half)
        by_col = jnp.broadcast_to(table[None, :, :], (side, side, half)).reshape(patches, half)
        place = jnp.concatenate([by_row, by_col], axis=1)
        rows_x = dot_exact(hot.astype(F32), latent) + hidden_ref[rows, :] * vec_ref[0:1, :] + place
        x_ref[rows, :] = rows_x
        unit, _ = normalize(rows_x)
        attention_rows(unit, vec_ref, flat_ref, qkv_ref, mixed_ref, lse_ref, part_ref, rows, head_dim, None, attn_ref)
        return carry

    lax.fori_loop(0, images, step, 0)


def mlp_kernel(tile, x_ref, mine_ref, other_ref, vec_ref, up_ref, down_ref, x1_ref, part_ref, low_ref, acc_ref):
    number = pl.program_id(0)
    count = x_ref.shape[0] // tile

    def first(step, carry):
        rows = pl.ds(pl.multiple_of(step * tile, tile), tile)
        after = x_ref[rows, :] + both(mine_ref, other_ref, rows)
        x1_ref[rows, :] = after
        unit, _ = normalize(after)
        low_ref[rows, :] = (unit * vec_ref[3:4, :] + vec_ref[4:5, :]).astype(BF16)
        return carry

    @pl.when(number == 0)
    def _():
        lax.fori_loop(0, count, first, 0)
        acc_ref[...] = jnp.zeros_like(acc_ref)

    def step(piece, carry):
        rows = pl.ds(pl.multiple_of(piece * tile, tile), tile)
        up = dot_nn(low_ref[rows, :], up_ref[...])
        _, _, half = gelu_parts(up)
        acc_ref[rows, :] += dot_nt((up * half).astype(BF16), down_ref[...])
        return carry

    lax.fori_loop(0, count, step, 0)

    @pl.when(number == pl.num_programs(0) - 1)
    def _():
        part_ref[...] = acc_ref[...].astype(BF16)


def head_kernel(core_ref, inverse_ref, x1_ref, mine_ref, other_ref, vec_ref, bias_ref, predict_ref, target_ref,
                band_ref, weight_ref, gy_ref, gpred_ref, gbias_ref, loss_ref, gain_ref, shift_ref, low_ref):
    number = pl.program_id(0)

    @pl.when(number == 0)
    def _():
        for ref in (gpred_ref, gbias_ref, loss_ref, gain_ref, shift_ref):
            ref[...] = jnp.zeros_like(ref)

    every = pl.ds(0, x1_ref.shape[0])
    unit, rstd = normalize(x1_ref[...] + both(mine_ref, other_ref, every))
    gain = vec_ref[5:6, :]
    final = (unit * gain + vec_ref[6:7, :]).astype(BF16)
    mismatch = dot_nn(final, predict_ref[...]) + bias_ref[...] - target_ref[...].astype(F32)
    band = band_ref[...]
    level = jnp.where(band == 0, inverse_ref[0], jnp.where(band == 1, inverse_ref[1], inverse_ref[2]))
    level = level * weight_ref[...]
    square = mismatch * mismatch + EPS_C
    root = lax.rsqrt(square)
    loss_ref[...] += jnp.sum(level * (square * root), axis=0, keepdims=True)
    grad = level * (mismatch * root)
    gbias_ref[...] += jnp.sum(grad, axis=0, keepdims=True)
    low_ref[...] = grad.astype(BF16)
    share = gpred_ref.shape[1]
    columns = pl.ds(pl.multiple_of(core_ref[0] * share, share), share)
    gpred_ref[...] += dot_tn(final, low_ref[:, columns])
    grad_final = dot_nt(low_ref[...], predict_ref[...])
    grad_in, gain_sum, shift_sum = norm_back(grad_final, gain, unit, rstd)
    gy_ref[...] = grad_in
    gain_ref[...] += gain_sum
    shift_ref[...] += shift_sum


def mlp_back_kernel(tile, gy_ref, x1_ref, vec_ref, up_ref, down_ref, gup_ref, gdown_ref, part_ref,
                    low_ref, lowt_ref, grad_ref, gradt_ref, gu_ref, z_ref, acc_ref):
    number = pl.program_id(0)
    count = x1_ref.shape[0] // tile

    def first(step, carry):
        rows = pl.ds(pl.multiple_of(step * tile, tile), tile)
        unit, _ = normalize(x1_ref[rows, :])
        low = (unit * vec_ref[3:4, :] + vec_ref[4:5, :]).astype(BF16)
        low_ref[rows, :] = low
        lowt_ref[:, rows] = low.T
        grad = gy_ref[rows, :].astype(BF16)
        grad_ref[rows, :] = grad
        gradt_ref[:, rows] = grad.T
        return carry

    @pl.when(number == 0)
    def _():
        lax.fori_loop(0, count, first, 0)
        acc_ref[...] = jnp.zeros_like(acc_ref)

    def step(piece, carry):
        rows = pl.ds(pl.multiple_of(piece * tile, tile), tile)
        up = dot_nn(low_ref[rows, :], up_ref[...])
        square, bent, half = gelu_parts(up)
        z_ref[rows, :] = (up * half).astype(BF16)
        slope = half + (0.5 * GELU_C) * up * (1.0 - bent * bent) * (1.0 + (3.0 * 0.044715) * square)
        grad_up = (dot_nn(grad_ref[rows, :], down_ref[...]) * slope).astype(BF16)
        gu_ref[rows, :] = grad_up
        acc_ref[rows, :] += dot_nt(grad_up, up_ref[...])
        return carry

    lax.fori_loop(0, count, step, 0)
    gup_ref[...] = dot_nn(lowt_ref[...], gu_ref[...]).astype(BF16)
    gdown_ref[...] = dot_nn(gradt_ref[...], z_ref[...]).astype(BF16)

    @pl.when(number == pl.num_programs(0) - 1)
    def _():
        part_ref[...] = acc_ref[...].astype(BF16)


def attn_back_kernel(length, group, head_dim, gy_ref, x1_ref, mine_ref, other_ref, x_ref, qkv_ref, mixed_ref, lse_ref,
                     vec_ref, attn_ref, gx_ref, gqk_ref, gvo_ref, gain_ref, shift_ref, part_ref,
                     flat_ref, lowt_ref, gradt_ref, gmix_ref, gqkv_ref):
    width = mixed_ref.shape[0]
    transposed_weights(attn_ref, flat_ref)
    gain_ref[...] = jnp.zeros_like(gain_ref)
    shift_ref[...] = jnp.zeros_like(shift_ref)
    mask = group_mask(group, length)

    def step(number, carry):
        rows = pl.ds(pl.multiple_of(number * group, group), group)
        unit, rstd = normalize(x1_ref[rows, :])
        grad_in, gain_sum, shift_sum = norm_back(both(mine_ref, other_ref, rows), vec_ref[3:4, :], unit, rstd)
        grad_in = grad_in + gy_ref[rows, :]
        gx_ref[rows, :] = grad_in
        gain_ref[...] += gain_sum
        shift_ref[...] += shift_sum
        low_grad = grad_in.astype(BF16)
        gradt_ref[:, rows] = low_grad.T
        gmix_ref[...] = dot_nt(flat_ref[3 * width :, :], low_grad).astype(BF16)
        attend_back(qkv_ref, gmix_ref, lse_ref, gqkv_ref, rows, width, head_dim, mask)
        part_ref[rows, :] = dot_nn(gqkv_ref[:, rows].T, flat_ref[: 3 * width, :]).astype(BF16)
        unit_a, _ = normalize(x_ref[rows, :])
        lowt_ref[:, rows] = (unit_a * vec_ref[1:2, :] + vec_ref[2:3, :]).astype(BF16).T
        return carry

    lax.fori_loop(0, x_ref.shape[0] // group, step, 0)
    gqk_ref[0] = dot_nt(lowt_ref[...], gqkv_ref[:width, :]).astype(BF16)
    gqk_ref[1] = dot_nt(lowt_ref[...], gqkv_ref[width : 2 * width, :]).astype(BF16)
    gvo_ref[0] = dot_nt(lowt_ref[...], gqkv_ref[2 * width :, :]).astype(BF16)
    gvo_ref[1] = dot_nt(gradt_ref[...], mixed_ref[...]).astype(BF16)


def between_kernel(length, core_ref, gx_ref, x_ref, mine_ref, other_ref, vec_ref, kept_ref, hidden_ref, final_ref, x2_ref,
                   evec_ref, bridge_ref, gain_ref, shift_ref, mask_ref, gbridge_ref, egain_ref, eshift_ref, gy_ref,
                   latent_ref):
    images = kept_ref.shape[0] // length
    patches = x_ref.shape[0] // images
    for ref in (gain_ref, shift_ref, mask_ref):
        ref[...] = jnp.zeros_like(ref)

    def step(image, carry):
        rows = pl.ds(pl.multiple_of(image * patches, patches), patches)
        unit, rstd = normalize(x_ref[rows, :])
        grad_in, gain_sum, shift_sum = norm_back(both(mine_ref, other_ref, rows), vec_ref[1:2, :], unit, rstd)
        grad_in = grad_in + gx_ref[rows, :]
        gain_ref[...] += gain_sum
        shift_ref[...] += shift_sum
        mask_ref[...] += jnp.sum(grad_in * hidden_ref[rows, :], axis=0, keepdims=True)
        kept_rows = pl.ds(pl.multiple_of(image * length, length), length)
        hot = lax.broadcasted_iota(jnp.int32, (length, patches), 1) == kept_ref[kept_rows, :]
        latent_ref[kept_rows, :] = dot_nn(hot.astype(BF16), grad_in.astype(BF16)).astype(BF16)
        return carry

    lax.fori_loop(0, images, step, 0)
    share = gbridge_ref.shape[1]
    columns = pl.ds(pl.multiple_of(core_ref[0] * share, share), share)
    gbridge_ref[...] = dot_tn(final_ref[...], latent_ref[:, columns]).astype(BF16)
    grad_final = dot_nt(latent_ref[...], bridge_ref[...])
    unit, rstd = normalize(x2_ref[...])
    gy_ref[...], egain_ref[...], eshift_ref[...] = norm_back(grad_final, evec_ref[5:6, :], unit, rstd)


def enc_out_kernel(core_ref, gx_ref, x_ref, mine_ref, other_ref, vec_ref, pixk_ref,
                   gain_ref, shift_ref, ebias_ref, gembed_ref):
    every = pl.ds(0, x_ref.shape[0])
    unit, rstd = normalize(x_ref[...])
    grad_in, gain_ref[...], shift_ref[...] = norm_back(both(mine_ref, other_ref, every), vec_ref[1:2, :], unit, rstd)
    grad_in = grad_in + gx_ref[...]
    ebias_ref[...] = jnp.sum(grad_in, axis=0, keepdims=True)
    share = gembed_ref.shape[1]
    columns = pl.ds(pl.multiple_of(core_ref[0] * share, share), share)
    gembed_ref[...] = dot_tn(grad_in.astype(BF16), pixk_ref[:, columns]).astype(BF16)


def shape(dims, dtype):
    return jax.ShapeDtypeStruct(dims, dtype)


def run(kernel, outs, scratch, args, flops, scalars=0):
    moved = sum(math.prod(a.shape) * a.dtype.itemsize for a in list(args) + list(outs))
    in_vmem = pl.BlockSpec(memory_space=pltpu.VMEM)
    return pl.pallas_call(
        kernel,
        out_shape=tuple(outs),
        in_specs=[pl.BlockSpec(memory_space=pltpu.SMEM)] * scalars + [in_vmem] * (len(args) - scalars),
        out_specs=tuple([in_vmem] * len(outs)),
        scratch_shapes=scratch,
        compiler_params=pltpu.CompilerParams(vmem_limit_bytes=VMEM_LIMIT),
        cost_estimate=pl.CostEstimate(flops=flops, bytes_accessed=moved, transcendentals=0),
    )(*args)


def other_core(block):
    return lax.ppermute(block, "mp", [(0, 1), (1, 0)])


def mlp_forward(x, mine, vec, up, down):
    rows, width = x.shape
    hidden = up.shape[1]
    block = min(hidden, 512)
    tile = min(rows, 512)
    other = other_core(mine)
    whole = pl.BlockSpec((rows, width), lambda i: (0, 0))
    cols = pl.BlockSpec((width, block), lambda i: (0, i))
    return pl.pallas_call(
        functools.partial(mlp_kernel, tile),
        out_shape=(shape((rows, width), F32), shape((rows, width), BF16)),
        grid=(hidden // block,),
        in_specs=[whole] * 3 + [pl.BlockSpec((8, width), lambda i: (0, 0)), cols, cols],
        out_specs=(whole, whole),
        scratch_shapes=[pltpu.VMEM((rows, width), BF16), pltpu.VMEM((rows, width), F32)],
        compiler_params=pltpu.CompilerParams(vmem_limit_bytes=VMEM_LIMIT),
        cost_estimate=pl.CostEstimate(flops=4 * rows * width * hidden, bytes_accessed=rows * width * 14 + width * hidden * 4,
                                      transcendentals=rows * hidden),
    )(x, mine, other, vec, up, down)


def mlp_backward(gy, x1, vec, up, down):
    rows, width = x1.shape
    hidden = up.shape[1]
    block = min(hidden, 512)
    tile = min(rows, 256)
    whole = pl.BlockSpec((rows, width), lambda i: (0, 0))
    cols = pl.BlockSpec((width, block), lambda i: (0, i))
    return pl.pallas_call(
        functools.partial(mlp_back_kernel, tile),
        out_shape=(shape((width, hidden), BF16), shape((width, hidden), BF16), shape((rows, width), BF16)),
        grid=(hidden // block,),
        in_specs=[whole] * 2 + [pl.BlockSpec((8, width), lambda i: (0, 0)), cols, cols],
        out_specs=(cols, cols, whole),
        scratch_shapes=[
            pltpu.VMEM((rows, width), BF16), pltpu.VMEM((width, rows), BF16),
            pltpu.VMEM((rows, width), BF16), pltpu.VMEM((width, rows), BF16),
            pltpu.VMEM((rows, block), BF16), pltpu.VMEM((rows, block), BF16),
            pltpu.VMEM((rows, width), F32)],
        compiler_params=pltpu.CompilerParams(vmem_limit_bytes=VMEM_LIMIT),
        cost_estimate=pl.CostEstimate(flops=10 * rows * width * hidden, bytes_accessed=rows * width * 10 + width * hidden * 8,
                                      transcendentals=rows * hidden),
    )(gy, x1, vec, up, down)


def head(core, inverse, x1, mine, vec, bias, predict, target, band, weight, patches):
    rows, width = x1.shape
    pixels = target.shape[1]
    share = pixels // 2
    other = other_core(mine)
    smem = pl.BlockSpec(memory_space=pltpu.SMEM)
    row_w = pl.BlockSpec((patches, width), lambda i: (i, 0))
    row_p = pl.BlockSpec((patches, pixels), lambda i: (i, 0))
    fix = lambda a, b: pl.BlockSpec((a, b), lambda i: (0, 0))
    return pl.pallas_call(
        head_kernel,
        out_shape=(shape((rows, width), F32), shape((width, share), F32), shape((1, pixels), F32),
                   shape((1, pixels), F32), shape((1, width), F32), shape((1, width), F32)),
        grid=(rows // patches,),
        in_specs=[smem, smem, row_w, row_w, row_w, fix(8, width), fix(1, pixels), fix(width, pixels), row_p, row_p,
                  pl.BlockSpec((patches, 1), lambda i: (i, 0))],
        out_specs=(row_w, fix(width, share), fix(1, pixels), fix(1, pixels), fix(1, width), fix(1, width)),
        scratch_shapes=[pltpu.VMEM((patches, pixels), BF16)],
        compiler_params=pltpu.CompilerParams(vmem_limit_bytes=VMEM_LIMIT),
        cost_estimate=pl.CostEstimate(flops=5 * rows * width * pixels, bytes_accessed=rows * (width * 12 + pixels * 6),
                                      transcendentals=rows * pixels),
    )(core, inverse, x1, mine, other, vec, bias, predict, target, band, weight)


def attn_backward(gy, x1, mine, x, saved, vec, attn, length, group, head_dim):
    qkv, mixed, lse = saved
    rows, width = x.shape
    local = mixed.shape[0]
    return run(
        functools.partial(attn_back_kernel, length, group, head_dim),
        [shape((rows, width), F32), shape((2, width, local), BF16), shape((2, width, local), BF16),
         shape((1, width), F32), shape((1, width), F32), shape((rows, width), BF16)],
        [pltpu.VMEM((4 * local, width), BF16), pltpu.VMEM((width, rows), BF16), pltpu.VMEM((width, rows), BF16),
         pltpu.VMEM((local, group), BF16), pltpu.VMEM((3 * local, rows), BF16)],
        (gy, x1, mine, other_core(mine), x, qkv, mixed, lse, vec, attn),
        18 * rows * width * local)


def sine_table(gsd_values, feature_width, grid_side):
    quarter = feature_width // 4
    frequency = jnp.exp(-jnp.log(10000.0) * jnp.arange(quarter).astype(F32) / quarter)
    gsd_ratio = gsd_values.astype(F32)[:, None, None] / REF_GSD
    line = jnp.arange(grid_side, dtype=jnp.int32).astype(F32)
    arg = line[None, :, None] * gsd_ratio * frequency
    return jnp.concatenate([jnp.sin(arg), jnp.cos(arg)], axis=-1)


def dp_bits():
    return lax.axis_size("dp").bit_length() - 1


def orders():
    bits = dp_bits()
    high = list(range(bits - 1, 1, -1))
    return (high + [0, 1], high + [1, 0])


def swap(block, bit):
    size = lax.axis_size("dp")
    return lax.ppermute(block, "dp", [(i, i ^ (1 << bit)) for i in range(size)])


def my_bit(bit):
    return (lax.axis_index("dp") >> bit) & 1


def gather_dp(block, axis, order):
    lead, rest = (block.shape[:axis], block.shape[axis:])
    done = []
    cur = block
    for bit in order:
        other = swap(cur, bit)
        mine = my_bit(bit) == 1
        place = axis + sum(1 for b in done if b > bit)
        cur = jnp.stack([jnp.where(mine, other, cur), jnp.where(mine, cur, other)], axis=place)
        done.append(bit)
    return cur.reshape(lead + (rest[0] * lax.axis_size("dp"),) + rest[1:])


def reduce_dp(block, axis, order, wire):
    bits = dp_bits()
    lead, rest = (block.shape[:axis], block.shape[axis:])
    shard = rest[0] // lax.axis_size("dp")
    cur = block.reshape(lead + (2,) * bits + (shard,) + rest[1:])
    left = list(range(bits - 1, -1, -1))
    for bit in reversed(order):
        place = axis + left.index(bit)
        mine = my_bit(bit)
        keep = lax.dynamic_index_in_dim(cur, mine, place, keepdims=False)
        give = lax.dynamic_index_in_dim(cur, 1 - mine, place, keepdims=False)
        other = swap(give.astype(wire), bit)
        cur = keep.astype(F32) + other.astype(F32)
        left.remove(bit)
    return cur


def join_cores(mine, core):
    other = other_core(mine)
    return jnp.concatenate([jnp.where(core == 0, mine, other), jnp.where(core == 0, other, mine)], axis=1)


def total_dp(value):
    for bit in range(dp_bits()):
        value = value + swap(value, bit)
    return value


def adam_update(master, gradient, first_old, second_old, step_rate, decay_rate):
    first_new = BETA_ONE * first_old + (1.0 - BETA_ONE) * gradient
    second_new = BETA_TWO * second_old + (1.0 - BETA_TWO) * gradient * gradient
    first_hat = first_new / (1.0 - BETA_ONE**STEP)
    second_hat = second_new / (1.0 - BETA_TWO**STEP)
    updated = master - step_rate * (
        first_hat / (jnp.sqrt(second_hat) + ADAM_EPS) + decay_rate * master
    )
    return (updated, first_new, second_new)


def per_device(
    pixels,
    target,
    band_ids,
    kept_index,
    intersection,
    gsd_scale,
    enc_attn,
    enc_mlp,
    dec_attn,
    dec_mlp,
    patch_embed,
    bridge,
    predict,
    vectors,
    first_enc_attn,
    first_enc_mlp,
    first_dec_attn,
    first_dec_mlp,
    first_patch_embed,
    first_bridge,
    first_predict,
    first_vectors,
    second_enc_attn,
    second_enc_mlp,
    second_dec_attn,
    second_dec_mlp,
    second_patch_embed,
    second_bridge,
    second_predict,
    second_vectors,
    ema_enc_attn,
    ema_enc_mlp,
    ema_patch_embed,
):
    masters = (enc_attn, enc_mlp, dec_attn, dec_mlp, patch_embed, bridge, predict, vectors)
    firsts = (
        first_enc_attn,
        first_enc_mlp,
        first_dec_attn,
        first_dec_mlp,
        first_patch_embed,
        first_bridge,
        first_predict,
        first_vectors,
    )
    seconds = (
        second_enc_attn,
        second_enc_mlp,
        second_dec_attn,
        second_dec_mlp,
        second_patch_embed,
        second_bridge,
        second_predict,
        second_vectors,
    )
    order_a, order_b = orders()
    low = jnp.bfloat16
    embed_w = gather_dp(patch_embed.astype(low).T, 0, order_a)
    vector_low = gather_dp(vectors.astype(low).reshape(1, -1), 0, order_b).reshape(-1)
    enc_attn_w = jnp.concatenate([
        gather_dp(enc_attn[:2].astype(low), 1, order_a),
        gather_dp(enc_attn[2:].astype(low), 1, order_b)])
    enc_mlp_w = [
        gather_dp(enc_mlp[0].astype(low), 0, order_a),
        gather_dp(enc_mlp[1].astype(low), 0, order_b)]
    bridge_w = gather_dp(bridge.astype(low), 0, order_a)
    dec_attn_w = jnp.concatenate([
        gather_dp(dec_attn[:2].astype(low), 1, order_a),
        gather_dp(dec_attn[2:].astype(low), 1, order_b)])
    dec_mlp_w = [
        gather_dp(dec_mlp[0].astype(low), 0, order_a),
        gather_dp(dec_mlp[1].astype(low), 0, order_b)]
    predict_w = gather_dp(predict.astype(low), 0, order_b)
    pieces = split_vectors(vector_low.astype(jnp.float32), D, E)
    images, keep_count = kept_index.shape
    patch_count = intersection.shape[1]
    patch_index = jnp.arange(patch_count, dtype=jnp.int32)
    kept_flags = jnp.any(kept_index[:, :, None] == patch_index[None, None, :], axis=1).astype(
        jnp.float32
    )
    patch_weight = ((1.0 - kept_flags) * (1.0 - 0.5 * intersection.astype(jnp.float32))).reshape(
        -1, 1
    )
    local_counts = jnp.stack(
        [
            jnp.sum(patch_weight * (band_ids == band_level).astype(jnp.float32))
            for band_level in range(NB)
        ]
    )
    band_weight = total_dp(local_counts)
    inverse = 1.0 / band_weight
    core = lax.axis_index("mp").astype(jnp.int32).reshape(1)
    hidden_rows = (1.0 - kept_flags).reshape(-1, 1)
    kept_column = kept_index.reshape(-1, 1)
    rows, rows_d = images * keep_count, images * patch_count
    local, local_d = enc_attn_w.shape[2], dec_attn_w.shape[2]
    pixel_count = pixels.shape[1]
    evec = jnp.stack(pieces[:7] + [jnp.zeros_like(pieces[0])])
    dvec = jnp.stack(pieces[7:14] + [jnp.zeros_like(pieces[7])])
    group = 2 * keep_count
    x0, *enc_saved, part, kept_pixels = run(
        functools.partial(enc_in_kernel, keep_count, group, DH),
        [shape((rows, D), F32), shape((3 * local, rows), BF16), shape((local, rows), BF16),
         shape((local // DH, rows), F32), shape((rows, D), BF16), shape((rows, pixel_count), BF16)],
        [pltpu.VMEM((4 * local, D), BF16)],
        (pixels, kept_column, sine_table(gsd_scale, D, GRID), embed_w, evec, enc_attn_w),
        rows * D * (2 * pixel_count + 8 * local))
    x1, part = mlp_forward(x0, part, evec, *enc_mlp_w)
    x2, final_enc, xd, *dec_saved, part = run(
        functools.partial(dec_in_kernel, keep_count, DDH),
        [shape((rows, D), F32), shape((rows, D), BF16), shape((rows_d, E), F32), shape((3 * local_d, rows_d), BF16),
         shape((local_d, rows_d), BF16), shape((local_d // DDH, rows_d), F32), shape((rows_d, E), BF16)],
        [pltpu.VMEM((4 * local_d, E), BF16), pltpu.VMEM((rows, E), F32)],
        (x1, part, other_core(part), evec, bridge_w, kept_index, hidden_rows, sine_table(gsd_scale, E, GRID), dvec,
         dec_attn_w),
        rows_d * E * 8 * local_d + 2 * rows * D * E)
    xd1, part = mlp_forward(xd, part, dvec, *dec_mlp_w)
    gyd, grad_predict, grad_pbias, loss_parts, grad_dec_fg, grad_dec_fb = head(
        core, inverse, xd1, part, dvec, pieces[14].reshape(1, -1), predict_w, target, band_ids, patch_weight, patch_count)
    loss = total_dp(jnp.sum(loss_parts))
    grad_dec_up, grad_dec_down, part = mlp_backward(gyd, xd1, dvec, *dec_mlp_w)
    gxd, grad_dec_qk, grad_dec_vo, grad_dec_gb, grad_dec_bb, part = attn_backward(
        gyd, xd1, part, xd, dec_saved, dvec, dec_attn_w, patch_count, patch_count, DDH)
    one_d, one_e = shape((1, D), F32), shape((1, E), F32)
    grad_dec_ga, grad_dec_ba, grad_mask, grad_bridge, grad_enc_fg, grad_enc_fb, gye = run(
        functools.partial(between_kernel, keep_count),
        [one_e, one_e, one_e, shape((D, E // 2), BF16), one_d, one_d, shape((rows, D), F32)],
        [pltpu.VMEM((rows, E), BF16)],
        (core, gxd, xd, part, other_core(part), dvec, kept_column, hidden_rows, final_enc, x2, evec, bridge_w),
        3 * rows * D * E, 1)
    grad_enc_up, grad_enc_down, part = mlp_backward(gye, x1, evec, *enc_mlp_w)
    gxe, grad_enc_qk, grad_enc_vo, grad_enc_gb, grad_enc_bb, part = attn_backward(
        gye, x1, part, x0, enc_saved, evec, enc_attn_w, keep_count, group, DH)
    grad_enc_ga, grad_enc_ba, grad_ebias, grad_embed = run(
        enc_out_kernel,
        [one_d, one_d, one_d, shape((D, pixel_count // 2), BF16)],
        [], (core, gxe, x0, part, other_core(part), evec, kept_pixels), rows * D * pixel_count, 1)
    grad_vectors = jnp.concatenate(
        [grad_ebias, grad_enc_ga, grad_enc_ba, grad_enc_gb, grad_enc_bb, grad_enc_fg, grad_enc_fb, grad_mask,
         grad_dec_ga, grad_dec_ba, grad_dec_gb, grad_dec_bb, grad_dec_fg, grad_dec_fb, grad_pbias], axis=1).reshape(-1)
    reduced = (
        jnp.concatenate([
            reduce_dp(grad_enc_qk, 1, order_a, low),
            reduce_dp(grad_enc_vo, 1, order_b, low)]),
        jnp.stack([
            reduce_dp(grad_enc_up, 0, order_a, low),
            reduce_dp(grad_enc_down, 0, order_b, low)]),
        jnp.concatenate([
            reduce_dp(grad_dec_qk, 1, order_a, low),
            reduce_dp(grad_dec_vo, 1, order_b, low)]),
        jnp.stack([
            reduce_dp(grad_dec_up, 0, order_a, low),
            reduce_dp(grad_dec_down, 0, order_b, low)]),
        join_cores(reduce_dp(grad_embed, 0, order_a, low), core).T,
        join_cores(reduce_dp(grad_bridge, 0, order_a, low), core),
        join_cores(reduce_dp(grad_predict, 0, order_b, low), core),
        reduce_dp(grad_vectors, 0, order_b, F32),
    )
    shares = (1.0, 1.0, 1.0, 1.0, 0.5, 0.5, 0.5, 0.5)
    squares = jnp.zeros((), jnp.float32)
    for position, gradient in enumerate(reduced):
        squares = squares + shares[position] * jnp.sum(gradient * gradient)
    total_squares = total_dp(squares)
    total_squares = total_squares + lax.ppermute(total_squares, "mp", [(0, 1), (1, 0)])
    grad_norm = jnp.sqrt(total_squares)
    factor = CLIP / jnp.maximum(grad_norm, CLIP)
    news, new_firsts, new_seconds = ([], [], [])
    for position, master in enumerate(masters):
        is_vec = position == 7
        updated, first_new, second_new = adam_update(
            master,
            reduced[position] * factor,
            firsts[position],
            seconds[position],
            RATE_VEC if is_vec else RATE_MAT,
            0.0 if is_vec else DECAY_MAT,
        )
        news.append(updated)
        new_firsts.append(first_new)
        new_seconds.append(second_new)
    ema_attn = EMA_KEEP * ema_enc_attn + (1.0 - EMA_KEEP) * news[0]
    ema_mlp = EMA_KEEP * ema_enc_mlp + (1.0 - EMA_KEEP) * news[1]
    ema_embed = EMA_KEEP * ema_patch_embed + (1.0 - EMA_KEEP) * news[4]
    return (
        loss,
        band_weight,
        grad_norm,
        news[0],
        news[1],
        news[2],
        news[3],
        news[4],
        news[5],
        news[6],
        news[7],
        new_firsts[0],
        new_firsts[1],
        new_firsts[2],
        new_firsts[3],
        new_firsts[4],
        new_firsts[5],
        new_firsts[6],
        new_firsts[7],
        new_seconds[0],
        new_seconds[1],
        new_seconds[2],
        new_seconds[3],
        new_seconds[4],
        new_seconds[5],
        new_seconds[6],
        new_seconds[7],
        ema_attn,
        ema_mlp,
        ema_embed,
    )


def solution(mesh):
    return jax.shard_map(
        per_device,
        mesh=mesh,
        in_specs=(
            P("dp", None),
            P("dp", None),
            P("dp", None),
            P("dp", None),
            P("dp", None),
            P("dp"),
            P(None, "dp", "mp"),
            P(None, "dp", "mp"),
            P(None, "dp", "mp"),
            P(None, "dp", "mp"),
            P(None, "dp"),
            P("dp", None),
            P("dp", None),
            P("dp"),
            P(None, "dp", "mp"),
            P(None, "dp", "mp"),
            P(None, "dp", "mp"),
            P(None, "dp", "mp"),
            P(None, "dp"),
            P("dp", None),
            P("dp", None),
            P("dp"),
            P(None, "dp", "mp"),
            P(None, "dp", "mp"),
            P(None, "dp", "mp"),
            P(None, "dp", "mp"),
            P(None, "dp"),
            P("dp", None),
            P("dp", None),
            P("dp"),
            P(None, "dp", "mp"),
            P(None, "dp", "mp"),
            P(None, "dp"),
        ),
        out_specs=(
            P(),
            P(),
            P(),
            P(None, "dp", "mp"),
            P(None, "dp", "mp"),
            P(None, "dp", "mp"),
            P(None, "dp", "mp"),
            P(None, "dp"),
            P("dp", None),
            P("dp", None),
            P("dp"),
            P(None, "dp", "mp"),
            P(None, "dp", "mp"),
            P(None, "dp", "mp"),
            P(None, "dp", "mp"),
            P(None, "dp"),
            P("dp", None),
            P("dp", None),
            P("dp"),
            P(None, "dp", "mp"),
            P(None, "dp", "mp"),
            P(None, "dp", "mp"),
            P(None, "dp", "mp"),
            P(None, "dp"),
            P("dp", None),
            P("dp", None),
            P("dp"),
            P(None, "dp", "mp"),
            P(None, "dp", "mp"),
            P(None, "dp"),
        ),
        check_vma=False,
    )
```

```python
import functools
import math

import jax
import jax.numpy as jnp
from jax import lax
from jax.experimental import pallas as pl
from jax.experimental.pallas import tpu as pltpu
from jax.sharding import PartitionSpec as P

D = 1024
DH = 64
E = 512
DDH = 32
GRID = 16
NB = 3
STEP = 10


EPS_LN = 1e-06
EPS_C = 0.01
CLIP = 0.0002
BETA_ONE = 0.9
BETA_TWO = 0.999
ADAM_EPS = 1e-12
RATE_MAT = 0.06
RATE_VEC = 0.5
DECAY_MAT = 0.05
EMA_KEEP = 0.9
REF_GSD = 4.0


def split_vectors(flat_vec, enc_width, dec_width):
    lengths = [enc_width] * 7 + [dec_width] * 7
    pieces = []
    offset = 0
    for length in lengths:
        pieces.append(flat_vec[offset : offset + length])
        offset = offset + length
    pieces.append(flat_vec[offset:])
    return pieces


F32 = jnp.float32
BF16 = jnp.bfloat16
VMEM_LIMIT = 58 * 2**20
GELU_C = math.sqrt(2.0 / math.pi)


def dot_nn(left, right):
    return jnp.dot(left, right, preferred_element_type=F32)


def dot_nt(left, right):
    return lax.dot_general(left, right, (((1,), (1,)), ((), ())), preferred_element_type=F32)


def dot_tn(left, right):
    return lax.dot_general(left, right, (((0,), (0,)), ((), ())), preferred_element_type=F32)


def dot_exact(left, right):
    return jnp.dot(left, right, preferred_element_type=F32, precision=lax.Precision.HIGHEST)


def normalize(rows):
    centred = rows - jnp.mean(rows, axis=-1, keepdims=True)
    rstd = lax.rsqrt(jnp.mean(centred * centred, axis=-1, keepdims=True) + EPS_LN)
    return centred * rstd, rstd


def norm_back(grad, gain, unit, rstd):
    scaled = grad * gain
    mean_one = jnp.mean(scaled, axis=-1, keepdims=True)
    mean_two = jnp.mean(scaled * unit, axis=-1, keepdims=True)
    grad_in = rstd * (scaled - mean_one - unit * mean_two)
    return (
        grad_in,
        jnp.sum(grad * unit, axis=0, keepdims=True),
        jnp.sum(grad, axis=0, keepdims=True),
    )


def both(mine_ref, other_ref, rows):
    return mine_ref[rows, :].astype(F32) + other_ref[rows, :].astype(F32)


def gelu_parts(up):
    square = up * up
    bent = jnp.tanh(GELU_C * up * (1.0 + 0.044715 * square))
    half = 0.5 * (1.0 + bent)
    return square, bent, half


def group_mask(group, length):
    if group == length:
        return None
    row_image = lax.broadcasted_iota(jnp.int32, (group, group), 0) // length
    col_image = lax.broadcasted_iota(jnp.int32, (group, group), 1) // length
    return row_image == col_image


def attend(qkv_ref, mixed_ref, lse_ref, cols, width, head_dim, mask):
    scale = head_dim ** (-0.5)
    for head in range(width // head_dim):
        at = pl.ds(head * head_dim, head_dim)
        queries = qkv_ref[at, cols]
        keys = qkv_ref[pl.ds(width + head * head_dim, head_dim), cols]
        values = qkv_ref[pl.ds(2 * width + head * head_dim, head_dim), cols]
        scores = dot_tn(keys, queries) * scale
        if mask is not None:
            scores = jnp.where(mask, scores, -1e30)
        top = jnp.max(scores, axis=0, keepdims=True)
        weights = jnp.exp(scores - top)
        total = jnp.sum(weights, axis=0, keepdims=True)
        lse_ref[pl.ds(head, 1), cols] = top + jnp.log(total)
        soft = (weights * (1.0 / total)).astype(BF16)
        mixed_ref[at, cols] = dot_nn(values, soft).astype(BF16)


def attend_back(qkv_ref, grad_ref, lse_ref, out_ref, cols, width, head_dim, mask):
    scale = head_dim ** (-0.5)
    for head in range(width // head_dim):
        at = pl.ds(head * head_dim, head_dim)
        at_k = pl.ds(width + head * head_dim, head_dim)
        at_v = pl.ds(2 * width + head * head_dim, head_dim)
        queries, keys, values = qkv_ref[at, cols], qkv_ref[at_k, cols], qkv_ref[at_v, cols]
        grad = grad_ref[at, :]
        scores = dot_tn(keys, queries) * scale
        if mask is not None:
            scores = jnp.where(mask, scores, -1e30)
        soft = jnp.exp(scores - lse_ref[pl.ds(head, 1), cols])
        out_ref[at_v, cols] = dot_nt(grad, soft.astype(BF16)).astype(BF16)
        grad_soft = dot_tn(values, grad)
        inner = jnp.sum(soft * grad_soft, axis=0, keepdims=True)
        grad_scores = (soft * (grad_soft - inner)).astype(BF16)
        out_ref[at, cols] = (dot_nn(keys, grad_scores) * scale).astype(BF16)
        out_ref[at_k, cols] = (dot_nt(queries, grad_scores) * scale).astype(BF16)


def transposed_weights(attn_ref, flat_ref):
    width = attn_ref.shape[1] // 4
    for part in range(4):
        at = pl.ds(part * width, width)
        flat_ref[at, :] = attn_ref[:, at].T


def attention_rows(unit, vec_ref, flat_ref, qkv_ref, mixed_ref, lse_ref, part_ref, rows, head_dim, mask, attn_ref):
    width = mixed_ref.shape[0]
    low = (unit * vec_ref[1:2, :] + vec_ref[2:3, :]).astype(BF16)
    qkv_ref[:, rows] = dot_nt(flat_ref[: 3 * width, :], low).astype(BF16)
    attend(qkv_ref, mixed_ref, lse_ref, rows, width, head_dim, mask)
    part_ref[rows, :] = dot_nt(mixed_ref[:, rows].T, attn_ref[:, 3 * width :]).astype(BF16)


def enc_in_kernel(length, group, head_dim, pix_ref, kept_ref, table_ref, embed_ref, vec_ref, attn_ref,
                  x_ref, qkv_ref, mixed_ref, lse_ref, part_ref, pixk_ref, flat_ref):
    images, patches = table_ref.shape[0], pix_ref.shape[0] // table_ref.shape[0]
    side = table_ref.shape[1]
    transposed_weights(attn_ref, flat_ref)

    def pick(image, carry):
        rows = pl.ds(image * length, length)
        index = kept_ref[rows, :]
        hot = lax.broadcasted_iota(jnp.int32, (length, patches), 1) == index
        pixels = pix_ref[pl.ds(image * patches, patches), :]
        pixk_ref[rows, :] = dot_nn(hot.astype(BF16), pixels).astype(BF16)
        grid_at = lax.broadcasted_iota(jnp.int32, (length, side), 1)
        table = table_ref[image]
        half = table.shape[1]
        x_ref[rows, :half] = dot_exact((grid_at == index // side).astype(F32), table)
        x_ref[rows, half:] = dot_exact((grid_at == index % side).astype(F32), table)
        return carry

    lax.fori_loop(0, images, pick, 0)
    mask = group_mask(group, length)

    def step(number, carry):
        rows = pl.ds(pl.multiple_of(number * group, group), group)
        share = embed_ref.shape[2]
        rows_x = dot_nt(pixk_ref[rows, :share], embed_ref[0]) + dot_nt(pixk_ref[rows, share:], embed_ref[1])
        rows_x = rows_x + vec_ref[0:1, :] + x_ref[rows, :]
        x_ref[rows, :] = rows_x
        unit, _ = normalize(rows_x)
        attention_rows(unit, vec_ref, flat_ref, qkv_ref, mixed_ref, lse_ref, part_ref, rows, head_dim, mask, attn_ref)
        return carry

    lax.fori_loop(0, x_ref.shape[0] // group, step, 0)


def dec_in_kernel(length, head_dim, x1_ref, mine_ref, other_ref, evec_ref, bridge_ref, kept_ref, hidden_ref,
                  table_ref, vec_ref, attn_ref,
                  x2_ref, final_ref, x_ref, qkv_ref, mixed_ref, lse_ref, part_ref, flat_ref, latent_ref):
    images, side, half = table_ref.shape
    patches = side * side
    transposed_weights(attn_ref, flat_ref)
    every = pl.ds(0, x1_ref.shape[0])
    out = x1_ref[...] + both(mine_ref, other_ref, every)
    x2_ref[...] = out
    unit, _ = normalize(out)
    final = (unit * evec_ref[5:6, :] + evec_ref[6:7, :]).astype(BF16)
    final_ref[...] = final
    share = bridge_ref.shape[2]
    latent_ref[:, :share] = dot_nn(final, bridge_ref[0])
    latent_ref[:, share:] = dot_nn(final, bridge_ref[1])

    def step(image, carry):
        rows = pl.ds(pl.multiple_of(image * patches, patches), patches)
        hot = lax.broadcasted_iota(jnp.int32, (patches, length), 0) == kept_ref[pl.ds(image, 1), :]
        latent = latent_ref[pl.ds(image * length, length), :]
        table = table_ref[image]
        by_row = jnp.broadcast_to(table[:, None, :], (side, side, half)).reshape(patches, half)
        by_col = jnp.broadcast_to(table[None, :, :], (side, side, half)).reshape(patches, half)
        place = jnp.concatenate([by_row, by_col], axis=1)
        rows_x = dot_exact(hot.astype(F32), latent) + hidden_ref[rows, :] * vec_ref[0:1, :] + place
        x_ref[rows, :] = rows_x
        unit, _ = normalize(rows_x)
        attention_rows(unit, vec_ref, flat_ref, qkv_ref, mixed_ref, lse_ref, part_ref, rows, head_dim, None, attn_ref)
        return carry

    lax.fori_loop(0, images, step, 0)


def mlp_kernel(tile, x_ref, mine_ref, other_ref, vec_ref, up_ref, down_ref, x1_ref, part_ref, low_ref, acc_ref):
    number = pl.program_id(0)
    count = x_ref.shape[0] // tile

    def first(step, carry):
        rows = pl.ds(pl.multiple_of(step * tile, tile), tile)
        after = x_ref[rows, :] + both(mine_ref, other_ref, rows)
        x1_ref[rows, :] = after
        unit, _ = normalize(after)
        low_ref[rows, :] = (unit * vec_ref[3:4, :] + vec_ref[4:5, :]).astype(BF16)
        return carry

    @pl.when(number == 0)
    def _():
        lax.fori_loop(0, count, first, 0)
        acc_ref[...] = jnp.zeros_like(acc_ref)

    def step(piece, carry):
        rows = pl.ds(pl.multiple_of(piece * tile, tile), tile)
        up = dot_nn(low_ref[rows, :], up_ref[...])
        _, _, half = gelu_parts(up)
        acc_ref[rows, :] += dot_nt((up * half).astype(BF16), down_ref[...])
        return carry

    lax.fori_loop(0, count, step, 0)

    @pl.when(number == pl.num_programs(0) - 1)
    def _():
        part_ref[...] = acc_ref[...].astype(BF16)


def head_kernel(core_ref, inverse_ref, x1_ref, mine_ref, other_ref, vec_ref, bias_ref, predict_ref, target_ref,
                band_ref, weight_ref, gy_ref, glow_ref, gbias_ref, loss_ref, gain_ref, shift_ref, low_ref, gpred_ref):
    number = pl.program_id(0)

    @pl.when(number == 0)
    def _():
        for ref in (gpred_ref, gbias_ref, loss_ref, gain_ref, shift_ref):
            ref[...] = jnp.zeros_like(ref)

    every = pl.ds(0, x1_ref.shape[0])
    unit, rstd = normalize(x1_ref[...] + both(mine_ref, other_ref, every))
    gain = vec_ref[5:6, :]
    final = (unit * gain + vec_ref[6:7, :]).astype(BF16)
    share = gpred_ref.shape[1]
    predicted = jnp.concatenate([dot_nn(final, predict_ref[0]), dot_nn(final, predict_ref[1])], axis=1)
    mismatch = predicted + bias_ref[...] - target_ref[...].astype(F32)
    band = band_ref[...]
    level = jnp.where(band == 0, inverse_ref[0], jnp.where(band == 1, inverse_ref[1], inverse_ref[2]))
    level = level * weight_ref[...]
    square = mismatch * mismatch + EPS_C
    root = lax.rsqrt(square)
    loss_ref[...] += jnp.sum(level * (square * root), axis=0, keepdims=True)
    grad = level * (mismatch * root)
    gbias_ref[...] += jnp.sum(grad, axis=0, keepdims=True)
    low_ref[...] = grad.astype(BF16)
    columns = pl.ds(pl.multiple_of(core_ref[0] * share, share), share)
    gpred_ref[...] += dot_tn(final, low_ref[:, columns])
    grad_final = dot_nt(low_ref[:, :share], predict_ref[0]) + dot_nt(low_ref[:, share:], predict_ref[1])
    grad_in, gain_sum, shift_sum = norm_back(grad_final, gain, unit, rstd)
    gy_ref[...] = grad_in
    gain_ref[...] += gain_sum
    shift_ref[...] += shift_sum

    @pl.when(number == pl.num_programs(0) - 1)
    def _():
        glow_ref[...] = gpred_ref[...].astype(BF16)


def mlp_back_kernel(tile, gy_ref, x1_ref, vec_ref, up_ref, down_ref, gup_ref, gdown_ref, part_ref,
                    low_ref, lowt_ref, grad_ref, gradt_ref, gu_ref, z_ref, acc_ref):
    number = pl.program_id(0)
    count = x1_ref.shape[0] // tile

    def first(step, carry):
        rows = pl.ds(pl.multiple_of(step * tile, tile), tile)
        unit, _ = normalize(x1_ref[rows, :])
        low = (unit * vec_ref[3:4, :] + vec_ref[4:5, :]).astype(BF16)
        low_ref[rows, :] = low
        lowt_ref[:, rows] = low.T
        grad = gy_ref[rows, :].astype(BF16)
        grad_ref[rows, :] = grad
        gradt_ref[:, rows] = grad.T
        return carry

    @pl.when(number == 0)
    def _():
        lax.fori_loop(0, count, first, 0)
        acc_ref[...] = jnp.zeros_like(acc_ref)

    def step(piece, carry):
        rows = pl.ds(pl.multiple_of(piece * tile, tile), tile)
        up = dot_nn(low_ref[rows, :], up_ref[...])
        square, bent, half = gelu_parts(up)
        z_ref[rows, :] = (up * half).astype(BF16)
        slope = half + (0.5 * GELU_C) * up * (1.0 - bent * bent) * (1.0 + (3.0 * 0.044715) * square)
        grad_up = (dot_nn(grad_ref[rows, :], down_ref[...]) * slope).astype(BF16)
        gu_ref[rows, :] = grad_up
        acc_ref[rows, :] += dot_nt(grad_up, up_ref[...])
        return carry

    lax.fori_loop(0, count, step, 0)
    gup_ref[...] = dot_nn(lowt_ref[...], gu_ref[...]).astype(BF16)
    gdown_ref[...] = dot_nn(gradt_ref[...], z_ref[...]).astype(BF16)

    @pl.when(number == pl.num_programs(0) - 1)
    def _():
        part_ref[...] = acc_ref[...].astype(BF16)


def attn_back_kernel(length, group, head_dim, gy_ref, x1_ref, mine_ref, other_ref, x_ref, qkv_ref, mixed_ref, lse_ref,
                     vec_ref, attn_ref, gx_ref, grad_ref, gain_ref, shift_ref, part_ref,
                     flat_ref, lowt_ref, gradt_ref, gmix_ref, gqkv_ref):
    width = mixed_ref.shape[0]
    transposed_weights(attn_ref, flat_ref)
    gain_ref[...] = jnp.zeros_like(gain_ref)
    shift_ref[...] = jnp.zeros_like(shift_ref)
    mask = group_mask(group, length)

    def step(number, carry):
        rows = pl.ds(pl.multiple_of(number * group, group), group)
        unit, rstd = normalize(x1_ref[rows, :])
        grad_in, gain_sum, shift_sum = norm_back(both(mine_ref, other_ref, rows), vec_ref[3:4, :], unit, rstd)
        grad_in = grad_in + gy_ref[rows, :]
        gx_ref[rows, :] = grad_in
        gain_ref[...] += gain_sum
        shift_ref[...] += shift_sum
        low_grad = grad_in.astype(BF16)
        gradt_ref[:, rows] = low_grad.T
        gmix_ref[...] = dot_nt(flat_ref[3 * width :, :], low_grad).astype(BF16)
        attend_back(qkv_ref, gmix_ref, lse_ref, gqkv_ref, rows, width, head_dim, mask)
        part_ref[rows, :] = dot_nn(gqkv_ref[:, rows].T, flat_ref[: 3 * width, :]).astype(BF16)
        unit_a, _ = normalize(x_ref[rows, :])
        lowt_ref[:, rows] = (unit_a * vec_ref[1:2, :] + vec_ref[2:3, :]).astype(BF16).T
        return carry

    lax.fori_loop(0, x_ref.shape[0] // group, step, 0)
    grad_ref[:, : 3 * width] = dot_nt(lowt_ref[...], gqkv_ref[...]).astype(BF16)
    grad_ref[:, 3 * width :] = dot_nt(gradt_ref[...], mixed_ref[...]).astype(BF16)


def between_kernel(length, core_ref, gx_ref, x_ref, mine_ref, other_ref, vec_ref, kept_ref, hidden_ref, final_ref, x2_ref,
                   evec_ref, bridge_ref, gain_ref, shift_ref, mask_ref, gbridge_ref, egain_ref, eshift_ref, gy_ref,
                   latent_ref):
    images = kept_ref.shape[0] // length
    patches = x_ref.shape[0] // images
    for ref in (gain_ref, shift_ref, mask_ref):
        ref[...] = jnp.zeros_like(ref)

    def step(image, carry):
        rows = pl.ds(pl.multiple_of(image * patches, patches), patches)
        unit, rstd = normalize(x_ref[rows, :])
        grad_in, gain_sum, shift_sum = norm_back(both(mine_ref, other_ref, rows), vec_ref[1:2, :], unit, rstd)
        grad_in = grad_in + gx_ref[rows, :]
        gain_ref[...] += gain_sum
        shift_ref[...] += shift_sum
        mask_ref[...] += jnp.sum(grad_in * hidden_ref[rows, :], axis=0, keepdims=True)
        kept_rows = pl.ds(pl.multiple_of(image * length, length), length)
        hot = lax.broadcasted_iota(jnp.int32, (length, patches), 1) == kept_ref[kept_rows, :]
        latent_ref[kept_rows, :] = dot_nn(hot.astype(BF16), grad_in.astype(BF16)).astype(BF16)
        return carry

    lax.fori_loop(0, images, step, 0)
    share = gbridge_ref.shape[1]
    columns = pl.ds(pl.multiple_of(core_ref[0] * share, share), share)
    gbridge_ref[...] = dot_tn(final_ref[...], latent_ref[:, columns]).astype(BF16)
    grad_final = dot_nt(latent_ref[:, :share], bridge_ref[0]) + dot_nt(latent_ref[:, share:], bridge_ref[1])
    unit, rstd = normalize(x2_ref[...])
    gy_ref[...], egain_ref[...], eshift_ref[...] = norm_back(grad_final, evec_ref[5:6, :], unit, rstd)


def enc_out_kernel(core_ref, gx_ref, x_ref, mine_ref, other_ref, vec_ref, pixk_ref,
                   gain_ref, shift_ref, ebias_ref, gembed_ref):
    every = pl.ds(0, x_ref.shape[0])
    unit, rstd = normalize(x_ref[...])
    grad_in, gain_ref[...], shift_ref[...] = norm_back(both(mine_ref, other_ref, every), vec_ref[1:2, :], unit, rstd)
    grad_in = grad_in + gx_ref[...]
    ebias_ref[...] = jnp.sum(grad_in, axis=0, keepdims=True)
    share = gembed_ref.shape[1]
    columns = pl.ds(pl.multiple_of(core_ref[0] * share, share), share)
    gembed_ref[...] = dot_tn(grad_in.astype(BF16), pixk_ref[:, columns]).astype(BF16)


def shape(dims, dtype):
    return jax.ShapeDtypeStruct(dims, dtype)


def run(kernel, outs, scratch, args, flops, scalars=0):
    moved = sum(math.prod(a.shape) * a.dtype.itemsize for a in list(args) + list(outs))
    in_vmem = pl.BlockSpec(memory_space=pltpu.VMEM)
    return pl.pallas_call(
        kernel,
        out_shape=tuple(outs),
        in_specs=[pl.BlockSpec(memory_space=pltpu.SMEM)] * scalars + [in_vmem] * (len(args) - scalars),
        out_specs=tuple([in_vmem] * len(outs)),
        scratch_shapes=scratch,
        compiler_params=pltpu.CompilerParams(vmem_limit_bytes=VMEM_LIMIT),
        cost_estimate=pl.CostEstimate(flops=flops, bytes_accessed=moved, transcendentals=0),
    )(*args)


def other_core(block):
    return lax.ppermute(block, "mp", [(0, 1), (1, 0)])


def mlp_forward(x, mine, vec, stack):
    rows, width = x.shape
    hidden = stack.shape[1] // 2
    block = min(hidden, 512)
    tile = min(rows, 512)
    other = other_core(mine)
    whole = pl.BlockSpec((rows, width), lambda i: (0, 0))
    cols = pl.BlockSpec((width, block), lambda i: (0, i))
    later = pl.BlockSpec((width, block), lambda i: (0, i + hidden // block))
    return pl.pallas_call(
        functools.partial(mlp_kernel, tile),
        out_shape=(shape((rows, width), F32), shape((rows, width), BF16)),
        grid=(hidden // block,),
        in_specs=[whole] * 3 + [pl.BlockSpec((8, width), lambda i: (0, 0)), cols, later],
        out_specs=(whole, whole),
        scratch_shapes=[pltpu.VMEM((rows, width), BF16), pltpu.VMEM((rows, width), F32)],
        compiler_params=pltpu.CompilerParams(vmem_limit_bytes=VMEM_LIMIT),
        cost_estimate=pl.CostEstimate(flops=4 * rows * width * hidden, bytes_accessed=rows * width * 14 + width * hidden * 4,
                                      transcendentals=rows * hidden),
    )(x, mine, other, vec, stack, stack)


def mlp_backward(gy, x1, vec, stack):
    rows, width = x1.shape
    hidden = stack.shape[1] // 2
    block = min(hidden, 512)
    tile = min(rows, 256)
    whole = pl.BlockSpec((rows, width), lambda i: (0, 0))
    cols = pl.BlockSpec((width, block), lambda i: (0, i))
    later = pl.BlockSpec((width, block), lambda i: (0, i + hidden // block))
    return pl.pallas_call(
        functools.partial(mlp_back_kernel, tile),
        out_shape=(shape((width, hidden), BF16), shape((width, hidden), BF16), shape((rows, width), BF16)),
        grid=(hidden // block,),
        in_specs=[whole] * 2 + [pl.BlockSpec((8, width), lambda i: (0, 0)), cols, later],
        out_specs=(cols, cols, whole),
        scratch_shapes=[
            pltpu.VMEM((rows, width), BF16), pltpu.VMEM((width, rows), BF16),
            pltpu.VMEM((rows, width), BF16), pltpu.VMEM((width, rows), BF16),
            pltpu.VMEM((rows, block), BF16), pltpu.VMEM((rows, block), BF16),
            pltpu.VMEM((rows, width), F32)],
        compiler_params=pltpu.CompilerParams(vmem_limit_bytes=VMEM_LIMIT),
        cost_estimate=pl.CostEstimate(flops=10 * rows * width * hidden, bytes_accessed=rows * width * 10 + width * hidden * 8,
                                      transcendentals=rows * hidden),
    )(gy, x1, vec, stack, stack)


def head(core, inverse, x1, mine, vec, bias, predict, target, band, weight, patches):
    rows, width = x1.shape
    pixels = target.shape[1]
    share = pixels // 2
    other = other_core(mine)
    smem = pl.BlockSpec(memory_space=pltpu.SMEM)
    row_w = pl.BlockSpec((patches, width), lambda i: (i, 0))
    row_p = pl.BlockSpec((patches, pixels), lambda i: (i, 0))
    fix = lambda a, b: pl.BlockSpec((a, b), lambda i: (0, 0))
    return pl.pallas_call(
        head_kernel,
        out_shape=(shape((rows, width), F32), shape((width, share), BF16), shape((1, pixels), F32),
                   shape((1, pixels), F32), shape((1, width), F32), shape((1, width), F32)),
        grid=(rows // patches,),
        in_specs=[smem, smem, row_w, row_w, row_w, fix(8, width), fix(1, pixels), pl.BlockSpec((2, width, share), lambda i: (0, 0, 0)), row_p, row_p,
                  pl.BlockSpec((patches, 1), lambda i: (i, 0))],
        out_specs=(row_w, fix(width, share), fix(1, pixels), fix(1, pixels), fix(1, width), fix(1, width)),
        scratch_shapes=[pltpu.VMEM((patches, pixels), BF16), pltpu.VMEM((width, share), F32)],
        compiler_params=pltpu.CompilerParams(vmem_limit_bytes=VMEM_LIMIT),
        cost_estimate=pl.CostEstimate(flops=5 * rows * width * pixels, bytes_accessed=rows * (width * 12 + pixels * 6),
                                      transcendentals=rows * pixels),
    )(core, inverse, x1, mine, other, vec, bias, predict, target, band, weight)


def attn_backward(gy, x1, mine, x, saved, vec, attn, length, group, head_dim):
    qkv, mixed, lse = saved
    rows, width = x.shape
    local = mixed.shape[0]
    return run(
        functools.partial(attn_back_kernel, length, group, head_dim),
        [shape((rows, width), F32), shape((width, 4 * local), BF16),
         shape((1, width), F32), shape((1, width), F32), shape((rows, width), BF16)],
        [pltpu.VMEM((4 * local, width), BF16), pltpu.VMEM((width, rows), BF16), pltpu.VMEM((width, rows), BF16),
         pltpu.VMEM((local, group), BF16), pltpu.VMEM((3 * local, rows), BF16)],
        (gy, x1, mine, other_core(mine), x, qkv, mixed, lse, vec, attn),
        18 * rows * width * local)


def sine_table(gsd_values, feature_width, grid_side):
    quarter = feature_width // 4
    frequency = jnp.exp(-jnp.log(10000.0) * jnp.arange(quarter).astype(F32) / quarter)
    gsd_ratio = gsd_values.astype(F32)[:, None, None] / REF_GSD
    line = jnp.arange(grid_side, dtype=jnp.int32).astype(F32)
    arg = line[None, :, None] * gsd_ratio * frequency
    return jnp.concatenate([jnp.sin(arg), jnp.cos(arg)], axis=-1)


def dp_bits():
    return lax.axis_size("dp").bit_length() - 1


def orders():
    bits = dp_bits()
    high = list(range(bits - 1, 1, -1))
    return (high + [0, 1], high + [1, 0])


def swap(block, bit):
    size = lax.axis_size("dp")
    return lax.ppermute(block, "dp", [(i, i ^ (1 << bit)) for i in range(size)])


def my_bit(bit):
    return (lax.axis_index("dp") >> bit) & 1


def gather_dp(block, axis, order):
    lead, rest = (block.shape[:axis], block.shape[axis:])
    done = []
    cur = block
    for bit in order:
        other = swap(cur, bit)
        mine = my_bit(bit) == 1
        place = axis + sum(1 for b in done if b > bit)
        cur = jnp.stack([jnp.where(mine, other, cur), jnp.where(mine, cur, other)], axis=place)
        done.append(bit)
    return cur.reshape(lead + (rest[0] * lax.axis_size("dp"),) + rest[1:])


def reduce_dp(block, axis, order, wire):
    bits = dp_bits()
    lead, rest = (block.shape[:axis], block.shape[axis:])
    shard = rest[0] // lax.axis_size("dp")
    cur = block.reshape(lead + (2,) * bits + (shard,) + rest[1:])
    left = list(range(bits - 1, -1, -1))
    for bit in reversed(order):
        place = axis + left.index(bit)
        mine = my_bit(bit)
        keep = lax.dynamic_index_in_dim(cur, mine, place, keepdims=False)
        give = lax.dynamic_index_in_dim(cur, 1 - mine, place, keepdims=False)
        other = swap(give.astype(wire), bit)
        cur = keep.astype(F32) + other.astype(F32)
        left.remove(bit)
    return cur


def join_cores(mine, core):
    other = other_core(mine)
    return jnp.concatenate([jnp.where(core == 0, mine, other), jnp.where(core == 0, other, mine)], axis=1)


def total_dp(value):
    for bit in range(dp_bits()):
        value = value + swap(value, bit)
    return value


def place_of():
    index = lax.axis_index("dp")
    core = lax.axis_index("mp")
    low, high = lax.rem(index, 4), index // 4
    bit_x, bit_y = lax.rem(low, 2), low // 2
    low_x, low_y = low + 1 - 2 * bit_x, low + 2 - 4 * bit_y
    return core, low, high, low_x, low_y


def greet(partners):
    barrier = pltpu.get_barrier_semaphore()
    for partner in partners:
        pl.semaphore_signal(barrier, inc=1, device_id=partner, device_id_type=pl.DeviceIdType.MESH)
    pl.semaphore_wait(barrier, len(partners))


def blocks_of(widths, limit):
    found = []
    for number, width in enumerate(widths):
        start = 0
        while start < width:
            size = min(limit, width - start)
            found.append((number, start, size))
            start += size
    return found


def gather_kernel(highs, shared, groups, count, *refs):
    shards, fulls = refs[:count], refs[count : 2 * count]
    own_sem, zs_sem, zr_sem, cs_sem, cr_sem, fs_sem, fr_sem, ms_sem, mr_sem = refs[2 * count :]
    core, low, high, low_x, low_y = place_of()
    at_x, at_y = (high * 4 + low_x, core), (high * 4 + low_y, core)
    at_high = [(lax.rem(high + k, highs) * 4 + low, core) for k in range(1, highs)]
    sibling = (high * 4 + low, 1 - core)
    greet([at_x, at_y, sibling] + at_high)

    def full(group):
        number, start, size = group
        ref = fulls[number].at[core] if shared[number] else fulls[number]
        return ref, pl.ds(start, size)

    def remote(source, target, send, receive, device):
        return pltpu.make_async_remote_copy(
            src_ref=source, dst_ref=target, send_sem=send, recv_sem=receive,
            device_id=device, device_id_type=pl.DeviceIdType.MESH)

    def first(at):
        ref, cols = full(groups[at])
        shard = shards[groups[at][0]].at[:, cols]
        mine = ref.at[high, low, :, cols]
        copies = [pltpu.make_async_copy(shard, mine, own_sem.at[at])]
        for k in range(1, highs):
            copies.append(remote(shard, mine, zs_sem.at[at, k - 1], zr_sem.at[at, k - 1], at_high[k - 1]))
        return copies

    def column(at):
        ref, cols = full(groups[at])
        part = ref.at[:, low, :, cols]
        return [remote(part, part, cs_sem.at[at, 0], cr_sem.at[at, 0], at_x),
                remote(part, part, cs_sem.at[at, 1], cr_sem.at[at, 1], at_y)]

    def forward(at):
        ref, cols = full(groups[at])
        if at % 2 == 0:
            part = ref.at[:, low_x, :, cols]
            return remote(part, part, fs_sem.at[at], fr_sem.at[at], at_y)
        part = ref.at[:, low_y, :, cols]
        return remote(part, part, fs_sem.at[at], fr_sem.at[at], at_x)

    total = len(groups)
    pairs = (total + 1) // 2
    in_pair = lambda pair: [at for at in (2 * pair, 2 * pair + 1) if at < total]
    for step in range(pairs + 2):
        if step < pairs:
            for at in in_pair(step):
                for copy in first(at):
                    copy.start()
        if 0 <= step - 1 < pairs:
            for at in in_pair(step - 1):
                for copy in first(at):
                    copy.wait()
                for copy in column(at):
                    copy.start()
        if 0 <= step - 2 < pairs:
            for at in in_pair(step - 2):
                column(at)[at % 2].wait()
                forward(at).start()
    swaps = []
    for at in range(total):
        column(at)[1 - at % 2].wait()
        forward(at).wait()
    for number in range(count):
        if shared[number]:
            part = fulls[number].at[core]
            swap = remote(part, part, ms_sem.at[number], mr_sem.at[number], sibling)
            swap.start()
            swaps.append(swap)
    for swap in swaps:
        swap.wait()


def gather_all(shards, shared):
    size = lax.axis_size("dp")
    if any(a.shape[0] % 16 for a in shards if a.dtype == BF16):
        order_a, order_b = orders()
        fulls = []
        for number, shard in enumerate(shards):
            full = gather_dp(shard, 0, (order_a, order_b)[number % 2])
            if shared[number]:
                other, zero = other_core(full), lax.axis_index("mp") == 0
                full = jnp.stack([jnp.where(zero, full, other), jnp.where(zero, other, full)])
            fulls.append(full)
        return fulls
    highs = size // 4
    count = len(shards)
    groups = blocks_of([a.shape[1] for a in shards], 1024)
    outs = []
    for shard, split in zip(shards, shared):
        dims = (highs, 4) + shard.shape
        outs.append(shape((2,) + dims if split else dims, shard.dtype))
    dma = pltpu.SemaphoreType.DMA
    total = len(groups)
    any_space = pl.BlockSpec(memory_space=pl.ANY)
    fulls = pl.pallas_call(
        functools.partial(gather_kernel, highs, shared, groups, count),
        out_shape=tuple(outs),
        in_specs=[any_space] * count,
        out_specs=tuple([any_space] * count),
        scratch_shapes=[dma((total,)), dma((total, highs - 1)), dma((total, highs - 1)), dma((total, 2)), dma((total, 2)),
                        dma((total,)), dma((total,)), dma((count,)), dma((count,))],
        compiler_params=pltpu.CompilerParams(collective_id=0, has_side_effects=True),
        cost_estimate=pl.CostEstimate(flops=0, bytes_accessed=sum(a.size * a.dtype.itemsize * size for a in shards),
                                      transcendentals=0),
    )(*shards)
    return [full.reshape(((2,) if split else ()) + (size * shard.shape[0], shard.shape[1]))
            for full, split, shard in zip(fulls, shared, shards)]


def reduce_kernel(highs, weights, groups, count, loss_ref, *refs):
    grads, outs, sums_ref = refs[:count], refs[count : 2 * count], refs[2 * count]
    refs = refs[2 * count + 1 :]
    total = len(groups)
    buffers, refs = refs[: 6 * total], refs[6 * total :]
    plane_ref, norm_ref, near_ref, far_ref = refs[:4]
    load_sem, as_sem, ar_sem, bs_sem, br_sem, zs_sem, zr_sem, ns_sem, nr_sem, hs_sem, hr_sem = refs[4:]
    core, low, high, low_x, low_y = place_of()
    low_d = 3 - low
    spot = low * 2 + core
    dev_x, dev_y = (high * 4 + low_x, core), (high * 4 + low_y, core)
    at_high = [(lax.rem(high + k, highs) * 4 + low, core) for k in range(1, highs)]
    near = [(high * 4 + lax.rem(spot + k, 8) // 2, lax.rem(lax.rem(spot + k, 8), 2)) for k in range(1, 8)]
    greet(near + at_high)

    def remote(source, target, send, receive, device):
        return pltpu.make_async_remote_copy(
            src_ref=source, dst_ref=target, send_sem=send, recv_sem=receive,
            device_id=device, device_id_type=pl.DeviceIdType.MESH)

    def route(at):
        if at % 2 == 0:
            return low_y, dev_y, low_x, dev_x
        return low_x, dev_x, low_y, dev_y

    def grad(at, which):
        number, start, size = groups[at]
        return grads[number].at[:, which, :, pl.ds(start, size)]

    def loads(at):
        _, _, low_two, _ = route(at)
        return [pltpu.make_async_copy(grad(at, low_two), buffers[6 * at], load_sem.at[at, 0]),
                pltpu.make_async_copy(grad(at, low), buffers[6 * at + 1], load_sem.at[at, 1])]

    def one(at):
        low_one, dev_one, _, _ = route(at)
        return [remote(grad(at, low_d), buffers[6 * at + 2], as_sem.at[at, 0], ar_sem.at[at, 0], dev_one),
                remote(grad(at, low_one), buffers[6 * at + 3], as_sem.at[at, 1], ar_sem.at[at, 1], dev_one)]

    def two(at):
        return remote(buffers[6 * at], buffers[6 * at + 4], bs_sem.at[at], br_sem.at[at], route(at)[3])

    def three(at):
        return [remote(buffers[6 * at + 1].at[lax.rem(high + k, highs)], buffers[6 * at + 5].at[k - 1],
                       zs_sem.at[at, k - 1], zr_sem.at[at, k - 1], at_high[k - 1]) for k in range(1, highs)]

    pairs = (total + 1) // 2
    in_pair = lambda pair: [at for at in (2 * pair, 2 * pair + 1) if at < total]
    norm_ref[...] = jnp.zeros_like(norm_ref)
    kept = {}
    for step in range(pairs + 3):
        if step < pairs:
            for at in in_pair(step):
                for copy in one(at) + loads(at):
                    copy.start()
        if 0 <= step - 1 < pairs:
            for at in in_pair(step - 1):
                mine = buffers[6 * at]
                loads(at)[0].wait()
                one(at)[0].wait()
                mine[...] = (mine[...].astype(F32) + buffers[6 * at + 2][...].astype(F32)).astype(mine.dtype)
                two(at).start()
        if 0 <= step - 2 < pairs:
            for at in in_pair(step - 2):
                number, start, size = groups[at]
                mine = buffers[6 * at + 1]
                loads(at)[1].wait()
                one(at)[1].wait()
                two(at).wait()
                rows = mine.shape[1]
                plane = plane_ref.at[at % 4, :, :rows, :size]
                plane[...] = (mine[...].astype(F32) + buffers[6 * at + 3][...].astype(F32)
                              + buffers[6 * at + 4][...].astype(F32))
                outs[number][:, pl.ds(start, size)] = plane[high]
                mine[...] = plane[...].astype(mine.dtype)
                for copy in three(at):
                    copy.start()
        if 0 <= step - 3 < pairs:
            for at in in_pair(step - 3):
                number, start, size = groups[at]
                for copy in three(at):
                    copy.wait()
                cols = pl.ds(start, size)
                done = outs[number][:, cols]
                for k in range(highs - 1):
                    done = done + buffers[6 * at + 5][k].astype(F32)
                outs[number][:, cols] = done
                norm_ref[0:1, 0:1] += weights[number] * jnp.sum(done * done, keepdims=True)
    norm_ref[1:2, 0:1] = jnp.sum(loss_ref[...], keepdims=True)
    near_ref[spot] = norm_ref[...]
    copies = [remote(norm_ref, near_ref.at[spot], ns_sem.at[k], nr_sem.at[k], near[k]) for k in range(7)]
    for copy in copies:
        copy.start()
    for copy in copies:
        copy.wait()
    local = near_ref[0]
    for k in range(1, 8):
        local = local + near_ref[k]
    norm_ref[...] = local
    far_ref[high] = local
    copies = [remote(norm_ref, far_ref.at[high], hs_sem.at[k], hr_sem.at[k], at_high[k]) for k in range(highs - 1)]
    for copy in copies:
        copy.start()
    for copy in copies:
        copy.wait()
    every = far_ref[0]
    for k in range(1, highs):
        every = every + far_ref[k]
    sums_ref[...] = every


def reduce_all(grads, weights, loss_parts):
    size = lax.axis_size("dp")
    highs = size // 4
    if any((a.shape[0] // size) % 16 for a in grads if a.dtype == BF16):
        order_a, order_b = orders()
        outs = [reduce_dp(a, 0, (order_a, order_b)[number % 2], a.dtype) for number, a in enumerate(grads)]
        sums = jnp.stack([sum(w * jnp.sum(a * a) for w, a in zip(weights, outs)), jnp.sum(loss_parts)])
        sums = total_dp(sums)
        sums = sums + other_core(sums)
        return outs, sums[0], 0.5 * sums[1]
    count = len(grads)
    groups = blocks_of([a.shape[1] for a in grads], 512)
    shards = [a.shape[0] // size for a in grads]
    total = len(groups)
    buffers = []
    for number, _, width in groups:
        piece = pltpu.VMEM((highs, shards[number], width), grads[number].dtype)
        buffers += [piece] * 5 + [pltpu.VMEM((highs - 1, shards[number], width), grads[number].dtype)]
    dma = pltpu.SemaphoreType.DMA
    small = (8, 128)
    in_vmem = pl.BlockSpec(memory_space=pltpu.VMEM)
    any_space = pl.BlockSpec(memory_space=pl.ANY)
    result = pl.pallas_call(
        functools.partial(reduce_kernel, highs, weights, groups, count),
        out_shape=tuple([shape((rows, a.shape[1]), F32) for rows, a in zip(shards, grads)] + [shape(small, F32)]),
        in_specs=[in_vmem] + [any_space] * count,
        out_specs=tuple([in_vmem] * (count + 1)),
        scratch_shapes=buffers + [
            pltpu.VMEM((4, highs, max(shards), max(g[2] for g in groups)), F32), pltpu.VMEM(small, F32),
            pltpu.VMEM((8,) + small, F32), pltpu.VMEM((highs,) + small, F32),
            dma((total, 2)), dma((total, 2)), dma((total, 2)), dma((total,)), dma((total,)),
            dma((total, highs - 1)), dma((total, highs - 1)), dma((7,)), dma((7,)), dma((highs - 1,)), dma((highs - 1,))],
        compiler_params=pltpu.CompilerParams(collective_id=1, has_side_effects=True, vmem_limit_bytes=VMEM_LIMIT),
        cost_estimate=pl.CostEstimate(flops=0, bytes_accessed=sum(a.size * a.dtype.itemsize for a in grads),
                                      transcendentals=0),
    )(loss_parts, *[a.reshape(highs, 4, rows, a.shape[1]) for rows, a in zip(shards, grads)])
    return list(result[:count]), result[count][0, 0], 0.5 * result[count][1, 0]


def adam_update(master, gradient, first_old, second_old, step_rate, decay_rate):
    first_new = BETA_ONE * first_old + (1.0 - BETA_ONE) * gradient
    second_new = BETA_TWO * second_old + (1.0 - BETA_TWO) * gradient * gradient
    first_hat = first_new / (1.0 - BETA_ONE**STEP)
    second_hat = second_new / (1.0 - BETA_TWO**STEP)
    updated = master - step_rate * (
        first_hat / (jnp.sqrt(second_hat) + ADAM_EPS) + decay_rate * master
    )
    return (updated, first_new, second_new)


def per_device(
    pixels,
    target,
    band_ids,
    kept_index,
    intersection,
    gsd_scale,
    enc_attn,
    enc_mlp,
    dec_attn,
    dec_mlp,
    patch_embed,
    bridge,
    predict,
    vectors,
    first_enc_attn,
    first_enc_mlp,
    first_dec_attn,
    first_dec_mlp,
    first_patch_embed,
    first_bridge,
    first_predict,
    first_vectors,
    second_enc_attn,
    second_enc_mlp,
    second_dec_attn,
    second_dec_mlp,
    second_patch_embed,
    second_bridge,
    second_predict,
    second_vectors,
    ema_enc_attn,
    ema_enc_mlp,
    ema_patch_embed,
):
    masters = (enc_attn, enc_mlp, dec_attn, dec_mlp, patch_embed, bridge, predict, vectors)
    firsts = (
        first_enc_attn,
        first_enc_mlp,
        first_dec_attn,
        first_dec_mlp,
        first_patch_embed,
        first_bridge,
        first_predict,
        first_vectors,
    )
    seconds = (
        second_enc_attn,
        second_enc_mlp,
        second_dec_attn,
        second_dec_mlp,
        second_patch_embed,
        second_bridge,
        second_predict,
        second_vectors,
    )
    images, keep_count = kept_index.shape
    patch_count = intersection.shape[1]
    patch_index = jnp.arange(patch_count, dtype=jnp.int32)
    kept_flags = jnp.any(kept_index[:, :, None] == patch_index[None, None, :], axis=1).astype(
        jnp.float32
    )
    patch_weight = ((1.0 - kept_flags) * (1.0 - 0.5 * intersection.astype(jnp.float32))).reshape(
        -1, 1
    )
    local_counts = jnp.stack(
        [
            jnp.sum(patch_weight * (band_ids == band_level).astype(jnp.float32))
            for band_level in range(NB)
        ]
    )
    core_at = lax.axis_index("mp")
    size = lax.axis_size("dp")
    low = jnp.bfloat16

    def flat(stack):
        return jnp.concatenate([part.astype(low) for part in stack], axis=1)

    def core_half(block):
        return lax.dynamic_slice_in_dim(block, core_at * (block.shape[1] // 2), block.shape[1] // 2, 1).astype(low)

    vec_shard = vectors.shape[0]
    vec_room = -(-(vec_shard + NB) // 1024) * 1024
    vec_rows = jnp.concatenate([lax.reduce_precision(vectors, 8, 7), local_counts,
                                jnp.zeros((vec_room - vec_shard - NB,), F32)]).reshape(-1, 128)
    enc_attn_w, enc_mlp_w, dec_attn_w, dec_mlp_w, embed_w, bridge_w, predict_w, vec_full = gather_all(
        [flat(enc_attn), flat(enc_mlp), flat(dec_attn), flat(dec_mlp), core_half(patch_embed.T), core_half(bridge),
         core_half(predict), vec_rows],
        (False, False, False, False, True, True, True, False))
    vec_full = vec_full.reshape(size, vec_room)
    pieces = split_vectors(vec_full[:, :vec_shard].reshape(-1), D, E)
    band_weight = jnp.sum(vec_full[:, vec_shard : vec_shard + NB], axis=0)
    inverse = 1.0 / band_weight
    core = lax.axis_index("mp").astype(jnp.int32).reshape(1)
    hidden_rows = (1.0 - kept_flags).reshape(-1, 1)
    kept_column = kept_index.reshape(-1, 1)
    rows, rows_d = images * keep_count, images * patch_count
    local, local_d = enc_attn_w.shape[1] // 4, dec_attn_w.shape[1] // 4
    pixel_count = pixels.shape[1]
    evec = jnp.stack(pieces[:7] + [jnp.zeros_like(pieces[0])])
    dvec = jnp.stack(pieces[7:14] + [jnp.zeros_like(pieces[7])])
    group = 2 * keep_count
    x0, *enc_saved, part, kept_pixels = run(
        functools.partial(enc_in_kernel, keep_count, group, DH),
        [shape((rows, D), F32), shape((3 * local, rows), BF16), shape((local, rows), BF16),
         shape((local // DH, rows), F32), shape((rows, D), BF16), shape((rows, pixel_count), BF16)],
        [pltpu.VMEM((4 * local, D), BF16)],
        (pixels, kept_column, sine_table(gsd_scale, D, GRID), embed_w, evec, enc_attn_w),
        rows * D * (2 * pixel_count + 8 * local))
    x1, part = mlp_forward(x0, part, evec, enc_mlp_w)
    x2, final_enc, xd, *dec_saved, part = run(
        functools.partial(dec_in_kernel, keep_count, DDH),
        [shape((rows, D), F32), shape((rows, D), BF16), shape((rows_d, E), F32), shape((3 * local_d, rows_d), BF16),
         shape((local_d, rows_d), BF16), shape((local_d // DDH, rows_d), F32), shape((rows_d, E), BF16)],
        [pltpu.VMEM((4 * local_d, E), BF16), pltpu.VMEM((rows, E), F32)],
        (x1, part, other_core(part), evec, bridge_w, kept_index, hidden_rows, sine_table(gsd_scale, E, GRID), dvec,
         dec_attn_w),
        rows_d * E * 8 * local_d + 2 * rows * D * E)
    xd1, part = mlp_forward(xd, part, dvec, dec_mlp_w)
    gyd, grad_predict, grad_pbias, loss_parts, grad_dec_fg, grad_dec_fb = head(
        core, inverse, xd1, part, dvec, pieces[14].reshape(1, -1), predict_w, target, band_ids, patch_weight, patch_count)
    grad_dec_up, grad_dec_down, part = mlp_backward(gyd, xd1, dvec, dec_mlp_w)
    gxd, grad_dec_attn, grad_dec_gb, grad_dec_bb, part = attn_backward(
        gyd, xd1, part, xd, dec_saved, dvec, dec_attn_w, patch_count, patch_count, DDH)
    one_d, one_e = shape((1, D), F32), shape((1, E), F32)
    grad_dec_ga, grad_dec_ba, grad_mask, grad_bridge, grad_enc_fg, grad_enc_fb, gye = run(
        functools.partial(between_kernel, keep_count),
        [one_e, one_e, one_e, shape((D, E // 2), BF16), one_d, one_d, shape((rows, D), F32)],
        [pltpu.VMEM((rows, E), BF16)],
        (core, gxd, xd, part, other_core(part), dvec, kept_column, hidden_rows, final_enc, x2, evec, bridge_w),
        3 * rows * D * E, 1)
    grad_enc_up, grad_enc_down, part = mlp_backward(gye, x1, evec, enc_mlp_w)
    gxe, grad_enc_attn, grad_enc_gb, grad_enc_bb, part = attn_backward(
        gye, x1, part, x0, enc_saved, evec, enc_attn_w, keep_count, group, DH)
    grad_enc_ga, grad_enc_ba, grad_ebias, grad_embed = run(
        enc_out_kernel,
        [one_d, one_d, one_d, shape((D, pixel_count // 2), BF16)],
        [], (core, gxe, x0, part, other_core(part), evec, kept_pixels), rows * D * pixel_count, 1)
    grad_vectors = jnp.concatenate(
        [grad_ebias, grad_enc_ga, grad_enc_ba, grad_enc_gb, grad_enc_bb, grad_enc_fg, grad_enc_fb, grad_mask,
         grad_dec_ga, grad_dec_ba, grad_dec_gb, grad_dec_bb, grad_dec_fg, grad_dec_fb, grad_pbias], axis=1).reshape(-1)
    vec_grads = jnp.pad(grad_vectors.reshape(size, vec_shard), ((0, 0), (0, vec_room - vec_shard)))
    sums, total_squares, loss = reduce_all(
        [grad_enc_attn, grad_enc_up, grad_enc_down, grad_dec_attn, grad_dec_up, grad_dec_down, grad_embed, grad_bridge,
         grad_predict, vec_grads.reshape(-1, 128)],
        (1.0,) * 9 + (0.5,), loss_parts)
    reduced = (
        jnp.stack(jnp.split(sums[0], 4, axis=1)),
        jnp.stack(sums[1:3]),
        jnp.stack(jnp.split(sums[3], 4, axis=1)),
        jnp.stack(sums[4:6]),
        join_cores(sums[6], core).T,
        join_cores(sums[7], core),
        join_cores(sums[8], core),
        sums[9].reshape(-1)[:vec_shard],
    )
    grad_norm = jnp.sqrt(total_squares)
    factor = CLIP / jnp.maximum(grad_norm, CLIP)
    news, new_firsts, new_seconds = ([], [], [])
    for position, master in enumerate(masters):
        is_vec = position == 7
        updated, first_new, second_new = adam_update(
            master,
            reduced[position] * factor,
            firsts[position],
            seconds[position],
            RATE_VEC if is_vec else RATE_MAT,
            0.0 if is_vec else DECAY_MAT,
        )
        news.append(updated)
        new_firsts.append(first_new)
        new_seconds.append(second_new)
    ema_attn = EMA_KEEP * ema_enc_attn + (1.0 - EMA_KEEP) * news[0]
    ema_mlp = EMA_KEEP * ema_enc_mlp + (1.0 - EMA_KEEP) * news[1]
    ema_embed = EMA_KEEP * ema_patch_embed + (1.0 - EMA_KEEP) * news[4]
    return (
        loss,
        band_weight,
        grad_norm,
        news[0],
        news[1],
        news[2],
        news[3],
        news[4],
        news[5],
        news[6],
        news[7],
        new_firsts[0],
        new_firsts[1],
        new_firsts[2],
        new_firsts[3],
        new_firsts[4],
        new_firsts[5],
        new_firsts[6],
        new_firsts[7],
        new_seconds[0],
        new_seconds[1],
        new_seconds[2],
        new_seconds[3],
        new_seconds[4],
        new_seconds[5],
        new_seconds[6],
        new_seconds[7],
        ema_attn,
        ema_mlp,
        ema_embed,
    )


def solution(mesh):
    return jax.shard_map(
        per_device,
        mesh=mesh,
        in_specs=(
            P("dp", None),
            P("dp", None),
            P("dp", None),
            P("dp", None),
            P("dp", None),
            P("dp"),
            P(None, "dp", "mp"),
            P(None, "dp", "mp"),
            P(None, "dp", "mp"),
            P(None, "dp", "mp"),
            P(None, "dp"),
            P("dp", None),
            P("dp", None),
            P("dp"),
            P(None, "dp", "mp"),
            P(None, "dp", "mp"),
            P(None, "dp", "mp"),
            P(None, "dp", "mp"),
            P(None, "dp"),
            P("dp", None),
            P("dp", None),
            P("dp"),
            P(None, "dp", "mp"),
            P(None, "dp", "mp"),
            P(None, "dp", "mp"),
            P(None, "dp", "mp"),
            P(None, "dp"),
            P("dp", None),
            P("dp", None),
            P("dp"),
            P(None, "dp", "mp"),
            P(None, "dp", "mp"),
            P(None, "dp"),
        ),
        out_specs=(
            P(),
            P(),
            P(),
            P(None, "dp", "mp"),
            P(None, "dp", "mp"),
            P(None, "dp", "mp"),
            P(None, "dp", "mp"),
            P(None, "dp"),
            P("dp", None),
            P("dp", None),
            P("dp"),
            P(None, "dp", "mp"),
            P(None, "dp", "mp"),
            P(None, "dp", "mp"),
            P(None, "dp", "mp"),
            P(None, "dp"),
            P("dp", None),
            P("dp", None),
            P("dp"),
            P(None, "dp", "mp"),
            P(None, "dp", "mp"),
            P(None, "dp", "mp"),
            P(None, "dp", "mp"),
            P(None, "dp"),
            P("dp", None),
            P("dp", None),
            P("dp"),
            P(None, "dp", "mp"),
            P(None, "dp", "mp"),
            P(None, "dp"),
        ),
        check_vma=False,
    )
```

```python
import functools
import math

import jax
import jax.numpy as jnp
from jax import lax
from jax.experimental import pallas as pl
from jax.experimental.pallas import tpu as pltpu
from jax.sharding import PartitionSpec as P

D = 1024
DH = 64
E = 512
DDH = 32
GRID = 16
NB = 3
STEP = 10


EPS_LN = 1e-06
EPS_C = 0.01
CLIP = 0.0002
BETA_ONE = 0.9
BETA_TWO = 0.999
ADAM_EPS = 1e-12
RATE_MAT = 0.06
RATE_VEC = 0.5
DECAY_MAT = 0.05
EMA_KEEP = 0.9
REF_GSD = 4.0


def split_vectors(flat_vec, enc_width, dec_width):
    lengths = [enc_width] * 7 + [dec_width] * 7
    pieces = []
    offset = 0
    for length in lengths:
        pieces.append(flat_vec[offset : offset + length])
        offset = offset + length
    pieces.append(flat_vec[offset:])
    return pieces


F32 = jnp.float32
BF16 = jnp.bfloat16
VMEM_LIMIT = 58 * 2**20
GELU_C = math.sqrt(2.0 / math.pi)


def dot_nn(left, right):
    return jnp.dot(left, right, preferred_element_type=F32)


def dot_nt(left, right):
    return lax.dot_general(left, right, (((1,), (1,)), ((), ())), preferred_element_type=F32)


def dot_tn(left, right):
    return lax.dot_general(left, right, (((0,), (0,)), ((), ())), preferred_element_type=F32)


def dot_exact(left, right):
    return jnp.dot(left, right, preferred_element_type=F32, precision=lax.Precision.HIGHEST)


def normalize(rows):
    centred = rows - jnp.mean(rows, axis=-1, keepdims=True)
    rstd = lax.rsqrt(jnp.mean(centred * centred, axis=-1, keepdims=True) + EPS_LN)
    return centred * rstd, rstd


def norm_back(grad, gain, unit, rstd):
    scaled = grad * gain
    mean_one = jnp.mean(scaled, axis=-1, keepdims=True)
    mean_two = jnp.mean(scaled * unit, axis=-1, keepdims=True)
    grad_in = rstd * (scaled - mean_one - unit * mean_two)
    return (
        grad_in,
        jnp.sum(grad * unit, axis=0, keepdims=True),
        jnp.sum(grad, axis=0, keepdims=True),
    )


def both(mine_ref, other_ref, rows):
    return mine_ref[rows, :].astype(F32) + other_ref[rows, :].astype(F32)


def gelu_parts(up):
    square = up * up
    bent = jnp.tanh(GELU_C * up * (1.0 + 0.044715 * square))
    half = 0.5 * (1.0 + bent)
    return square, bent, half


def group_mask(group, length):
    if group == length:
        return None
    row_image = lax.broadcasted_iota(jnp.int32, (group, group), 0) // length
    col_image = lax.broadcasted_iota(jnp.int32, (group, group), 1) // length
    return row_image == col_image


def attend(qkv_ref, mixed_ref, lse_ref, cols, width, head_dim, mask):
    scale = head_dim ** (-0.5)
    for head in range(width // head_dim):
        at = pl.ds(head * head_dim, head_dim)
        queries = qkv_ref[at, cols]
        keys = qkv_ref[pl.ds(width + head * head_dim, head_dim), cols]
        values = qkv_ref[pl.ds(2 * width + head * head_dim, head_dim), cols]
        scores = dot_tn(keys, queries) * scale
        if mask is not None:
            scores = jnp.where(mask, scores, -1e30)
        top = jnp.max(scores, axis=0, keepdims=True)
        weights = jnp.exp(scores - top)
        total = jnp.sum(weights, axis=0, keepdims=True)
        lse_ref[pl.ds(head, 1), cols] = top + jnp.log(total)
        soft = (weights * (1.0 / total)).astype(BF16)
        mixed_ref[at, cols] = dot_nn(values, soft).astype(BF16)


def attend_back(qkv_ref, grad_ref, lse_ref, out_ref, cols, width, head_dim, mask):
    scale = head_dim ** (-0.5)
    for head in range(width // head_dim):
        at = pl.ds(head * head_dim, head_dim)
        at_k = pl.ds(width + head * head_dim, head_dim)
        at_v = pl.ds(2 * width + head * head_dim, head_dim)
        queries, keys, values = qkv_ref[at, cols], qkv_ref[at_k, cols], qkv_ref[at_v, cols]
        grad = grad_ref[at, :]
        scores = dot_tn(keys, queries) * scale
        if mask is not None:
            scores = jnp.where(mask, scores, -1e30)
        soft = jnp.exp(scores - lse_ref[pl.ds(head, 1), cols])
        out_ref[at_v, cols] = dot_nt(grad, soft.astype(BF16)).astype(BF16)
        grad_soft = dot_tn(values, grad)
        inner = jnp.sum(soft * grad_soft, axis=0, keepdims=True)
        grad_scores = (soft * (grad_soft - inner)).astype(BF16)
        out_ref[at, cols] = (dot_nn(keys, grad_scores) * scale).astype(BF16)
        out_ref[at_k, cols] = (dot_nt(queries, grad_scores) * scale).astype(BF16)


def transposed_weights(attn_ref, flat_ref):
    width = attn_ref.shape[1] // 4
    for part in range(4):
        at = pl.ds(part * width, width)
        flat_ref[at, :] = attn_ref[:, at].T


def attention_rows(unit, vec_ref, flat_ref, qkv_ref, mixed_ref, lse_ref, part_ref, rows, head_dim, mask, attn_ref):
    width = mixed_ref.shape[0]
    low = (unit * vec_ref[1:2, :] + vec_ref[2:3, :]).astype(BF16)
    qkv_ref[:, rows] = dot_nt(flat_ref[: 3 * width, :], low).astype(BF16)
    attend(qkv_ref, mixed_ref, lse_ref, rows, width, head_dim, mask)
    part_ref[rows, :] = dot_nt(mixed_ref[:, rows].T, attn_ref[:, 3 * width :]).astype(BF16)


def enc_in_kernel(length, group, head_dim, pix_ref, kept_ref, table_ref, embed_ref, vec_ref, attn_ref,
                  x_ref, qkv_ref, mixed_ref, lse_ref, part_ref, pixk_ref, flat_ref):
    images, patches = table_ref.shape[0], pix_ref.shape[0] // table_ref.shape[0]
    side = table_ref.shape[1]
    transposed_weights(attn_ref, flat_ref)

    def pick(image, carry):
        rows = pl.ds(image * length, length)
        index = kept_ref[rows, :]
        hot = lax.broadcasted_iota(jnp.int32, (length, patches), 1) == index
        pixels = pix_ref[pl.ds(image * patches, patches), :]
        pixk_ref[rows, :] = dot_nn(hot.astype(BF16), pixels).astype(BF16)
        grid_at = lax.broadcasted_iota(jnp.int32, (length, side), 1)
        table = table_ref[image]
        half = table.shape[1]
        x_ref[rows, :half] = dot_exact((grid_at == index // side).astype(F32), table)
        x_ref[rows, half:] = dot_exact((grid_at == index % side).astype(F32), table)
        return carry

    lax.fori_loop(0, images, pick, 0)
    mask = group_mask(group, length)

    def step(number, carry):
        rows = pl.ds(pl.multiple_of(number * group, group), group)
        share = embed_ref.shape[2]
        rows_x = dot_nt(pixk_ref[rows, :share], embed_ref[0]) + dot_nt(pixk_ref[rows, share:], embed_ref[1])
        rows_x = rows_x + vec_ref[0:1, :] + x_ref[rows, :]
        x_ref[rows, :] = rows_x
        unit, _ = normalize(rows_x)
        attention_rows(unit, vec_ref, flat_ref, qkv_ref, mixed_ref, lse_ref, part_ref, rows, head_dim, mask, attn_ref)
        return carry

    lax.fori_loop(0, x_ref.shape[0] // group, step, 0)


def dec_in_kernel(length, head_dim, x1_ref, mine_ref, other_ref, evec_ref, bridge_ref, kept_ref, hidden_ref,
                  table_ref, vec_ref, attn_ref,
                  x2_ref, final_ref, x_ref, qkv_ref, mixed_ref, lse_ref, part_ref, flat_ref, latent_ref):
    images, side, half = table_ref.shape
    patches = side * side
    transposed_weights(attn_ref, flat_ref)
    every = pl.ds(0, x1_ref.shape[0])
    out = x1_ref[...] + both(mine_ref, other_ref, every)
    x2_ref[...] = out
    unit, _ = normalize(out)
    final = (unit * evec_ref[5:6, :] + evec_ref[6:7, :]).astype(BF16)
    final_ref[...] = final
    share = bridge_ref.shape[2]
    latent_ref[:, :share] = dot_nn(final, bridge_ref[0])
    latent_ref[:, share:] = dot_nn(final, bridge_ref[1])

    def step(image, carry):
        rows = pl.ds(pl.multiple_of(image * patches, patches), patches)
        hot = lax.broadcasted_iota(jnp.int32, (patches, length), 0) == kept_ref[pl.ds(image, 1), :]
        latent = latent_ref[pl.ds(image * length, length), :]
        table = table_ref[image]
        by_row = jnp.broadcast_to(table[:, None, :], (side, side, half)).reshape(patches, half)
        by_col = jnp.broadcast_to(table[None, :, :], (side, side, half)).reshape(patches, half)
        place = jnp.concatenate([by_row, by_col], axis=1)
        rows_x = dot_exact(hot.astype(F32), latent) + hidden_ref[rows, :] * vec_ref[0:1, :] + place
        x_ref[rows, :] = rows_x
        unit, _ = normalize(rows_x)
        attention_rows(unit, vec_ref, flat_ref, qkv_ref, mixed_ref, lse_ref, part_ref, rows, head_dim, None, attn_ref)
        return carry

    lax.fori_loop(0, images, step, 0)


def mlp_kernel(tile, x_ref, mine_ref, other_ref, vec_ref, up_ref, down_ref, x1_ref, part_ref, low_ref, acc_ref):
    number = pl.program_id(0)
    count = x_ref.shape[0] // tile

    def first(step, carry):
        rows = pl.ds(pl.multiple_of(step * tile, tile), tile)
        after = x_ref[rows, :] + both(mine_ref, other_ref, rows)
        x1_ref[rows, :] = after
        unit, _ = normalize(after)
        low_ref[rows, :] = (unit * vec_ref[3:4, :] + vec_ref[4:5, :]).astype(BF16)
        return carry

    @pl.when(number == 0)
    def _():
        lax.fori_loop(0, count, first, 0)
        acc_ref[...] = jnp.zeros_like(acc_ref)

    def step(piece, carry):
        rows = pl.ds(pl.multiple_of(piece * tile, tile), tile)
        up = dot_nn(low_ref[rows, :], up_ref[...])
        _, _, half = gelu_parts(up)
        acc_ref[rows, :] += dot_nt((up * half).astype(BF16), down_ref[...])
        return carry

    lax.fori_loop(0, count, step, 0)

    @pl.when(number == pl.num_programs(0) - 1)
    def _():
        part_ref[...] = acc_ref[...].astype(BF16)


def head_kernel(core_ref, inverse_ref, x1_ref, mine_ref, other_ref, vec_ref, bias_ref, predict_ref, target_ref,
                band_ref, weight_ref, gy_ref, glow_ref, gbias_ref, loss_ref, gain_ref, shift_ref, low_ref, gpred_ref):
    number = pl.program_id(0)

    @pl.when(number == 0)
    def _():
        for ref in (gpred_ref, gbias_ref, loss_ref, gain_ref, shift_ref):
            ref[...] = jnp.zeros_like(ref)

    every = pl.ds(0, x1_ref.shape[0])
    unit, rstd = normalize(x1_ref[...] + both(mine_ref, other_ref, every))
    gain = vec_ref[5:6, :]
    final = (unit * gain + vec_ref[6:7, :]).astype(BF16)
    share = gpred_ref.shape[1]
    predicted = jnp.concatenate([dot_nn(final, predict_ref[0]), dot_nn(final, predict_ref[1])], axis=1)
    mismatch = predicted + bias_ref[...] - target_ref[...].astype(F32)
    band = band_ref[...]
    level = jnp.where(band == 0, inverse_ref[0], jnp.where(band == 1, inverse_ref[1], inverse_ref[2]))
    level = level * weight_ref[...]
    square = mismatch * mismatch + EPS_C
    root = lax.rsqrt(square)
    loss_ref[...] += jnp.sum(level * (square * root), axis=0, keepdims=True)
    grad = level * (mismatch * root)
    gbias_ref[...] += jnp.sum(grad, axis=0, keepdims=True)
    low_ref[...] = grad.astype(BF16)
    columns = pl.ds(pl.multiple_of(core_ref[0] * share, share), share)
    gpred_ref[...] += dot_tn(final, low_ref[:, columns])
    grad_final = dot_nt(low_ref[:, :share], predict_ref[0]) + dot_nt(low_ref[:, share:], predict_ref[1])
    grad_in, gain_sum, shift_sum = norm_back(grad_final, gain, unit, rstd)
    gy_ref[...] = grad_in
    gain_ref[...] += gain_sum
    shift_ref[...] += shift_sum

    @pl.when(number == pl.num_programs(0) - 1)
    def _():
        glow_ref[...] = gpred_ref[...].astype(BF16)


def mlp_back_kernel(tile, gy_ref, x1_ref, vec_ref, up_ref, down_ref, gup_ref, gdown_ref, part_ref,
                    low_ref, lowt_ref, grad_ref, gradt_ref, gu_ref, z_ref, acc_ref):
    number = pl.program_id(0)
    count = x1_ref.shape[0] // tile

    def first(step, carry):
        rows = pl.ds(pl.multiple_of(step * tile, tile), tile)
        unit, _ = normalize(x1_ref[rows, :])
        low = (unit * vec_ref[3:4, :] + vec_ref[4:5, :]).astype(BF16)
        low_ref[rows, :] = low
        lowt_ref[:, rows] = low.T
        grad = gy_ref[rows, :].astype(BF16)
        grad_ref[rows, :] = grad
        gradt_ref[:, rows] = grad.T
        return carry

    @pl.when(number == 0)
    def _():
        lax.fori_loop(0, count, first, 0)
        acc_ref[...] = jnp.zeros_like(acc_ref)

    def step(piece, carry):
        rows = pl.ds(pl.multiple_of(piece * tile, tile), tile)
        up = dot_nn(low_ref[rows, :], up_ref[...])
        square, bent, half = gelu_parts(up)
        z_ref[rows, :] = (up * half).astype(BF16)
        slope = half + (0.5 * GELU_C) * up * (1.0 - bent * bent) * (1.0 + (3.0 * 0.044715) * square)
        grad_up = (dot_nn(grad_ref[rows, :], down_ref[...]) * slope).astype(BF16)
        gu_ref[rows, :] = grad_up
        acc_ref[rows, :] += dot_nt(grad_up, up_ref[...])
        return carry

    lax.fori_loop(0, count, step, 0)
    gup_ref[...] = dot_nn(lowt_ref[...], gu_ref[...]).astype(BF16)
    gdown_ref[...] = dot_nn(gradt_ref[...], z_ref[...]).astype(BF16)

    @pl.when(number == pl.num_programs(0) - 1)
    def _():
        part_ref[...] = acc_ref[...].astype(BF16)


def attn_back_kernel(length, group, head_dim, gy_ref, x1_ref, mine_ref, other_ref, x_ref, qkv_ref, mixed_ref, lse_ref,
                     vec_ref, attn_ref, gx_ref, grad_ref, gain_ref, shift_ref, part_ref,
                     flat_ref, lowt_ref, gradt_ref, gmix_ref, gqkv_ref):
    width = mixed_ref.shape[0]
    transposed_weights(attn_ref, flat_ref)
    gain_ref[...] = jnp.zeros_like(gain_ref)
    shift_ref[...] = jnp.zeros_like(shift_ref)
    mask = group_mask(group, length)

    def step(number, carry):
        rows = pl.ds(pl.multiple_of(number * group, group), group)
        unit, rstd = normalize(x1_ref[rows, :])
        grad_in, gain_sum, shift_sum = norm_back(both(mine_ref, other_ref, rows), vec_ref[3:4, :], unit, rstd)
        grad_in = grad_in + gy_ref[rows, :]
        gx_ref[rows, :] = grad_in
        gain_ref[...] += gain_sum
        shift_ref[...] += shift_sum
        low_grad = grad_in.astype(BF16)
        gradt_ref[:, rows] = low_grad.T
        gmix_ref[...] = dot_nt(flat_ref[3 * width :, :], low_grad).astype(BF16)
        attend_back(qkv_ref, gmix_ref, lse_ref, gqkv_ref, rows, width, head_dim, mask)
        part_ref[rows, :] = dot_nn(gqkv_ref[:, rows].T, flat_ref[: 3 * width, :]).astype(BF16)
        unit_a, _ = normalize(x_ref[rows, :])
        lowt_ref[:, rows] = (unit_a * vec_ref[1:2, :] + vec_ref[2:3, :]).astype(BF16).T
        return carry

    lax.fori_loop(0, x_ref.shape[0] // group, step, 0)
    grad_ref[:, : 3 * width] = dot_nt(lowt_ref[...], gqkv_ref[...]).astype(BF16)
    grad_ref[:, 3 * width :] = dot_nt(gradt_ref[...], mixed_ref[...]).astype(BF16)


def between_kernel(length, core_ref, gx_ref, x_ref, mine_ref, other_ref, vec_ref, kept_ref, hidden_ref, final_ref, x2_ref,
                   evec_ref, bridge_ref, gain_ref, shift_ref, mask_ref, gbridge_ref, egain_ref, eshift_ref, gy_ref,
                   latent_ref):
    images = kept_ref.shape[0] // length
    patches = x_ref.shape[0] // images
    for ref in (gain_ref, shift_ref, mask_ref):
        ref[...] = jnp.zeros_like(ref)

    def step(image, carry):
        rows = pl.ds(pl.multiple_of(image * patches, patches), patches)
        unit, rstd = normalize(x_ref[rows, :])
        grad_in, gain_sum, shift_sum = norm_back(both(mine_ref, other_ref, rows), vec_ref[1:2, :], unit, rstd)
        grad_in = grad_in + gx_ref[rows, :]
        gain_ref[...] += gain_sum
        shift_ref[...] += shift_sum
        mask_ref[...] += jnp.sum(grad_in * hidden_ref[rows, :], axis=0, keepdims=True)
        kept_rows = pl.ds(pl.multiple_of(image * length, length), length)
        hot = lax.broadcasted_iota(jnp.int32, (length, patches), 1) == kept_ref[kept_rows, :]
        latent_ref[kept_rows, :] = dot_nn(hot.astype(BF16), grad_in.astype(BF16)).astype(BF16)
        return carry

    lax.fori_loop(0, images, step, 0)
    share = gbridge_ref.shape[1]
    columns = pl.ds(pl.multiple_of(core_ref[0] * share, share), share)
    gbridge_ref[...] = dot_tn(final_ref[...], latent_ref[:, columns]).astype(BF16)
    grad_final = dot_nt(latent_ref[:, :share], bridge_ref[0]) + dot_nt(latent_ref[:, share:], bridge_ref[1])
    unit, rstd = normalize(x2_ref[...])
    gy_ref[...], egain_ref[...], eshift_ref[...] = norm_back(grad_final, evec_ref[5:6, :], unit, rstd)


def enc_out_kernel(core_ref, gx_ref, x_ref, mine_ref, other_ref, vec_ref, pixk_ref,
                   gain_ref, shift_ref, ebias_ref, gembed_ref):
    every = pl.ds(0, x_ref.shape[0])
    unit, rstd = normalize(x_ref[...])
    grad_in, gain_ref[...], shift_ref[...] = norm_back(both(mine_ref, other_ref, every), vec_ref[1:2, :], unit, rstd)
    grad_in = grad_in + gx_ref[...]
    ebias_ref[...] = jnp.sum(grad_in, axis=0, keepdims=True)
    share = gembed_ref.shape[1]
    columns = pl.ds(pl.multiple_of(core_ref[0] * share, share), share)
    gembed_ref[...] = dot_tn(grad_in.astype(BF16), pixk_ref[:, columns]).astype(BF16)


def shape(dims, dtype):
    return jax.ShapeDtypeStruct(dims, dtype)


def run(kernel, outs, scratch, args, flops, scalars=0):
    moved = sum(math.prod(a.shape) * a.dtype.itemsize for a in list(args) + list(outs))
    in_vmem = pl.BlockSpec(memory_space=pltpu.VMEM)
    return pl.pallas_call(
        kernel,
        out_shape=tuple(outs),
        in_specs=[pl.BlockSpec(memory_space=pltpu.SMEM)] * scalars + [in_vmem] * (len(args) - scalars),
        out_specs=tuple([in_vmem] * len(outs)),
        scratch_shapes=scratch,
        compiler_params=pltpu.CompilerParams(vmem_limit_bytes=VMEM_LIMIT),
        cost_estimate=pl.CostEstimate(flops=flops, bytes_accessed=moved, transcendentals=0),
    )(*args)


def other_core(block):
    return lax.ppermute(block, "mp", [(0, 1), (1, 0)])


def mlp_forward(x, mine, vec, stack):
    rows, width = x.shape
    hidden = stack.shape[1] // 2
    block = min(hidden, 512)
    tile = min(rows, 512)
    other = other_core(mine)
    whole = pl.BlockSpec((rows, width), lambda i: (0, 0))
    cols = pl.BlockSpec((width, block), lambda i: (0, i))
    later = pl.BlockSpec((width, block), lambda i: (0, i + hidden // block))
    return pl.pallas_call(
        functools.partial(mlp_kernel, tile),
        out_shape=(shape((rows, width), F32), shape((rows, width), BF16)),
        grid=(hidden // block,),
        in_specs=[whole] * 3 + [pl.BlockSpec((8, width), lambda i: (0, 0)), cols, later],
        out_specs=(whole, whole),
        scratch_shapes=[pltpu.VMEM((rows, width), BF16), pltpu.VMEM((rows, width), F32)],
        compiler_params=pltpu.CompilerParams(vmem_limit_bytes=VMEM_LIMIT),
        cost_estimate=pl.CostEstimate(flops=4 * rows * width * hidden, bytes_accessed=rows * width * 14 + width * hidden * 4,
                                      transcendentals=rows * hidden),
    )(x, mine, other, vec, stack, stack)


def mlp_backward(gy, x1, vec, stack):
    rows, width = x1.shape
    hidden = stack.shape[1] // 2
    block = min(hidden, 512)
    tile = min(rows, 256)
    whole = pl.BlockSpec((rows, width), lambda i: (0, 0))
    cols = pl.BlockSpec((width, block), lambda i: (0, i))
    later = pl.BlockSpec((width, block), lambda i: (0, i + hidden // block))
    return pl.pallas_call(
        functools.partial(mlp_back_kernel, tile),
        out_shape=(shape((width, hidden), BF16), shape((width, hidden), BF16), shape((rows, width), BF16)),
        grid=(hidden // block,),
        in_specs=[whole] * 2 + [pl.BlockSpec((8, width), lambda i: (0, 0)), cols, later],
        out_specs=(cols, cols, whole),
        scratch_shapes=[
            pltpu.VMEM((rows, width), BF16), pltpu.VMEM((width, rows), BF16),
            pltpu.VMEM((rows, width), BF16), pltpu.VMEM((width, rows), BF16),
            pltpu.VMEM((rows, block), BF16), pltpu.VMEM((rows, block), BF16),
            pltpu.VMEM((rows, width), F32)],
        compiler_params=pltpu.CompilerParams(vmem_limit_bytes=VMEM_LIMIT),
        cost_estimate=pl.CostEstimate(flops=10 * rows * width * hidden, bytes_accessed=rows * width * 10 + width * hidden * 8,
                                      transcendentals=rows * hidden),
    )(gy, x1, vec, stack, stack)


def head(core, inverse, x1, mine, vec, bias, predict, target, band, weight, patches):
    rows, width = x1.shape
    pixels = target.shape[1]
    share = pixels // 2
    other = other_core(mine)
    smem = pl.BlockSpec(memory_space=pltpu.SMEM)
    row_w = pl.BlockSpec((patches, width), lambda i: (i, 0))
    row_p = pl.BlockSpec((patches, pixels), lambda i: (i, 0))
    fix = lambda a, b: pl.BlockSpec((a, b), lambda i: (0, 0))
    return pl.pallas_call(
        head_kernel,
        out_shape=(shape((rows, width), F32), shape((width, share), BF16), shape((1, pixels), F32),
                   shape((1, pixels), F32), shape((1, width), F32), shape((1, width), F32)),
        grid=(rows // patches,),
        in_specs=[smem, smem, row_w, row_w, row_w, fix(8, width), fix(1, pixels), pl.BlockSpec((2, width, share), lambda i: (0, 0, 0)), row_p, row_p,
                  pl.BlockSpec((patches, 1), lambda i: (i, 0))],
        out_specs=(row_w, fix(width, share), fix(1, pixels), fix(1, pixels), fix(1, width), fix(1, width)),
        scratch_shapes=[pltpu.VMEM((patches, pixels), BF16), pltpu.VMEM((width, share), F32)],
        compiler_params=pltpu.CompilerParams(vmem_limit_bytes=VMEM_LIMIT),
        cost_estimate=pl.CostEstimate(flops=5 * rows * width * pixels, bytes_accessed=rows * (width * 12 + pixels * 6),
                                      transcendentals=rows * pixels),
    )(core, inverse, x1, mine, other, vec, bias, predict, target, band, weight)


def attn_backward(gy, x1, mine, x, saved, vec, attn, length, group, head_dim):
    qkv, mixed, lse = saved
    rows, width = x.shape
    local = mixed.shape[0]
    return run(
        functools.partial(attn_back_kernel, length, group, head_dim),
        [shape((rows, width), F32), shape((width, 4 * local), BF16),
         shape((1, width), F32), shape((1, width), F32), shape((rows, width), BF16)],
        [pltpu.VMEM((4 * local, width), BF16), pltpu.VMEM((width, rows), BF16), pltpu.VMEM((width, rows), BF16),
         pltpu.VMEM((local, group), BF16), pltpu.VMEM((3 * local, rows), BF16)],
        (gy, x1, mine, other_core(mine), x, qkv, mixed, lse, vec, attn),
        18 * rows * width * local)


def sine_table(gsd_values, feature_width, grid_side):
    quarter = feature_width // 4
    frequency = jnp.exp(-jnp.log(10000.0) * jnp.arange(quarter).astype(F32) / quarter)
    gsd_ratio = gsd_values.astype(F32)[:, None, None] / REF_GSD
    line = jnp.arange(grid_side, dtype=jnp.int32).astype(F32)
    arg = line[None, :, None] * gsd_ratio * frequency
    return jnp.concatenate([jnp.sin(arg), jnp.cos(arg)], axis=-1)


def dp_bits():
    return lax.axis_size("dp").bit_length() - 1


def orders():
    bits = dp_bits()
    high = list(range(bits - 1, 1, -1))
    return (high + [0, 1], high + [1, 0])


def swap(block, bit):
    size = lax.axis_size("dp")
    return lax.ppermute(block, "dp", [(i, i ^ (1 << bit)) for i in range(size)])


def my_bit(bit):
    return (lax.axis_index("dp") >> bit) & 1


def gather_dp(block, axis, order):
    lead, rest = (block.shape[:axis], block.shape[axis:])
    done = []
    cur = block
    for bit in order:
        other = swap(cur, bit)
        mine = my_bit(bit) == 1
        place = axis + sum(1 for b in done if b > bit)
        cur = jnp.stack([jnp.where(mine, other, cur), jnp.where(mine, cur, other)], axis=place)
        done.append(bit)
    return cur.reshape(lead + (rest[0] * lax.axis_size("dp"),) + rest[1:])


def reduce_dp(block, axis, order, wire):
    bits = dp_bits()
    lead, rest = (block.shape[:axis], block.shape[axis:])
    shard = rest[0] // lax.axis_size("dp")
    cur = block.reshape(lead + (2,) * bits + (shard,) + rest[1:])
    left = list(range(bits - 1, -1, -1))
    for bit in reversed(order):
        place = axis + left.index(bit)
        mine = my_bit(bit)
        keep = lax.dynamic_index_in_dim(cur, mine, place, keepdims=False)
        give = lax.dynamic_index_in_dim(cur, 1 - mine, place, keepdims=False)
        other = swap(give.astype(wire), bit)
        cur = keep.astype(F32) + other.astype(F32)
        left.remove(bit)
    return cur


def join_cores(mine, core):
    other = other_core(mine)
    return jnp.concatenate([jnp.where(core == 0, mine, other), jnp.where(core == 0, other, mine)], axis=1)


def total_dp(value):
    for bit in range(dp_bits()):
        value = value + swap(value, bit)
    return value


def place_of():
    index = lax.axis_index("dp")
    core = lax.axis_index("mp")
    low, high = lax.rem(index, 4), index // 4
    bit_x, bit_y = lax.rem(low, 2), low // 2
    low_x, low_y = low + 1 - 2 * bit_x, low + 2 - 4 * bit_y
    return core, low, high, low_x, low_y


def greet(partners):
    barrier = pltpu.get_barrier_semaphore()
    for partner in partners:
        pl.semaphore_signal(barrier, inc=1, device_id=partner, device_id_type=pl.DeviceIdType.MESH)
    pl.semaphore_wait(barrier, len(partners))


def blocks_of(widths, limit):
    found = []
    for number, width in enumerate(widths):
        start = 0
        while start < width:
            size = min(limit, width - start)
            found.append((number, start, size))
            start += size
    return found


def remote(source, target, send, receive, device):
    return pltpu.make_async_remote_copy(
        src_ref=source, dst_ref=target, send_sem=send, recv_sem=receive,
        device_id=device, device_id_type=pl.DeviceIdType.MESH)


def small_gather_kernel(size, part_ref, full_ref, send_sem, receive_sem):
    index, core = lax.axis_index("dp"), lax.axis_index("mp")
    peers = [(lax.rem(index + k, size), core) for k in range(1, size)]
    greet(peers)
    full_ref[index] = part_ref[...]
    copies = [remote(part_ref, full_ref.at[index], send_sem.at[k], receive_sem.at[k], peers[k])
              for k in range(size - 1)]
    for copy in copies:
        copy.start()
    for copy in copies:
        copy.wait()


def small_gather(part):
    size = lax.axis_size("dp")
    in_vmem = pl.BlockSpec(memory_space=pltpu.VMEM)
    dma = pltpu.SemaphoreType.DMA
    return pl.pallas_call(
        functools.partial(small_gather_kernel, size),
        out_shape=shape((size,) + part.shape, part.dtype),
        in_specs=[in_vmem],
        out_specs=in_vmem,
        scratch_shapes=[dma((size - 1,)), dma((size - 1,))],
        compiler_params=pltpu.CompilerParams(collective_id=2, has_side_effects=True),
    )(part)


def total_blocks(block_ref, near_ref, far_ref, sems, low, high, core, highs, stage):
    send, receive = sems
    if stage == 0:
        spots = [(high * 4 + lax.rem(low + k, 4), core) for k in range(1, 4)]
        return [remote(block_ref, near_ref.at[low], send.at[k], receive.at[k], spots[k]) for k in range(3)]
    spots = [(lax.rem(high + k, highs) * 4 + low, core) for k in range(1, highs)]
    return [remote(block_ref, far_ref.at[high], send.at[3 + k], receive.at[3 + k], spots[k]) for k in range(highs - 1)]


def forward_kernel(highs, shared, groups, count, length, group, head_dim, *refs):
    shards, refs = refs[:count], refs[count:]
    pix_ref, band_ref, weight_ref, kept_ref, table_ref, vec_ref = refs[:6]
    fulls, refs = refs[6 : 6 + count], refs[6 + count :]
    x_ref, qkv_ref, mixed_ref, lse_ref, pixk_ref, x1_ref, last_ref, far_out_ref, counts_ref = refs[:9]
    refs = refs[9:]
    (bands_v, embed_v, attn_v, mlp_v, flat_ref, part_ref, other_ref, low_ref, acc_ref, block_ref, near_ref,
     far_ref) = refs[:12]
    (own_sem, zs_sem, zr_sem, cs_sem, cr_sem, fs_sem, fr_sem, ms_sem, mr_sem, load_sem, xs_sem, xr_sem, ts_sem,
     tr_sem) = refs[12:]
    core, low, high, low_x, low_y = place_of()
    at_x, at_y = (high * 4 + low_x, core), (high * 4 + low_y, core)
    at_high = [(lax.rem(high + k, highs) * 4 + low, core) for k in range(1, highs)]
    sibling = (high * 4 + low, 1 - core)
    near = [(high * 4 + lax.rem(low + k, 4), core) for k in range(1, 4)]
    greet([sibling] + near + at_high)

    def full(at):
        number, start, size = groups[at]
        ref = fulls[number].at[core] if shared[number] else fulls[number]
        return ref, pl.ds(start, size)

    def first(at):
        ref, cols = full(at)
        shard = shards[groups[at][0]].at[:, cols]
        mine = ref.at[high, low, :, cols]
        copies = [pltpu.make_async_copy(shard, mine, own_sem.at[at])]
        for k in range(1, highs):
            copies.append(remote(shard, mine, zs_sem.at[at, k - 1], zr_sem.at[at, k - 1], at_high[k - 1]))
        return copies

    def column(at):
        ref, cols = full(at)
        part = ref.at[:, low, :, cols]
        return [remote(part, part, cs_sem.at[at, 0], cr_sem.at[at, 0], at_x),
                remote(part, part, cs_sem.at[at, 1], cr_sem.at[at, 1], at_y)]

    def forward(at):
        ref, cols = full(at)
        which, device = (low_x, at_y) if at % 2 == 0 else (low_y, at_x)
        part = ref.at[:, which, :, cols]
        return remote(part, part, fs_sem.at[at], fr_sem.at[at], device)

    def swap(number):
        part = fulls[number].at[core]
        return remote(part, part, ms_sem.at[number], mr_sem.at[number], sibling)

    def exchange(at, source, target):
        return remote(source, target, xs_sem.at[at], xr_sem.at[at], sibling)

    total = len(groups)
    pairs = (total + 1) // 2
    in_pair = lambda pair: [at for at in (2 * pair, 2 * pair + 1) if at < total]
    pair_of = lambda number: max(at for at in range(total) if groups[at][0] == number) // 2
    images, side = table_ref.shape[0], table_ref.shape[1]
    patches = pix_ref.shape[0] // images
    width = mixed_ref.shape[0]
    mask = group_mask(group, length)

    def pick(image, carry):
        rows = pl.ds(image * length, length)
        index = kept_ref[rows, :]
        hot = lax.broadcasted_iota(jnp.int32, (length, patches), 1) == index
        pixels = pix_ref[pl.ds(image * patches, patches), :]
        pixk_ref[rows, :] = dot_nn(hot.astype(BF16), pixels).astype(BF16)
        grid_at = lax.broadcasted_iota(jnp.int32, (length, side), 1)
        table = table_ref[image]
        half = table.shape[1]
        x_ref[rows, :half] = dot_exact((grid_at == index // side).astype(F32), table)
        x_ref[rows, half:] = dot_exact((grid_at == index % side).astype(F32), table)
        return carry

    def tally(image, carry):
        rows = pl.ds(image * patches, patches)
        band, weight = bands_v[rows, :], weight_ref[rows, :]
        for level in range(NB):
            row = jnp.sum(jnp.where(band == level, weight, 0.0), axis=0, keepdims=True)
            for start in range(0, row.shape[1], 128):
                block_ref[level : level + 1, :] += row[:, start : start + 128]
        return carry

    def rows_step(number, carry):
        rows = pl.ds(pl.multiple_of(number * group, group), group)
        share = embed_v.shape[-1]
        embed = lambda half: embed_v[half].reshape(-1, share)
        rows_x = dot_nt(pixk_ref[rows, :share], embed(0)) + dot_nt(pixk_ref[rows, share:], embed(1))
        rows_x = rows_x + vec_ref[0:1, :] + x_ref[rows, :]
        x_ref[rows, :] = rows_x
        unit, _ = normalize(rows_x)
        low_a = (unit * vec_ref[1:2, :] + vec_ref[2:3, :]).astype(BF16)
        qkv_ref[:, rows] = dot_nt(flat_ref[: 3 * width, :], low_a).astype(BF16)
        attend(qkv_ref, mixed_ref, lse_ref, rows, width, head_dim, mask)
        part_ref[rows, :] = dot_nn(mixed_ref[:, rows].T, flat_ref[3 * width :, :]).astype(BF16)
        return carry

    def mlp_first():
        after = x_ref[...] + both(part_ref, other_ref, pl.ds(0, x_ref.shape[0]))
        x1_ref[...] = after
        unit, _ = normalize(after)
        low_ref[...] = (unit * vec_ref[3:4, :] + vec_ref[4:5, :]).astype(BF16)
        acc_ref[...] = jnp.zeros_like(acc_ref)

    def mlp_block(piece, carry):
        size = 512
        hidden = mlp_v.shape[-1] // 2
        start = pl.multiple_of(piece * size, size)
        wide = x_ref.shape[1]
        up = dot_nn(low_ref[...], mlp_v[:, :, :, pl.ds(start, size)].reshape(wide, size))
        _, _, half = gelu_parts(up)
        down = mlp_v[:, :, :, pl.ds(pl.multiple_of(hidden + start, size), size)].reshape(wide, size)
        acc_ref[...] += dot_nt((up * half).astype(BF16), down)
        return carry

    load_bands = pltpu.make_async_copy(band_ref, bands_v, load_sem.at[0])
    load_attn = pltpu.make_async_copy(fulls[1], attn_v, load_sem.at[1])
    load_embed = pltpu.make_async_copy(fulls[0], embed_v, load_sem.at[2])
    load_mlp = pltpu.make_async_copy(fulls[2], mlp_v, load_sem.at[3])
    stages = functools.partial(total_blocks, block_ref, near_ref, far_ref, (ts_sem, tr_sem), low, high, core, highs)
    embed_at, attn_at, mlp_at = pair_of(0) + 3, pair_of(1) + 3, pair_of(2) + 3
    row_groups = x_ref.shape[0] // group
    swapped = set()
    for step in range(pairs + 3):
        if step < pairs:
            for at in in_pair(step):
                for copy in first(at):
                    copy.start()
        if 0 <= step - 1 < pairs:
            for at in in_pair(step - 1):
                for copy in first(at):
                    copy.wait()
                for copy in column(at):
                    copy.start()
        if 0 <= step - 2 < pairs:
            for at in in_pair(step - 2):
                column(at)[at % 2].wait()
                forward(at).start()
        if 0 <= step - 3 < pairs:
            for at in in_pair(step - 3):
                column(at)[1 - at % 2].wait()
                forward(at).wait()
        for number in range(count):
            if shared[number] and number not in swapped and pair_of(number) + 3 <= step:
                swap(number).start()
                swapped.add(number)
        if step == 0:
            load_bands.start()
            lax.fori_loop(0, images, pick, 0)
            block_ref[...] = jnp.zeros_like(block_ref)
            load_bands.wait()
            lax.fori_loop(0, images, tally, 0)
            near_ref[low] = block_ref[...]
            for copy in stages(0):
                copy.start()
        if step == 1:
            for copy in stages(0):
                copy.wait()
            block_ref[...] = (near_ref[0] + near_ref[1]) + (near_ref[2] + near_ref[3])
            far_ref[high] = block_ref[...]
            for copy in stages(1):
                copy.start()
        if step == 2:
            for copy in stages(1):
                copy.wait()
            counts = far_ref[0]
            for k in range(1, highs):
                counts = counts + far_ref[k]
            counts_ref[...] = counts
        if step == attn_at:
            swap(0).wait()
            load_attn.start()
            load_embed.start()
            load_attn.wait()
            for part in range(4):
                at = pl.ds(part * width, width)
                flat_ref[at, :] = attn_v[:, :, :, at].reshape(-1, width).T
            load_embed.wait()
        if attn_at <= step < mlp_at - 1:
            share = -(-row_groups // (mlp_at - 1 - attn_at))
            start, stop = (step - attn_at) * share, min((step - attn_at + 1) * share, row_groups)
            if start < stop:
                lax.fori_loop(start, stop, rows_step, 0)
                if stop == row_groups:
                    exchange(0, part_ref, other_ref).start()
        if step == mlp_at:
            load_mlp.start()
            exchange(0, part_ref, other_ref).wait()
            mlp_first()
            load_mlp.wait()
            lax.fori_loop(0, mlp_v.shape[-1] // 1024, mlp_block, 0)
            last_ref[...] = acc_ref[...].astype(BF16)
            exchange(1, last_ref, far_out_ref).start()
    exchange(1, last_ref, far_out_ref).wait()
    for number in range(1, count):
        if shared[number]:
            swap(number).wait()


def forward_all(shards, shared, pixels, band_ids, patch_weight, kept_column, table, evec):
    size = lax.axis_size("dp")
    highs = size // 4
    count = len(shards)
    groups = blocks_of([a.shape[1] for a in shards], 512)
    total = len(groups)
    rows, wide, local = kept_column.shape[0], evec.shape[1], shards[1].shape[1] // 4
    images = table.shape[0]
    length = rows // images
    group = 2 * length
    fulls = []
    for shard, split in zip(shards, shared):
        dims = (highs, 4) + shard.shape
        fulls.append(shape((2,) + dims if split else dims, shard.dtype))
    outs = [shape((rows, wide), F32), shape((3 * local, rows), BF16), shape((local, rows), BF16),
            shape((local // DH, rows), F32), shape((rows, pixels.shape[1]), BF16), shape((rows, wide), F32),
            shape((rows, wide), BF16), shape((rows, wide), BF16), shape((8, 128), F32)]
    dma = pltpu.SemaphoreType.DMA
    small = (8, 128)
    in_vmem = pl.BlockSpec(memory_space=pltpu.VMEM)
    any_space = pl.BlockSpec(memory_space=pl.ANY)
    result = pl.pallas_call(
        functools.partial(forward_kernel, highs, shared, groups, count, length, group, DH),
        out_shape=tuple(fulls + outs),
        in_specs=[any_space] * count + [in_vmem, any_space] + [in_vmem] * 4,
        out_specs=tuple([any_space] * count + [in_vmem] * len(outs)),
        scratch_shapes=[
            pltpu.VMEM(band_ids.shape, jnp.int32), pltpu.VMEM(fulls[0].shape, BF16), pltpu.VMEM(fulls[1].shape, BF16),
            pltpu.VMEM(fulls[2].shape, BF16), pltpu.VMEM((4 * local, wide), BF16), pltpu.VMEM((rows, wide), BF16),
            pltpu.VMEM((rows, wide), BF16), pltpu.VMEM((rows, wide), BF16), pltpu.VMEM((rows, wide), F32),
            pltpu.VMEM(small, F32), pltpu.VMEM((4,) + small, F32), pltpu.VMEM((highs,) + small, F32),
            dma((total,)), dma((total, highs - 1)), dma((total, highs - 1)), dma((total, 2)), dma((total, 2)),
            dma((total,)), dma((total,)), dma((count,)), dma((count,)), dma((4,)), dma((2,)), dma((2,)),
            dma((highs + 2,)), dma((highs + 2,))],
        compiler_params=pltpu.CompilerParams(collective_id=0, has_side_effects=True, vmem_limit_bytes=VMEM_LIMIT),
        cost_estimate=pl.CostEstimate(flops=0, bytes_accessed=sum(a.size * a.dtype.itemsize * size for a in shards),
                                      transcendentals=0),
    )(*shards, pixels, band_ids, patch_weight, kept_column, table, evec)
    weights = [full.reshape(((2,) if split else ()) + (size * shard.shape[0], shard.shape[1]))
               for full, split, shard in zip(result[:count], shared, shards)]
    return weights, result[count:]


def gather_all(shards, shared):
    order_a, order_b = orders()
    fulls = []
    for number, shard in enumerate(shards):
        full = gather_dp(shard, 0, (order_a, order_b)[number % 2])
        if shared[number]:
            other, zero = other_core(full), lax.axis_index("mp") == 0
            full = jnp.stack([jnp.where(zero, full, other), jnp.where(zero, other, full)])
        fulls.append(full)
    return fulls


def reduce_kernel(highs, weights, groups, count, loss_ref, *refs):
    grads, outs, sums_ref = refs[:count], refs[count : 2 * count], refs[2 * count]
    refs = refs[2 * count + 1 :]
    total = len(groups)
    buffers, refs = refs[: 6 * total], refs[6 * total :]
    plane_ref, norm_ref, near_ref, far_ref = refs[:4]
    load_sem, as_sem, ar_sem, bs_sem, br_sem, zs_sem, zr_sem, ns_sem, nr_sem, hs_sem, hr_sem = refs[4:]
    core, low, high, low_x, low_y = place_of()
    low_d = 3 - low
    spot = low * 2 + core
    dev_x, dev_y = (high * 4 + low_x, core), (high * 4 + low_y, core)
    at_high = [(lax.rem(high + k, highs) * 4 + low, core) for k in range(1, highs)]
    near = [(high * 4 + lax.rem(spot + k, 8) // 2, lax.rem(lax.rem(spot + k, 8), 2)) for k in range(1, 8)]
    greet(near + at_high)

    def route(at):
        if at % 2 == 0:
            return low_y, dev_y, low_x, dev_x
        return low_x, dev_x, low_y, dev_y

    def grad(at, which):
        number, start, size = groups[at]
        return grads[number].at[:, which, :, pl.ds(start, size)]

    def loads(at):
        _, _, low_two, _ = route(at)
        return [pltpu.make_async_copy(grad(at, low_two), buffers[6 * at], load_sem.at[at, 0]),
                pltpu.make_async_copy(grad(at, low), buffers[6 * at + 1], load_sem.at[at, 1])]

    def one(at):
        low_one, dev_one, _, _ = route(at)
        return [remote(grad(at, low_d), buffers[6 * at + 2], as_sem.at[at, 0], ar_sem.at[at, 0], dev_one),
                remote(grad(at, low_one), buffers[6 * at + 3], as_sem.at[at, 1], ar_sem.at[at, 1], dev_one)]

    def two(at):
        return remote(buffers[6 * at], buffers[6 * at + 4], bs_sem.at[at], br_sem.at[at], route(at)[3])

    def three(at):
        return [remote(buffers[6 * at + 1].at[lax.rem(high + k, highs)], buffers[6 * at + 5].at[k - 1],
                       zs_sem.at[at, k - 1], zr_sem.at[at, k - 1], at_high[k - 1]) for k in range(1, highs)]

    pairs = (total + 1) // 2
    in_pair = lambda pair: [at for at in (2 * pair, 2 * pair + 1) if at < total]
    norm_ref[...] = jnp.zeros_like(norm_ref)
    kept = {}
    for step in range(pairs + 3):
        if step < pairs:
            for at in in_pair(step):
                for copy in one(at) + loads(at):
                    copy.start()
        if 0 <= step - 1 < pairs:
            for at in in_pair(step - 1):
                mine = buffers[6 * at]
                loads(at)[0].wait()
                one(at)[0].wait()
                mine[...] = (mine[...].astype(F32) + buffers[6 * at + 2][...].astype(F32)).astype(mine.dtype)
                two(at).start()
        if 0 <= step - 2 < pairs:
            for at in in_pair(step - 2):
                number, start, size = groups[at]
                mine = buffers[6 * at + 1]
                loads(at)[1].wait()
                one(at)[1].wait()
                two(at).wait()
                rows = mine.shape[1]
                plane = plane_ref.at[at % 4, :, :rows, :size]
                plane[...] = (mine[...].astype(F32) + buffers[6 * at + 3][...].astype(F32)
                              + buffers[6 * at + 4][...].astype(F32))
                outs[number][:, pl.ds(start, size)] = plane[high]
                mine[...] = plane[...].astype(mine.dtype)
                for copy in three(at):
                    copy.start()
        if 0 <= step - 3 < pairs:
            for at in in_pair(step - 3):
                number, start, size = groups[at]
                for copy in three(at):
                    copy.wait()
                cols = pl.ds(start, size)
                done = outs[number][:, cols]
                for k in range(highs - 1):
                    done = done + buffers[6 * at + 5][k].astype(F32)
                outs[number][:, cols] = done
                norm_ref[0:1, 0:1] += weights[number] * jnp.sum(done * done, keepdims=True)
    norm_ref[1:2, 0:1] = jnp.sum(loss_ref[...], keepdims=True)
    near_ref[spot] = norm_ref[...]
    copies = [remote(norm_ref, near_ref.at[spot], ns_sem.at[k], nr_sem.at[k], near[k]) for k in range(7)]
    for copy in copies:
        copy.start()
    for copy in copies:
        copy.wait()
    local = near_ref[0]
    for k in range(1, 8):
        local = local + near_ref[k]
    norm_ref[...] = local
    far_ref[high] = local
    copies = [remote(norm_ref, far_ref.at[high], hs_sem.at[k], hr_sem.at[k], at_high[k]) for k in range(highs - 1)]
    for copy in copies:
        copy.start()
    for copy in copies:
        copy.wait()
    every = far_ref[0]
    for k in range(1, highs):
        every = every + far_ref[k]
    sums_ref[...] = every


def reduce_all(grads, weights, loss_parts):
    size = lax.axis_size("dp")
    highs = size // 4
    if any((a.shape[0] // size) % 16 for a in grads if a.dtype == BF16):
        order_a, order_b = orders()
        outs = [reduce_dp(a, 0, (order_a, order_b)[number % 2], a.dtype) for number, a in enumerate(grads)]
        sums = jnp.stack([sum(w * jnp.sum(a * a) for w, a in zip(weights, outs)), jnp.sum(loss_parts)])
        sums = total_dp(sums)
        sums = sums + other_core(sums)
        return outs, sums[0], 0.5 * sums[1]
    count = len(grads)
    groups = blocks_of([a.shape[1] for a in grads], 512)
    shards = [a.shape[0] // size for a in grads]
    total = len(groups)
    buffers = []
    for number, _, width in groups:
        piece = pltpu.VMEM((highs, shards[number], width), grads[number].dtype)
        buffers += [piece] * 5 + [pltpu.VMEM((highs - 1, shards[number], width), grads[number].dtype)]
    dma = pltpu.SemaphoreType.DMA
    small = (8, 128)
    in_vmem = pl.BlockSpec(memory_space=pltpu.VMEM)
    any_space = pl.BlockSpec(memory_space=pl.ANY)
    result = pl.pallas_call(
        functools.partial(reduce_kernel, highs, weights, groups, count),
        out_shape=tuple([shape((rows, a.shape[1]), F32) for rows, a in zip(shards, grads)] + [shape(small, F32)]),
        in_specs=[in_vmem] + [any_space] * count,
        out_specs=tuple([in_vmem] * (count + 1)),
        scratch_shapes=buffers + [
            pltpu.VMEM((4, highs, max(shards), max(g[2] for g in groups)), F32), pltpu.VMEM(small, F32),
            pltpu.VMEM((8,) + small, F32), pltpu.VMEM((highs,) + small, F32),
            dma((total, 2)), dma((total, 2)), dma((total, 2)), dma((total,)), dma((total,)),
            dma((total, highs - 1)), dma((total, highs - 1)), dma((7,)), dma((7,)), dma((highs - 1,)), dma((highs - 1,))],
        compiler_params=pltpu.CompilerParams(collective_id=1, has_side_effects=True, vmem_limit_bytes=VMEM_LIMIT),
        cost_estimate=pl.CostEstimate(flops=0, bytes_accessed=sum(a.size * a.dtype.itemsize for a in grads),
                                      transcendentals=0),
    )(loss_parts, *[a.reshape(highs, 4, rows, a.shape[1]) for rows, a in zip(shards, grads)])
    return list(result[:count]), result[count][0, 0], 0.5 * result[count][1, 0]


def adam_update(master, gradient, first_old, second_old, step_rate, decay_rate):
    first_new = BETA_ONE * first_old + (1.0 - BETA_ONE) * gradient
    second_new = BETA_TWO * second_old + (1.0 - BETA_TWO) * gradient * gradient
    first_hat = first_new / (1.0 - BETA_ONE**STEP)
    second_hat = second_new / (1.0 - BETA_TWO**STEP)
    updated = master - step_rate * (
        first_hat / (jnp.sqrt(second_hat) + ADAM_EPS) + decay_rate * master
    )
    return (updated, first_new, second_new)


def per_device(
    pixels,
    target,
    band_ids,
    kept_index,
    intersection,
    gsd_scale,
    enc_attn,
    enc_mlp,
    dec_attn,
    dec_mlp,
    patch_embed,
    bridge,
    predict,
    vectors,
    first_enc_attn,
    first_enc_mlp,
    first_dec_attn,
    first_dec_mlp,
    first_patch_embed,
    first_bridge,
    first_predict,
    first_vectors,
    second_enc_attn,
    second_enc_mlp,
    second_dec_attn,
    second_dec_mlp,
    second_patch_embed,
    second_bridge,
    second_predict,
    second_vectors,
    ema_enc_attn,
    ema_enc_mlp,
    ema_patch_embed,
):
    masters = (enc_attn, enc_mlp, dec_attn, dec_mlp, patch_embed, bridge, predict, vectors)
    firsts = (
        first_enc_attn,
        first_enc_mlp,
        first_dec_attn,
        first_dec_mlp,
        first_patch_embed,
        first_bridge,
        first_predict,
        first_vectors,
    )
    seconds = (
        second_enc_attn,
        second_enc_mlp,
        second_dec_attn,
        second_dec_mlp,
        second_patch_embed,
        second_bridge,
        second_predict,
        second_vectors,
    )
    images, keep_count = kept_index.shape
    patch_count = intersection.shape[1]
    patch_index = jnp.arange(patch_count, dtype=jnp.int32)
    kept_flags = jnp.any(kept_index[:, :, None] == patch_index[None, None, :], axis=1).astype(
        jnp.float32
    )
    patch_weight = ((1.0 - kept_flags) * (1.0 - 0.5 * intersection.astype(jnp.float32))).reshape(
        -1, 1
    )
    core_at = lax.axis_index("mp")
    size = lax.axis_size("dp")
    low = jnp.bfloat16

    def flat(stack):
        return jnp.concatenate([part.astype(low) for part in stack], axis=1)

    def core_half(block):
        return lax.dynamic_slice_in_dim(block, core_at * (block.shape[1] // 2), block.shape[1] // 2, 1).astype(low)

    vec_shard = vectors.shape[0]
    vec_room = -(-vec_shard // 1024) * 1024
    vec_rows = jnp.pad(lax.reduce_precision(vectors, 8, 7), (0, vec_room - vec_shard)).reshape(-1, 128)
    whole_tiles = patch_embed.shape[1] % 16 == 0 and dec_attn.shape[1] % 16 == 0
    vec_full = small_gather(vec_rows) if whole_tiles else gather_dp(vec_rows, 0, orders()[0])
    pieces = split_vectors(vec_full.reshape(size, vec_room)[:, :vec_shard].reshape(-1), D, E)
    evec = jnp.stack(pieces[:7] + [jnp.zeros_like(pieces[0])])
    dvec = jnp.stack(pieces[7:14] + [jnp.zeros_like(pieces[7])])
    kept_column = kept_index.reshape(-1, 1)
    rows, rows_d = images * keep_count, images * patch_count
    pixel_count = pixels.shape[1]
    group = 2 * keep_count
    shards = [core_half(patch_embed.T), flat(enc_attn), flat(enc_mlp), flat(dec_attn), flat(dec_mlp), core_half(bridge),
              core_half(predict)]
    shared = (True, False, False, False, False, True, True)
    enc_table = sine_table(gsd_scale, D, GRID)
    if whole_tiles:
        weights, results = forward_all(shards, shared, pixels, band_ids, patch_weight, kept_column, enc_table, evec)
        embed_w, enc_attn_w, enc_mlp_w, dec_attn_w, dec_mlp_w, bridge_w, predict_w = weights
        x0, *enc_saved, kept_pixels, x1, part, other, counts = results
        band_weight = jnp.sum(counts[:NB], axis=1)
    else:
        weights = gather_all(shards, shared)
        embed_w, enc_attn_w, enc_mlp_w, dec_attn_w, dec_mlp_w, bridge_w, predict_w = weights
        local = enc_attn_w.shape[1] // 4
        band_weight = total_dp(jnp.stack([
            jnp.sum(jnp.where(band_ids == level, patch_weight, 0.0)) for level in range(NB)]))
        x0, *enc_saved, part, kept_pixels = run(
            functools.partial(enc_in_kernel, keep_count, group, DH),
            [shape((rows, D), F32), shape((3 * local, rows), BF16), shape((local, rows), BF16),
             shape((local // DH, rows), F32), shape((rows, D), BF16), shape((rows, pixel_count), BF16)],
            [pltpu.VMEM((4 * local, D), BF16)],
            (pixels, kept_column, enc_table, embed_w, evec, enc_attn_w),
            rows * D * (2 * pixel_count + 8 * local))
        x1, part = mlp_forward(x0, part, evec, enc_mlp_w)
        other = other_core(part)
    inverse = 1.0 / band_weight
    core = lax.axis_index("mp").astype(jnp.int32).reshape(1)
    hidden_rows = (1.0 - kept_flags).reshape(-1, 1)
    local_d = dec_attn_w.shape[1] // 4
    x2, final_enc, xd, *dec_saved, part = run(
        functools.partial(dec_in_kernel, keep_count, DDH),
        [shape((rows, D), F32), shape((rows, D), BF16), shape((rows_d, E), F32), shape((3 * local_d, rows_d), BF16),
         shape((local_d, rows_d), BF16), shape((local_d // DDH, rows_d), F32), shape((rows_d, E), BF16)],
        [pltpu.VMEM((4 * local_d, E), BF16), pltpu.VMEM((rows, E), F32)],
        (x1, part, other, evec, bridge_w, kept_index, hidden_rows, sine_table(gsd_scale, E, GRID), dvec,
         dec_attn_w),
        rows_d * E * 8 * local_d + 2 * rows * D * E)
    xd1, part = mlp_forward(xd, part, dvec, dec_mlp_w)
    gyd, grad_predict, grad_pbias, loss_parts, grad_dec_fg, grad_dec_fb = head(
        core, inverse, xd1, part, dvec, pieces[14].reshape(1, -1), predict_w, target, band_ids, patch_weight, patch_count)
    grad_dec_up, grad_dec_down, part = mlp_backward(gyd, xd1, dvec, dec_mlp_w)
    gxd, grad_dec_attn, grad_dec_gb, grad_dec_bb, part = attn_backward(
        gyd, xd1, part, xd, dec_saved, dvec, dec_attn_w, patch_count, patch_count, DDH)
    one_d, one_e = shape((1, D), F32), shape((1, E), F32)
    grad_dec_ga, grad_dec_ba, grad_mask, grad_bridge, grad_enc_fg, grad_enc_fb, gye = run(
        functools.partial(between_kernel, keep_count),
        [one_e, one_e, one_e, shape((D, E // 2), BF16), one_d, one_d, shape((rows, D), F32)],
        [pltpu.VMEM((rows, E), BF16)],
        (core, gxd, xd, part, other_core(part), dvec, kept_column, hidden_rows, final_enc, x2, evec, bridge_w),
        3 * rows * D * E, 1)
    grad_enc_up, grad_enc_down, part = mlp_backward(gye, x1, evec, enc_mlp_w)
    gxe, grad_enc_attn, grad_enc_gb, grad_enc_bb, part = attn_backward(
        gye, x1, part, x0, enc_saved, evec, enc_attn_w, keep_count, group, DH)
    grad_enc_ga, grad_enc_ba, grad_ebias, grad_embed = run(
        enc_out_kernel,
        [one_d, one_d, one_d, shape((D, pixel_count // 2), BF16)],
        [], (core, gxe, x0, part, other_core(part), evec, kept_pixels), rows * D * pixel_count, 1)
    grad_vectors = jnp.concatenate(
        [grad_ebias, grad_enc_ga, grad_enc_ba, grad_enc_gb, grad_enc_bb, grad_enc_fg, grad_enc_fb, grad_mask,
         grad_dec_ga, grad_dec_ba, grad_dec_gb, grad_dec_bb, grad_dec_fg, grad_dec_fb, grad_pbias], axis=1).reshape(-1)
    vec_grads = jnp.pad(grad_vectors.reshape(size, vec_shard), ((0, 0), (0, vec_room - vec_shard)))
    sums, total_squares, loss = reduce_all(
        [grad_enc_attn, grad_enc_up, grad_enc_down, grad_dec_attn, grad_dec_up, grad_dec_down, grad_embed, grad_bridge,
         grad_predict, vec_grads.reshape(-1, 128)],
        (1.0,) * 9 + (0.5,), loss_parts)
    reduced = (
        jnp.stack(jnp.split(sums[0], 4, axis=1)),
        jnp.stack(sums[1:3]),
        jnp.stack(jnp.split(sums[3], 4, axis=1)),
        jnp.stack(sums[4:6]),
        join_cores(sums[6], core).T,
        join_cores(sums[7], core),
        join_cores(sums[8], core),
        sums[9].reshape(-1)[:vec_shard],
    )
    grad_norm = jnp.sqrt(total_squares)
    factor = CLIP / jnp.maximum(grad_norm, CLIP)
    news, new_firsts, new_seconds = ([], [], [])
    for position, master in enumerate(masters):
        is_vec = position == 7
        updated, first_new, second_new = adam_update(
            master,
            reduced[position] * factor,
            firsts[position],
            seconds[position],
            RATE_VEC if is_vec else RATE_MAT,
            0.0 if is_vec else DECAY_MAT,
        )
        news.append(updated)
        new_firsts.append(first_new)
        new_seconds.append(second_new)
    ema_attn = EMA_KEEP * ema_enc_attn + (1.0 - EMA_KEEP) * news[0]
    ema_mlp = EMA_KEEP * ema_enc_mlp + (1.0 - EMA_KEEP) * news[1]
    ema_embed = EMA_KEEP * ema_patch_embed + (1.0 - EMA_KEEP) * news[4]
    return (
        loss,
        band_weight,
        grad_norm,
        news[0],
        news[1],
        news[2],
        news[3],
        news[4],
        news[5],
        news[6],
        news[7],
        new_firsts[0],
        new_firsts[1],
        new_firsts[2],
        new_firsts[3],
        new_firsts[4],
        new_firsts[5],
        new_firsts[6],
        new_firsts[7],
        new_seconds[0],
        new_seconds[1],
        new_seconds[2],
        new_seconds[3],
        new_seconds[4],
        new_seconds[5],
        new_seconds[6],
        new_seconds[7],
        ema_attn,
        ema_mlp,
        ema_embed,
    )


def solution(mesh):
    return jax.shard_map(
        per_device,
        mesh=mesh,
        in_specs=(
            P("dp", None),
            P("dp", None),
            P("dp", None),
            P("dp", None),
            P("dp", None),
            P("dp"),
            P(None, "dp", "mp"),
            P(None, "dp", "mp"),
            P(None, "dp", "mp"),
            P(None, "dp", "mp"),
            P(None, "dp"),
            P("dp", None),
            P("dp", None),
            P("dp"),
            P(None, "dp", "mp"),
            P(None, "dp", "mp"),
            P(None, "dp", "mp"),
            P(None, "dp", "mp"),
            P(None, "dp"),
            P("dp", None),
            P("dp", None),
            P("dp"),
            P(None, "dp", "mp"),
            P(None, "dp", "mp"),
            P(None, "dp", "mp"),
            P(None, "dp", "mp"),
            P(None, "dp"),
            P("dp", None),
            P("dp", None),
            P("dp"),
            P(None, "dp", "mp"),
            P(None, "dp", "mp"),
            P(None, "dp"),
        ),
        out_specs=(
            P(),
            P(),
            P(),
            P(None, "dp", "mp"),
            P(None, "dp", "mp"),
            P(None, "dp", "mp"),
            P(None, "dp", "mp"),
            P(None, "dp"),
            P("dp", None),
            P("dp", None),
            P("dp"),
            P(None, "dp", "mp"),
            P(None, "dp", "mp"),
            P(None, "dp", "mp"),
            P(None, "dp", "mp"),
            P(None, "dp"),
            P("dp", None),
            P("dp", None),
            P("dp"),
            P(None, "dp", "mp"),
            P(None, "dp", "mp"),
            P(None, "dp", "mp"),
            P(None, "dp", "mp"),
            P(None, "dp"),
            P("dp", None),
            P("dp", None),
            P("dp"),
            P(None, "dp", "mp"),
            P(None, "dp", "mp"),
            P(None, "dp"),
        ),
        check_vma=False,
    )
```

```python
import functools
import math

import jax
import jax.numpy as jnp
from jax import lax
from jax.experimental import pallas as pl
from jax.experimental.pallas import tpu as pltpu
from jax.sharding import PartitionSpec as P

D = 1024
DH = 64
E = 512
DDH = 32
GRID = 16
NB = 3
STEP = 10


EPS_LN = 1e-06
EPS_C = 0.01
CLIP = 0.0002
BETA_ONE = 0.9
BETA_TWO = 0.999
ADAM_EPS = 1e-12
RATE_MAT = 0.06
RATE_VEC = 0.5
DECAY_MAT = 0.05
EMA_KEEP = 0.9
REF_GSD = 4.0


def split_vectors(flat_vec, enc_width, dec_width):
    lengths = [enc_width] * 7 + [dec_width] * 7
    pieces = []
    offset = 0
    for length in lengths:
        pieces.append(flat_vec[offset : offset + length])
        offset = offset + length
    pieces.append(flat_vec[offset:])
    return pieces


F32 = jnp.float32
BF16 = jnp.bfloat16
VMEM_LIMIT = 58 * 2**20
GELU_C = math.sqrt(2.0 / math.pi)


def dot_nn(left, right):
    return jnp.dot(left, right, preferred_element_type=F32)


def dot_nt(left, right):
    return lax.dot_general(left, right, (((1,), (1,)), ((), ())), preferred_element_type=F32)


def dot_tn(left, right):
    return lax.dot_general(left, right, (((0,), (0,)), ((), ())), preferred_element_type=F32)


def dot_exact(left, right):
    return jnp.dot(left, right, preferred_element_type=F32, precision=lax.Precision.HIGHEST)


def normalize(rows):
    centred = rows - jnp.mean(rows, axis=-1, keepdims=True)
    rstd = lax.rsqrt(jnp.mean(centred * centred, axis=-1, keepdims=True) + EPS_LN)
    return centred * rstd, rstd


def norm_back(grad, gain, unit, rstd):
    scaled = grad * gain
    mean_one = jnp.mean(scaled, axis=-1, keepdims=True)
    mean_two = jnp.mean(scaled * unit, axis=-1, keepdims=True)
    grad_in = rstd * (scaled - mean_one - unit * mean_two)
    return (
        grad_in,
        jnp.sum(grad * unit, axis=0, keepdims=True),
        jnp.sum(grad, axis=0, keepdims=True),
    )


def both(mine_ref, other_ref, rows):
    return mine_ref[rows, :].astype(F32) + other_ref[rows, :].astype(F32)


def gelu_parts(up):
    square = up * up
    bent = jnp.tanh(GELU_C * up * (1.0 + 0.044715 * square))
    half = 0.5 * (1.0 + bent)
    return square, bent, half


def group_mask(group, length):
    if group == length:
        return None
    row_image = lax.broadcasted_iota(jnp.int32, (group, group), 0) // length
    col_image = lax.broadcasted_iota(jnp.int32, (group, group), 1) // length
    return row_image == col_image


def attend(qkv_ref, mixed_ref, lse_ref, cols, width, head_dim, mask):
    scale = head_dim ** (-0.5)
    for head in range(width // head_dim):
        at = pl.ds(head * head_dim, head_dim)
        queries = qkv_ref[at, cols]
        keys = qkv_ref[pl.ds(width + head * head_dim, head_dim), cols]
        values = qkv_ref[pl.ds(2 * width + head * head_dim, head_dim), cols]
        scores = dot_tn(keys, queries) * scale
        if mask is not None:
            scores = jnp.where(mask, scores, -1e30)
        top = jnp.max(scores, axis=0, keepdims=True)
        weights = jnp.exp(scores - top)
        total = jnp.sum(weights, axis=0, keepdims=True)
        lse_ref[pl.ds(head, 1), cols] = top + jnp.log(total)
        soft = (weights * (1.0 / total)).astype(BF16)
        mixed_ref[at, cols] = dot_nn(values, soft).astype(BF16)


def attend_back(qkv_ref, grad_ref, lse_ref, out_ref, cols, width, head_dim, mask):
    scale = head_dim ** (-0.5)
    for head in range(width // head_dim):
        at = pl.ds(head * head_dim, head_dim)
        at_k = pl.ds(width + head * head_dim, head_dim)
        at_v = pl.ds(2 * width + head * head_dim, head_dim)
        queries, keys, values = qkv_ref[at, cols], qkv_ref[at_k, cols], qkv_ref[at_v, cols]
        grad = grad_ref[at, :]
        scores = dot_tn(keys, queries) * scale
        if mask is not None:
            scores = jnp.where(mask, scores, -1e30)
        soft = jnp.exp(scores - lse_ref[pl.ds(head, 1), cols])
        out_ref[at_v, cols] = dot_nt(grad, soft.astype(BF16)).astype(BF16)
        grad_soft = dot_tn(values, grad)
        inner = jnp.sum(soft * grad_soft, axis=0, keepdims=True)
        grad_scores = (soft * (grad_soft - inner)).astype(BF16)
        out_ref[at, cols] = (dot_nn(keys, grad_scores) * scale).astype(BF16)
        out_ref[at_k, cols] = (dot_nt(queries, grad_scores) * scale).astype(BF16)


def transposed_weights(attn_ref, flat_ref):
    width = attn_ref.shape[1] // 4
    for part in range(4):
        at = pl.ds(part * width, width)
        flat_ref[at, :] = attn_ref[:, at].T


def attention_rows(unit, vec_ref, flat_ref, qkv_ref, mixed_ref, lse_ref, part_ref, rows, head_dim, mask, attn_ref):
    width = mixed_ref.shape[0]
    low = (unit * vec_ref[1:2, :] + vec_ref[2:3, :]).astype(BF16)
    qkv_ref[:, rows] = dot_nt(flat_ref[: 3 * width, :], low).astype(BF16)
    attend(qkv_ref, mixed_ref, lse_ref, rows, width, head_dim, mask)
    part_ref[rows, :] = dot_nt(mixed_ref[:, rows].T, attn_ref[:, 3 * width :]).astype(BF16)


def enc_in_kernel(length, group, head_dim, pix_ref, kept_ref, table_ref, embed_ref, vec_ref, attn_ref,
                  x_ref, qkv_ref, mixed_ref, lse_ref, part_ref, pixk_ref, flat_ref):
    images, patches = table_ref.shape[0], pix_ref.shape[0] // table_ref.shape[0]
    side = table_ref.shape[1]
    transposed_weights(attn_ref, flat_ref)

    def pick(image, carry):
        rows = pl.ds(image * length, length)
        index = kept_ref[rows, :]
        hot = lax.broadcasted_iota(jnp.int32, (length, patches), 1) == index
        pixels = pix_ref[pl.ds(image * patches, patches), :]
        pixk_ref[rows, :] = dot_nn(hot.astype(BF16), pixels).astype(BF16)
        grid_at = lax.broadcasted_iota(jnp.int32, (length, side), 1)
        table = table_ref[image]
        half = table.shape[1]
        x_ref[rows, :half] = dot_exact((grid_at == index // side).astype(F32), table)
        x_ref[rows, half:] = dot_exact((grid_at == index % side).astype(F32), table)
        return carry

    lax.fori_loop(0, images, pick, 0)
    mask = group_mask(group, length)

    def step(number, carry):
        rows = pl.ds(pl.multiple_of(number * group, group), group)
        share = embed_ref.shape[2]
        rows_x = dot_nt(pixk_ref[rows, :share], embed_ref[0]) + dot_nt(pixk_ref[rows, share:], embed_ref[1])
        rows_x = rows_x + vec_ref[0:1, :] + x_ref[rows, :]
        x_ref[rows, :] = rows_x
        unit, _ = normalize(rows_x)
        attention_rows(unit, vec_ref, flat_ref, qkv_ref, mixed_ref, lse_ref, part_ref, rows, head_dim, mask, attn_ref)
        return carry

    lax.fori_loop(0, x_ref.shape[0] // group, step, 0)


def dec_in_kernel(length, head_dim, x1_ref, mine_ref, other_ref, evec_ref, bridge_ref, kept_ref, hidden_ref,
                  table_ref, vec_ref, attn_ref,
                  x2_ref, final_ref, x_ref, qkv_ref, mixed_ref, lse_ref, part_ref, flat_ref, latent_ref):
    images, side, half = table_ref.shape
    patches = side * side
    transposed_weights(attn_ref, flat_ref)
    every = pl.ds(0, x1_ref.shape[0])
    out = x1_ref[...] + both(mine_ref, other_ref, every)
    x2_ref[...] = out
    unit, _ = normalize(out)
    final = (unit * evec_ref[5:6, :] + evec_ref[6:7, :]).astype(BF16)
    final_ref[...] = final
    share = bridge_ref.shape[2]
    latent_ref[:, :share] = dot_nn(final, bridge_ref[0])
    latent_ref[:, share:] = dot_nn(final, bridge_ref[1])

    def step(image, carry):
        rows = pl.ds(pl.multiple_of(image * patches, patches), patches)
        hot = lax.broadcasted_iota(jnp.int32, (patches, length), 0) == kept_ref[pl.ds(image, 1), :]
        latent = latent_ref[pl.ds(image * length, length), :]
        table = table_ref[image]
        by_row = jnp.broadcast_to(table[:, None, :], (side, side, half)).reshape(patches, half)
        by_col = jnp.broadcast_to(table[None, :, :], (side, side, half)).reshape(patches, half)
        place = jnp.concatenate([by_row, by_col], axis=1)
        rows_x = dot_exact(hot.astype(F32), latent) + hidden_ref[rows, :] * vec_ref[0:1, :] + place
        x_ref[rows, :] = rows_x
        unit, _ = normalize(rows_x)
        attention_rows(unit, vec_ref, flat_ref, qkv_ref, mixed_ref, lse_ref, part_ref, rows, head_dim, None, attn_ref)
        return carry

    lax.fori_loop(0, images, step, 0)


def mlp_kernel(tile, x_ref, mine_ref, other_ref, vec_ref, up_ref, down_ref, x1_ref, part_ref, low_ref, acc_ref):
    number = pl.program_id(0)
    count = x_ref.shape[0] // tile

    def first(step, carry):
        rows = pl.ds(pl.multiple_of(step * tile, tile), tile)
        after = x_ref[rows, :] + both(mine_ref, other_ref, rows)
        x1_ref[rows, :] = after
        unit, _ = normalize(after)
        low_ref[rows, :] = (unit * vec_ref[3:4, :] + vec_ref[4:5, :]).astype(BF16)
        return carry

    @pl.when(number == 0)
    def _():
        lax.fori_loop(0, count, first, 0)
        acc_ref[...] = jnp.zeros_like(acc_ref)

    def step(piece, carry):
        rows = pl.ds(pl.multiple_of(piece * tile, tile), tile)
        up = dot_nn(low_ref[rows, :], up_ref[...])
        _, _, half = gelu_parts(up)
        acc_ref[rows, :] += dot_nt((up * half).astype(BF16), down_ref[...])
        return carry

    lax.fori_loop(0, count, step, 0)

    @pl.when(number == pl.num_programs(0) - 1)
    def _():
        part_ref[...] = acc_ref[...].astype(BF16)


def head_kernel(core_ref, inverse_ref, x1_ref, mine_ref, other_ref, vec_ref, bias_ref, predict_ref, target_ref,
                band_ref, weight_ref, gy_ref, glow_ref, gbias_ref, loss_ref, gain_ref, shift_ref, low_ref, gpred_ref):
    number = pl.program_id(0)

    @pl.when(number == 0)
    def _():
        for ref in (gpred_ref, gbias_ref, loss_ref, gain_ref, shift_ref):
            ref[...] = jnp.zeros_like(ref)

    every = pl.ds(0, x1_ref.shape[0])
    unit, rstd = normalize(x1_ref[...] + both(mine_ref, other_ref, every))
    gain = vec_ref[5:6, :]
    final = (unit * gain + vec_ref[6:7, :]).astype(BF16)
    share = gpred_ref.shape[1]
    predicted = jnp.concatenate([dot_nn(final, predict_ref[0]), dot_nn(final, predict_ref[1])], axis=1)
    mismatch = predicted + bias_ref[...] - target_ref[...].astype(F32)
    band = band_ref[...]
    level = jnp.where(band == 0, inverse_ref[0], jnp.where(band == 1, inverse_ref[1], inverse_ref[2]))
    level = level * weight_ref[...]
    square = mismatch * mismatch + EPS_C
    root = lax.rsqrt(square)
    loss_ref[...] += jnp.sum(level * (square * root), axis=0, keepdims=True)
    grad = level * (mismatch * root)
    gbias_ref[...] += jnp.sum(grad, axis=0, keepdims=True)
    low_ref[...] = grad.astype(BF16)
    columns = pl.ds(pl.multiple_of(core_ref[0] * share, share), share)
    gpred_ref[...] += dot_tn(final, low_ref[:, columns])
    grad_final = dot_nt(low_ref[:, :share], predict_ref[0]) + dot_nt(low_ref[:, share:], predict_ref[1])
    grad_in, gain_sum, shift_sum = norm_back(grad_final, gain, unit, rstd)
    gy_ref[...] = grad_in
    gain_ref[...] += gain_sum
    shift_ref[...] += shift_sum

    @pl.when(number == pl.num_programs(0) - 1)
    def _():
        glow_ref[...] = gpred_ref[...].astype(BF16)


def mlp_back_kernel(tile, gy_ref, x1_ref, vec_ref, up_ref, down_ref, gup_ref, gdown_ref, part_ref,
                    low_ref, lowt_ref, grad_ref, gradt_ref, gu_ref, z_ref, acc_ref):
    number = pl.program_id(0)
    count = x1_ref.shape[0] // tile

    def first(step, carry):
        rows = pl.ds(pl.multiple_of(step * tile, tile), tile)
        unit, _ = normalize(x1_ref[rows, :])
        low = (unit * vec_ref[3:4, :] + vec_ref[4:5, :]).astype(BF16)
        low_ref[rows, :] = low
        lowt_ref[:, rows] = low.T
        grad = gy_ref[rows, :].astype(BF16)
        grad_ref[rows, :] = grad
        gradt_ref[:, rows] = grad.T
        return carry

    @pl.when(number == 0)
    def _():
        lax.fori_loop(0, count, first, 0)
        acc_ref[...] = jnp.zeros_like(acc_ref)

    def step(piece, carry):
        rows = pl.ds(pl.multiple_of(piece * tile, tile), tile)
        up = dot_nn(low_ref[rows, :], up_ref[...])
        square, bent, half = gelu_parts(up)
        z_ref[rows, :] = (up * half).astype(BF16)
        slope = half + (0.5 * GELU_C) * up * (1.0 - bent * bent) * (1.0 + (3.0 * 0.044715) * square)
        grad_up = (dot_nn(grad_ref[rows, :], down_ref[...]) * slope).astype(BF16)
        gu_ref[rows, :] = grad_up
        acc_ref[rows, :] += dot_nt(grad_up, up_ref[...])
        return carry

    lax.fori_loop(0, count, step, 0)
    gup_ref[...] = dot_nn(lowt_ref[...], gu_ref[...]).astype(BF16)
    gdown_ref[...] = dot_nn(gradt_ref[...], z_ref[...]).astype(BF16)

    @pl.when(number == pl.num_programs(0) - 1)
    def _():
        part_ref[...] = acc_ref[...].astype(BF16)


def attn_back_kernel(length, group, head_dim, gy_ref, x1_ref, mine_ref, other_ref, x_ref, qkv_ref, mixed_ref, lse_ref,
                     vec_ref, attn_ref, gx_ref, grad_ref, gain_ref, shift_ref, part_ref,
                     flat_ref, lowt_ref, gradt_ref, gmix_ref, gqkv_ref):
    width = mixed_ref.shape[0]
    transposed_weights(attn_ref, flat_ref)
    gain_ref[...] = jnp.zeros_like(gain_ref)
    shift_ref[...] = jnp.zeros_like(shift_ref)
    mask = group_mask(group, length)

    def step(number, carry):
        rows = pl.ds(pl.multiple_of(number * group, group), group)
        unit, rstd = normalize(x1_ref[rows, :])
        grad_in, gain_sum, shift_sum = norm_back(both(mine_ref, other_ref, rows), vec_ref[3:4, :], unit, rstd)
        grad_in = grad_in + gy_ref[rows, :]
        gx_ref[rows, :] = grad_in
        gain_ref[...] += gain_sum
        shift_ref[...] += shift_sum
        low_grad = grad_in.astype(BF16)
        gradt_ref[:, rows] = low_grad.T
        gmix_ref[...] = dot_nt(flat_ref[3 * width :, :], low_grad).astype(BF16)
        attend_back(qkv_ref, gmix_ref, lse_ref, gqkv_ref, rows, width, head_dim, mask)
        part_ref[rows, :] = dot_nn(gqkv_ref[:, rows].T, flat_ref[: 3 * width, :]).astype(BF16)
        unit_a, _ = normalize(x_ref[rows, :])
        lowt_ref[:, rows] = (unit_a * vec_ref[1:2, :] + vec_ref[2:3, :]).astype(BF16).T
        return carry

    lax.fori_loop(0, x_ref.shape[0] // group, step, 0)
    grad_ref[:, : 3 * width] = dot_nt(lowt_ref[...], gqkv_ref[...]).astype(BF16)
    grad_ref[:, 3 * width :] = dot_nt(gradt_ref[...], mixed_ref[...]).astype(BF16)


def between_kernel(length, core_ref, gx_ref, x_ref, mine_ref, other_ref, vec_ref, kept_ref, hidden_ref, final_ref, x2_ref,
                   evec_ref, bridge_ref, gain_ref, shift_ref, mask_ref, gbridge_ref, egain_ref, eshift_ref, gy_ref,
                   latent_ref):
    images = kept_ref.shape[0] // length
    patches = x_ref.shape[0] // images
    for ref in (gain_ref, shift_ref, mask_ref):
        ref[...] = jnp.zeros_like(ref)

    def step(image, carry):
        rows = pl.ds(pl.multiple_of(image * patches, patches), patches)
        unit, rstd = normalize(x_ref[rows, :])
        grad_in, gain_sum, shift_sum = norm_back(both(mine_ref, other_ref, rows), vec_ref[1:2, :], unit, rstd)
        grad_in = grad_in + gx_ref[rows, :]
        gain_ref[...] += gain_sum
        shift_ref[...] += shift_sum
        mask_ref[...] += jnp.sum(grad_in * hidden_ref[rows, :], axis=0, keepdims=True)
        kept_rows = pl.ds(pl.multiple_of(image * length, length), length)
        hot = lax.broadcasted_iota(jnp.int32, (length, patches), 1) == kept_ref[kept_rows, :]
        latent_ref[kept_rows, :] = dot_nn(hot.astype(BF16), grad_in.astype(BF16)).astype(BF16)
        return carry

    lax.fori_loop(0, images, step, 0)
    share = gbridge_ref.shape[1]
    columns = pl.ds(pl.multiple_of(core_ref[0] * share, share), share)
    gbridge_ref[...] = dot_tn(final_ref[...], latent_ref[:, columns]).astype(BF16)
    grad_final = dot_nt(latent_ref[:, :share], bridge_ref[0]) + dot_nt(latent_ref[:, share:], bridge_ref[1])
    unit, rstd = normalize(x2_ref[...])
    gy_ref[...], egain_ref[...], eshift_ref[...] = norm_back(grad_final, evec_ref[5:6, :], unit, rstd)


def enc_out_kernel(core_ref, gx_ref, x_ref, mine_ref, other_ref, vec_ref, pixk_ref,
                   gain_ref, shift_ref, ebias_ref, gembed_ref):
    every = pl.ds(0, x_ref.shape[0])
    unit, rstd = normalize(x_ref[...])
    grad_in, gain_ref[...], shift_ref[...] = norm_back(both(mine_ref, other_ref, every), vec_ref[1:2, :], unit, rstd)
    grad_in = grad_in + gx_ref[...]
    ebias_ref[...] = jnp.sum(grad_in, axis=0, keepdims=True)
    share = gembed_ref.shape[1]
    columns = pl.ds(pl.multiple_of(core_ref[0] * share, share), share)
    gembed_ref[...] = dot_tn(grad_in.astype(BF16), pixk_ref[:, columns]).astype(BF16)


def shape(dims, dtype):
    return jax.ShapeDtypeStruct(dims, dtype)


def run(kernel, outs, scratch, args, flops, scalars=0):
    moved = sum(math.prod(a.shape) * a.dtype.itemsize for a in list(args) + list(outs))
    in_vmem = pl.BlockSpec(memory_space=pltpu.VMEM)
    return pl.pallas_call(
        kernel,
        out_shape=tuple(outs),
        in_specs=[pl.BlockSpec(memory_space=pltpu.SMEM)] * scalars + [in_vmem] * (len(args) - scalars),
        out_specs=tuple([in_vmem] * len(outs)),
        scratch_shapes=scratch,
        compiler_params=pltpu.CompilerParams(vmem_limit_bytes=VMEM_LIMIT),
        cost_estimate=pl.CostEstimate(flops=flops, bytes_accessed=moved, transcendentals=0),
    )(*args)


def other_core(block):
    return lax.ppermute(block, "mp", [(0, 1), (1, 0)])


def mlp_forward(x, mine, vec, stack):
    rows, width = x.shape
    hidden = stack.shape[1] // 2
    block = min(hidden, 512)
    tile = min(rows, 512)
    other = other_core(mine)
    whole = pl.BlockSpec((rows, width), lambda i: (0, 0))
    cols = pl.BlockSpec((width, block), lambda i: (0, i))
    later = pl.BlockSpec((width, block), lambda i: (0, i + hidden // block))
    return pl.pallas_call(
        functools.partial(mlp_kernel, tile),
        out_shape=(shape((rows, width), F32), shape((rows, width), BF16)),
        grid=(hidden // block,),
        in_specs=[whole] * 3 + [pl.BlockSpec((8, width), lambda i: (0, 0)), cols, later],
        out_specs=(whole, whole),
        scratch_shapes=[pltpu.VMEM((rows, width), BF16), pltpu.VMEM((rows, width), F32)],
        compiler_params=pltpu.CompilerParams(vmem_limit_bytes=VMEM_LIMIT),
        cost_estimate=pl.CostEstimate(flops=4 * rows * width * hidden, bytes_accessed=rows * width * 14 + width * hidden * 4,
                                      transcendentals=rows * hidden),
    )(x, mine, other, vec, stack, stack)


def mlp_backward(gy, x1, vec, stack):
    rows, width = x1.shape
    hidden = stack.shape[1] // 2
    block = min(hidden, 512)
    tile = min(rows, 256)
    whole = pl.BlockSpec((rows, width), lambda i: (0, 0))
    cols = pl.BlockSpec((width, block), lambda i: (0, i))
    later = pl.BlockSpec((width, block), lambda i: (0, i + hidden // block))
    return pl.pallas_call(
        functools.partial(mlp_back_kernel, tile),
        out_shape=(shape((width, hidden), BF16), shape((width, hidden), BF16), shape((rows, width), BF16)),
        grid=(hidden // block,),
        in_specs=[whole] * 2 + [pl.BlockSpec((8, width), lambda i: (0, 0)), cols, later],
        out_specs=(cols, cols, whole),
        scratch_shapes=[
            pltpu.VMEM((rows, width), BF16), pltpu.VMEM((width, rows), BF16),
            pltpu.VMEM((rows, width), BF16), pltpu.VMEM((width, rows), BF16),
            pltpu.VMEM((rows, block), BF16), pltpu.VMEM((rows, block), BF16),
            pltpu.VMEM((rows, width), F32)],
        compiler_params=pltpu.CompilerParams(vmem_limit_bytes=VMEM_LIMIT),
        cost_estimate=pl.CostEstimate(flops=10 * rows * width * hidden, bytes_accessed=rows * width * 10 + width * hidden * 8,
                                      transcendentals=rows * hidden),
    )(gy, x1, vec, stack, stack)


def head(core, inverse, x1, mine, vec, bias, predict, target, band, weight, patches):
    rows, width = x1.shape
    pixels = target.shape[1]
    share = pixels // 2
    other = other_core(mine)
    smem = pl.BlockSpec(memory_space=pltpu.SMEM)
    row_w = pl.BlockSpec((patches, width), lambda i: (i, 0))
    row_p = pl.BlockSpec((patches, pixels), lambda i: (i, 0))
    fix = lambda a, b: pl.BlockSpec((a, b), lambda i: (0, 0))
    return pl.pallas_call(
        head_kernel,
        out_shape=(shape((rows, width), F32), shape((width, share), BF16), shape((1, pixels), F32),
                   shape((1, pixels), F32), shape((1, width), F32), shape((1, width), F32)),
        grid=(rows // patches,),
        in_specs=[smem, smem, row_w, row_w, row_w, fix(8, width), fix(1, pixels), pl.BlockSpec((2, width, share), lambda i: (0, 0, 0)), row_p, row_p,
                  pl.BlockSpec((patches, 1), lambda i: (i, 0))],
        out_specs=(row_w, fix(width, share), fix(1, pixels), fix(1, pixels), fix(1, width), fix(1, width)),
        scratch_shapes=[pltpu.VMEM((patches, pixels), BF16), pltpu.VMEM((width, share), F32)],
        compiler_params=pltpu.CompilerParams(vmem_limit_bytes=VMEM_LIMIT),
        cost_estimate=pl.CostEstimate(flops=5 * rows * width * pixels, bytes_accessed=rows * (width * 12 + pixels * 6),
                                      transcendentals=rows * pixels),
    )(core, inverse, x1, mine, other, vec, bias, predict, target, band, weight)


def attn_backward(gy, x1, mine, x, saved, vec, attn, length, group, head_dim):
    qkv, mixed, lse = saved
    rows, width = x.shape
    local = mixed.shape[0]
    return run(
        functools.partial(attn_back_kernel, length, group, head_dim),
        [shape((rows, width), F32), shape((width, 4 * local), BF16),
         shape((1, width), F32), shape((1, width), F32), shape((rows, width), BF16)],
        [pltpu.VMEM((4 * local, width), BF16), pltpu.VMEM((width, rows), BF16), pltpu.VMEM((width, rows), BF16),
         pltpu.VMEM((local, group), BF16), pltpu.VMEM((3 * local, rows), BF16)],
        (gy, x1, mine, other_core(mine), x, qkv, mixed, lse, vec, attn),
        18 * rows * width * local)


def sine_table(gsd_values, feature_width, grid_side):
    quarter = feature_width // 4
    frequency = jnp.exp(-jnp.log(10000.0) * jnp.arange(quarter).astype(F32) / quarter)
    gsd_ratio = gsd_values.astype(F32)[:, None, None] / REF_GSD
    line = jnp.arange(grid_side, dtype=jnp.int32).astype(F32)
    arg = line[None, :, None] * gsd_ratio * frequency
    return jnp.concatenate([jnp.sin(arg), jnp.cos(arg)], axis=-1)


def dp_bits():
    return lax.axis_size("dp").bit_length() - 1


def orders():
    bits = dp_bits()
    high = list(range(bits - 1, 1, -1))
    return (high + [0, 1], high + [1, 0])


def swap(block, bit):
    size = lax.axis_size("dp")
    return lax.ppermute(block, "dp", [(i, i ^ (1 << bit)) for i in range(size)])


def my_bit(bit):
    return (lax.axis_index("dp") >> bit) & 1


def gather_dp(block, axis, order):
    lead, rest = (block.shape[:axis], block.shape[axis:])
    done = []
    cur = block
    for bit in order:
        other = swap(cur, bit)
        mine = my_bit(bit) == 1
        place = axis + sum(1 for b in done if b > bit)
        cur = jnp.stack([jnp.where(mine, other, cur), jnp.where(mine, cur, other)], axis=place)
        done.append(bit)
    return cur.reshape(lead + (rest[0] * lax.axis_size("dp"),) + rest[1:])


def reduce_dp(block, axis, order, wire):
    bits = dp_bits()
    lead, rest = (block.shape[:axis], block.shape[axis:])
    shard = rest[0] // lax.axis_size("dp")
    cur = block.reshape(lead + (2,) * bits + (shard,) + rest[1:])
    left = list(range(bits - 1, -1, -1))
    for bit in reversed(order):
        place = axis + left.index(bit)
        mine = my_bit(bit)
        keep = lax.dynamic_index_in_dim(cur, mine, place, keepdims=False)
        give = lax.dynamic_index_in_dim(cur, 1 - mine, place, keepdims=False)
        other = swap(give.astype(wire), bit)
        cur = keep.astype(F32) + other.astype(F32)
        left.remove(bit)
    return cur


def join_cores(mine, core):
    other = other_core(mine)
    return jnp.concatenate([jnp.where(core == 0, mine, other), jnp.where(core == 0, other, mine)], axis=1)


def total_dp(value):
    for bit in range(dp_bits()):
        value = value + swap(value, bit)
    return value


def place_of():
    index = lax.axis_index("dp")
    core = lax.axis_index("mp")
    low, high = lax.rem(index, 4), index // 4
    bit_x, bit_y = lax.rem(low, 2), low // 2
    low_x, low_y = low + 1 - 2 * bit_x, low + 2 - 4 * bit_y
    return core, low, high, low_x, low_y


def greet(partners):
    barrier = pltpu.get_barrier_semaphore()
    for partner in partners:
        pl.semaphore_signal(barrier, inc=1, device_id=partner, device_id_type=pl.DeviceIdType.MESH)
    pl.semaphore_wait(barrier, len(partners))


def blocks_of(widths, limit):
    found = []
    for number, width in enumerate(widths):
        start = 0
        while start < width:
            size = min(limit, width - start)
            found.append((number, start, size))
            start += size
    return found


def remote(source, target, send, receive, device):
    return pltpu.make_async_remote_copy(
        src_ref=source, dst_ref=target, send_sem=send, recv_sem=receive,
        device_id=device, device_id_type=pl.DeviceIdType.MESH)


def small_gather_kernel(size, part_ref, full_ref, send_sem, receive_sem):
    index, core = lax.axis_index("dp"), lax.axis_index("mp")
    peers = [(lax.rem(index + k, size), core) for k in range(1, size)]
    greet(peers)
    full_ref[index] = part_ref[...]
    copies = [remote(part_ref, full_ref.at[index], send_sem.at[k], receive_sem.at[k], peers[k])
              for k in range(size - 1)]
    for copy in copies:
        copy.start()
    for copy in copies:
        copy.wait()


def small_gather(part):
    size = lax.axis_size("dp")
    in_vmem = pl.BlockSpec(memory_space=pltpu.VMEM)
    dma = pltpu.SemaphoreType.DMA
    return pl.pallas_call(
        functools.partial(small_gather_kernel, size),
        out_shape=shape((size,) + part.shape, part.dtype),
        in_specs=[in_vmem],
        out_specs=in_vmem,
        scratch_shapes=[dma((size - 1,)), dma((size - 1,))],
        compiler_params=pltpu.CompilerParams(collective_id=2, has_side_effects=True),
    )(part)


def total_blocks(block_ref, near_ref, far_ref, sems, low, high, core, highs, stage):
    send, receive = sems
    if stage == 0:
        spots = [(high * 4 + lax.rem(low + k, 4), core) for k in range(1, 4)]
        return [remote(block_ref, near_ref.at[low], send.at[k], receive.at[k], spots[k]) for k in range(3)]
    spots = [(lax.rem(high + k, highs) * 4 + low, core) for k in range(1, highs)]
    return [remote(block_ref, far_ref.at[high], send.at[3 + k], receive.at[3 + k], spots[k]) for k in range(highs - 1)]


def forward_kernel(highs, shared, groups, count, length, group, head_dim, *refs):
    shards, refs = refs[:count], refs[count:]
    pix_ref, band_ref, weight_ref, kept_ref, table_ref, vec_ref = refs[:6]
    fulls, refs = refs[6 : 6 + count], refs[6 + count :]
    x_ref, qkv_ref, mixed_ref, lse_ref, pixk_ref, x1_ref, last_ref, far_out_ref, counts_ref, flat_ref = refs[:10]
    refs = refs[10:]
    (bands_v, embed_v, attn_v, mlp_v, part_ref, other_ref, low_ref, acc_ref, block_ref, near_ref,
     far_ref) = refs[:11]
    (own_sem, zs_sem, zr_sem, cs_sem, cr_sem, fs_sem, fr_sem, ms_sem, mr_sem, load_sem, xs_sem, xr_sem, ts_sem,
     tr_sem) = refs[11:]
    core, low, high, low_x, low_y = place_of()
    at_x, at_y = (high * 4 + low_x, core), (high * 4 + low_y, core)
    at_high = [(lax.rem(high + k, highs) * 4 + low, core) for k in range(1, highs)]
    sibling = (high * 4 + low, 1 - core)
    near = [(high * 4 + lax.rem(low + k, 4), core) for k in range(1, 4)]
    greet([sibling] + near + at_high)

    def full(at):
        number, start, size = groups[at]
        ref = fulls[number].at[core] if shared[number] else fulls[number]
        return ref, pl.ds(start, size)

    def first(at):
        ref, cols = full(at)
        shard = shards[groups[at][0]].at[:, cols]
        mine = ref.at[high, low, :, cols]
        copies = [pltpu.make_async_copy(shard, mine, own_sem.at[at])]
        for k in range(1, highs):
            copies.append(remote(shard, mine, zs_sem.at[at, k - 1], zr_sem.at[at, k - 1], at_high[k - 1]))
        return copies

    def column(at):
        ref, cols = full(at)
        part = ref.at[:, low, :, cols]
        return [remote(part, part, cs_sem.at[at, 0], cr_sem.at[at, 0], at_x),
                remote(part, part, cs_sem.at[at, 1], cr_sem.at[at, 1], at_y)]

    def forward(at):
        ref, cols = full(at)
        which, device = (low_x, at_y) if at % 2 == 0 else (low_y, at_x)
        part = ref.at[:, which, :, cols]
        return remote(part, part, fs_sem.at[at], fr_sem.at[at], device)

    def swap(number):
        part = fulls[number].at[core]
        return remote(part, part, ms_sem.at[number], mr_sem.at[number], sibling)

    def exchange(at, source, target):
        return remote(source, target, xs_sem.at[at], xr_sem.at[at], sibling)

    total = len(groups)
    pairs = (total + 1) // 2
    in_pair = lambda pair: [at for at in (2 * pair, 2 * pair + 1) if at < total]
    pair_of = lambda number: max(at for at in range(total) if groups[at][0] == number) // 2
    images, side = table_ref.shape[0], table_ref.shape[1]
    patches = pix_ref.shape[0] // images
    width = mixed_ref.shape[0]
    mask = group_mask(group, length)

    def pick(image, carry):
        rows = pl.ds(image * length, length)
        index = kept_ref[rows, :]
        hot = lax.broadcasted_iota(jnp.int32, (length, patches), 1) == index
        pixels = pix_ref[pl.ds(image * patches, patches), :]
        pixk_ref[rows, :] = dot_nn(hot.astype(BF16), pixels).astype(BF16)
        grid_at = lax.broadcasted_iota(jnp.int32, (length, side), 1)
        table = table_ref[image]
        half = table.shape[1]
        x_ref[rows, :half] = dot_exact((grid_at == index // side).astype(F32), table)
        x_ref[rows, half:] = dot_exact((grid_at == index % side).astype(F32), table)
        return carry

    def tally(image, carry):
        rows = pl.ds(image * patches, patches)
        band, weight = bands_v[rows, :], weight_ref[rows, :]
        for level in range(NB):
            row = jnp.sum(jnp.where(band == level, weight, 0.0), axis=0, keepdims=True)
            for start in range(0, row.shape[1], 128):
                block_ref[level : level + 1, :] += row[:, start : start + 128]
        return carry

    def rows_step(number, carry):
        rows = pl.ds(pl.multiple_of(number * group, group), group)
        share = embed_v.shape[-1]
        embed = lambda half: embed_v[half].reshape(-1, share)
        rows_x = dot_nt(pixk_ref[rows, :share], embed(0)) + dot_nt(pixk_ref[rows, share:], embed(1))
        rows_x = rows_x + vec_ref[0:1, :] + x_ref[rows, :]
        x_ref[rows, :] = rows_x
        unit, _ = normalize(rows_x)
        low_a = (unit * vec_ref[1:2, :] + vec_ref[2:3, :]).astype(BF16)
        qkv_ref[:, rows] = dot_nt(flat_ref[: 3 * width, :], low_a).astype(BF16)
        attend(qkv_ref, mixed_ref, lse_ref, rows, width, head_dim, mask)
        part_ref[rows, :] = dot_nn(mixed_ref[:, rows].T, flat_ref[3 * width :, :]).astype(BF16)
        return carry

    def mlp_first():
        after = x_ref[...] + both(part_ref, other_ref, pl.ds(0, x_ref.shape[0]))
        x1_ref[...] = after
        unit, _ = normalize(after)
        low_ref[...] = (unit * vec_ref[3:4, :] + vec_ref[4:5, :]).astype(BF16)
        acc_ref[...] = jnp.zeros_like(acc_ref)

    def mlp_block(piece, carry):
        size = 512
        hidden = mlp_v.shape[-1] // 2
        start = pl.multiple_of(piece * size, size)
        wide = x_ref.shape[1]
        up = dot_nn(low_ref[...], mlp_v[:, :, :, pl.ds(start, size)].reshape(wide, size))
        _, _, half = gelu_parts(up)
        down = mlp_v[:, :, :, pl.ds(pl.multiple_of(hidden + start, size), size)].reshape(wide, size)
        acc_ref[...] += dot_nt((up * half).astype(BF16), down)
        return carry

    load_bands = pltpu.make_async_copy(band_ref, bands_v, load_sem.at[0])
    load_attn = pltpu.make_async_copy(fulls[1], attn_v, load_sem.at[1])
    load_embed = pltpu.make_async_copy(fulls[0], embed_v, load_sem.at[2])
    load_mlp = pltpu.make_async_copy(fulls[2], mlp_v, load_sem.at[3])
    stages = functools.partial(total_blocks, block_ref, near_ref, far_ref, (ts_sem, tr_sem), low, high, core, highs)
    embed_at, attn_at, mlp_at = pair_of(0) + 3, pair_of(1) + 3, pair_of(2) + 3
    row_groups = x_ref.shape[0] // group
    swapped = set()
    for step in range(pairs + 3):
        if step < pairs:
            for at in in_pair(step):
                for copy in first(at):
                    copy.start()
        if 0 <= step - 1 < pairs:
            for at in in_pair(step - 1):
                for copy in first(at):
                    copy.wait()
                for copy in column(at):
                    copy.start()
        if 0 <= step - 2 < pairs:
            for at in in_pair(step - 2):
                column(at)[at % 2].wait()
                forward(at).start()
        if 0 <= step - 3 < pairs:
            for at in in_pair(step - 3):
                column(at)[1 - at % 2].wait()
                forward(at).wait()
        for number in range(count):
            if shared[number] and number not in swapped and pair_of(number) + 3 <= step:
                swap(number).start()
                swapped.add(number)
        if step == 0:
            load_bands.start()
            lax.fori_loop(0, images, pick, 0)
            block_ref[...] = jnp.zeros_like(block_ref)
            load_bands.wait()
            lax.fori_loop(0, images, tally, 0)
            near_ref[low] = block_ref[...]
            for copy in stages(0):
                copy.start()
        if step == 1:
            for copy in stages(0):
                copy.wait()
            block_ref[...] = (near_ref[0] + near_ref[1]) + (near_ref[2] + near_ref[3])
            far_ref[high] = block_ref[...]
            for copy in stages(1):
                copy.start()
        if step == 2:
            for copy in stages(1):
                copy.wait()
            counts = far_ref[0]
            for k in range(1, highs):
                counts = counts + far_ref[k]
            counts_ref[...] = counts
        if step == attn_at:
            swap(0).wait()
            load_attn.start()
            load_embed.start()
            load_attn.wait()
            for part in range(4):
                at = pl.ds(part * width, width)
                flat_ref[at, :] = attn_v[:, :, :, at].reshape(-1, width).T
            load_embed.wait()
        if attn_at <= step < mlp_at - 1:
            share = -(-row_groups // (mlp_at - 1 - attn_at))
            start, stop = (step - attn_at) * share, min((step - attn_at + 1) * share, row_groups)
            if start < stop:
                lax.fori_loop(start, stop, rows_step, 0)
                if stop == row_groups:
                    exchange(0, part_ref, other_ref).start()
        if step == mlp_at:
            load_mlp.start()
            exchange(0, part_ref, other_ref).wait()
            mlp_first()
            load_mlp.wait()
            lax.fori_loop(0, mlp_v.shape[-1] // 1024, mlp_block, 0)
            last_ref[...] = acc_ref[...].astype(BF16)
            exchange(1, last_ref, far_out_ref).start()
    exchange(1, last_ref, far_out_ref).wait()
    for number in range(1, count):
        if shared[number]:
            swap(number).wait()


def forward_all(shards, shared, pixels, band_ids, patch_weight, kept_column, table, evec):
    size = lax.axis_size("dp")
    highs = size // 4
    count = len(shards)
    groups = blocks_of([a.shape[1] for a in shards], 512)
    total = len(groups)
    rows, wide, local = kept_column.shape[0], evec.shape[1], shards[1].shape[1] // 4
    images = table.shape[0]
    length = rows // images
    group = 2 * length
    fulls = []
    for shard, split in zip(shards, shared):
        dims = (highs, 4) + shard.shape
        fulls.append(shape((2,) + dims if split else dims, shard.dtype))
    outs = [shape((rows, wide), F32), shape((3 * local, rows), BF16), shape((local, rows), BF16),
            shape((local // DH, rows), F32), shape((rows, pixels.shape[1]), BF16), shape((rows, wide), F32),
            shape((rows, wide), BF16), shape((rows, wide), BF16), shape((8, 128), F32), shape((4 * local, wide), BF16)]
    dma = pltpu.SemaphoreType.DMA
    small = (8, 128)
    in_vmem = pl.BlockSpec(memory_space=pltpu.VMEM)
    any_space = pl.BlockSpec(memory_space=pl.ANY)
    result = pl.pallas_call(
        functools.partial(forward_kernel, highs, shared, groups, count, length, group, DH),
        out_shape=tuple(fulls + outs),
        in_specs=[any_space] * count + [in_vmem, any_space] + [in_vmem] * 4,
        out_specs=tuple([any_space] * count + [in_vmem] * len(outs)),
        scratch_shapes=[
            pltpu.VMEM(band_ids.shape, jnp.int32), pltpu.VMEM(fulls[0].shape, BF16), pltpu.VMEM(fulls[1].shape, BF16),
            pltpu.VMEM(fulls[2].shape, BF16), pltpu.VMEM((rows, wide), BF16),
            pltpu.VMEM((rows, wide), BF16), pltpu.VMEM((rows, wide), BF16), pltpu.VMEM((rows, wide), F32),
            pltpu.VMEM(small, F32), pltpu.VMEM((4,) + small, F32), pltpu.VMEM((highs,) + small, F32),
            dma((total,)), dma((total, highs - 1)), dma((total, highs - 1)), dma((total, 2)), dma((total, 2)),
            dma((total,)), dma((total,)), dma((count,)), dma((count,)), dma((4,)), dma((2,)), dma((2,)),
            dma((highs + 2,)), dma((highs + 2,))],
        compiler_params=pltpu.CompilerParams(collective_id=0, has_side_effects=True, vmem_limit_bytes=VMEM_LIMIT),
        cost_estimate=pl.CostEstimate(flops=0, bytes_accessed=sum(a.size * a.dtype.itemsize * size for a in shards),
                                      transcendentals=0),
    )(*shards, pixels, band_ids, patch_weight, kept_column, table, evec)
    weights = [full.reshape(((2,) if split else ()) + (size * shard.shape[0], shard.shape[1]))
               for full, split, shard in zip(result[:count], shared, shards)]
    return weights, result[count:]


def gather_all(shards, shared):
    order_a, order_b = orders()
    fulls = []
    for number, shard in enumerate(shards):
        full = gather_dp(shard, 0, (order_a, order_b)[number % 2])
        if shared[number]:
            other, zero = other_core(full), lax.axis_index("mp") == 0
            full = jnp.stack([jnp.where(zero, full, other), jnp.where(zero, other, full)])
        fulls.append(full)
    return fulls


class Reducer:
    def __init__(self, highs, groups, weights, grads, outs, near, second, far, load_two, load_own, plane, norm, sems):
        self.highs, self.groups, self.weights = highs, groups, weights
        self.grads, self.outs = grads, outs
        self.near, self.second, self.far = near, second, far
        self.load_two, self.load_own, self.plane, self.norm = load_two, load_own, plane, norm
        self.load_sem, self.as_sem, self.ar_sem, self.bs_sem, self.br_sem, self.zs_sem, self.zr_sem = sems
        self.core, self.low, self.high, self.low_x, self.low_y = place_of()
        self.dev_x, self.dev_y = (self.high * 4 + self.low_x, self.core), (self.high * 4 + self.low_y, self.core)
        self.at_high = [(lax.rem(self.high + k, highs) * 4 + self.low, self.core) for k in range(1, highs)]
        self.pairs = (len(groups) + 1) // 2

    def in_pair(self, pair):
        return [at for at in (2 * pair, 2 * pair + 1) if 0 <= at < len(self.groups)] if 0 <= pair < self.pairs else []

    def route(self, at):
        if at % 2 == 0:
            return self.low_y, self.dev_y, self.low_x, self.dev_x
        return self.low_x, self.dev_x, self.low_y, self.dev_y

    def grad(self, at, which):
        number, start, size = self.groups[at]
        return self.grads[number].at[:, which, :, pl.ds(start, size)]

    def slot(self, ref, at, count):
        number, _, size = self.groups[at]
        return ref.at[at % count, :, pl.ds(0, self.outs[number].shape[0]), pl.ds(0, size)]

    def two_ref(self, at):
        return self.slot(self.load_two, at, 6)

    def own_ref(self, at):
        return self.slot(self.load_own, at, 8)

    def loads(self, at):
        return [pltpu.make_async_copy(self.grad(at, self.route(at)[2]), self.two_ref(at), self.load_sem.at[at, 0]),
                pltpu.make_async_copy(self.grad(at, self.low), self.own_ref(at), self.load_sem.at[at, 1])]

    def one(self, at):
        low_one, dev_one, _, _ = self.route(at)
        return [remote(self.grad(at, 3 - self.low), self.near[2 * at], self.as_sem.at[at, 0], self.ar_sem.at[at, 0], dev_one),
                remote(self.grad(at, low_one), self.near[2 * at + 1], self.as_sem.at[at, 1], self.ar_sem.at[at, 1], dev_one)]

    def two(self, at):
        return remote(self.two_ref(at), self.second[at], self.bs_sem.at[at], self.br_sem.at[at], self.route(at)[3])

    def three(self, at):
        return [remote(self.own_ref(at).at[lax.rem(self.high + k, self.highs)], self.far[at].at[k - 1],
                       self.zs_sem.at[at, k - 1], self.zr_sem.at[at, k - 1], self.at_high[k - 1])
                for k in range(1, self.highs)]

    def step(self, step):
        for at in self.in_pair(step):
            for copy in self.one(at) + self.loads(at):
                copy.start()
        for at in self.in_pair(step - 1):
            mine = self.two_ref(at)
            self.loads(at)[0].wait()
            self.one(at)[0].wait()
            mine[...] = (mine[...].astype(F32) + self.near[2 * at][...].astype(F32)).astype(BF16)
            self.two(at).start()
        for at in self.in_pair(step - 2):
            number, start, size = self.groups[at]
            mine = self.own_ref(at)
            self.loads(at)[1].wait()
            self.one(at)[1].wait()
            self.two(at).wait()
            plane = self.slot(self.plane, at, 2)
            plane[...] = (mine[...].astype(F32) + self.near[2 * at + 1][...].astype(F32)
                          + self.second[at][...].astype(F32))
            self.outs[number][:, pl.ds(start, size)] = plane[self.high]
            mine[...] = plane[...].astype(BF16)
            for copy in self.three(at):
                copy.start()
        for at in self.in_pair(step - 3):
            number, start, size = self.groups[at]
            for copy in self.three(at):
                copy.wait()
            cols = pl.ds(start, size)
            done = self.outs[number][:, cols]
            for k in range(self.highs - 1):
                done = done + self.far[at][k].astype(F32)
            self.outs[number][:, cols] = done
            self.norm[0:1, 0:1] += self.weights[number] * jnp.sum(done * done, keepdims=True)


def reducer_scratch(highs, groups, shards):
    piece = lambda lead, group: pltpu.VMEM((lead, shards[group[0]], group[2]), BF16)
    near = [piece(highs, group) for group in groups for _ in range(2)]
    second = [piece(highs, group) for group in groups]
    far = [piece(highs - 1, group) for group in groups]
    slot = (highs, max(shards), max(group[2] for group in groups))
    loads = [pltpu.VMEM((6,) + slot, BF16), pltpu.VMEM((8,) + slot, BF16), pltpu.VMEM((2,) + slot, F32)]
    dma, total = pltpu.SemaphoreType.DMA, len(groups)
    sems = [dma((total, 2)), dma((total, 2)), dma((total, 2)), dma((total,)), dma((total,)),
            dma((total, highs - 1)), dma((total, highs - 1))]
    return near + second + far + loads + sems


def make_reducer(highs, groups, weights, grads, outs, norm, refs):
    total = len(groups)
    near, second, far, refs = refs[: 2 * total], refs[2 * total : 3 * total], refs[3 * total : 4 * total], refs[4 * total :]
    return Reducer(highs, groups, weights, grads, outs, near, second, far, *refs[:3], norm, refs[3:10]), refs[10:]


def backward_kernel(highs, weights, groups, ready, count, length, group, head_dim, *refs):
    given = count - 4
    gy_ref, x1_ref, vec_ref, vgrad_ref, loss_ref, lse_ref = refs[:6]
    x_any, qkv_any, mixed_any, flat_any, pixk_any, mlp_any = refs[6:12]
    refs = refs[12:]
    grads, refs = refs[:given], refs[given:]
    outs, sums_ref, vsum_ref, refs = refs[:count], refs[count], refs[count + 1], refs[count + 2 :]
    made, refs = refs[:4], refs[4:]
    grads = tuple(grads) + tuple(made)
    (x_ref, qkv_ref, mixed_ref, flat_ref, pixk_ref, wmlp_ref, low_ref, lowt_ref, grad_ref, gradt_ref, acc_ref, part_ref,
     other_ref, last_ref, gmix_ref, gqkv_ref, stage_ref, norm_ref, spots_ref, far_ref, vnear_ref, vfar_ref) = refs[:22]
    (load_sem, wload_sem, store_sem, xs_sem, xr_sem, ns_sem, nr_sem, hs_sem, hr_sem, ts_sem, tr_sem) = refs[22:33]
    red, _ = make_reducer(highs, groups, weights, grads, outs, norm_ref, refs[33:])
    core, low, high = red.core, red.low, red.high
    spot = low * 2 + core
    sibling = (high * 4 + low, 1 - core)
    near = [(high * 4 + lax.rem(spot + k, 8) // 2, lax.rem(lax.rem(spot + k, 8), 2)) for k in range(1, 8)]
    greet(near + red.at_high)
    rows, wide = x_ref.shape
    width = mixed_ref.shape[0]
    hidden = mlp_any.shape[-1] // 2
    size = 512
    tiles = hidden // size
    mask = group_mask(group, length)

    late = [pltpu.make_async_copy(source, target, load_sem.at[at]) for at, (source, target) in enumerate(
        ((x_any, x_ref), (qkv_any, qkv_ref), (mixed_any, mixed_ref), (flat_any, flat_ref), (pixk_any, pixk_ref)))]

    def weight_loads(tile):
        return [pltpu.make_async_copy(mlp_any.at[:, :, :, pl.ds(half * hidden + tile * size, size)],
                                      wmlp_ref.at[tile % 2, half], wload_sem.at[tile % 2, half]) for half in range(2)]

    def store(slot, target, start, columns=512):
        return pltpu.make_async_copy(stage_ref.at[slot, :, :, :, pl.ds(0, columns)],
                                     target.at[:, :, :, pl.ds(start, columns)], store_sem.at[slot])

    def exchange(at, target):
        return remote(part_ref, target, xs_sem.at[at], xr_sem.at[at], sibling)

    def staged(slot, value):
        columns = value.shape[1]
        stage_ref[slot, :, :, :, :columns] = value.astype(BF16).reshape(stage_ref.shape[1:4] + (columns,))

    def mlp_first():
        unit, _ = normalize(x1_ref[...])
        value = (unit * vec_ref[3:4, :] + vec_ref[4:5, :]).astype(BF16)
        low_ref[...] = value
        lowt_ref[...] = value.T
        value = gy_ref[...].astype(BF16)
        grad_ref[...] = value
        gradt_ref[...] = value.T
        acc_ref[...] = jnp.zeros_like(acc_ref)

    def mlp_block(tile):
        for copy in weight_loads(tile):
            copy.wait()
        if tile + 1 < tiles:
            for copy in weight_loads(tile + 1):
                copy.start()
        w_up = wmlp_ref[tile % 2, 0].reshape(wide, size)
        w_down = wmlp_ref[tile % 2, 1].reshape(wide, size)
        up = dot_nn(low_ref[...], w_up)
        square, bent, half = gelu_parts(up)
        mid = (up * half).astype(BF16)
        slope = half + (0.5 * GELU_C) * up * (1.0 - bent * bent) * (1.0 + (3.0 * 0.044715) * square)
        grad_up = (dot_nn(grad_ref[...], w_down) * slope).astype(BF16)
        acc_ref[...] += dot_nt(grad_up, w_up)
        slot = 2 * (tile % 2)
        if tile >= 2:
            store(slot, made[0], (tile - 2) * size).wait()
            store(slot + 1, made[1], (tile - 2) * size).wait()
        staged(slot, dot_nn(lowt_ref[...], grad_up))
        store(slot, made[0], tile * size).start()
        staged(slot + 1, dot_nn(gradt_ref[...], mid))
        store(slot + 1, made[1], tile * size).start()

    def mlp_last():
        part_ref[...] = acc_ref[...].astype(BF16)
        exchange(0, other_ref).start()

    def stores_done(tile):
        slot = 2 * (tile % 2)
        store(slot, made[0], tile * size).wait()
        store(slot + 1, made[1], tile * size).wait()

    def rows_step(number, carry):
        at = pl.ds(pl.multiple_of(number * group, group), group)
        unit, rstd = normalize(x1_ref[at, :])
        grad_in, gain_sum, shift_sum = norm_back(both(part_ref, other_ref, at), vec_ref[3:4, :], unit, rstd)
        grad_in = grad_in + gy_ref[at, :]
        gy_ref[at, :] = grad_in
        vsum_ref[3:4, :] += gain_sum
        vsum_ref[4:5, :] += shift_sum
        low_grad = grad_in.astype(BF16)
        gradt_ref[:, at] = low_grad.T
        gmix_ref[...] = dot_nt(flat_ref[3 * width :, :], low_grad).astype(BF16)
        attend_back(qkv_ref, gmix_ref, lse_ref, gqkv_ref, at, width, head_dim, mask)
        part_ref[at, :] = dot_nn(gqkv_ref[:, at].T, flat_ref[: 3 * width, :]).astype(BF16)
        unit_a, _ = normalize(x_ref[at, :])
        lowt_ref[:, at] = (unit_a * vec_ref[1:2, :] + vec_ref[2:3, :]).astype(BF16).T
        return carry

    def attn_grads():
        for slot in range(4):
            if slot < 3:
                value = dot_nt(lowt_ref[...], gqkv_ref[pl.ds(slot * width, width), :])
            else:
                value = dot_nt(gradt_ref[...], mixed_ref[...])
            staged(slot, value)
            store(slot, made[2], slot * width, width).start()

    def enc_out():
        unit, rstd = normalize(x_ref[...])
        grad_in, gain_sum, shift_sum = norm_back(both(part_ref, last_ref, pl.ds(0, rows)), vec_ref[1:2, :], unit, rstd)
        grad_in = grad_in + gy_ref[...]
        vsum_ref[0:1, :] = jnp.sum(grad_in, axis=0, keepdims=True)
        vsum_ref[1:2, :] = gain_sum
        vsum_ref[2:3, :] = shift_sum
        share = made[3].shape[-1]
        columns = pl.ds(pl.multiple_of(core * share, share), share)
        staged(0, dot_tn(grad_in.astype(BF16), pixk_ref[:, columns]))
        store(0, made[3], 0, share).start()

    stages = functools.partial(total_blocks, vsum_ref, vnear_ref, vfar_ref, (ts_sem, tr_sem), low, high, core, highs)
    mlp_ready, attn_ready, embed_ready = ready
    row_groups = rows // group
    norm_ref[...] = jnp.zeros_like(norm_ref)
    vsum_ref[...] = vgrad_ref[...]
    for copy in weight_loads(0):
        copy.start()
    for step in range(red.pairs + 3):
        if tiles - 2 <= step - mlp_ready < tiles:
            stores_done(step - mlp_ready)
        if step == attn_ready:
            for slot in range(4):
                store(slot, made[2], slot * width, width).wait()
        if step == embed_ready:
            store(0, made[3], 0, made[3].shape[-1]).wait()
        red.step(step)
        if step == 0:
            for copy in late:
                copy.start()
            mlp_first()
        if step < tiles:
            mlp_block(step)
            if step == tiles - 1:
                mlp_last()
        if tiles <= step < attn_ready - 1:
            if step == tiles:
                for copy in late:
                    copy.wait()
                exchange(0, other_ref).wait()
            share = -(-row_groups // (attn_ready - 1 - tiles))
            start, stop = (step - tiles) * share, min((step - tiles + 1) * share, row_groups)
            if start < stop:
                lax.fori_loop(start, stop, rows_step, 0)
                if stop == row_groups:
                    exchange(1, last_ref).start()
        if step == attn_ready - 1:
            attn_grads()
        if step == embed_ready - 1:
            exchange(1, last_ref).wait()
            enc_out()
            vnear_ref[low] = vsum_ref[...]
            for copy in stages(0):
                copy.start()
        if step == embed_ready:
            for copy in stages(0):
                copy.wait()
            vsum_ref[...] = (vnear_ref[0] + vnear_ref[1]) + (vnear_ref[2] + vnear_ref[3])
            vfar_ref[high] = vsum_ref[...]
            for copy in stages(1):
                copy.start()
        if step == embed_ready + 1:
            for copy in stages(1):
                copy.wait()
            every = vfar_ref[0]
            for k in range(1, highs):
                every = every + vfar_ref[k]
            vsum_ref[...] = every
            norm_ref[0:1, 0:1] += jnp.sum(every * every, keepdims=True) * (1.0 / (8 * highs))
    norm_ref[1:2, 0:1] = jnp.sum(loss_ref[...], keepdims=True)
    spots_ref[spot] = norm_ref[...]
    copies = [remote(norm_ref, spots_ref.at[spot], ns_sem.at[k], nr_sem.at[k], near[k]) for k in range(7)]
    for copy in copies:
        copy.start()
    for copy in copies:
        copy.wait()
    local = spots_ref[0]
    for k in range(1, 8):
        local = local + spots_ref[k]
    norm_ref[...] = local
    far_ref[high] = local
    copies = [remote(norm_ref, far_ref.at[high], hs_sem.at[k], hr_sem.at[k], red.at_high[k]) for k in range(highs - 1)]
    for copy in copies:
        copy.start()
    for copy in copies:
        copy.wait()
    every = far_ref[0]
    for k in range(1, highs):
        every = every + far_ref[k]
    sums_ref[...] = every


def backward_all(gy, x1, evec, vec_grads, loss_parts, enc_saved, x0, flat, pixk, mlp, grads, length, head_dim):
    size = lax.axis_size("dp")
    highs = size // 4
    qkv, mixed, lse = enc_saved
    rows, wide = x1.shape
    width = mixed.shape[0]
    hidden = mlp.shape[1] // 2
    group = 2 * length
    shard = wide // size
    lead = (highs, 4, shard)
    fresh = [lead + (hidden,), lead + (hidden,), lead + (4 * width,), lead + (pixk.shape[1] // 2,)]
    widths = [a.shape[1] for a in grads] + [dims[-1] for dims in fresh]
    shards = [a.shape[0] // size for a in grads] + [shard] * 4
    count, given = len(widths), len(grads)
    blocks = blocks_of(widths, 512)
    first = [b for b in blocks if b[0] < given]
    if len(first) % 2:
        raise ValueError("odd blocks")
    middle = [b for at in range(0, hidden, 512) for b in ((given, at, 512), (given + 1, at, 512))]
    attn = [b for b in blocks if b[0] == given + 2]
    groups = first + middle + attn + [b for b in blocks if b[0] == given + 3]
    ready = (len(first) // 2, (len(first) + len(middle)) // 2, (len(first) + len(middle) + len(attn)) // 2)
    dma = pltpu.SemaphoreType.DMA
    small, vec_block = (8, 128), vec_grads.shape
    in_vmem = pl.BlockSpec(memory_space=pltpu.VMEM)
    any_space = pl.BlockSpec(memory_space=pl.ANY)
    result = pl.pallas_call(
        functools.partial(backward_kernel, highs, (1.0,) * count, groups, ready, count, length, group, head_dim),
        out_shape=tuple([shape((r, w), F32) for r, w in zip(shards, widths)] + [shape(small, F32), shape(vec_block, F32)]
                        + [shape(dims, BF16) for dims in fresh]),
        in_specs=[in_vmem] * 6 + [any_space] * (6 + given),
        out_specs=tuple([in_vmem] * (count + 2) + [any_space] * 4),
        scratch_shapes=[
            pltpu.VMEM((rows, wide), F32), pltpu.VMEM(qkv.shape, BF16), pltpu.VMEM(mixed.shape, BF16),
            pltpu.VMEM(flat.shape, BF16), pltpu.VMEM(pixk.shape, BF16), pltpu.VMEM((2, 2) + lead + (512,), BF16),
            pltpu.VMEM((rows, wide), BF16), pltpu.VMEM((wide, rows), BF16), pltpu.VMEM((rows, wide), BF16),
            pltpu.VMEM((wide, rows), BF16), pltpu.VMEM((rows, wide), F32), pltpu.VMEM((rows, wide), BF16),
            pltpu.VMEM((rows, wide), BF16), pltpu.VMEM((rows, wide), BF16), pltpu.VMEM((width, group), BF16),
            pltpu.VMEM((3 * width, rows), BF16), pltpu.VMEM((4,) + lead + (512,), BF16), pltpu.VMEM(small, F32),
            pltpu.VMEM((8,) + small, F32), pltpu.VMEM((highs,) + small, F32), pltpu.VMEM((4,) + vec_block, F32),
            pltpu.VMEM((highs,) + vec_block, F32),
            dma((5,)), dma((2, 2)), dma((4,)), dma((2,)), dma((2,)), dma((7,)), dma((7,)), dma((highs - 1,)),
            dma((highs - 1,)), dma((highs + 2,)), dma((highs + 2,))] + reducer_scratch(highs, groups, shards),
        compiler_params=pltpu.CompilerParams(collective_id=1, has_side_effects=True, vmem_limit_bytes=62 * 2**20),
        cost_estimate=pl.CostEstimate(flops=0, bytes_accessed=sum(a.size * 2 for a in grads), transcendentals=0),
    )(gy, x1, evec, vec_grads, loss_parts, lse, x0, qkv, mixed, flat, pixk, mlp.reshape(lead + (2 * hidden,)),
      *[a.reshape(highs, 4, r, a.shape[1]) for r, a in zip(shards, grads)])
    return list(result[:count]), result[count][0, 0], 0.5 * result[count][1, 0], result[count + 1]


def reduce_plain(grads, loss_parts, vec_grads):
    order_a, order_b = orders()
    outs = [reduce_dp(a, 0, (order_a, order_b)[number % 2], a.dtype) for number, a in enumerate(grads)]
    vec_sums = total_dp(vec_grads)
    sums = jnp.stack([sum(jnp.sum(a * a) for a in outs), jnp.sum(loss_parts)])
    sums = total_dp(sums)
    sums = sums + other_core(sums)
    return outs, sums[0] + jnp.sum(vec_sums * vec_sums), 0.5 * sums[1], vec_sums


def adam_update(master, gradient, first_old, second_old, step_rate, decay_rate):
    first_new = BETA_ONE * first_old + (1.0 - BETA_ONE) * gradient
    second_new = BETA_TWO * second_old + (1.0 - BETA_TWO) * gradient * gradient
    first_hat = first_new / (1.0 - BETA_ONE**STEP)
    second_hat = second_new / (1.0 - BETA_TWO**STEP)
    updated = master - step_rate * (
        first_hat / (jnp.sqrt(second_hat) + ADAM_EPS) + decay_rate * master
    )
    return (updated, first_new, second_new)


def per_device(
    pixels,
    target,
    band_ids,
    kept_index,
    intersection,
    gsd_scale,
    enc_attn,
    enc_mlp,
    dec_attn,
    dec_mlp,
    patch_embed,
    bridge,
    predict,
    vectors,
    first_enc_attn,
    first_enc_mlp,
    first_dec_attn,
    first_dec_mlp,
    first_patch_embed,
    first_bridge,
    first_predict,
    first_vectors,
    second_enc_attn,
    second_enc_mlp,
    second_dec_attn,
    second_dec_mlp,
    second_patch_embed,
    second_bridge,
    second_predict,
    second_vectors,
    ema_enc_attn,
    ema_enc_mlp,
    ema_patch_embed,
):
    masters = (enc_attn, enc_mlp, dec_attn, dec_mlp, patch_embed, bridge, predict, vectors)
    firsts = (
        first_enc_attn,
        first_enc_mlp,
        first_dec_attn,
        first_dec_mlp,
        first_patch_embed,
        first_bridge,
        first_predict,
        first_vectors,
    )
    seconds = (
        second_enc_attn,
        second_enc_mlp,
        second_dec_attn,
        second_dec_mlp,
        second_patch_embed,
        second_bridge,
        second_predict,
        second_vectors,
    )
    images, keep_count = kept_index.shape
    patch_count = intersection.shape[1]
    patch_index = jnp.arange(patch_count, dtype=jnp.int32)
    kept_flags = jnp.any(kept_index[:, :, None] == patch_index[None, None, :], axis=1).astype(
        jnp.float32
    )
    patch_weight = ((1.0 - kept_flags) * (1.0 - 0.5 * intersection.astype(jnp.float32))).reshape(
        -1, 1
    )
    core_at = lax.axis_index("mp")
    size = lax.axis_size("dp")
    low = jnp.bfloat16

    def flat(stack):
        return jnp.concatenate([part.astype(low) for part in stack], axis=1)

    def core_half(block):
        return lax.dynamic_slice_in_dim(block, core_at * (block.shape[1] // 2), block.shape[1] // 2, 1).astype(low)

    vec_shard = vectors.shape[0]
    vec_room = -(-vec_shard // 1024) * 1024
    vec_rows = jnp.pad(lax.reduce_precision(vectors, 8, 7), (0, vec_room - vec_shard)).reshape(-1, 128)
    whole_tiles = patch_embed.shape[1] % 16 == 0 and dec_attn.shape[1] % 16 == 0
    vec_full = small_gather(vec_rows) if whole_tiles else gather_dp(vec_rows, 0, orders()[0])
    pieces = split_vectors(vec_full.reshape(size, vec_room)[:, :vec_shard].reshape(-1), D, E)
    evec = jnp.stack(pieces[:7] + [jnp.zeros_like(pieces[0])])
    dvec = jnp.stack(pieces[7:14] + [jnp.zeros_like(pieces[7])])
    kept_column = kept_index.reshape(-1, 1)
    rows, rows_d = images * keep_count, images * patch_count
    pixel_count = pixels.shape[1]
    group = 2 * keep_count
    shards = [core_half(patch_embed.T), flat(enc_attn), flat(enc_mlp), flat(dec_attn), flat(dec_mlp), core_half(bridge),
              core_half(predict)]
    shared = (True, False, False, False, False, True, True)
    enc_table = sine_table(gsd_scale, D, GRID)
    if whole_tiles:
        weights, results = forward_all(shards, shared, pixels, band_ids, patch_weight, kept_column, enc_table, evec)
        embed_w, enc_attn_w, enc_mlp_w, dec_attn_w, dec_mlp_w, bridge_w, predict_w = weights
        x0, *enc_saved, kept_pixels, x1, part, other, counts, enc_flat = results
        band_weight = jnp.sum(counts[:NB], axis=1)
    else:
        weights = gather_all(shards, shared)
        embed_w, enc_attn_w, enc_mlp_w, dec_attn_w, dec_mlp_w, bridge_w, predict_w = weights
        local = enc_attn_w.shape[1] // 4
        band_weight = total_dp(jnp.stack([
            jnp.sum(jnp.where(band_ids == level, patch_weight, 0.0)) for level in range(NB)]))
        x0, *enc_saved, part, kept_pixels = run(
            functools.partial(enc_in_kernel, keep_count, group, DH),
            [shape((rows, D), F32), shape((3 * local, rows), BF16), shape((local, rows), BF16),
             shape((local // DH, rows), F32), shape((rows, D), BF16), shape((rows, pixel_count), BF16)],
            [pltpu.VMEM((4 * local, D), BF16)],
            (pixels, kept_column, enc_table, embed_w, evec, enc_attn_w),
            rows * D * (2 * pixel_count + 8 * local))
        x1, part = mlp_forward(x0, part, evec, enc_mlp_w)
        other = other_core(part)
    inverse = 1.0 / band_weight
    core = lax.axis_index("mp").astype(jnp.int32).reshape(1)
    hidden_rows = (1.0 - kept_flags).reshape(-1, 1)
    local_d = dec_attn_w.shape[1] // 4
    x2, final_enc, xd, *dec_saved, part = run(
        functools.partial(dec_in_kernel, keep_count, DDH),
        [shape((rows, D), F32), shape((rows, D), BF16), shape((rows_d, E), F32), shape((3 * local_d, rows_d), BF16),
         shape((local_d, rows_d), BF16), shape((local_d // DDH, rows_d), F32), shape((rows_d, E), BF16)],
        [pltpu.VMEM((4 * local_d, E), BF16), pltpu.VMEM((rows, E), F32)],
        (x1, part, other, evec, bridge_w, kept_index, hidden_rows, sine_table(gsd_scale, E, GRID), dvec,
         dec_attn_w),
        rows_d * E * 8 * local_d + 2 * rows * D * E)
    xd1, part = mlp_forward(xd, part, dvec, dec_mlp_w)
    gyd, grad_predict, grad_pbias, loss_parts, grad_dec_fg, grad_dec_fb = head(
        core, inverse, xd1, part, dvec, pieces[14].reshape(1, -1), predict_w, target, band_ids, patch_weight, patch_count)
    grad_dec_up, grad_dec_down, part = mlp_backward(gyd, xd1, dvec, dec_mlp_w)
    gxd, grad_dec_attn, grad_dec_gb, grad_dec_bb, part = attn_backward(
        gyd, xd1, part, xd, dec_saved, dvec, dec_attn_w, patch_count, patch_count, DDH)
    one_d, one_e = shape((1, D), F32), shape((1, E), F32)
    grad_dec_ga, grad_dec_ba, grad_mask, grad_bridge, grad_enc_fg, grad_enc_fb, gye = run(
        functools.partial(between_kernel, keep_count),
        [one_e, one_e, one_e, shape((D, E // 2), BF16), one_d, one_d, shape((rows, D), F32)],
        [pltpu.VMEM((rows, E), BF16)],
        (core, gxd, xd, part, other_core(part), dvec, kept_column, hidden_rows, final_enc, x2, evec, bridge_w),
        3 * rows * D * E, 1)
    wide_row = lambda row: jnp.pad(row, ((0, 0), (0, D - row.shape[1])))
    no_row = jnp.zeros((1, D), F32)
    late_rows = [grad_enc_fg, grad_enc_fb] + [wide_row(row) for row in (
        grad_mask, grad_dec_ga, grad_dec_ba, grad_dec_gb, grad_dec_bb, grad_dec_fg, grad_dec_fb, grad_pbias)] + [no_row]
    dec_grads = [grad_predict, grad_dec_up, grad_dec_down, grad_dec_attn, grad_bridge]
    if whole_tiles:
        sums, total_squares, loss, vec_sums = backward_all(
            gye, x1, evec, jnp.concatenate([no_row] * 5 + late_rows), loss_parts, enc_saved, x0, enc_flat, kept_pixels,
            enc_mlp_w, dec_grads, keep_count, DH)
    else:
        grad_enc_up, grad_enc_down, part = mlp_backward(gye, x1, evec, enc_mlp_w)
        gxe, grad_enc_attn, grad_enc_gb, grad_enc_bb, part = attn_backward(
            gye, x1, part, x0, enc_saved, evec, enc_attn_w, keep_count, group, DH)
        grad_enc_ga, grad_enc_ba, grad_ebias, grad_embed = run(
            enc_out_kernel,
            [one_d, one_d, one_d, shape((D, pixel_count // 2), BF16)],
            [], (core, gxe, x0, part, other_core(part), evec, kept_pixels), rows * D * pixel_count, 1)
        vec_grads = jnp.concatenate([grad_ebias, grad_enc_ga, grad_enc_ba, grad_enc_gb, grad_enc_bb] + late_rows)
        sums, total_squares, loss, vec_sums = reduce_plain(
            dec_grads + [grad_enc_up, grad_enc_down, grad_enc_attn, grad_embed], loss_parts, vec_grads)
    vec_grad = jnp.concatenate([vec_sums[:7].reshape(-1), vec_sums[7:14, :E].reshape(-1), vec_sums[14, :pixel_count]])
    vec_grad = lax.dynamic_slice_in_dim(vec_grad, lax.axis_index("dp") * vec_shard, vec_shard)
    reduced = (
        jnp.stack(jnp.split(sums[7], 4, axis=1)),
        jnp.stack(sums[5:7]),
        jnp.stack(jnp.split(sums[3], 4, axis=1)),
        jnp.stack(sums[1:3]),
        join_cores(sums[8], core).T,
        join_cores(sums[4], core),
        join_cores(sums[0], core),
        vec_grad,
    )
    grad_norm = jnp.sqrt(total_squares)
    factor = CLIP / jnp.maximum(grad_norm, CLIP)
    news, new_firsts, new_seconds = ([], [], [])
    for position, master in enumerate(masters):
        is_vec = position == 7
        updated, first_new, second_new = adam_update(
            master,
            reduced[position] * factor,
            firsts[position],
            seconds[position],
            RATE_VEC if is_vec else RATE_MAT,
            0.0 if is_vec else DECAY_MAT,
        )
        news.append(updated)
        new_firsts.append(first_new)
        new_seconds.append(second_new)
    ema_attn = EMA_KEEP * ema_enc_attn + (1.0 - EMA_KEEP) * news[0]
    ema_mlp = EMA_KEEP * ema_enc_mlp + (1.0 - EMA_KEEP) * news[1]
    ema_embed = EMA_KEEP * ema_patch_embed + (1.0 - EMA_KEEP) * news[4]
    return (
        loss,
        band_weight,
        grad_norm,
        news[0],
        news[1],
        news[2],
        news[3],
        news[4],
        news[5],
        news[6],
        news[7],
        new_firsts[0],
        new_firsts[1],
        new_firsts[2],
        new_firsts[3],
        new_firsts[4],
        new_firsts[5],
        new_firsts[6],
        new_firsts[7],
        new_seconds[0],
        new_seconds[1],
        new_seconds[2],
        new_seconds[3],
        new_seconds[4],
        new_seconds[5],
        new_seconds[6],
        new_seconds[7],
        ema_attn,
        ema_mlp,
        ema_embed,
    )


def solution(mesh):
    return jax.shard_map(
        per_device,
        mesh=mesh,
        in_specs=(
            P("dp", None),
            P("dp", None),
            P("dp", None),
            P("dp", None),
            P("dp", None),
            P("dp"),
            P(None, "dp", "mp"),
            P(None, "dp", "mp"),
            P(None, "dp", "mp"),
            P(None, "dp", "mp"),
            P(None, "dp"),
            P("dp", None),
            P("dp", None),
            P("dp"),
            P(None, "dp", "mp"),
            P(None, "dp", "mp"),
            P(None, "dp", "mp"),
            P(None, "dp", "mp"),
            P(None, "dp"),
            P("dp", None),
            P("dp", None),
            P("dp"),
            P(None, "dp", "mp"),
            P(None, "dp", "mp"),
            P(None, "dp", "mp"),
            P(None, "dp", "mp"),
            P(None, "dp"),
            P("dp", None),
            P("dp", None),
            P("dp"),
            P(None, "dp", "mp"),
            P(None, "dp", "mp"),
            P(None, "dp"),
        ),
        out_specs=(
            P(),
            P(),
            P(),
            P(None, "dp", "mp"),
            P(None, "dp", "mp"),
            P(None, "dp", "mp"),
            P(None, "dp", "mp"),
            P(None, "dp"),
            P("dp", None),
            P("dp", None),
            P("dp"),
            P(None, "dp", "mp"),
            P(None, "dp", "mp"),
            P(None, "dp", "mp"),
            P(None, "dp", "mp"),
            P(None, "dp"),
            P("dp", None),
            P("dp", None),
            P("dp"),
            P(None, "dp", "mp"),
            P(None, "dp", "mp"),
            P(None, "dp", "mp"),
            P(None, "dp", "mp"),
            P(None, "dp"),
            P("dp", None),
            P("dp", None),
            P("dp"),
            P(None, "dp", "mp"),
            P(None, "dp", "mp"),
            P(None, "dp"),
        ),
        check_vma=False,
    )
```

```python
import functools
import math

import jax
import jax.numpy as jnp
from jax import lax
from jax.experimental import pallas as pl
from jax.experimental.pallas import tpu as pltpu
from jax.sharding import PartitionSpec as P

D = 1024
DH = 64
E = 512
DDH = 32
GRID = 16
NB = 3
STEP = 10


EPS_LN = 1e-06
EPS_C = 0.01
CLIP = 0.0002
BETA_ONE = 0.9
BETA_TWO = 0.999
ADAM_EPS = 1e-12
RATE_MAT = 0.06
RATE_VEC = 0.5
DECAY_MAT = 0.05
EMA_KEEP = 0.9
REF_GSD = 4.0


def split_vectors(flat_vec, enc_width, dec_width):
    lengths = [enc_width] * 7 + [dec_width] * 7
    pieces = []
    offset = 0
    for length in lengths:
        pieces.append(flat_vec[offset : offset + length])
        offset = offset + length
    pieces.append(flat_vec[offset:])
    return pieces


F32 = jnp.float32
BF16 = jnp.bfloat16
VMEM_LIMIT = 58 * 2**20
GELU_C = math.sqrt(2.0 / math.pi)


def dot_nn(left, right):
    return jnp.dot(left, right, preferred_element_type=F32)


def dot_nt(left, right):
    return lax.dot_general(left, right, (((1,), (1,)), ((), ())), preferred_element_type=F32)


def dot_tn(left, right):
    return lax.dot_general(left, right, (((0,), (0,)), ((), ())), preferred_element_type=F32)


def dot_exact(left, right):
    return jnp.dot(left, right, preferred_element_type=F32, precision=lax.Precision.HIGHEST)


def normalize(rows):
    centred = rows - jnp.mean(rows, axis=-1, keepdims=True)
    rstd = lax.rsqrt(jnp.mean(centred * centred, axis=-1, keepdims=True) + EPS_LN)
    return centred * rstd, rstd


def norm_back(grad, gain, unit, rstd):
    scaled = grad * gain
    mean_one = jnp.mean(scaled, axis=-1, keepdims=True)
    mean_two = jnp.mean(scaled * unit, axis=-1, keepdims=True)
    grad_in = rstd * (scaled - mean_one - unit * mean_two)
    return (
        grad_in,
        jnp.sum(grad * unit, axis=0, keepdims=True),
        jnp.sum(grad, axis=0, keepdims=True),
    )


def both(mine_ref, other_ref, rows):
    return mine_ref[rows, :].astype(F32) + other_ref[rows, :].astype(F32)


def gelu_parts(up):
    square = up * up
    bent = jnp.tanh(GELU_C * up * (1.0 + 0.044715 * square))
    half = 0.5 * (1.0 + bent)
    return square, bent, half


def group_mask(group, length):
    if group == length:
        return None
    row_image = lax.broadcasted_iota(jnp.int32, (group, group), 0) // length
    col_image = lax.broadcasted_iota(jnp.int32, (group, group), 1) // length
    return row_image == col_image


def attend(qkv_ref, mixed_ref, lse_ref, cols, width, head_dim, mask):
    scale = head_dim ** (-0.5)
    for head in range(width // head_dim):
        at = pl.ds(head * head_dim, head_dim)
        queries = qkv_ref[at, cols]
        keys = qkv_ref[pl.ds(width + head * head_dim, head_dim), cols]
        values = qkv_ref[pl.ds(2 * width + head * head_dim, head_dim), cols]
        scores = dot_tn(keys, queries) * scale
        if mask is not None:
            scores = jnp.where(mask, scores, -1e30)
        top = jnp.max(scores, axis=0, keepdims=True)
        weights = jnp.exp(scores - top)
        total = jnp.sum(weights, axis=0, keepdims=True)
        lse_ref[pl.ds(head, 1), cols] = top + jnp.log(total)
        soft = (weights * (1.0 / total)).astype(BF16)
        mixed_ref[at, cols] = dot_nn(values, soft).astype(BF16)


def attend_back(qkv_ref, grad_ref, lse_ref, out_ref, cols, width, head_dim, mask):
    scale = head_dim ** (-0.5)
    for head in range(width // head_dim):
        at = pl.ds(head * head_dim, head_dim)
        at_k = pl.ds(width + head * head_dim, head_dim)
        at_v = pl.ds(2 * width + head * head_dim, head_dim)
        queries, keys, values = qkv_ref[at, cols], qkv_ref[at_k, cols], qkv_ref[at_v, cols]
        grad = grad_ref[at, :]
        scores = dot_tn(keys, queries) * scale
        if mask is not None:
            scores = jnp.where(mask, scores, -1e30)
        soft = jnp.exp(scores - lse_ref[pl.ds(head, 1), cols])
        out_ref[at_v, cols] = dot_nt(grad, soft.astype(BF16)).astype(BF16)
        grad_soft = dot_tn(values, grad)
        inner = jnp.sum(soft * grad_soft, axis=0, keepdims=True)
        grad_scores = (soft * (grad_soft - inner)).astype(BF16)
        out_ref[at, cols] = (dot_nn(keys, grad_scores) * scale).astype(BF16)
        out_ref[at_k, cols] = (dot_nt(queries, grad_scores) * scale).astype(BF16)


def transposed_weights(attn_ref, flat_ref):
    width = attn_ref.shape[1] // 4
    for part in range(4):
        at = pl.ds(part * width, width)
        flat_ref[at, :] = attn_ref[:, at].T


def attention_rows(unit, vec_ref, flat_ref, qkv_ref, mixed_ref, lse_ref, part_ref, rows, head_dim, mask, attn_ref):
    width = mixed_ref.shape[0]
    low = (unit * vec_ref[1:2, :] + vec_ref[2:3, :]).astype(BF16)
    qkv_ref[:, rows] = dot_nt(flat_ref[: 3 * width, :], low).astype(BF16)
    attend(qkv_ref, mixed_ref, lse_ref, rows, width, head_dim, mask)
    part_ref[rows, :] = dot_nt(mixed_ref[:, rows].T, attn_ref[:, 3 * width :]).astype(BF16)


def enc_in_kernel(length, group, head_dim, pix_ref, kept_ref, table_ref, embed_ref, vec_ref, attn_ref,
                  x_ref, qkv_ref, mixed_ref, lse_ref, part_ref, pixk_ref, flat_ref):
    images, patches = table_ref.shape[0], pix_ref.shape[0] // table_ref.shape[0]
    side = table_ref.shape[1]
    transposed_weights(attn_ref, flat_ref)

    def pick(image, carry):
        rows = pl.ds(image * length, length)
        index = kept_ref[rows, :]
        hot = lax.broadcasted_iota(jnp.int32, (length, patches), 1) == index
        pixels = pix_ref[pl.ds(image * patches, patches), :]
        pixk_ref[rows, :] = dot_nn(hot.astype(BF16), pixels).astype(BF16)
        grid_at = lax.broadcasted_iota(jnp.int32, (length, side), 1)
        table = table_ref[image]
        half = table.shape[1]
        x_ref[rows, :half] = dot_exact((grid_at == index // side).astype(F32), table)
        x_ref[rows, half:] = dot_exact((grid_at == index % side).astype(F32), table)
        return carry

    lax.fori_loop(0, images, pick, 0)
    mask = group_mask(group, length)

    def step(number, carry):
        rows = pl.ds(pl.multiple_of(number * group, group), group)
        share = embed_ref.shape[2]
        rows_x = dot_nt(pixk_ref[rows, :share], embed_ref[0]) + dot_nt(pixk_ref[rows, share:], embed_ref[1])
        rows_x = rows_x + vec_ref[0:1, :] + x_ref[rows, :]
        x_ref[rows, :] = rows_x
        unit, _ = normalize(rows_x)
        attention_rows(unit, vec_ref, flat_ref, qkv_ref, mixed_ref, lse_ref, part_ref, rows, head_dim, mask, attn_ref)
        return carry

    lax.fori_loop(0, x_ref.shape[0] // group, step, 0)


def dec_in_kernel(length, head_dim, x1_ref, mine_ref, other_ref, evec_ref, bridge_ref, kept_ref, hidden_ref,
                  table_ref, vec_ref, attn_ref,
                  x2_ref, final_ref, x_ref, qkv_ref, mixed_ref, lse_ref, part_ref, flat_ref, latent_ref):
    images, side, half = table_ref.shape
    patches = side * side
    transposed_weights(attn_ref, flat_ref)
    every = pl.ds(0, x1_ref.shape[0])
    out = x1_ref[...] + both(mine_ref, other_ref, every)
    x2_ref[...] = out
    unit, _ = normalize(out)
    final = (unit * evec_ref[5:6, :] + evec_ref[6:7, :]).astype(BF16)
    final_ref[...] = final
    share = bridge_ref.shape[2]
    latent_ref[:, :share] = dot_nn(final, bridge_ref[0])
    latent_ref[:, share:] = dot_nn(final, bridge_ref[1])

    def step(image, carry):
        rows = pl.ds(pl.multiple_of(image * patches, patches), patches)
        hot = lax.broadcasted_iota(jnp.int32, (patches, length), 0) == kept_ref[pl.ds(image, 1), :]
        latent = latent_ref[pl.ds(image * length, length), :]
        table = table_ref[image]
        by_row = jnp.broadcast_to(table[:, None, :], (side, side, half)).reshape(patches, half)
        by_col = jnp.broadcast_to(table[None, :, :], (side, side, half)).reshape(patches, half)
        place = jnp.concatenate([by_row, by_col], axis=1)
        rows_x = dot_exact(hot.astype(F32), latent) + hidden_ref[rows, :] * vec_ref[0:1, :] + place
        x_ref[rows, :] = rows_x
        unit, _ = normalize(rows_x)
        attention_rows(unit, vec_ref, flat_ref, qkv_ref, mixed_ref, lse_ref, part_ref, rows, head_dim, None, attn_ref)
        return carry

    lax.fori_loop(0, images, step, 0)


def mlp_kernel(tile, x_ref, mine_ref, other_ref, vec_ref, up_ref, down_ref, x1_ref, part_ref, low_ref, acc_ref):
    number = pl.program_id(0)
    count = x_ref.shape[0] // tile

    def first(step, carry):
        rows = pl.ds(pl.multiple_of(step * tile, tile), tile)
        after = x_ref[rows, :] + both(mine_ref, other_ref, rows)
        x1_ref[rows, :] = after
        unit, _ = normalize(after)
        low_ref[rows, :] = (unit * vec_ref[3:4, :] + vec_ref[4:5, :]).astype(BF16)
        return carry

    @pl.when(number == 0)
    def _():
        lax.fori_loop(0, count, first, 0)
        acc_ref[...] = jnp.zeros_like(acc_ref)

    def step(piece, carry):
        rows = pl.ds(pl.multiple_of(piece * tile, tile), tile)
        up = dot_nn(low_ref[rows, :], up_ref[...])
        _, _, half = gelu_parts(up)
        acc_ref[rows, :] += dot_nt((up * half).astype(BF16), down_ref[...])
        return carry

    lax.fori_loop(0, count, step, 0)

    @pl.when(number == pl.num_programs(0) - 1)
    def _():
        part_ref[...] = acc_ref[...].astype(BF16)


def head_kernel(core_ref, inverse_ref, x1_ref, mine_ref, other_ref, vec_ref, bias_ref, predict_ref, target_ref,
                band_ref, weight_ref, gy_ref, glow_ref, gbias_ref, loss_ref, gain_ref, shift_ref, low_ref, gpred_ref):
    number = pl.program_id(0)

    @pl.when(number == 0)
    def _():
        for ref in (gpred_ref, gbias_ref, loss_ref, gain_ref, shift_ref):
            ref[...] = jnp.zeros_like(ref)

    every = pl.ds(0, x1_ref.shape[0])
    unit, rstd = normalize(x1_ref[...] + both(mine_ref, other_ref, every))
    gain = vec_ref[5:6, :]
    final = (unit * gain + vec_ref[6:7, :]).astype(BF16)
    share = gpred_ref.shape[1]
    predicted = jnp.concatenate([dot_nn(final, predict_ref[0]), dot_nn(final, predict_ref[1])], axis=1)
    mismatch = predicted + bias_ref[...] - target_ref[...].astype(F32)
    band = band_ref[...]
    level = jnp.where(band == 0, inverse_ref[0], jnp.where(band == 1, inverse_ref[1], inverse_ref[2]))
    level = level * weight_ref[...]
    square = mismatch * mismatch + EPS_C
    root = lax.rsqrt(square)
    loss_ref[...] += jnp.sum(level * (square * root), axis=0, keepdims=True)
    grad = level * (mismatch * root)
    gbias_ref[...] += jnp.sum(grad, axis=0, keepdims=True)
    low_ref[...] = grad.astype(BF16)
    columns = pl.ds(pl.multiple_of(core_ref[0] * share, share), share)
    gpred_ref[...] += dot_tn(final, low_ref[:, columns])
    grad_final = dot_nt(low_ref[:, :share], predict_ref[0]) + dot_nt(low_ref[:, share:], predict_ref[1])
    grad_in, gain_sum, shift_sum = norm_back(grad_final, gain, unit, rstd)
    gy_ref[...] = grad_in
    gain_ref[...] += gain_sum
    shift_ref[...] += shift_sum

    @pl.when(number == pl.num_programs(0) - 1)
    def _():
        glow_ref[...] = gpred_ref[...].astype(BF16)


def mlp_back_kernel(tile, gy_ref, x1_ref, vec_ref, up_ref, down_ref, gup_ref, gdown_ref, part_ref,
                    low_ref, lowt_ref, grad_ref, gradt_ref, gu_ref, z_ref, acc_ref):
    number = pl.program_id(0)
    count = x1_ref.shape[0] // tile

    def first(step, carry):
        rows = pl.ds(pl.multiple_of(step * tile, tile), tile)
        unit, _ = normalize(x1_ref[rows, :])
        low = (unit * vec_ref[3:4, :] + vec_ref[4:5, :]).astype(BF16)
        low_ref[rows, :] = low
        lowt_ref[:, rows] = low.T
        grad = gy_ref[rows, :].astype(BF16)
        grad_ref[rows, :] = grad
        gradt_ref[:, rows] = grad.T
        return carry

    @pl.when(number == 0)
    def _():
        lax.fori_loop(0, count, first, 0)
        acc_ref[...] = jnp.zeros_like(acc_ref)

    def step(piece, carry):
        rows = pl.ds(pl.multiple_of(piece * tile, tile), tile)
        up = dot_nn(low_ref[rows, :], up_ref[...])
        square, bent, half = gelu_parts(up)
        z_ref[rows, :] = (up * half).astype(BF16)
        slope = half + (0.5 * GELU_C) * up * (1.0 - bent * bent) * (1.0 + (3.0 * 0.044715) * square)
        grad_up = (dot_nn(grad_ref[rows, :], down_ref[...]) * slope).astype(BF16)
        gu_ref[rows, :] = grad_up
        acc_ref[rows, :] += dot_nt(grad_up, up_ref[...])
        return carry

    lax.fori_loop(0, count, step, 0)
    gup_ref[...] = dot_nn(lowt_ref[...], gu_ref[...]).astype(BF16)
    gdown_ref[...] = dot_nn(gradt_ref[...], z_ref[...]).astype(BF16)

    @pl.when(number == pl.num_programs(0) - 1)
    def _():
        part_ref[...] = acc_ref[...].astype(BF16)


def attn_back_kernel(length, group, head_dim, gy_ref, x1_ref, mine_ref, other_ref, x_ref, qkv_ref, mixed_ref, lse_ref,
                     vec_ref, attn_ref, gx_ref, grad_ref, gain_ref, shift_ref, part_ref,
                     flat_ref, lowt_ref, gradt_ref, gmix_ref, gqkv_ref):
    width = mixed_ref.shape[0]
    transposed_weights(attn_ref, flat_ref)
    gain_ref[...] = jnp.zeros_like(gain_ref)
    shift_ref[...] = jnp.zeros_like(shift_ref)
    mask = group_mask(group, length)

    def step(number, carry):
        rows = pl.ds(pl.multiple_of(number * group, group), group)
        unit, rstd = normalize(x1_ref[rows, :])
        grad_in, gain_sum, shift_sum = norm_back(both(mine_ref, other_ref, rows), vec_ref[3:4, :], unit, rstd)
        grad_in = grad_in + gy_ref[rows, :]
        gx_ref[rows, :] = grad_in
        gain_ref[...] += gain_sum
        shift_ref[...] += shift_sum
        low_grad = grad_in.astype(BF16)
        gradt_ref[:, rows] = low_grad.T
        gmix_ref[...] = dot_nt(flat_ref[3 * width :, :], low_grad).astype(BF16)
        attend_back(qkv_ref, gmix_ref, lse_ref, gqkv_ref, rows, width, head_dim, mask)
        part_ref[rows, :] = dot_nn(gqkv_ref[:, rows].T, flat_ref[: 3 * width, :]).astype(BF16)
        unit_a, _ = normalize(x_ref[rows, :])
        lowt_ref[:, rows] = (unit_a * vec_ref[1:2, :] + vec_ref[2:3, :]).astype(BF16).T
        return carry

    lax.fori_loop(0, x_ref.shape[0] // group, step, 0)
    grad_ref[:, : 3 * width] = dot_nt(lowt_ref[...], gqkv_ref[...]).astype(BF16)
    grad_ref[:, 3 * width :] = dot_nt(gradt_ref[...], mixed_ref[...]).astype(BF16)


def between_kernel(length, core_ref, gx_ref, x_ref, mine_ref, other_ref, vec_ref, kept_ref, hidden_ref, final_ref, x2_ref,
                   evec_ref, bridge_ref, gain_ref, shift_ref, mask_ref, gbridge_ref, egain_ref, eshift_ref, gy_ref,
                   latent_ref):
    images = kept_ref.shape[0] // length
    patches = x_ref.shape[0] // images
    for ref in (gain_ref, shift_ref, mask_ref):
        ref[...] = jnp.zeros_like(ref)

    def step(image, carry):
        rows = pl.ds(pl.multiple_of(image * patches, patches), patches)
        unit, rstd = normalize(x_ref[rows, :])
        grad_in, gain_sum, shift_sum = norm_back(both(mine_ref, other_ref, rows), vec_ref[1:2, :], unit, rstd)
        grad_in = grad_in + gx_ref[rows, :]
        gain_ref[...] += gain_sum
        shift_ref[...] += shift_sum
        mask_ref[...] += jnp.sum(grad_in * hidden_ref[rows, :], axis=0, keepdims=True)
        kept_rows = pl.ds(pl.multiple_of(image * length, length), length)
        hot = lax.broadcasted_iota(jnp.int32, (length, patches), 1) == kept_ref[kept_rows, :]
        latent_ref[kept_rows, :] = dot_nn(hot.astype(BF16), grad_in.astype(BF16)).astype(BF16)
        return carry

    lax.fori_loop(0, images, step, 0)
    share = gbridge_ref.shape[1]
    columns = pl.ds(pl.multiple_of(core_ref[0] * share, share), share)
    gbridge_ref[...] = dot_tn(final_ref[...], latent_ref[:, columns]).astype(BF16)
    grad_final = dot_nt(latent_ref[:, :share], bridge_ref[0]) + dot_nt(latent_ref[:, share:], bridge_ref[1])
    unit, rstd = normalize(x2_ref[...])
    gy_ref[...], egain_ref[...], eshift_ref[...] = norm_back(grad_final, evec_ref[5:6, :], unit, rstd)


def enc_out_kernel(core_ref, gx_ref, x_ref, mine_ref, other_ref, vec_ref, pixk_ref,
                   gain_ref, shift_ref, ebias_ref, gembed_ref):
    every = pl.ds(0, x_ref.shape[0])
    unit, rstd = normalize(x_ref[...])
    grad_in, gain_ref[...], shift_ref[...] = norm_back(both(mine_ref, other_ref, every), vec_ref[1:2, :], unit, rstd)
    grad_in = grad_in + gx_ref[...]
    ebias_ref[...] = jnp.sum(grad_in, axis=0, keepdims=True)
    share = gembed_ref.shape[1]
    columns = pl.ds(pl.multiple_of(core_ref[0] * share, share), share)
    gembed_ref[...] = dot_tn(grad_in.astype(BF16), pixk_ref[:, columns]).astype(BF16)


def shape(dims, dtype):
    return jax.ShapeDtypeStruct(dims, dtype)


def run(kernel, outs, scratch, args, flops, scalars=0):
    moved = sum(math.prod(a.shape) * a.dtype.itemsize for a in list(args) + list(outs))
    in_vmem = pl.BlockSpec(memory_space=pltpu.VMEM)
    return pl.pallas_call(
        kernel,
        out_shape=tuple(outs),
        in_specs=[pl.BlockSpec(memory_space=pltpu.SMEM)] * scalars + [in_vmem] * (len(args) - scalars),
        out_specs=tuple([in_vmem] * len(outs)),
        scratch_shapes=scratch,
        compiler_params=pltpu.CompilerParams(vmem_limit_bytes=VMEM_LIMIT),
        cost_estimate=pl.CostEstimate(flops=flops, bytes_accessed=moved, transcendentals=0),
    )(*args)


def other_core(block):
    return lax.ppermute(block, "mp", [(0, 1), (1, 0)])


def mlp_forward(x, mine, vec, stack):
    rows, width = x.shape
    hidden = stack.shape[1] // 2
    block = min(hidden, 512)
    tile = min(rows, 512)
    other = other_core(mine)
    whole = pl.BlockSpec((rows, width), lambda i: (0, 0))
    cols = pl.BlockSpec((width, block), lambda i: (0, i))
    later = pl.BlockSpec((width, block), lambda i: (0, i + hidden // block))
    return pl.pallas_call(
        functools.partial(mlp_kernel, tile),
        out_shape=(shape((rows, width), F32), shape((rows, width), BF16)),
        grid=(hidden // block,),
        in_specs=[whole] * 3 + [pl.BlockSpec((8, width), lambda i: (0, 0)), cols, later],
        out_specs=(whole, whole),
        scratch_shapes=[pltpu.VMEM((rows, width), BF16), pltpu.VMEM((rows, width), F32)],
        compiler_params=pltpu.CompilerParams(vmem_limit_bytes=VMEM_LIMIT),
        cost_estimate=pl.CostEstimate(flops=4 * rows * width * hidden, bytes_accessed=rows * width * 14 + width * hidden * 4,
                                      transcendentals=rows * hidden),
    )(x, mine, other, vec, stack, stack)


def mlp_backward(gy, x1, vec, stack):
    rows, width = x1.shape
    hidden = stack.shape[1] // 2
    block = min(hidden, 512)
    tile = min(rows, 256)
    whole = pl.BlockSpec((rows, width), lambda i: (0, 0))
    cols = pl.BlockSpec((width, block), lambda i: (0, i))
    later = pl.BlockSpec((width, block), lambda i: (0, i + hidden // block))
    return pl.pallas_call(
        functools.partial(mlp_back_kernel, tile),
        out_shape=(shape((width, hidden), BF16), shape((width, hidden), BF16), shape((rows, width), BF16)),
        grid=(hidden // block,),
        in_specs=[whole] * 2 + [pl.BlockSpec((8, width), lambda i: (0, 0)), cols, later],
        out_specs=(cols, cols, whole),
        scratch_shapes=[
            pltpu.VMEM((rows, width), BF16), pltpu.VMEM((width, rows), BF16),
            pltpu.VMEM((rows, width), BF16), pltpu.VMEM((width, rows), BF16),
            pltpu.VMEM((rows, block), BF16), pltpu.VMEM((rows, block), BF16),
            pltpu.VMEM((rows, width), F32)],
        compiler_params=pltpu.CompilerParams(vmem_limit_bytes=VMEM_LIMIT),
        cost_estimate=pl.CostEstimate(flops=10 * rows * width * hidden, bytes_accessed=rows * width * 10 + width * hidden * 8,
                                      transcendentals=rows * hidden),
    )(gy, x1, vec, stack, stack)


def head(core, inverse, x1, mine, vec, bias, predict, target, band, weight, patches):
    rows, width = x1.shape
    pixels = target.shape[1]
    share = pixels // 2
    other = other_core(mine)
    smem = pl.BlockSpec(memory_space=pltpu.SMEM)
    row_w = pl.BlockSpec((patches, width), lambda i: (i, 0))
    row_p = pl.BlockSpec((patches, pixels), lambda i: (i, 0))
    fix = lambda a, b: pl.BlockSpec((a, b), lambda i: (0, 0))
    return pl.pallas_call(
        head_kernel,
        out_shape=(shape((rows, width), F32), shape((width, share), BF16), shape((1, pixels), F32),
                   shape((1, pixels), F32), shape((1, width), F32), shape((1, width), F32)),
        grid=(rows // patches,),
        in_specs=[smem, smem, row_w, row_w, row_w, fix(8, width), fix(1, pixels), pl.BlockSpec((2, width, share), lambda i: (0, 0, 0)), row_p, row_p,
                  pl.BlockSpec((patches, 1), lambda i: (i, 0))],
        out_specs=(row_w, fix(width, share), fix(1, pixels), fix(1, pixels), fix(1, width), fix(1, width)),
        scratch_shapes=[pltpu.VMEM((patches, pixels), BF16), pltpu.VMEM((width, share), F32)],
        compiler_params=pltpu.CompilerParams(vmem_limit_bytes=VMEM_LIMIT),
        cost_estimate=pl.CostEstimate(flops=5 * rows * width * pixels, bytes_accessed=rows * (width * 12 + pixels * 6),
                                      transcendentals=rows * pixels),
    )(core, inverse, x1, mine, other, vec, bias, predict, target, band, weight)


def attn_backward(gy, x1, mine, x, saved, vec, attn, length, group, head_dim):
    qkv, mixed, lse = saved
    rows, width = x.shape
    local = mixed.shape[0]
    return run(
        functools.partial(attn_back_kernel, length, group, head_dim),
        [shape((rows, width), F32), shape((width, 4 * local), BF16),
         shape((1, width), F32), shape((1, width), F32), shape((rows, width), BF16)],
        [pltpu.VMEM((4 * local, width), BF16), pltpu.VMEM((width, rows), BF16), pltpu.VMEM((width, rows), BF16),
         pltpu.VMEM((local, group), BF16), pltpu.VMEM((3 * local, rows), BF16)],
        (gy, x1, mine, other_core(mine), x, qkv, mixed, lse, vec, attn),
        18 * rows * width * local)


def sine_table(gsd_values, feature_width, grid_side):
    quarter = feature_width // 4
    frequency = jnp.exp(-jnp.log(10000.0) * jnp.arange(quarter).astype(F32) / quarter)
    gsd_ratio = gsd_values.astype(F32)[:, None, None] / REF_GSD
    line = jnp.arange(grid_side, dtype=jnp.int32).astype(F32)
    arg = line[None, :, None] * gsd_ratio * frequency
    return jnp.concatenate([jnp.sin(arg), jnp.cos(arg)], axis=-1)


def dp_bits():
    return lax.axis_size("dp").bit_length() - 1


def orders():
    bits = dp_bits()
    high = list(range(bits - 1, 1, -1))
    return (high + [0, 1], high + [1, 0])


def swap(block, bit):
    size = lax.axis_size("dp")
    return lax.ppermute(block, "dp", [(i, i ^ (1 << bit)) for i in range(size)])


def my_bit(bit):
    return (lax.axis_index("dp") >> bit) & 1


def gather_dp(block, axis, order):
    lead, rest = (block.shape[:axis], block.shape[axis:])
    done = []
    cur = block
    for bit in order:
        other = swap(cur, bit)
        mine = my_bit(bit) == 1
        place = axis + sum(1 for b in done if b > bit)
        cur = jnp.stack([jnp.where(mine, other, cur), jnp.where(mine, cur, other)], axis=place)
        done.append(bit)
    return cur.reshape(lead + (rest[0] * lax.axis_size("dp"),) + rest[1:])


def reduce_dp(block, axis, order, wire):
    bits = dp_bits()
    lead, rest = (block.shape[:axis], block.shape[axis:])
    shard = rest[0] // lax.axis_size("dp")
    cur = block.reshape(lead + (2,) * bits + (shard,) + rest[1:])
    left = list(range(bits - 1, -1, -1))
    for bit in reversed(order):
        place = axis + left.index(bit)
        mine = my_bit(bit)
        keep = lax.dynamic_index_in_dim(cur, mine, place, keepdims=False)
        give = lax.dynamic_index_in_dim(cur, 1 - mine, place, keepdims=False)
        other = swap(give.astype(wire), bit)
        cur = keep.astype(F32) + other.astype(F32)
        left.remove(bit)
    return cur


def join_cores(mine, core):
    other = other_core(mine)
    return jnp.concatenate([jnp.where(core == 0, mine, other), jnp.where(core == 0, other, mine)], axis=1)


def total_dp(value):
    for bit in range(dp_bits()):
        value = value + swap(value, bit)
    return value


def place_of():
    index = lax.axis_index("dp")
    core = lax.axis_index("mp")
    low, high = lax.rem(index, 4), index // 4
    bit_x, bit_y = lax.rem(low, 2), low // 2
    low_x, low_y = low + 1 - 2 * bit_x, low + 2 - 4 * bit_y
    return core, low, high, low_x, low_y


def greet(partners):
    barrier = pltpu.get_barrier_semaphore()
    for partner in partners:
        pl.semaphore_signal(barrier, inc=1, device_id=partner, device_id_type=pl.DeviceIdType.MESH)
    pl.semaphore_wait(barrier, len(partners))


def blocks_of(widths, limit):
    found = []
    for number, width in enumerate(widths):
        start = 0
        while start < width:
            size = min(limit, width - start)
            found.append((number, start, size))
            start += size
    return found


def remote(source, target, send, receive, device):
    return pltpu.make_async_remote_copy(
        src_ref=source, dst_ref=target, send_sem=send, recv_sem=receive,
        device_id=device, device_id_type=pl.DeviceIdType.MESH)


def small_gather_kernel(size, part_ref, full_ref, send_sem, receive_sem):
    index, core = lax.axis_index("dp"), lax.axis_index("mp")
    peers = [(lax.rem(index + k, size), core) for k in range(1, size)]
    greet(peers)
    full_ref[index] = part_ref[...]
    copies = [remote(part_ref, full_ref.at[index], send_sem.at[k], receive_sem.at[k], peers[k])
              for k in range(size - 1)]
    for copy in copies:
        copy.start()
    for copy in copies:
        copy.wait()


def small_gather(part):
    size = lax.axis_size("dp")
    in_vmem = pl.BlockSpec(memory_space=pltpu.VMEM)
    dma = pltpu.SemaphoreType.DMA
    return pl.pallas_call(
        functools.partial(small_gather_kernel, size),
        out_shape=shape((size,) + part.shape, part.dtype),
        in_specs=[in_vmem],
        out_specs=in_vmem,
        scratch_shapes=[dma((size - 1,)), dma((size - 1,))],
        compiler_params=pltpu.CompilerParams(collective_id=2, has_side_effects=True),
    )(part)


def total_blocks(block_ref, near_ref, far_ref, sems, low, high, core, highs, stage):
    send, receive = sems
    if stage == 0:
        spots = [(high * 4 + lax.rem(low + k, 4), core) for k in range(1, 4)]
        return [remote(block_ref, near_ref.at[low], send.at[k], receive.at[k], spots[k]) for k in range(3)]
    spots = [(lax.rem(high + k, highs) * 4 + low, core) for k in range(1, highs)]
    return [remote(block_ref, far_ref.at[high], send.at[3 + k], receive.at[3 + k], spots[k]) for k in range(highs - 1)]


def forward_kernel(highs, shared, groups, count, length, group, head_dim, *refs):
    shards, refs = refs[:count], refs[count:]
    pix_ref, band_ref, weight_ref, kept_ref, table_ref, vec_ref = refs[:6]
    fulls, refs = refs[6 : 6 + count], refs[6 + count :]
    x_ref, qkv_ref, mixed_ref, lse_ref, pixk_ref, x1_ref, last_ref, far_out_ref, counts_ref, flat_ref = refs[:10]
    refs = refs[10:]
    (bands_v, embed_v, attn_v, mlp_v, part_ref, other_ref, low_ref, acc_ref, block_ref, near_ref,
     far_ref) = refs[:11]
    (own_sem, zs_sem, zr_sem, cs_sem, cr_sem, fs_sem, fr_sem, ms_sem, mr_sem, load_sem, xs_sem, xr_sem, ts_sem,
     tr_sem) = refs[11:]
    core, low, high, low_x, low_y = place_of()
    at_x, at_y = (high * 4 + low_x, core), (high * 4 + low_y, core)
    at_high = [(lax.rem(high + k, highs) * 4 + low, core) for k in range(1, highs)]
    sibling = (high * 4 + low, 1 - core)
    near = [(high * 4 + lax.rem(low + k, 4), core) for k in range(1, 4)]
    greet([sibling] + near + at_high)

    def full(at):
        number, start, size = groups[at]
        ref = fulls[number].at[core] if shared[number] else fulls[number]
        return ref, pl.ds(start, size)

    def first(at):
        ref, cols = full(at)
        shard = shards[groups[at][0]].at[:, cols]
        mine = ref.at[high, low, :, cols]
        copies = [pltpu.make_async_copy(shard, mine, own_sem.at[at])]
        for k in range(1, highs):
            copies.append(remote(shard, mine, zs_sem.at[at, k - 1], zr_sem.at[at, k - 1], at_high[k - 1]))
        return copies

    def column(at):
        ref, cols = full(at)
        part = ref.at[:, low, :, cols]
        return [remote(part, part, cs_sem.at[at, 0], cr_sem.at[at, 0], at_x),
                remote(part, part, cs_sem.at[at, 1], cr_sem.at[at, 1], at_y)]

    def forward(at):
        ref, cols = full(at)
        which, device = (low_x, at_y) if at % 2 == 0 else (low_y, at_x)
        part = ref.at[:, which, :, cols]
        return remote(part, part, fs_sem.at[at], fr_sem.at[at], device)

    def swap(number):
        part = fulls[number].at[core]
        return remote(part, part, ms_sem.at[number], mr_sem.at[number], sibling)

    def exchange(at, source, target):
        return remote(source, target, xs_sem.at[at], xr_sem.at[at], sibling)

    total = len(groups)
    pairs = (total + 1) // 2
    in_pair = lambda pair: [at for at in (2 * pair, 2 * pair + 1) if at < total]
    pair_of = lambda number: max(at for at in range(total) if groups[at][0] == number) // 2
    images, side = table_ref.shape[0], table_ref.shape[1]
    patches = pix_ref.shape[0] // images
    width = mixed_ref.shape[0]
    mask = group_mask(group, length)

    def pick(image, carry):
        rows = pl.ds(image * length, length)
        index = kept_ref[rows, :]
        hot = lax.broadcasted_iota(jnp.int32, (length, patches), 1) == index
        pixels = pix_ref[pl.ds(image * patches, patches), :]
        pixk_ref[rows, :] = dot_nn(hot.astype(BF16), pixels).astype(BF16)
        grid_at = lax.broadcasted_iota(jnp.int32, (length, side), 1)
        table = table_ref[image]
        half = table.shape[1]
        x_ref[rows, :half] = dot_exact((grid_at == index // side).astype(F32), table)
        x_ref[rows, half:] = dot_exact((grid_at == index % side).astype(F32), table)
        return carry

    def tally(image, carry):
        rows = pl.ds(image * patches, patches)
        band, weight = bands_v[rows, :], weight_ref[rows, :]
        for level in range(NB):
            row = jnp.sum(jnp.where(band == level, weight, 0.0), axis=0, keepdims=True)
            for start in range(0, row.shape[1], 128):
                block_ref[level : level + 1, :] += row[:, start : start + 128]
        return carry

    def rows_step(number, carry):
        rows = pl.ds(pl.multiple_of(number * group, group), group)
        share = embed_v.shape[-1]
        embed = lambda half: embed_v[half].reshape(-1, share)
        rows_x = dot_nt(pixk_ref[rows, :share], embed(0)) + dot_nt(pixk_ref[rows, share:], embed(1))
        rows_x = rows_x + vec_ref[0:1, :] + x_ref[rows, :]
        x_ref[rows, :] = rows_x
        unit, _ = normalize(rows_x)
        low_a = (unit * vec_ref[1:2, :] + vec_ref[2:3, :]).astype(BF16)
        qkv_ref[:, rows] = dot_nt(flat_ref[: 3 * width, :], low_a).astype(BF16)
        attend(qkv_ref, mixed_ref, lse_ref, rows, width, head_dim, mask)
        part_ref[rows, :] = dot_nn(mixed_ref[:, rows].T, flat_ref[3 * width :, :]).astype(BF16)
        return carry

    def mlp_first():
        after = x_ref[...] + both(part_ref, other_ref, pl.ds(0, x_ref.shape[0]))
        x1_ref[...] = after
        unit, _ = normalize(after)
        low_ref[...] = (unit * vec_ref[3:4, :] + vec_ref[4:5, :]).astype(BF16)
        acc_ref[...] = jnp.zeros_like(acc_ref)

    def mlp_block(piece, carry):
        size = 512
        hidden = mlp_v.shape[-1] // 2
        start = pl.multiple_of(piece * size, size)
        wide = x_ref.shape[1]
        up = dot_nn(low_ref[...], mlp_v[:, :, :, pl.ds(start, size)].reshape(wide, size))
        _, _, half = gelu_parts(up)
        down = mlp_v[:, :, :, pl.ds(pl.multiple_of(hidden + start, size), size)].reshape(wide, size)
        acc_ref[...] += dot_nt((up * half).astype(BF16), down)
        return carry

    load_bands = pltpu.make_async_copy(band_ref, bands_v, load_sem.at[0])
    load_attn = pltpu.make_async_copy(fulls[1], attn_v, load_sem.at[1])
    load_embed = pltpu.make_async_copy(fulls[0], embed_v, load_sem.at[2])
    load_mlp = pltpu.make_async_copy(fulls[2], mlp_v, load_sem.at[3])
    stages = functools.partial(total_blocks, block_ref, near_ref, far_ref, (ts_sem, tr_sem), low, high, core, highs)
    embed_at, attn_at, mlp_at = pair_of(0) + 3, pair_of(1) + 3, pair_of(2) + 3
    row_groups = x_ref.shape[0] // group
    swapped = set()
    for step in range(pairs + 3):
        if step < pairs:
            for at in in_pair(step):
                for copy in first(at):
                    copy.start()
        if 0 <= step - 1 < pairs:
            for at in in_pair(step - 1):
                for copy in first(at):
                    copy.wait()
                for copy in column(at):
                    copy.start()
        if 0 <= step - 2 < pairs:
            for at in in_pair(step - 2):
                column(at)[at % 2].wait()
                forward(at).start()
        if 0 <= step - 3 < pairs:
            for at in in_pair(step - 3):
                column(at)[1 - at % 2].wait()
                forward(at).wait()
        for number in range(count):
            if shared[number] and number not in swapped and pair_of(number) + 3 <= step:
                swap(number).start()
                swapped.add(number)
        if step == 0:
            load_bands.start()
            lax.fori_loop(0, images, pick, 0)
            block_ref[...] = jnp.zeros_like(block_ref)
            load_bands.wait()
            lax.fori_loop(0, images, tally, 0)
            near_ref[low] = block_ref[...]
            for copy in stages(0):
                copy.start()
        if step == 1:
            for copy in stages(0):
                copy.wait()
            block_ref[...] = (near_ref[0] + near_ref[1]) + (near_ref[2] + near_ref[3])
            far_ref[high] = block_ref[...]
            for copy in stages(1):
                copy.start()
        if step == 2:
            for copy in stages(1):
                copy.wait()
            counts = far_ref[0]
            for k in range(1, highs):
                counts = counts + far_ref[k]
            counts_ref[...] = counts
        if step == attn_at:
            swap(0).wait()
            load_attn.start()
            load_embed.start()
            load_attn.wait()
            for part in range(4):
                at = pl.ds(part * width, width)
                flat_ref[at, :] = attn_v[:, :, :, at].reshape(-1, width).T
            load_embed.wait()
        if attn_at <= step < mlp_at - 1:
            share = -(-row_groups // (mlp_at - 1 - attn_at))
            start, stop = (step - attn_at) * share, min((step - attn_at + 1) * share, row_groups)
            if start < stop:
                lax.fori_loop(start, stop, rows_step, 0)
                if stop == row_groups:
                    exchange(0, part_ref, other_ref).start()
        if step == mlp_at:
            load_mlp.start()
            exchange(0, part_ref, other_ref).wait()
            mlp_first()
            load_mlp.wait()
            lax.fori_loop(0, mlp_v.shape[-1] // 1024, mlp_block, 0)
            last_ref[...] = acc_ref[...].astype(BF16)
            exchange(1, last_ref, far_out_ref).start()
    exchange(1, last_ref, far_out_ref).wait()
    for number in range(1, count):
        if shared[number]:
            swap(number).wait()


def forward_all(shards, shared, pixels, band_ids, patch_weight, kept_column, table, evec):
    size = lax.axis_size("dp")
    highs = size // 4
    count = len(shards)
    groups = blocks_of([a.shape[1] for a in shards], 512)
    total = len(groups)
    rows, wide, local = kept_column.shape[0], evec.shape[1], shards[1].shape[1] // 4
    images = table.shape[0]
    length = rows // images
    group = 2 * length
    fulls = []
    for shard, split in zip(shards, shared):
        dims = (highs, 4) + shard.shape
        fulls.append(shape((2,) + dims if split else dims, shard.dtype))
    outs = [shape((rows, wide), F32), shape((3 * local, rows), BF16), shape((local, rows), BF16),
            shape((local // DH, rows), F32), shape((rows, pixels.shape[1]), BF16), shape((rows, wide), F32),
            shape((rows, wide), BF16), shape((rows, wide), BF16), shape((8, 128), F32), shape((4 * local, wide), BF16)]
    dma = pltpu.SemaphoreType.DMA
    small = (8, 128)
    in_vmem = pl.BlockSpec(memory_space=pltpu.VMEM)
    any_space = pl.BlockSpec(memory_space=pl.ANY)
    result = pl.pallas_call(
        functools.partial(forward_kernel, highs, shared, groups, count, length, group, DH),
        out_shape=tuple(fulls + outs),
        in_specs=[any_space] * count + [in_vmem, any_space] + [in_vmem] * 4,
        out_specs=tuple([any_space] * count + [in_vmem] * len(outs)),
        scratch_shapes=[
            pltpu.VMEM(band_ids.shape, jnp.int32), pltpu.VMEM(fulls[0].shape, BF16), pltpu.VMEM(fulls[1].shape, BF16),
            pltpu.VMEM(fulls[2].shape, BF16), pltpu.VMEM((rows, wide), BF16),
            pltpu.VMEM((rows, wide), BF16), pltpu.VMEM((rows, wide), BF16), pltpu.VMEM((rows, wide), F32),
            pltpu.VMEM(small, F32), pltpu.VMEM((4,) + small, F32), pltpu.VMEM((highs,) + small, F32),
            dma((total,)), dma((total, highs - 1)), dma((total, highs - 1)), dma((total, 2)), dma((total, 2)),
            dma((total,)), dma((total,)), dma((count,)), dma((count,)), dma((4,)), dma((2,)), dma((2,)),
            dma((highs + 2,)), dma((highs + 2,))],
        compiler_params=pltpu.CompilerParams(collective_id=0, has_side_effects=True, vmem_limit_bytes=VMEM_LIMIT),
        cost_estimate=pl.CostEstimate(flops=0, bytes_accessed=sum(a.size * a.dtype.itemsize * size for a in shards),
                                      transcendentals=0),
    )(*shards, pixels, band_ids, patch_weight, kept_column, table, evec)
    weights = [full.reshape(((2,) if split else ()) + (size * shard.shape[0], shard.shape[1]))
               for full, split, shard in zip(result[:count], shared, shards)]
    return weights, result[count:]


def gather_all(shards, shared):
    order_a, order_b = orders()
    fulls = []
    for number, shard in enumerate(shards):
        full = gather_dp(shard, 0, (order_a, order_b)[number % 2])
        if shared[number]:
            other, zero = other_core(full), lax.axis_index("mp") == 0
            full = jnp.stack([jnp.where(zero, full, other), jnp.where(zero, other, full)])
        fulls.append(full)
    return fulls


def decoder_kernel(length, head_dim, inverse_ref, x1e_ref, mine_ref, other_ref, evec_ref, kept_ref, column_ref, rows_ref,
                   table_ref, vec_ref, bias_ref, target_any, band_any, attn_any, mlp_any, bridge_any, predict_any,
                   gy_out, gattn_ref, gup_ref, gdown_ref, gpred_ref, gbridge_ref, loss_ref, gbias_ref, sums_ref, esums_ref,
                   final_ref, glat_ref, x_ref, x1_ref, gy_ref, qkv_ref, mixed_ref, lse_ref, part_ref, from_ref,
                   lowt_ref, gradt_ref, z_ref, gu_ref, flat_ref, mlp_ref, bridge_ref, predict_ref, target_ref,
                   band_ref, gp_ref, gpred_acc, gmix_ref, load_sem, stream_sem, send_sem, receive_sem):
    core, index = lax.axis_index("mp"), lax.axis_index("dp")
    sibling = (index, 1 - core)
    greet([sibling])
    images, side, half = table_ref.shape
    patches = side * side
    width = mixed_ref.shape[0]
    hidden = z_ref.shape[1]
    share = predict_ref.shape[2]
    attn_ref = z_ref.at[pl.ds(0, attn_any.shape[0]), pl.ds(0, 4 * width)]

    loads = [pltpu.make_async_copy(source, target, load_sem.at[at]) for at, (source, target) in enumerate(
        ((attn_any, attn_ref), (bridge_any, bridge_ref), (mlp_any, mlp_ref), (predict_any, predict_ref)))]
    for copy in loads:
        copy.start()

    def rows_of(image):
        return pl.ds(pl.multiple_of(image * patches, patches), patches)

    def exchange(phase, image):
        rows = rows_of(image)
        return remote(part_ref.at[phase % 2, rows, :], from_ref.at[phase % 2, rows, :], send_sem.at[phase, image],
                      receive_sem.at[phase, image], sibling)

    def summed(phase, rows):
        return part_ref[phase % 2, rows, :].astype(F32) + from_ref[phase % 2, rows, :].astype(F32)

    def give(phase, image, value):
        part_ref[phase % 2, rows_of(image), :] = value.astype(BF16)
        exchange(phase, image).start()

    def stream(image):
        rows, slot = rows_of(image), lax.rem(image, 2)
        return [pltpu.make_async_copy(target_any.at[rows, :], target_ref.at[slot], stream_sem.at[0, slot]),
                pltpu.make_async_copy(band_any.at[rows, :], band_ref.at[slot], stream_sem.at[1, slot])]

    sums_ref[...] = jnp.zeros_like(sums_ref)
    loss_ref[...] = jnp.zeros_like(loss_ref)
    gbias_ref[...] = jnp.zeros_like(gbias_ref)
    gpred_acc[...] = jnp.zeros_like(gpred_acc)
    for copy in stream(0):
        copy.start()
    loads[0].wait()
    for part in range(4):
        at = pl.ds(part * width, width)
        flat_ref[at, :] = attn_ref[:, at].T
    loads[1].wait()
    ends = bridge_ref.shape[2]
    latent_ref = gy_ref

    def ends_rows(step):
        return pl.ds(pl.multiple_of(step * 128, 128), 128)

    def enc_end(step, carry):
        rows = ends_rows(step)
        out = x1e_ref[rows, :] + both(mine_ref, other_ref, rows)
        gy_out[rows, :] = out
        unit, _ = normalize(out)
        final = (unit * evec_ref[5:6, :] + evec_ref[6:7, :]).astype(BF16)
        final_ref[rows, :] = final
        latent_ref[rows, :ends] = dot_nn(final, bridge_ref[0])
        latent_ref[rows, ends:] = dot_nn(final, bridge_ref[1])
        return carry

    lax.fori_loop(0, x1e_ref.shape[0] // 128, enc_end, 0)

    def phase_a(image, carry):
        rows = rows_of(image)
        hot = lax.broadcasted_iota(jnp.int32, (patches, length), 0) == kept_ref[pl.ds(image, 1), :]
        latent = latent_ref[pl.ds(pl.multiple_of(image * length, length), length), :]
        table = table_ref[image]
        by_row = jnp.broadcast_to(table[:, None, :], (side, side, half)).reshape(patches, half)
        by_col = jnp.broadcast_to(table[None, :, :], (side, side, half)).reshape(patches, half)
        place = jnp.concatenate([by_row, by_col], axis=1)
        rows_x = dot_exact(hot.astype(F32), latent) + rows_ref[rows, 0:1] * vec_ref[0:1, :] + place
        x_ref[rows, :] = rows_x
        unit, _ = normalize(rows_x)
        low = (unit * vec_ref[1:2, :] + vec_ref[2:3, :]).astype(BF16)
        qkv_ref[:, rows] = dot_nt(flat_ref[: 3 * width, :], low).astype(BF16)
        attend(qkv_ref, mixed_ref, lse_ref, rows, width, head_dim, None)
        give(0, image, dot_nn(mixed_ref[:, rows].T, flat_ref[3 * width :, :]))
        return carry

    lax.fori_loop(0, images, phase_a, 0)
    loads[2].wait()
    loads[3].wait()

    def phase_b(image, carry):
        rows = rows_of(image)
        exchange(0, image).wait()
        after = x_ref[rows, :] + summed(0, rows)
        x1_ref[rows, :] = after
        unit, _ = normalize(after)
        low = (unit * vec_ref[3:4, :] + vec_ref[4:5, :]).astype(BF16)
        lowt_ref[:, rows] = low.T
        up = dot_nn(low, mlp_ref[:, :hidden])
        square, bent, rise = gelu_parts(up)
        mid = (up * rise).astype(BF16)
        z_ref[rows, :] = mid
        slope = rise + (0.5 * GELU_C) * up * (1.0 - bent * bent) * (1.0 + (3.0 * 0.044715) * square)
        gu_ref[rows, :] = slope.astype(BF16)
        give(1, image, dot_nt(mid, mlp_ref[:, hidden:]))
        return carry

    lax.fori_loop(0, images, phase_b, 0)

    def phase_c(image, carry):
        rows, slot = rows_of(image), lax.rem(image, 2)

        @pl.when(image + 1 < images)
        def _():
            for copy in stream(image + 1):
                copy.start()

        exchange(1, image).wait()
        unit, rstd = normalize(x1_ref[rows, :] + summed(1, rows))
        gain = vec_ref[5:6, :]
        final = (unit * gain + vec_ref[6:7, :]).astype(BF16)
        for copy in stream(image):
            copy.wait()
        predicted = jnp.concatenate([dot_nn(final, predict_ref[0]), dot_nn(final, predict_ref[1])], axis=1)
        mismatch = predicted + bias_ref[...] - target_ref[slot].astype(F32)
        band = band_ref[slot]
        level = jnp.where(band == 0, inverse_ref[0], jnp.where(band == 1, inverse_ref[1], inverse_ref[2]))
        level = level * rows_ref[rows, 1:2]
        square = mismatch * mismatch + EPS_C
        root = lax.rsqrt(square)
        loss_ref[...] += jnp.sum(level * (square * root), axis=0, keepdims=True)
        grad = level * (mismatch * root)
        gbias_ref[...] += jnp.sum(grad, axis=0, keepdims=True)
        gp_ref[...] = grad.astype(BF16)
        columns = pl.ds(pl.multiple_of(core * share, share), share)
        gpred_acc[...] += dot_tn(final, gp_ref[:, columns])
        grad_final = dot_nt(gp_ref[:, :share], predict_ref[0]) + dot_nt(gp_ref[:, share:], predict_ref[1])
        grad_in, gain_sum, shift_sum = norm_back(grad_final, gain, unit, rstd)
        gy_ref[rows, :] = grad_in
        sums_ref[5:6, :] += gain_sum
        sums_ref[6:7, :] += shift_sum
        low = grad_in.astype(BF16)
        gradt_ref[:, rows] = low.T
        grad_up = (dot_nn(low, mlp_ref[:, hidden:]) * gu_ref[rows, :].astype(F32)).astype(BF16)
        gu_ref[rows, :] = grad_up
        give(2, image, dot_nt(grad_up, mlp_ref[:, :hidden]))
        return carry

    lax.fori_loop(0, images, phase_c, 0)
    gpred_ref[...] = gpred_acc[...].astype(BF16)
    tile = 256
    for start in range(0, hidden, tile):
        at = pl.ds(start, tile)
        gup_ref[:, at] = dot_nn(lowt_ref[...], gu_ref[:, at]).astype(BF16)
        gdown_ref[:, at] = dot_nn(gradt_ref[...], z_ref[:, at]).astype(BF16)

    def phase_d(image, carry):
        rows = rows_of(image)
        exchange(2, image).wait()
        unit, rstd = normalize(x1_ref[rows, :])
        grad_in, gain_sum, shift_sum = norm_back(summed(2, rows), vec_ref[3:4, :], unit, rstd)
        grad_in = grad_in + gy_ref[rows, :]
        gy_ref[rows, :] = grad_in
        sums_ref[3:4, :] += gain_sum
        sums_ref[4:5, :] += shift_sum
        low = grad_in.astype(BF16)
        gradt_ref[:, rows] = low.T
        gmix_ref[...] = dot_nt(flat_ref[3 * width :, :], low).astype(BF16)
        attend_back(qkv_ref, gmix_ref, lse_ref, qkv_ref, rows, width, head_dim, None)
        unit_a, _ = normalize(x_ref[rows, :])
        lowt_ref[:, rows] = (unit_a * vec_ref[1:2, :] + vec_ref[2:3, :]).astype(BF16).T
        give(3, image, dot_nn(qkv_ref[:, rows].T, flat_ref[: 3 * width, :]))
        return carry

    lax.fori_loop(0, images, phase_d, 0)
    for part in range(3):
        at = pl.ds(part * width, width)
        gattn_ref[:, at] = dot_nt(lowt_ref[...], qkv_ref[at, :]).astype(BF16)
    gattn_ref[:, 3 * width :] = dot_nt(gradt_ref[...], mixed_ref[...]).astype(BF16)

    def phase_e(image, carry):
        rows = rows_of(image)
        exchange(3, image).wait()
        unit, rstd = normalize(x_ref[rows, :])
        grad_in, gain_sum, shift_sum = norm_back(summed(3, rows), vec_ref[1:2, :], unit, rstd)
        grad_in = grad_in + gy_ref[rows, :]
        sums_ref[1:2, :] += gain_sum
        sums_ref[2:3, :] += shift_sum
        sums_ref[0:1, :] += jnp.sum(grad_in * rows_ref[rows, 0:1], axis=0, keepdims=True)
        kept_rows = pl.ds(pl.multiple_of(image * length, length), length)
        hot = lax.broadcasted_iota(jnp.int32, (length, patches), 1) == column_ref[kept_rows, :]
        glat_ref[kept_rows, :] = dot_nn(hot.astype(BF16), grad_in.astype(BF16)).astype(BF16)
        return carry

    lax.fori_loop(0, images, phase_e, 0)
    columns = pl.ds(pl.multiple_of(core * ends, ends), ends)
    gbridge_ref[...] = dot_tn(final_ref[...], glat_ref[:, columns]).astype(BF16)
    esums_ref[...] = jnp.zeros_like(esums_ref)

    def enc_start(step, carry):
        rows = ends_rows(step)
        grad_final = dot_nt(glat_ref[rows, :ends], bridge_ref[0]) + dot_nt(glat_ref[rows, ends:], bridge_ref[1])
        unit, rstd = normalize(gy_out[rows, :])
        grad_in, gain_sum, shift_sum = norm_back(grad_final, evec_ref[5:6, :], unit, rstd)
        gy_out[rows, :] = grad_in
        esums_ref[0:1, :] += gain_sum
        esums_ref[1:2, :] += shift_sum
        return carry

    lax.fori_loop(0, x1e_ref.shape[0] // 128, enc_start, 0)


def decoder_all(inverse, x1e, mine, other, evec, kept_index, kept_column, row_values, table, dvec, bias, target, band,
                attn, mlp, bridge, predict):
    rows_e, wide = x1e.shape
    images, length = kept_index.shape
    rows, pixel_count = target.shape
    patches = rows // images
    low_wide = dvec.shape[1]
    width, hidden, share, ends = attn.shape[1] // 4, mlp.shape[1] // 2, predict.shape[2], bridge.shape[2]
    in_vmem = pl.BlockSpec(memory_space=pltpu.VMEM)
    any_space = pl.BlockSpec(memory_space=pl.ANY)
    dma = pltpu.SemaphoreType.DMA
    vm = pltpu.VMEM
    return pl.pallas_call(
        functools.partial(decoder_kernel, length, DDH),
        out_shape=(
            shape((rows_e, wide), F32), shape((low_wide, 4 * width), BF16), shape((low_wide, hidden), BF16),
            shape((low_wide, hidden), BF16), shape((low_wide, share), BF16), shape((wide, ends), BF16),
            shape((1, pixel_count), F32), shape((1, pixel_count), F32), shape((8, low_wide), F32), shape((8, wide), F32)),
        in_specs=[pl.BlockSpec(memory_space=pltpu.SMEM)] + [in_vmem] * 10 + [any_space] * 6,
        out_specs=tuple([in_vmem] * 10),
        scratch_shapes=[
            vm((rows_e, wide), BF16), vm((rows_e, low_wide), BF16), vm((rows, low_wide), F32),
            vm((rows, low_wide), F32), vm((rows, low_wide), F32), vm((3 * width, rows), BF16), vm((width, rows), BF16),
            vm((width // DDH, rows), F32), vm((2, rows, low_wide), BF16), vm((2, rows, low_wide), BF16),
            vm((low_wide, rows), BF16), vm((low_wide, rows), BF16), vm((rows, hidden), BF16), vm((rows, hidden), BF16),
            vm((4 * width, low_wide), BF16), vm(mlp.shape, BF16), vm(bridge.shape, BF16),
            vm(predict.shape, BF16), vm((2, patches, pixel_count), BF16), vm((2, patches, pixel_count), jnp.int32),
            vm((patches, pixel_count), BF16), vm((low_wide, share), F32), vm((width, patches), BF16),
            dma((4,)), dma((2, 2)), dma((4, images)), dma((4, images))],
        compiler_params=pltpu.CompilerParams(collective_id=3, has_side_effects=True, vmem_limit_bytes=62 * 2**20),
        cost_estimate=pl.CostEstimate(flops=0, bytes_accessed=2**25, transcendentals=0),
    )(inverse, x1e, mine, other, evec, kept_index, kept_column, row_values, table, dvec, bias, target, band, attn, mlp,
      bridge, predict)


class Reducer:
    def __init__(self, highs, groups, weights, grads, outs, near, second, far, load_two, load_own, plane, norm, sems):
        self.highs, self.groups, self.weights = highs, groups, weights
        self.grads, self.outs = grads, outs
        self.near, self.second, self.far = near, second, far
        self.load_two, self.load_own, self.plane, self.norm = load_two, load_own, plane, norm
        self.load_sem, self.as_sem, self.ar_sem, self.bs_sem, self.br_sem, self.zs_sem, self.zr_sem = sems
        self.core, self.low, self.high, self.low_x, self.low_y = place_of()
        self.dev_x, self.dev_y = (self.high * 4 + self.low_x, self.core), (self.high * 4 + self.low_y, self.core)
        self.at_high = [(lax.rem(self.high + k, highs) * 4 + self.low, self.core) for k in range(1, highs)]
        self.pairs = (len(groups) + 1) // 2

    def in_pair(self, pair):
        return [at for at in (2 * pair, 2 * pair + 1) if 0 <= at < len(self.groups)] if 0 <= pair < self.pairs else []

    def route(self, at):
        if at % 2 == 0:
            return self.low_y, self.dev_y, self.low_x, self.dev_x
        return self.low_x, self.dev_x, self.low_y, self.dev_y

    def grad(self, at, which):
        number, start, size = self.groups[at]
        return self.grads[number].at[:, which, :, pl.ds(start, size)]

    def slot(self, ref, at, count):
        number, _, size = self.groups[at]
        return ref.at[at % count, :, pl.ds(0, self.outs[number].shape[0]), pl.ds(0, size)]

    def two_ref(self, at):
        return self.slot(self.load_two, at, 6)

    def own_ref(self, at):
        return self.slot(self.load_own, at, 8)

    def loads(self, at):
        return [pltpu.make_async_copy(self.grad(at, self.route(at)[2]), self.two_ref(at), self.load_sem.at[at, 0]),
                pltpu.make_async_copy(self.grad(at, self.low), self.own_ref(at), self.load_sem.at[at, 1])]

    def one(self, at):
        low_one, dev_one, _, _ = self.route(at)
        return [remote(self.grad(at, 3 - self.low), self.near[2 * at], self.as_sem.at[at, 0], self.ar_sem.at[at, 0], dev_one),
                remote(self.grad(at, low_one), self.near[2 * at + 1], self.as_sem.at[at, 1], self.ar_sem.at[at, 1], dev_one)]

    def two(self, at):
        return remote(self.two_ref(at), self.second[at], self.bs_sem.at[at], self.br_sem.at[at], self.route(at)[3])

    def three(self, at):
        return [remote(self.own_ref(at).at[lax.rem(self.high + k, self.highs)], self.far[at].at[k - 1],
                       self.zs_sem.at[at, k - 1], self.zr_sem.at[at, k - 1], self.at_high[k - 1])
                for k in range(1, self.highs)]

    def step(self, step):
        for at in self.in_pair(step):
            for copy in self.one(at) + self.loads(at):
                copy.start()
        for at in self.in_pair(step - 1):
            mine = self.two_ref(at)
            self.loads(at)[0].wait()
            self.one(at)[0].wait()
            mine[...] = (mine[...].astype(F32) + self.near[2 * at][...].astype(F32)).astype(BF16)
            self.two(at).start()
        for at in self.in_pair(step - 2):
            number, start, size = self.groups[at]
            mine = self.own_ref(at)
            self.loads(at)[1].wait()
            self.one(at)[1].wait()
            self.two(at).wait()
            plane = self.slot(self.plane, at, 2)
            plane[...] = (mine[...].astype(F32) + self.near[2 * at + 1][...].astype(F32)
                          + self.second[at][...].astype(F32))
            self.outs[number][:, pl.ds(start, size)] = plane[self.high]
            mine[...] = plane[...].astype(BF16)
            for copy in self.three(at):
                copy.start()
        for at in self.in_pair(step - 3):
            number, start, size = self.groups[at]
            for copy in self.three(at):
                copy.wait()
            cols = pl.ds(start, size)
            done = self.outs[number][:, cols]
            for k in range(self.highs - 1):
                done = done + self.far[at][k].astype(F32)
            self.outs[number][:, cols] = done
            self.norm[0:1, 0:1] += self.weights[number] * jnp.sum(done * done, keepdims=True)


def reducer_scratch(highs, groups, shards):
    piece = lambda lead, group: pltpu.VMEM((lead, shards[group[0]], group[2]), BF16)
    near = [piece(highs, group) for group in groups for _ in range(2)]
    second = [piece(highs, group) for group in groups]
    far = [piece(highs - 1, group) for group in groups]
    slot = (highs, max(shards), max(group[2] for group in groups))
    loads = [pltpu.VMEM((6,) + slot, BF16), pltpu.VMEM((8,) + slot, BF16), pltpu.VMEM((2,) + slot, F32)]
    dma, total = pltpu.SemaphoreType.DMA, len(groups)
    sems = [dma((total, 2)), dma((total, 2)), dma((total, 2)), dma((total,)), dma((total,)),
            dma((total, highs - 1)), dma((total, highs - 1))]
    return near + second + far + loads + sems


def make_reducer(highs, groups, weights, grads, outs, norm, refs):
    total = len(groups)
    near, second, far, refs = refs[: 2 * total], refs[2 * total : 3 * total], refs[3 * total : 4 * total], refs[4 * total :]
    return Reducer(highs, groups, weights, grads, outs, near, second, far, *refs[:3], norm, refs[3:10]), refs[10:]


def backward_kernel(highs, weights, groups, ready, count, length, group, head_dim, *refs):
    given = count - 4
    gy_ref, x1_ref, vec_ref, vgrad_ref, loss_ref, lse_ref = refs[:6]
    x_any, qkv_any, mixed_any, flat_any, pixk_any, mlp_any = refs[6:12]
    refs = refs[12:]
    grads, refs = refs[:given], refs[given:]
    outs, sums_ref, vsum_ref, refs = refs[:count], refs[count], refs[count + 1], refs[count + 2 :]
    made, refs = refs[:4], refs[4:]
    grads = tuple(grads) + tuple(made)
    (x_ref, qkv_ref, mixed_ref, flat_ref, pixk_ref, wmlp_ref, low_ref, lowt_ref, grad_ref, gradt_ref, acc_ref, part_ref,
     other_ref, last_ref, gmix_ref, gqkv_ref, stage_ref, norm_ref, spots_ref, far_ref, vnear_ref, vfar_ref) = refs[:22]
    (load_sem, wload_sem, store_sem, xs_sem, xr_sem, ns_sem, nr_sem, hs_sem, hr_sem, ts_sem, tr_sem) = refs[22:33]
    red, _ = make_reducer(highs, groups, weights, grads, outs, norm_ref, refs[33:])
    core, low, high = red.core, red.low, red.high
    spot = low * 2 + core
    sibling = (high * 4 + low, 1 - core)
    near = [(high * 4 + lax.rem(spot + k, 8) // 2, lax.rem(lax.rem(spot + k, 8), 2)) for k in range(1, 8)]
    greet(near + red.at_high)
    rows, wide = x_ref.shape
    width = mixed_ref.shape[0]
    hidden = mlp_any.shape[-1] // 2
    size = 512
    tiles = hidden // size
    mask = group_mask(group, length)

    late = [pltpu.make_async_copy(source, target, load_sem.at[at]) for at, (source, target) in enumerate(
        ((x_any, x_ref), (qkv_any, qkv_ref), (mixed_any, mixed_ref), (flat_any, flat_ref), (pixk_any, pixk_ref)))]

    def weight_loads(tile):
        return [pltpu.make_async_copy(mlp_any.at[:, :, :, pl.ds(half * hidden + tile * size, size)],
                                      wmlp_ref.at[tile % 2, half], wload_sem.at[tile % 2, half]) for half in range(2)]

    def store(slot, target, start, columns=512):
        return pltpu.make_async_copy(stage_ref.at[slot, :, :, :, pl.ds(0, columns)],
                                     target.at[:, :, :, pl.ds(start, columns)], store_sem.at[slot])

    def exchange(at, target):
        return remote(part_ref, target, xs_sem.at[at], xr_sem.at[at], sibling)

    def staged(slot, value):
        columns = value.shape[1]
        stage_ref[slot, :, :, :, :columns] = value.astype(BF16).reshape(stage_ref.shape[1:4] + (columns,))

    def mlp_first():
        unit, _ = normalize(x1_ref[...])
        value = (unit * vec_ref[3:4, :] + vec_ref[4:5, :]).astype(BF16)
        low_ref[...] = value
        lowt_ref[...] = value.T
        value = gy_ref[...].astype(BF16)
        grad_ref[...] = value
        gradt_ref[...] = value.T
        acc_ref[...] = jnp.zeros_like(acc_ref)

    def mlp_block(tile):
        for copy in weight_loads(tile):
            copy.wait()
        if tile + 1 < tiles:
            for copy in weight_loads(tile + 1):
                copy.start()
        w_up = wmlp_ref[tile % 2, 0].reshape(wide, size)
        w_down = wmlp_ref[tile % 2, 1].reshape(wide, size)
        up = dot_nn(low_ref[...], w_up)
        square, bent, half = gelu_parts(up)
        mid = (up * half).astype(BF16)
        slope = half + (0.5 * GELU_C) * up * (1.0 - bent * bent) * (1.0 + (3.0 * 0.044715) * square)
        grad_up = (dot_nn(grad_ref[...], w_down) * slope).astype(BF16)
        acc_ref[...] += dot_nt(grad_up, w_up)
        slot = 2 * (tile % 2)
        if tile >= 2:
            store(slot, made[0], (tile - 2) * size).wait()
            store(slot + 1, made[1], (tile - 2) * size).wait()
        staged(slot, dot_nn(lowt_ref[...], grad_up))
        store(slot, made[0], tile * size).start()
        staged(slot + 1, dot_nn(gradt_ref[...], mid))
        store(slot + 1, made[1], tile * size).start()

    def mlp_last():
        part_ref[...] = acc_ref[...].astype(BF16)
        exchange(0, other_ref).start()

    def stores_done(tile):
        slot = 2 * (tile % 2)
        store(slot, made[0], tile * size).wait()
        store(slot + 1, made[1], tile * size).wait()

    def rows_step(number, carry):
        at = pl.ds(pl.multiple_of(number * group, group), group)
        unit, rstd = normalize(x1_ref[at, :])
        grad_in, gain_sum, shift_sum = norm_back(both(part_ref, other_ref, at), vec_ref[3:4, :], unit, rstd)
        grad_in = grad_in + gy_ref[at, :]
        gy_ref[at, :] = grad_in
        vsum_ref[3:4, :] += gain_sum
        vsum_ref[4:5, :] += shift_sum
        low_grad = grad_in.astype(BF16)
        gradt_ref[:, at] = low_grad.T
        gmix_ref[...] = dot_nt(flat_ref[3 * width :, :], low_grad).astype(BF16)
        attend_back(qkv_ref, gmix_ref, lse_ref, gqkv_ref, at, width, head_dim, mask)
        part_ref[at, :] = dot_nn(gqkv_ref[:, at].T, flat_ref[: 3 * width, :]).astype(BF16)
        unit_a, _ = normalize(x_ref[at, :])
        lowt_ref[:, at] = (unit_a * vec_ref[1:2, :] + vec_ref[2:3, :]).astype(BF16).T
        return carry

    def attn_grads():
        for slot in range(4):
            if slot < 3:
                value = dot_nt(lowt_ref[...], gqkv_ref[pl.ds(slot * width, width), :])
            else:
                value = dot_nt(gradt_ref[...], mixed_ref[...])
            staged(slot, value)
            store(slot, made[2], slot * width, width).start()

    def enc_out():
        unit, rstd = normalize(x_ref[...])
        grad_in, gain_sum, shift_sum = norm_back(both(part_ref, last_ref, pl.ds(0, rows)), vec_ref[1:2, :], unit, rstd)
        grad_in = grad_in + gy_ref[...]
        vsum_ref[0:1, :] = jnp.sum(grad_in, axis=0, keepdims=True)
        vsum_ref[1:2, :] = gain_sum
        vsum_ref[2:3, :] = shift_sum
        share = made[3].shape[-1]
        columns = pl.ds(pl.multiple_of(core * share, share), share)
        staged(0, dot_tn(grad_in.astype(BF16), pixk_ref[:, columns]))
        store(0, made[3], 0, share).start()

    stages = functools.partial(total_blocks, vsum_ref, vnear_ref, vfar_ref, (ts_sem, tr_sem), low, high, core, highs)
    mlp_ready, attn_ready, embed_ready = ready
    row_groups = rows // group
    norm_ref[...] = jnp.zeros_like(norm_ref)
    vsum_ref[...] = vgrad_ref[...]
    for copy in weight_loads(0):
        copy.start()
    for step in range(red.pairs + 3):
        if tiles - 2 <= step - mlp_ready < tiles:
            stores_done(step - mlp_ready)
        if step == attn_ready:
            for slot in range(4):
                store(slot, made[2], slot * width, width).wait()
        if step == embed_ready:
            store(0, made[3], 0, made[3].shape[-1]).wait()
        red.step(step)
        if step == 0:
            for copy in late:
                copy.start()
            mlp_first()
        if step < tiles:
            mlp_block(step)
            if step == tiles - 1:
                mlp_last()
        if tiles <= step < attn_ready - 1:
            if step == tiles:
                for copy in late:
                    copy.wait()
                exchange(0, other_ref).wait()
            share = -(-row_groups // (attn_ready - 1 - tiles))
            start, stop = (step - tiles) * share, min((step - tiles + 1) * share, row_groups)
            if start < stop:
                lax.fori_loop(start, stop, rows_step, 0)
                if stop == row_groups:
                    exchange(1, last_ref).start()
        if step == attn_ready - 1:
            attn_grads()
        if step == embed_ready - 1:
            exchange(1, last_ref).wait()
            enc_out()
            vnear_ref[low] = vsum_ref[...]
            for copy in stages(0):
                copy.start()
        if step == embed_ready:
            for copy in stages(0):
                copy.wait()
            vsum_ref[...] = (vnear_ref[0] + vnear_ref[1]) + (vnear_ref[2] + vnear_ref[3])
            vfar_ref[high] = vsum_ref[...]
            for copy in stages(1):
                copy.start()
        if step == embed_ready + 1:
            for copy in stages(1):
                copy.wait()
            every = vfar_ref[0]
            for k in range(1, highs):
                every = every + vfar_ref[k]
            vsum_ref[...] = every
            norm_ref[0:1, 0:1] += jnp.sum(every * every, keepdims=True) * (1.0 / (8 * highs))
    norm_ref[1:2, 0:1] = jnp.sum(loss_ref[...], keepdims=True)
    spots_ref[spot] = norm_ref[...]
    copies = [remote(norm_ref, spots_ref.at[spot], ns_sem.at[k], nr_sem.at[k], near[k]) for k in range(7)]
    for copy in copies:
        copy.start()
    for copy in copies:
        copy.wait()
    local = spots_ref[0]
    for k in range(1, 8):
        local = local + spots_ref[k]
    norm_ref[...] = local
    far_ref[high] = local
    copies = [remote(norm_ref, far_ref.at[high], hs_sem.at[k], hr_sem.at[k], red.at_high[k]) for k in range(highs - 1)]
    for copy in copies:
        copy.start()
    for copy in copies:
        copy.wait()
    every = far_ref[0]
    for k in range(1, highs):
        every = every + far_ref[k]
    sums_ref[...] = every


def backward_all(gy, x1, evec, vec_grads, loss_parts, enc_saved, x0, flat, pixk, mlp, grads, length, head_dim):
    size = lax.axis_size("dp")
    highs = size // 4
    qkv, mixed, lse = enc_saved
    rows, wide = x1.shape
    width = mixed.shape[0]
    hidden = mlp.shape[1] // 2
    group = 2 * length
    shard = wide // size
    lead = (highs, 4, shard)
    fresh = [lead + (hidden,), lead + (hidden,), lead + (4 * width,), lead + (pixk.shape[1] // 2,)]
    widths = [a.shape[1] for a in grads] + [dims[-1] for dims in fresh]
    shards = [a.shape[0] // size for a in grads] + [shard] * 4
    count, given = len(widths), len(grads)
    blocks = blocks_of(widths, 512)
    first = [b for b in blocks if b[0] < given]
    if len(first) % 2:
        raise ValueError("odd blocks")
    middle = [b for at in range(0, hidden, 512) for b in ((given, at, 512), (given + 1, at, 512))]
    attn = [b for b in blocks if b[0] == given + 2]
    groups = first + middle + attn + [b for b in blocks if b[0] == given + 3]
    ready = (len(first) // 2, (len(first) + len(middle)) // 2, (len(first) + len(middle) + len(attn)) // 2)
    dma = pltpu.SemaphoreType.DMA
    small, vec_block = (8, 128), vec_grads.shape
    in_vmem = pl.BlockSpec(memory_space=pltpu.VMEM)
    any_space = pl.BlockSpec(memory_space=pl.ANY)
    result = pl.pallas_call(
        functools.partial(backward_kernel, highs, (1.0,) * count, groups, ready, count, length, group, head_dim),
        out_shape=tuple([shape((r, w), F32) for r, w in zip(shards, widths)] + [shape(small, F32), shape(vec_block, F32)]
                        + [shape(dims, BF16) for dims in fresh]),
        in_specs=[in_vmem] * 6 + [any_space] * (6 + given),
        out_specs=tuple([in_vmem] * (count + 2) + [any_space] * 4),
        scratch_shapes=[
            pltpu.VMEM((rows, wide), F32), pltpu.VMEM(qkv.shape, BF16), pltpu.VMEM(mixed.shape, BF16),
            pltpu.VMEM(flat.shape, BF16), pltpu.VMEM(pixk.shape, BF16), pltpu.VMEM((2, 2) + lead + (512,), BF16),
            pltpu.VMEM((rows, wide), BF16), pltpu.VMEM((wide, rows), BF16), pltpu.VMEM((rows, wide), BF16),
            pltpu.VMEM((wide, rows), BF16), pltpu.VMEM((rows, wide), F32), pltpu.VMEM((rows, wide), BF16),
            pltpu.VMEM((rows, wide), BF16), pltpu.VMEM((rows, wide), BF16), pltpu.VMEM((width, group), BF16),
            pltpu.VMEM((3 * width, rows), BF16), pltpu.VMEM((4,) + lead + (512,), BF16), pltpu.VMEM(small, F32),
            pltpu.VMEM((8,) + small, F32), pltpu.VMEM((highs,) + small, F32), pltpu.VMEM((4,) + vec_block, F32),
            pltpu.VMEM((highs,) + vec_block, F32),
            dma((5,)), dma((2, 2)), dma((4,)), dma((2,)), dma((2,)), dma((7,)), dma((7,)), dma((highs - 1,)),
            dma((highs - 1,)), dma((highs + 2,)), dma((highs + 2,))] + reducer_scratch(highs, groups, shards),
        compiler_params=pltpu.CompilerParams(collective_id=1, has_side_effects=True, vmem_limit_bytes=62 * 2**20),
        cost_estimate=pl.CostEstimate(flops=0, bytes_accessed=sum(a.size * 2 for a in grads), transcendentals=0),
    )(gy, x1, evec, vec_grads, loss_parts, lse, x0, qkv, mixed, flat, pixk, mlp.reshape(lead + (2 * hidden,)),
      *[a.reshape(highs, 4, r, a.shape[1]) for r, a in zip(shards, grads)])
    return list(result[:count]), result[count][0, 0], 0.5 * result[count][1, 0], result[count + 1]


def reduce_plain(grads, loss_parts, vec_grads):
    order_a, order_b = orders()
    outs = [reduce_dp(a, 0, (order_a, order_b)[number % 2], a.dtype) for number, a in enumerate(grads)]
    vec_sums = total_dp(vec_grads)
    sums = jnp.stack([sum(jnp.sum(a * a) for a in outs), jnp.sum(loss_parts)])
    sums = total_dp(sums)
    sums = sums + other_core(sums)
    return outs, sums[0] + jnp.sum(vec_sums * vec_sums), 0.5 * sums[1], vec_sums


def adam_update(master, gradient, first_old, second_old, step_rate, decay_rate):
    first_new = BETA_ONE * first_old + (1.0 - BETA_ONE) * gradient
    second_new = BETA_TWO * second_old + (1.0 - BETA_TWO) * gradient * gradient
    first_hat = first_new / (1.0 - BETA_ONE**STEP)
    second_hat = second_new / (1.0 - BETA_TWO**STEP)
    updated = master - step_rate * (
        first_hat / (jnp.sqrt(second_hat) + ADAM_EPS) + decay_rate * master
    )
    return (updated, first_new, second_new)


def per_device(
    pixels,
    target,
    band_ids,
    kept_index,
    intersection,
    gsd_scale,
    enc_attn,
    enc_mlp,
    dec_attn,
    dec_mlp,
    patch_embed,
    bridge,
    predict,
    vectors,
    first_enc_attn,
    first_enc_mlp,
    first_dec_attn,
    first_dec_mlp,
    first_patch_embed,
    first_bridge,
    first_predict,
    first_vectors,
    second_enc_attn,
    second_enc_mlp,
    second_dec_attn,
    second_dec_mlp,
    second_patch_embed,
    second_bridge,
    second_predict,
    second_vectors,
    ema_enc_attn,
    ema_enc_mlp,
    ema_patch_embed,
):
    masters = (enc_attn, enc_mlp, dec_attn, dec_mlp, patch_embed, bridge, predict, vectors)
    firsts = (
        first_enc_attn,
        first_enc_mlp,
        first_dec_attn,
        first_dec_mlp,
        first_patch_embed,
        first_bridge,
        first_predict,
        first_vectors,
    )
    seconds = (
        second_enc_attn,
        second_enc_mlp,
        second_dec_attn,
        second_dec_mlp,
        second_patch_embed,
        second_bridge,
        second_predict,
        second_vectors,
    )
    images, keep_count = kept_index.shape
    patch_count = intersection.shape[1]
    patch_index = jnp.arange(patch_count, dtype=jnp.int32)
    kept_flags = jnp.any(kept_index[:, :, None] == patch_index[None, None, :], axis=1).astype(
        jnp.float32
    )
    patch_weight = ((1.0 - kept_flags) * (1.0 - 0.5 * intersection.astype(jnp.float32))).reshape(
        -1, 1
    )
    core_at = lax.axis_index("mp")
    size = lax.axis_size("dp")
    low = jnp.bfloat16

    def flat(stack):
        return jnp.concatenate([part.astype(low) for part in stack], axis=1)

    def core_half(block):
        return lax.dynamic_slice_in_dim(block, core_at * (block.shape[1] // 2), block.shape[1] // 2, 1).astype(low)

    vec_shard = vectors.shape[0]
    vec_room = -(-vec_shard // 1024) * 1024
    vec_rows = jnp.pad(lax.reduce_precision(vectors, 8, 7), (0, vec_room - vec_shard)).reshape(-1, 128)
    whole_tiles = patch_embed.shape[1] % 16 == 0 and dec_attn.shape[1] % 16 == 0
    vec_full = small_gather(vec_rows) if whole_tiles else gather_dp(vec_rows, 0, orders()[0])
    pieces = split_vectors(vec_full.reshape(size, vec_room)[:, :vec_shard].reshape(-1), D, E)
    evec = jnp.stack(pieces[:7] + [jnp.zeros_like(pieces[0])])
    dvec = jnp.stack(pieces[7:14] + [jnp.zeros_like(pieces[7])])
    kept_column = kept_index.reshape(-1, 1)
    rows, rows_d = images * keep_count, images * patch_count
    pixel_count = pixels.shape[1]
    group = 2 * keep_count
    shards = [core_half(patch_embed.T), flat(enc_attn), flat(enc_mlp), flat(dec_attn), flat(dec_mlp), core_half(bridge),
              core_half(predict)]
    shared = (True, False, False, False, False, True, True)
    enc_table = sine_table(gsd_scale, D, GRID)
    if whole_tiles:
        weights, results = forward_all(shards, shared, pixels, band_ids, patch_weight, kept_column, enc_table, evec)
        embed_w, enc_attn_w, enc_mlp_w, dec_attn_w, dec_mlp_w, bridge_w, predict_w = weights
        x0, *enc_saved, kept_pixels, x1, part, other, counts, enc_flat = results
        band_weight = jnp.sum(counts[:NB], axis=1)
    else:
        weights = gather_all(shards, shared)
        embed_w, enc_attn_w, enc_mlp_w, dec_attn_w, dec_mlp_w, bridge_w, predict_w = weights
        local = enc_attn_w.shape[1] // 4
        band_weight = total_dp(jnp.stack([
            jnp.sum(jnp.where(band_ids == level, patch_weight, 0.0)) for level in range(NB)]))
        x0, *enc_saved, part, kept_pixels = run(
            functools.partial(enc_in_kernel, keep_count, group, DH),
            [shape((rows, D), F32), shape((3 * local, rows), BF16), shape((local, rows), BF16),
             shape((local // DH, rows), F32), shape((rows, D), BF16), shape((rows, pixel_count), BF16)],
            [pltpu.VMEM((4 * local, D), BF16)],
            (pixels, kept_column, enc_table, embed_w, evec, enc_attn_w),
            rows * D * (2 * pixel_count + 8 * local))
        x1, part = mlp_forward(x0, part, evec, enc_mlp_w)
        other = other_core(part)
    inverse = 1.0 / band_weight
    core = lax.axis_index("mp").astype(jnp.int32).reshape(1)
    hidden_rows = (1.0 - kept_flags).reshape(-1, 1)
    one_d, one_e = shape((1, D), F32), shape((1, E), F32)
    dec_table = sine_table(gsd_scale, E, GRID)
    if whole_tiles:
        (gye, grad_dec_attn, grad_dec_up, grad_dec_down, grad_predict, grad_bridge, loss_parts, grad_pbias, dec_sums,
         enc_sums) = decoder_all(
            inverse, x1, part, other, evec, kept_index, kept_column, jnp.concatenate([hidden_rows, patch_weight], axis=1),
            dec_table, dvec, pieces[14].reshape(1, -1), target, band_ids, dec_attn_w, dec_mlp_w, bridge_w, predict_w)
        grad_mask, grad_dec_ga, grad_dec_ba, grad_dec_gb, grad_dec_bb, grad_dec_fg, grad_dec_fb = [
            dec_sums[i : i + 1] for i in range(7)]
        grad_enc_fg, grad_enc_fb = enc_sums[0:1], enc_sums[1:2]
    else:
        local_d = dec_attn_w.shape[1] // 4
        x2, final_enc, xd, *dec_saved, part = run(
            functools.partial(dec_in_kernel, keep_count, DDH),
            [shape((rows, D), F32), shape((rows, D), BF16), shape((rows_d, E), F32), shape((3 * local_d, rows_d), BF16),
             shape((local_d, rows_d), BF16), shape((local_d // DDH, rows_d), F32), shape((rows_d, E), BF16)],
            [pltpu.VMEM((4 * local_d, E), BF16), pltpu.VMEM((rows, E), F32)],
            (x1, part, other, evec, bridge_w, kept_index, hidden_rows, dec_table, dvec,
             dec_attn_w),
            rows_d * E * 8 * local_d + 2 * rows * D * E)
        xd1, part = mlp_forward(xd, part, dvec, dec_mlp_w)
        gyd, grad_predict, grad_pbias, loss_parts, grad_dec_fg, grad_dec_fb = head(
            core, inverse, xd1, part, dvec, pieces[14].reshape(1, -1), predict_w, target, band_ids, patch_weight, patch_count)
        grad_dec_up, grad_dec_down, part = mlp_backward(gyd, xd1, dvec, dec_mlp_w)
        gxd, grad_dec_attn, grad_dec_gb, grad_dec_bb, part = attn_backward(
            gyd, xd1, part, xd, dec_saved, dvec, dec_attn_w, patch_count, patch_count, DDH)
        grad_dec_ga, grad_dec_ba, grad_mask, grad_bridge, grad_enc_fg, grad_enc_fb, gye = run(
            functools.partial(between_kernel, keep_count),
            [one_e, one_e, one_e, shape((D, E // 2), BF16), one_d, one_d, shape((rows, D), F32)],
            [pltpu.VMEM((rows, E), BF16)],
            (core, gxd, xd, part, other_core(part), dvec, kept_column, hidden_rows, final_enc, x2, evec, bridge_w),
            3 * rows * D * E, 1)
    wide_row = lambda row: jnp.pad(row, ((0, 0), (0, D - row.shape[1])))
    no_row = jnp.zeros((1, D), F32)
    late_rows = [grad_enc_fg, grad_enc_fb] + [wide_row(row) for row in (
        grad_mask, grad_dec_ga, grad_dec_ba, grad_dec_gb, grad_dec_bb, grad_dec_fg, grad_dec_fb, grad_pbias)] + [no_row]
    dec_grads = [grad_predict, grad_dec_up, grad_dec_down, grad_dec_attn, grad_bridge]
    if whole_tiles:
        sums, total_squares, loss, vec_sums = backward_all(
            gye, x1, evec, jnp.concatenate([no_row] * 5 + late_rows), loss_parts, enc_saved, x0, enc_flat, kept_pixels,
            enc_mlp_w, dec_grads, keep_count, DH)
    else:
        grad_enc_up, grad_enc_down, part = mlp_backward(gye, x1, evec, enc_mlp_w)
        gxe, grad_enc_attn, grad_enc_gb, grad_enc_bb, part = attn_backward(
            gye, x1, part, x0, enc_saved, evec, enc_attn_w, keep_count, group, DH)
        grad_enc_ga, grad_enc_ba, grad_ebias, grad_embed = run(
            enc_out_kernel,
            [one_d, one_d, one_d, shape((D, pixel_count // 2), BF16)],
            [], (core, gxe, x0, part, other_core(part), evec, kept_pixels), rows * D * pixel_count, 1)
        vec_grads = jnp.concatenate([grad_ebias, grad_enc_ga, grad_enc_ba, grad_enc_gb, grad_enc_bb] + late_rows)
        sums, total_squares, loss, vec_sums = reduce_plain(
            dec_grads + [grad_enc_up, grad_enc_down, grad_enc_attn, grad_embed], loss_parts, vec_grads)
    vec_grad = jnp.concatenate([vec_sums[:7].reshape(-1), vec_sums[7:14, :E].reshape(-1), vec_sums[14, :pixel_count]])
    vec_grad = lax.dynamic_slice_in_dim(vec_grad, lax.axis_index("dp") * vec_shard, vec_shard)
    reduced = (
        jnp.stack(jnp.split(sums[7], 4, axis=1)),
        jnp.stack(sums[5:7]),
        jnp.stack(jnp.split(sums[3], 4, axis=1)),
        jnp.stack(sums[1:3]),
        join_cores(sums[8], core).T,
        join_cores(sums[4], core),
        join_cores(sums[0], core),
        vec_grad,
    )
    grad_norm = jnp.sqrt(total_squares)
    factor = CLIP / jnp.maximum(grad_norm, CLIP)
    news, new_firsts, new_seconds = ([], [], [])
    for position, master in enumerate(masters):
        is_vec = position == 7
        updated, first_new, second_new = adam_update(
            master,
            reduced[position] * factor,
            firsts[position],
            seconds[position],
            RATE_VEC if is_vec else RATE_MAT,
            0.0 if is_vec else DECAY_MAT,
        )
        news.append(updated)
        new_firsts.append(first_new)
        new_seconds.append(second_new)
    ema_attn = EMA_KEEP * ema_enc_attn + (1.0 - EMA_KEEP) * news[0]
    ema_mlp = EMA_KEEP * ema_enc_mlp + (1.0 - EMA_KEEP) * news[1]
    ema_embed = EMA_KEEP * ema_patch_embed + (1.0 - EMA_KEEP) * news[4]
    return (
        loss,
        band_weight,
        grad_norm,
        news[0],
        news[1],
        news[2],
        news[3],
        news[4],
        news[5],
        news[6],
        news[7],
        new_firsts[0],
        new_firsts[1],
        new_firsts[2],
        new_firsts[3],
        new_firsts[4],
        new_firsts[5],
        new_firsts[6],
        new_firsts[7],
        new_seconds[0],
        new_seconds[1],
        new_seconds[2],
        new_seconds[3],
        new_seconds[4],
        new_seconds[5],
        new_seconds[6],
        new_seconds[7],
        ema_attn,
        ema_mlp,
        ema_embed,
    )


def solution(mesh):
    return jax.shard_map(
        per_device,
        mesh=mesh,
        in_specs=(
            P("dp", None),
            P("dp", None),
            P("dp", None),
            P("dp", None),
            P("dp", None),
            P("dp"),
            P(None, "dp", "mp"),
            P(None, "dp", "mp"),
            P(None, "dp", "mp"),
            P(None, "dp", "mp"),
            P(None, "dp"),
            P("dp", None),
            P("dp", None),
            P("dp"),
            P(None, "dp", "mp"),
            P(None, "dp", "mp"),
            P(None, "dp", "mp"),
            P(None, "dp", "mp"),
            P(None, "dp"),
            P("dp", None),
            P("dp", None),
            P("dp"),
            P(None, "dp", "mp"),
            P(None, "dp", "mp"),
            P(None, "dp", "mp"),
            P(None, "dp", "mp"),
            P(None, "dp"),
            P("dp", None),
            P("dp", None),
            P("dp"),
            P(None, "dp", "mp"),
            P(None, "dp", "mp"),
            P(None, "dp"),
        ),
        out_specs=(
            P(),
            P(),
            P(),
            P(None, "dp", "mp"),
            P(None, "dp", "mp"),
            P(None, "dp", "mp"),
            P(None, "dp", "mp"),
            P(None, "dp"),
            P("dp", None),
            P("dp", None),
            P("dp"),
            P(None, "dp", "mp"),
            P(None, "dp", "mp"),
            P(None, "dp", "mp"),
            P(None, "dp", "mp"),
            P(None, "dp"),
            P("dp", None),
            P("dp", None),
            P("dp"),
            P(None, "dp", "mp"),
            P(None, "dp", "mp"),
            P(None, "dp", "mp"),
            P(None, "dp", "mp"),
            P(None, "dp"),
            P("dp", None),
            P("dp", None),
            P("dp"),
            P(None, "dp", "mp"),
            P(None, "dp", "mp"),
            P(None, "dp"),
        ),
        check_vma=False,
    )
```

```python
import functools
import math

import jax
import jax.numpy as jnp
from jax import lax
from jax.experimental import pallas as pl
from jax.experimental.pallas import tpu as pltpu
from jax.sharding import PartitionSpec as P

D = 1024
DH = 64
E = 512
DDH = 32
GRID = 16
NB = 3
STEP = 10


EPS_LN = 1e-06
EPS_C = 0.01
CLIP = 0.0002
BETA_ONE = 0.9
BETA_TWO = 0.999
ADAM_EPS = 1e-12
RATE_MAT = 0.06
RATE_VEC = 0.5
DECAY_MAT = 0.05
EMA_KEEP = 0.9
REF_GSD = 4.0


def split_vectors(flat_vec, enc_width, dec_width):
    lengths = [enc_width] * 7 + [dec_width] * 7
    pieces = []
    offset = 0
    for length in lengths:
        pieces.append(flat_vec[offset : offset + length])
        offset = offset + length
    pieces.append(flat_vec[offset:])
    return pieces


F32 = jnp.float32
BF16 = jnp.bfloat16
VMEM_LIMIT = 58 * 2**20
GELU_C = math.sqrt(2.0 / math.pi)


def dot_nn(left, right):
    return jnp.dot(left, right, preferred_element_type=F32)


def dot_nt(left, right):
    return lax.dot_general(left, right, (((1,), (1,)), ((), ())), preferred_element_type=F32)


def dot_tn(left, right):
    return lax.dot_general(left, right, (((0,), (0,)), ((), ())), preferred_element_type=F32)


def dot_exact(left, right):
    return jnp.dot(left, right, preferred_element_type=F32, precision=lax.Precision.HIGHEST)


def normalize(rows):
    centred = rows - jnp.mean(rows, axis=-1, keepdims=True)
    rstd = lax.rsqrt(jnp.mean(centred * centred, axis=-1, keepdims=True) + EPS_LN)
    return centred * rstd, rstd


def norm_back(grad, gain, unit, rstd):
    scaled = grad * gain
    mean_one = jnp.mean(scaled, axis=-1, keepdims=True)
    mean_two = jnp.mean(scaled * unit, axis=-1, keepdims=True)
    grad_in = rstd * (scaled - mean_one - unit * mean_two)
    return (
        grad_in,
        jnp.sum(grad * unit, axis=0, keepdims=True),
        jnp.sum(grad, axis=0, keepdims=True),
    )


def both(mine_ref, other_ref, rows):
    return mine_ref[rows, :].astype(F32) + other_ref[rows, :].astype(F32)


def gelu_parts(up):
    square = up * up
    bent = jnp.tanh(GELU_C * up * (1.0 + 0.044715 * square))
    half = 0.5 * (1.0 + bent)
    return square, bent, half


def group_mask(group, length):
    if group == length:
        return None
    row_image = lax.broadcasted_iota(jnp.int32, (group, group), 0) // length
    col_image = lax.broadcasted_iota(jnp.int32, (group, group), 1) // length
    return row_image == col_image


def attend(qkv_ref, mixed_ref, lse_ref, cols, width, head_dim, mask):
    scale = head_dim ** (-0.5)
    for head in range(width // head_dim):
        at = pl.ds(head * head_dim, head_dim)
        queries = qkv_ref[at, cols]
        keys = qkv_ref[pl.ds(width + head * head_dim, head_dim), cols]
        values = qkv_ref[pl.ds(2 * width + head * head_dim, head_dim), cols]
        scores = dot_tn(keys, queries) * scale
        if mask is not None:
            scores = jnp.where(mask, scores, -1e30)
        top = jnp.max(scores, axis=0, keepdims=True)
        weights = jnp.exp(scores - top)
        total = jnp.sum(weights, axis=0, keepdims=True)
        lse_ref[pl.ds(head, 1), cols] = top + jnp.log(total)
        soft = (weights * (1.0 / total)).astype(BF16)
        mixed_ref[at, cols] = dot_nn(values, soft).astype(BF16)


def attend_back(qkv_ref, grad_ref, lse_ref, out_ref, cols, width, head_dim, mask):
    scale = head_dim ** (-0.5)
    for head in range(width // head_dim):
        at = pl.ds(head * head_dim, head_dim)
        at_k = pl.ds(width + head * head_dim, head_dim)
        at_v = pl.ds(2 * width + head * head_dim, head_dim)
        queries, keys, values = qkv_ref[at, cols], qkv_ref[at_k, cols], qkv_ref[at_v, cols]
        grad = grad_ref[at, :]
        scores = dot_tn(keys, queries) * scale
        if mask is not None:
            scores = jnp.where(mask, scores, -1e30)
        soft = jnp.exp(scores - lse_ref[pl.ds(head, 1), cols])
        out_ref[at_v, cols] = dot_nt(grad, soft.astype(BF16)).astype(BF16)
        grad_soft = dot_tn(values, grad)
        inner = jnp.sum(soft * grad_soft, axis=0, keepdims=True)
        grad_scores = (soft * (grad_soft - inner)).astype(BF16)
        out_ref[at, cols] = (dot_nn(keys, grad_scores) * scale).astype(BF16)
        out_ref[at_k, cols] = (dot_nt(queries, grad_scores) * scale).astype(BF16)


def transposed_weights(attn_ref, flat_ref):
    width = attn_ref.shape[1] // 4
    for part in range(4):
        at = pl.ds(part * width, width)
        flat_ref[at, :] = attn_ref[:, at].T


def attention_rows(unit, vec_ref, flat_ref, qkv_ref, mixed_ref, lse_ref, part_ref, rows, head_dim, mask, attn_ref):
    width = mixed_ref.shape[0]
    low = (unit * vec_ref[1:2, :] + vec_ref[2:3, :]).astype(BF16)
    qkv_ref[:, rows] = dot_nt(flat_ref[: 3 * width, :], low).astype(BF16)
    attend(qkv_ref, mixed_ref, lse_ref, rows, width, head_dim, mask)
    part_ref[rows, :] = dot_nt(mixed_ref[:, rows].T, attn_ref[:, 3 * width :]).astype(BF16)


def enc_in_kernel(length, group, head_dim, pix_ref, kept_ref, table_ref, embed_ref, vec_ref, attn_ref,
                  x_ref, qkv_ref, mixed_ref, lse_ref, part_ref, pixk_ref, flat_ref):
    images, patches = table_ref.shape[0], pix_ref.shape[0] // table_ref.shape[0]
    side = table_ref.shape[1]
    transposed_weights(attn_ref, flat_ref)

    def pick(image, carry):
        rows = pl.ds(image * length, length)
        index = kept_ref[rows, :]
        hot = lax.broadcasted_iota(jnp.int32, (length, patches), 1) == index
        pixels = pix_ref[pl.ds(image * patches, patches), :]
        pixk_ref[rows, :] = dot_nn(hot.astype(BF16), pixels).astype(BF16)
        grid_at = lax.broadcasted_iota(jnp.int32, (length, side), 1)
        table = table_ref[image]
        half = table.shape[1]
        x_ref[rows, :half] = dot_exact((grid_at == index // side).astype(F32), table)
        x_ref[rows, half:] = dot_exact((grid_at == index % side).astype(F32), table)
        return carry

    lax.fori_loop(0, images, pick, 0)
    mask = group_mask(group, length)

    def step(number, carry):
        rows = pl.ds(pl.multiple_of(number * group, group), group)
        share = embed_ref.shape[2]
        rows_x = dot_nt(pixk_ref[rows, :share], embed_ref[0]) + dot_nt(pixk_ref[rows, share:], embed_ref[1])
        rows_x = rows_x + vec_ref[0:1, :] + x_ref[rows, :]
        x_ref[rows, :] = rows_x
        unit, _ = normalize(rows_x)
        attention_rows(unit, vec_ref, flat_ref, qkv_ref, mixed_ref, lse_ref, part_ref, rows, head_dim, mask, attn_ref)
        return carry

    lax.fori_loop(0, x_ref.shape[0] // group, step, 0)


def dec_in_kernel(length, head_dim, x1_ref, mine_ref, other_ref, evec_ref, bridge_ref, kept_ref, hidden_ref,
                  table_ref, vec_ref, attn_ref,
                  x2_ref, final_ref, x_ref, qkv_ref, mixed_ref, lse_ref, part_ref, flat_ref, latent_ref):
    images, side, half = table_ref.shape
    patches = side * side
    transposed_weights(attn_ref, flat_ref)
    every = pl.ds(0, x1_ref.shape[0])
    out = x1_ref[...] + both(mine_ref, other_ref, every)
    x2_ref[...] = out
    unit, _ = normalize(out)
    final = (unit * evec_ref[5:6, :] + evec_ref[6:7, :]).astype(BF16)
    final_ref[...] = final
    share = bridge_ref.shape[2]
    latent_ref[:, :share] = dot_nn(final, bridge_ref[0])
    latent_ref[:, share:] = dot_nn(final, bridge_ref[1])

    def step(image, carry):
        rows = pl.ds(pl.multiple_of(image * patches, patches), patches)
        hot = lax.broadcasted_iota(jnp.int32, (patches, length), 0) == kept_ref[pl.ds(image, 1), :]
        latent = latent_ref[pl.ds(image * length, length), :]
        table = table_ref[image]
        by_row = jnp.broadcast_to(table[:, None, :], (side, side, half)).reshape(patches, half)
        by_col = jnp.broadcast_to(table[None, :, :], (side, side, half)).reshape(patches, half)
        place = jnp.concatenate([by_row, by_col], axis=1)
        rows_x = dot_exact(hot.astype(F32), latent) + hidden_ref[rows, :] * vec_ref[0:1, :] + place
        x_ref[rows, :] = rows_x
        unit, _ = normalize(rows_x)
        attention_rows(unit, vec_ref, flat_ref, qkv_ref, mixed_ref, lse_ref, part_ref, rows, head_dim, None, attn_ref)
        return carry

    lax.fori_loop(0, images, step, 0)


def mlp_kernel(tile, x_ref, mine_ref, other_ref, vec_ref, up_ref, down_ref, x1_ref, part_ref, low_ref, acc_ref):
    number = pl.program_id(0)
    count = x_ref.shape[0] // tile

    def first(step, carry):
        rows = pl.ds(pl.multiple_of(step * tile, tile), tile)
        after = x_ref[rows, :] + both(mine_ref, other_ref, rows)
        x1_ref[rows, :] = after
        unit, _ = normalize(after)
        low_ref[rows, :] = (unit * vec_ref[3:4, :] + vec_ref[4:5, :]).astype(BF16)
        return carry

    @pl.when(number == 0)
    def _():
        lax.fori_loop(0, count, first, 0)
        acc_ref[...] = jnp.zeros_like(acc_ref)

    def step(piece, carry):
        rows = pl.ds(pl.multiple_of(piece * tile, tile), tile)
        up = dot_nn(low_ref[rows, :], up_ref[...])
        _, _, half = gelu_parts(up)
        acc_ref[rows, :] += dot_nt((up * half).astype(BF16), down_ref[...])
        return carry

    lax.fori_loop(0, count, step, 0)

    @pl.when(number == pl.num_programs(0) - 1)
    def _():
        part_ref[...] = acc_ref[...].astype(BF16)


def head_kernel(core_ref, inverse_ref, x1_ref, mine_ref, other_ref, vec_ref, bias_ref, predict_ref, target_ref,
                band_ref, weight_ref, gy_ref, glow_ref, gbias_ref, loss_ref, gain_ref, shift_ref, low_ref, gpred_ref):
    number = pl.program_id(0)

    @pl.when(number == 0)
    def _():
        for ref in (gpred_ref, gbias_ref, loss_ref, gain_ref, shift_ref):
            ref[...] = jnp.zeros_like(ref)

    every = pl.ds(0, x1_ref.shape[0])
    unit, rstd = normalize(x1_ref[...] + both(mine_ref, other_ref, every))
    gain = vec_ref[5:6, :]
    final = (unit * gain + vec_ref[6:7, :]).astype(BF16)
    share = gpred_ref.shape[1]
    predicted = jnp.concatenate([dot_nn(final, predict_ref[0]), dot_nn(final, predict_ref[1])], axis=1)
    mismatch = predicted + bias_ref[...] - target_ref[...].astype(F32)
    band = band_ref[...]
    level = jnp.where(band == 0, inverse_ref[0], jnp.where(band == 1, inverse_ref[1], inverse_ref[2]))
    level = level * weight_ref[...]
    square = mismatch * mismatch + EPS_C
    root = lax.rsqrt(square)
    loss_ref[...] += jnp.sum(level * (square * root), axis=0, keepdims=True)
    grad = level * (mismatch * root)
    gbias_ref[...] += jnp.sum(grad, axis=0, keepdims=True)
    low_ref[...] = grad.astype(BF16)
    columns = pl.ds(pl.multiple_of(core_ref[0] * share, share), share)
    gpred_ref[...] += dot_tn(final, low_ref[:, columns])
    grad_final = dot_nt(low_ref[:, :share], predict_ref[0]) + dot_nt(low_ref[:, share:], predict_ref[1])
    grad_in, gain_sum, shift_sum = norm_back(grad_final, gain, unit, rstd)
    gy_ref[...] = grad_in
    gain_ref[...] += gain_sum
    shift_ref[...] += shift_sum

    @pl.when(number == pl.num_programs(0) - 1)
    def _():
        glow_ref[...] = gpred_ref[...].astype(BF16)


def mlp_back_kernel(tile, gy_ref, x1_ref, vec_ref, up_ref, down_ref, gup_ref, gdown_ref, part_ref,
                    low_ref, lowt_ref, grad_ref, gradt_ref, gu_ref, z_ref, acc_ref):
    number = pl.program_id(0)
    count = x1_ref.shape[0] // tile

    def first(step, carry):
        rows = pl.ds(pl.multiple_of(step * tile, tile), tile)
        unit, _ = normalize(x1_ref[rows, :])
        low = (unit * vec_ref[3:4, :] + vec_ref[4:5, :]).astype(BF16)
        low_ref[rows, :] = low
        lowt_ref[:, rows] = low.T
        grad = gy_ref[rows, :].astype(BF16)
        grad_ref[rows, :] = grad
        gradt_ref[:, rows] = grad.T
        return carry

    @pl.when(number == 0)
    def _():
        lax.fori_loop(0, count, first, 0)
        acc_ref[...] = jnp.zeros_like(acc_ref)

    def step(piece, carry):
        rows = pl.ds(pl.multiple_of(piece * tile, tile), tile)
        up = dot_nn(low_ref[rows, :], up_ref[...])
        square, bent, half = gelu_parts(up)
        z_ref[rows, :] = (up * half).astype(BF16)
        slope = half + (0.5 * GELU_C) * up * (1.0 - bent * bent) * (1.0 + (3.0 * 0.044715) * square)
        grad_up = (dot_nn(grad_ref[rows, :], down_ref[...]) * slope).astype(BF16)
        gu_ref[rows, :] = grad_up
        acc_ref[rows, :] += dot_nt(grad_up, up_ref[...])
        return carry

    lax.fori_loop(0, count, step, 0)
    gup_ref[...] = dot_nn(lowt_ref[...], gu_ref[...]).astype(BF16)
    gdown_ref[...] = dot_nn(gradt_ref[...], z_ref[...]).astype(BF16)

    @pl.when(number == pl.num_programs(0) - 1)
    def _():
        part_ref[...] = acc_ref[...].astype(BF16)


def attn_back_kernel(length, group, head_dim, gy_ref, x1_ref, mine_ref, other_ref, x_ref, qkv_ref, mixed_ref, lse_ref,
                     vec_ref, attn_ref, gx_ref, grad_ref, gain_ref, shift_ref, part_ref,
                     flat_ref, lowt_ref, gradt_ref, gmix_ref, gqkv_ref):
    width = mixed_ref.shape[0]
    transposed_weights(attn_ref, flat_ref)
    gain_ref[...] = jnp.zeros_like(gain_ref)
    shift_ref[...] = jnp.zeros_like(shift_ref)
    mask = group_mask(group, length)

    def step(number, carry):
        rows = pl.ds(pl.multiple_of(number * group, group), group)
        unit, rstd = normalize(x1_ref[rows, :])
        grad_in, gain_sum, shift_sum = norm_back(both(mine_ref, other_ref, rows), vec_ref[3:4, :], unit, rstd)
        grad_in = grad_in + gy_ref[rows, :]
        gx_ref[rows, :] = grad_in
        gain_ref[...] += gain_sum
        shift_ref[...] += shift_sum
        low_grad = grad_in.astype(BF16)
        gradt_ref[:, rows] = low_grad.T
        gmix_ref[...] = dot_nt(flat_ref[3 * width :, :], low_grad).astype(BF16)
        attend_back(qkv_ref, gmix_ref, lse_ref, gqkv_ref, rows, width, head_dim, mask)
        part_ref[rows, :] = dot_nn(gqkv_ref[:, rows].T, flat_ref[: 3 * width, :]).astype(BF16)
        unit_a, _ = normalize(x_ref[rows, :])
        lowt_ref[:, rows] = (unit_a * vec_ref[1:2, :] + vec_ref[2:3, :]).astype(BF16).T
        return carry

    lax.fori_loop(0, x_ref.shape[0] // group, step, 0)
    grad_ref[:, : 3 * width] = dot_nt(lowt_ref[...], gqkv_ref[...]).astype(BF16)
    grad_ref[:, 3 * width :] = dot_nt(gradt_ref[...], mixed_ref[...]).astype(BF16)


def between_kernel(length, core_ref, gx_ref, x_ref, mine_ref, other_ref, vec_ref, kept_ref, hidden_ref, final_ref, x2_ref,
                   evec_ref, bridge_ref, gain_ref, shift_ref, mask_ref, gbridge_ref, egain_ref, eshift_ref, gy_ref,
                   latent_ref):
    images = kept_ref.shape[0] // length
    patches = x_ref.shape[0] // images
    for ref in (gain_ref, shift_ref, mask_ref):
        ref[...] = jnp.zeros_like(ref)

    def step(image, carry):
        rows = pl.ds(pl.multiple_of(image * patches, patches), patches)
        unit, rstd = normalize(x_ref[rows, :])
        grad_in, gain_sum, shift_sum = norm_back(both(mine_ref, other_ref, rows), vec_ref[1:2, :], unit, rstd)
        grad_in = grad_in + gx_ref[rows, :]
        gain_ref[...] += gain_sum
        shift_ref[...] += shift_sum
        mask_ref[...] += jnp.sum(grad_in * hidden_ref[rows, :], axis=0, keepdims=True)
        kept_rows = pl.ds(pl.multiple_of(image * length, length), length)
        hot = lax.broadcasted_iota(jnp.int32, (length, patches), 1) == kept_ref[kept_rows, :]
        latent_ref[kept_rows, :] = dot_nn(hot.astype(BF16), grad_in.astype(BF16)).astype(BF16)
        return carry

    lax.fori_loop(0, images, step, 0)
    share = gbridge_ref.shape[1]
    columns = pl.ds(pl.multiple_of(core_ref[0] * share, share), share)
    gbridge_ref[...] = dot_tn(final_ref[...], latent_ref[:, columns]).astype(BF16)
    grad_final = dot_nt(latent_ref[:, :share], bridge_ref[0]) + dot_nt(latent_ref[:, share:], bridge_ref[1])
    unit, rstd = normalize(x2_ref[...])
    gy_ref[...], egain_ref[...], eshift_ref[...] = norm_back(grad_final, evec_ref[5:6, :], unit, rstd)


def enc_out_kernel(core_ref, gx_ref, x_ref, mine_ref, other_ref, vec_ref, pixk_ref,
                   gain_ref, shift_ref, ebias_ref, gembed_ref):
    every = pl.ds(0, x_ref.shape[0])
    unit, rstd = normalize(x_ref[...])
    grad_in, gain_ref[...], shift_ref[...] = norm_back(both(mine_ref, other_ref, every), vec_ref[1:2, :], unit, rstd)
    grad_in = grad_in + gx_ref[...]
    ebias_ref[...] = jnp.sum(grad_in, axis=0, keepdims=True)
    share = gembed_ref.shape[1]
    columns = pl.ds(pl.multiple_of(core_ref[0] * share, share), share)
    gembed_ref[...] = dot_tn(grad_in.astype(BF16), pixk_ref[:, columns]).astype(BF16)


def shape(dims, dtype):
    return jax.ShapeDtypeStruct(dims, dtype)


def run(kernel, outs, scratch, args, flops, scalars=0):
    moved = sum(math.prod(a.shape) * a.dtype.itemsize for a in list(args) + list(outs))
    in_vmem = pl.BlockSpec(memory_space=pltpu.VMEM)
    return pl.pallas_call(
        kernel,
        out_shape=tuple(outs),
        in_specs=[pl.BlockSpec(memory_space=pltpu.SMEM)] * scalars + [in_vmem] * (len(args) - scalars),
        out_specs=tuple([in_vmem] * len(outs)),
        scratch_shapes=scratch,
        compiler_params=pltpu.CompilerParams(vmem_limit_bytes=VMEM_LIMIT),
        cost_estimate=pl.CostEstimate(flops=flops, bytes_accessed=moved, transcendentals=0),
    )(*args)


def other_core(block):
    return lax.ppermute(block, "mp", [(0, 1), (1, 0)])


def mlp_forward(x, mine, vec, stack):
    rows, width = x.shape
    hidden = stack.shape[1] // 2
    block = min(hidden, 512)
    tile = min(rows, 512)
    other = other_core(mine)
    whole = pl.BlockSpec((rows, width), lambda i: (0, 0))
    cols = pl.BlockSpec((width, block), lambda i: (0, i))
    later = pl.BlockSpec((width, block), lambda i: (0, i + hidden // block))
    return pl.pallas_call(
        functools.partial(mlp_kernel, tile),
        out_shape=(shape((rows, width), F32), shape((rows, width), BF16)),
        grid=(hidden // block,),
        in_specs=[whole] * 3 + [pl.BlockSpec((8, width), lambda i: (0, 0)), cols, later],
        out_specs=(whole, whole),
        scratch_shapes=[pltpu.VMEM((rows, width), BF16), pltpu.VMEM((rows, width), F32)],
        compiler_params=pltpu.CompilerParams(vmem_limit_bytes=VMEM_LIMIT),
        cost_estimate=pl.CostEstimate(flops=4 * rows * width * hidden, bytes_accessed=rows * width * 14 + width * hidden * 4,
                                      transcendentals=rows * hidden),
    )(x, mine, other, vec, stack, stack)


def mlp_backward(gy, x1, vec, stack):
    rows, width = x1.shape
    hidden = stack.shape[1] // 2
    block = min(hidden, 512)
    tile = min(rows, 256)
    whole = pl.BlockSpec((rows, width), lambda i: (0, 0))
    cols = pl.BlockSpec((width, block), lambda i: (0, i))
    later = pl.BlockSpec((width, block), lambda i: (0, i + hidden // block))
    return pl.pallas_call(
        functools.partial(mlp_back_kernel, tile),
        out_shape=(shape((width, hidden), BF16), shape((width, hidden), BF16), shape((rows, width), BF16)),
        grid=(hidden // block,),
        in_specs=[whole] * 2 + [pl.BlockSpec((8, width), lambda i: (0, 0)), cols, later],
        out_specs=(cols, cols, whole),
        scratch_shapes=[
            pltpu.VMEM((rows, width), BF16), pltpu.VMEM((width, rows), BF16),
            pltpu.VMEM((rows, width), BF16), pltpu.VMEM((width, rows), BF16),
            pltpu.VMEM((rows, block), BF16), pltpu.VMEM((rows, block), BF16),
            pltpu.VMEM((rows, width), F32)],
        compiler_params=pltpu.CompilerParams(vmem_limit_bytes=VMEM_LIMIT),
        cost_estimate=pl.CostEstimate(flops=10 * rows * width * hidden, bytes_accessed=rows * width * 10 + width * hidden * 8,
                                      transcendentals=rows * hidden),
    )(gy, x1, vec, stack, stack)


def head(core, inverse, x1, mine, vec, bias, predict, target, band, weight, patches):
    rows, width = x1.shape
    pixels = target.shape[1]
    share = pixels // 2
    other = other_core(mine)
    smem = pl.BlockSpec(memory_space=pltpu.SMEM)
    row_w = pl.BlockSpec((patches, width), lambda i: (i, 0))
    row_p = pl.BlockSpec((patches, pixels), lambda i: (i, 0))
    fix = lambda a, b: pl.BlockSpec((a, b), lambda i: (0, 0))
    return pl.pallas_call(
        head_kernel,
        out_shape=(shape((rows, width), F32), shape((width, share), BF16), shape((1, pixels), F32),
                   shape((1, pixels), F32), shape((1, width), F32), shape((1, width), F32)),
        grid=(rows // patches,),
        in_specs=[smem, smem, row_w, row_w, row_w, fix(8, width), fix(1, pixels), pl.BlockSpec((2, width, share), lambda i: (0, 0, 0)), row_p, row_p,
                  pl.BlockSpec((patches, 1), lambda i: (i, 0))],
        out_specs=(row_w, fix(width, share), fix(1, pixels), fix(1, pixels), fix(1, width), fix(1, width)),
        scratch_shapes=[pltpu.VMEM((patches, pixels), BF16), pltpu.VMEM((width, share), F32)],
        compiler_params=pltpu.CompilerParams(vmem_limit_bytes=VMEM_LIMIT),
        cost_estimate=pl.CostEstimate(flops=5 * rows * width * pixels, bytes_accessed=rows * (width * 12 + pixels * 6),
                                      transcendentals=rows * pixels),
    )(core, inverse, x1, mine, other, vec, bias, predict, target, band, weight)


def attn_backward(gy, x1, mine, x, saved, vec, attn, length, group, head_dim):
    qkv, mixed, lse = saved
    rows, width = x.shape
    local = mixed.shape[0]
    return run(
        functools.partial(attn_back_kernel, length, group, head_dim),
        [shape((rows, width), F32), shape((width, 4 * local), BF16),
         shape((1, width), F32), shape((1, width), F32), shape((rows, width), BF16)],
        [pltpu.VMEM((4 * local, width), BF16), pltpu.VMEM((width, rows), BF16), pltpu.VMEM((width, rows), BF16),
         pltpu.VMEM((local, group), BF16), pltpu.VMEM((3 * local, rows), BF16)],
        (gy, x1, mine, other_core(mine), x, qkv, mixed, lse, vec, attn),
        18 * rows * width * local)


def sine_table(gsd_values, feature_width, grid_side):
    quarter = feature_width // 4
    frequency = jnp.exp(-jnp.log(10000.0) * jnp.arange(quarter).astype(F32) / quarter)
    gsd_ratio = gsd_values.astype(F32)[:, None, None] / REF_GSD
    line = jnp.arange(grid_side, dtype=jnp.int32).astype(F32)
    arg = line[None, :, None] * gsd_ratio * frequency
    return jnp.concatenate([jnp.sin(arg), jnp.cos(arg)], axis=-1)


def dp_bits():
    return lax.axis_size("dp").bit_length() - 1


def orders():
    bits = dp_bits()
    high = list(range(bits - 1, 1, -1))
    return (high + [0, 1], high + [1, 0])


def swap(block, bit):
    size = lax.axis_size("dp")
    return lax.ppermute(block, "dp", [(i, i ^ (1 << bit)) for i in range(size)])


def my_bit(bit):
    return (lax.axis_index("dp") >> bit) & 1


def gather_dp(block, axis, order):
    lead, rest = (block.shape[:axis], block.shape[axis:])
    done = []
    cur = block
    for bit in order:
        other = swap(cur, bit)
        mine = my_bit(bit) == 1
        place = axis + sum(1 for b in done if b > bit)
        cur = jnp.stack([jnp.where(mine, other, cur), jnp.where(mine, cur, other)], axis=place)
        done.append(bit)
    return cur.reshape(lead + (rest[0] * lax.axis_size("dp"),) + rest[1:])


def reduce_dp(block, axis, order, wire):
    bits = dp_bits()
    lead, rest = (block.shape[:axis], block.shape[axis:])
    shard = rest[0] // lax.axis_size("dp")
    cur = block.reshape(lead + (2,) * bits + (shard,) + rest[1:])
    left = list(range(bits - 1, -1, -1))
    for bit in reversed(order):
        place = axis + left.index(bit)
        mine = my_bit(bit)
        keep = lax.dynamic_index_in_dim(cur, mine, place, keepdims=False)
        give = lax.dynamic_index_in_dim(cur, 1 - mine, place, keepdims=False)
        other = swap(give.astype(wire), bit)
        cur = keep.astype(F32) + other.astype(F32)
        left.remove(bit)
    return cur


def join_cores(mine, core):
    other = other_core(mine)
    return jnp.concatenate([jnp.where(core == 0, mine, other), jnp.where(core == 0, other, mine)], axis=1)


def total_dp(value):
    for bit in range(dp_bits()):
        value = value + swap(value, bit)
    return value


def place_of():
    index = lax.axis_index("dp")
    core = lax.axis_index("mp")
    low, high = lax.rem(index, 4), index // 4
    bit_x, bit_y = lax.rem(low, 2), low // 2
    low_x, low_y = low + 1 - 2 * bit_x, low + 2 - 4 * bit_y
    return core, low, high, low_x, low_y


def greet(partners):
    barrier = pltpu.get_barrier_semaphore()
    for partner in partners:
        pl.semaphore_signal(barrier, inc=1, device_id=partner, device_id_type=pl.DeviceIdType.MESH)
    pl.semaphore_wait(barrier, len(partners))


def blocks_of(widths, limit):
    found = []
    for number, width in enumerate(widths):
        start = 0
        while start < width:
            size = min(limit, width - start)
            found.append((number, start, size))
            start += size
    return found


def remote(source, target, send, receive, device):
    return pltpu.make_async_remote_copy(
        src_ref=source, dst_ref=target, send_sem=send, recv_sem=receive,
        device_id=device, device_id_type=pl.DeviceIdType.MESH)


def total_blocks(block_ref, near_ref, far_ref, sems, low, high, core, highs, stage):
    send, receive = sems
    if stage == 0:
        spots = [(high * 4 + lax.rem(low + k, 4), core) for k in range(1, 4)]
        return [remote(block_ref, near_ref.at[low], send.at[k], receive.at[k], spots[k]) for k in range(3)]
    spots = [(lax.rem(high + k, highs) * 4 + low, core) for k in range(1, highs)]
    return [remote(block_ref, far_ref.at[high], send.at[3 + k], receive.at[3 + k], spots[k]) for k in range(highs - 1)]


def forward_kernel(highs, shared, groups, count, length, group, head_dim, *refs):
    masters, refs = refs[:count], refs[count:]
    pix_any, band_ref, kept_ref, inter_ref, table_ref, placed_ref = refs[:6]
    fulls, refs = refs[6 : 6 + count], refs[6 + count :]
    (x_ref, qkv_ref, mixed_ref, lse_ref, pixk_ref, x1_ref, last_ref, far_out_ref, counts_ref, flat_ref, vec_ref, rows_ref,
     column_ref) = refs[:13]
    refs = refs[13:]
    shards, refs = refs[:count], refs[count:]
    (pix_ref, bands_v, embed_v, attn_v, mlp_v, part_ref, other_ref, low_ref, acc_ref, block_ref, near_ref,
     far_ref) = refs[:12]
    (own_sem, zs_sem, zr_sem, cs_sem, cr_sem, fs_sem, fr_sem, ms_sem, mr_sem, load_sem, xs_sem, xr_sem, ts_sem,
     tr_sem) = refs[12:]
    core, low, high, low_x, low_y = place_of()
    at_x, at_y = (high * 4 + low_x, core), (high * 4 + low_y, core)
    at_high = [(lax.rem(high + k, highs) * 4 + low, core) for k in range(1, highs)]
    sibling = (high * 4 + low, 1 - core)
    near = [(high * 4 + lax.rem(low + k, 4), core) for k in range(1, 4)]
    greet([sibling] + near + at_high)
    for master, shard, split in zip(masters, shards, shared):
        if len(master.shape) == 3:
            wide = master.shape[2]
            for part in range(master.shape[0]):
                shard[:, part * wide : (part + 1) * wide] = master[part].astype(BF16)
        else:
            share = shard.shape[1]
            shard[...] = master[:, pl.ds(pl.multiple_of(core * share, share), share)].astype(BF16)

    def full(at):
        number, start, size = groups[at]
        ref = fulls[number].at[core] if shared[number] else fulls[number]
        return ref, pl.ds(start, size)

    def first(at):
        ref, cols = full(at)
        shard = shards[groups[at][0]].at[:, cols]
        mine = ref.at[high, low, :, cols]
        copies = [pltpu.make_async_copy(shard, mine, own_sem.at[at])]
        for k in range(1, highs):
            copies.append(remote(shard, mine, zs_sem.at[at, k - 1], zr_sem.at[at, k - 1], at_high[k - 1]))
        return copies

    def column(at):
        ref, cols = full(at)
        part = ref.at[:, low, :, cols]
        return [remote(part, part, cs_sem.at[at, 0], cr_sem.at[at, 0], at_x),
                remote(part, part, cs_sem.at[at, 1], cr_sem.at[at, 1], at_y)]

    def forward(at):
        ref, cols = full(at)
        which, device = (low_x, at_y) if at % 2 == 0 else (low_y, at_x)
        part = ref.at[:, which, :, cols]
        return remote(part, part, fs_sem.at[at], fr_sem.at[at], device)

    def swap(number):
        part = fulls[number].at[core]
        return remote(part, part, ms_sem.at[number], mr_sem.at[number], sibling)

    def exchange(at, source, target):
        return remote(source, target, xs_sem.at[at], xr_sem.at[at], sibling)

    total = len(groups)
    pairs = (total + 1) // 2
    in_pair = lambda pair: [at for at in (2 * pair, 2 * pair + 1) if at < total]
    pair_of = lambda number: max(at for at in range(total) if groups[at][0] == number) // 2
    images, side = table_ref.shape[0], table_ref.shape[1]
    patches = side * side
    width = mixed_ref.shape[0]
    mask = group_mask(group, length)

    def lane_of(image, flipped):
        lanes = lax.broadcasted_iota(jnp.int32, flipped.shape, 1)
        return jnp.sum(jnp.where(lanes == image, flipped, 0.0), axis=1, keepdims=True)

    def pick(image, carry):
        rows = pl.ds(pl.multiple_of(image * length, length), length)
        index = lane_of(image, kept_ref[...].astype(F32).T).astype(jnp.int32)
        column_ref[rows, :] = index
        hot = lax.broadcasted_iota(jnp.int32, (length, patches), 1) == index
        pixels = pix_ref[pl.ds(pl.multiple_of(image * patches, patches), patches), :]
        pixk_ref[rows, :] = dot_nn(hot.astype(BF16), pixels).astype(BF16)
        grid_at = lax.broadcasted_iota(jnp.int32, (length, side), 1)
        table = table_ref[image]
        half = table.shape[1]
        x_ref[rows, :half] = dot_exact((grid_at == index // side).astype(F32), table)
        x_ref[rows, half:] = dot_exact((grid_at == index % side).astype(F32), table)
        return carry

    def tally(image, carry):
        rows = pl.ds(pl.multiple_of(image * patches, patches), patches)
        hot = lax.broadcasted_iota(jnp.int32, (patches, length), 0) == kept_ref[pl.ds(image, 1), :]
        hidden = 1.0 - jnp.max(jnp.where(hot, 1.0, 0.0), axis=1, keepdims=True)
        weight = hidden * (1.0 - 0.5 * lane_of(image, inter_ref[...].astype(F32).T))
        rows_ref[rows, 0:1] = hidden
        rows_ref[rows, 1:2] = weight
        band = bands_v[rows, :]
        for level in range(NB):
            row = jnp.sum(jnp.where(band == level, weight, 0.0), axis=0, keepdims=True)
            for start in range(0, row.shape[1], 128):
                block_ref[24 + level : 25 + level, 0:128] += row[:, start : start + 128]
        return carry

    def rows_step(number, carry):
        rows = pl.ds(pl.multiple_of(number * group, group), group)
        share = embed_v.shape[-1]
        embed = lambda half: embed_v[half].reshape(-1, share)
        rows_x = dot_nt(pixk_ref[rows, :share], embed(0)) + dot_nt(pixk_ref[rows, share:], embed(1))
        rows_x = rows_x + vec_ref[0:1, :] + x_ref[rows, :]
        x_ref[rows, :] = rows_x
        unit, _ = normalize(rows_x)
        low_a = (unit * vec_ref[1:2, :] + vec_ref[2:3, :]).astype(BF16)
        qkv_ref[:, rows] = dot_nt(flat_ref[: 3 * width, :], low_a).astype(BF16)
        attend(qkv_ref, mixed_ref, lse_ref, rows, width, head_dim, mask)
        part_ref[rows, :] = dot_nn(mixed_ref[:, rows].T, flat_ref[3 * width :, :]).astype(BF16)
        return carry

    def mlp_first():
        after = x_ref[...] + both(part_ref, other_ref, pl.ds(0, x_ref.shape[0]))
        x1_ref[...] = after
        unit, _ = normalize(after)
        low_ref[...] = (unit * vec_ref[3:4, :] + vec_ref[4:5, :]).astype(BF16)
        acc_ref[...] = jnp.zeros_like(acc_ref)

    def mlp_block(piece, carry):
        size = 512
        hidden = mlp_v.shape[-1] // 2
        start = pl.multiple_of(piece * size, size)
        wide = x_ref.shape[1]
        up = dot_nn(low_ref[...], mlp_v[:, :, :, pl.ds(start, size)].reshape(wide, size))
        _, _, half = gelu_parts(up)
        down = mlp_v[:, :, :, pl.ds(pl.multiple_of(hidden + start, size), size)].reshape(wide, size)
        acc_ref[...] += dot_nt((up * half).astype(BF16), down)
        return carry

    load_bands = pltpu.make_async_copy(band_ref, bands_v, load_sem.at[0])
    load_pixels = pltpu.make_async_copy(pix_any, pix_ref, load_sem.at[4])
    load_attn = pltpu.make_async_copy(fulls[1], attn_v, load_sem.at[1])
    load_embed = pltpu.make_async_copy(fulls[0], embed_v, load_sem.at[2])
    load_mlp = pltpu.make_async_copy(fulls[2], mlp_v, load_sem.at[3])
    stages = functools.partial(total_blocks, block_ref, near_ref, far_ref, (ts_sem, tr_sem), low, high, core, highs)
    embed_at, attn_at, mlp_at = pair_of(0) + 3, pair_of(1) + 3, pair_of(2) + 3
    row_groups = x_ref.shape[0] // group
    swapped = set()
    for step in range(pairs + 3):
        if step < pairs:
            for at in in_pair(step):
                for copy in first(at):
                    copy.start()
        if 0 <= step - 1 < pairs:
            for at in in_pair(step - 1):
                for copy in first(at):
                    copy.wait()
                for copy in column(at):
                    copy.start()
        if 0 <= step - 2 < pairs:
            for at in in_pair(step - 2):
                column(at)[at % 2].wait()
                forward(at).start()
        if 0 <= step - 3 < pairs:
            for at in in_pair(step - 3):
                column(at)[1 - at % 2].wait()
                forward(at).wait()
        for number in range(count):
            if shared[number] and number not in swapped and pair_of(number) + 3 <= step:
                swap(number).start()
                swapped.add(number)
        if step == 0:
            load_bands.start()
            load_pixels.start()
            block_ref[...] = jnp.zeros_like(block_ref)
            block_ref[:24, :] = placed_ref[...]
            load_bands.wait()
            lax.fori_loop(0, images, tally, 0)
            near_ref[low] = block_ref[...]
            for copy in stages(0):
                copy.start()
        if step == 1:
            for copy in stages(0):
                copy.wait()
            block_ref[...] = (near_ref[0] + near_ref[1]) + (near_ref[2] + near_ref[3])
            far_ref[high] = block_ref[...]
            for copy in stages(1):
                copy.start()
            load_pixels.wait()
            lax.fori_loop(0, images, pick, 0)
        if step == 2:
            for copy in stages(1):
                copy.wait()
            counts = far_ref[0]
            for k in range(1, highs):
                counts = counts + far_ref[k]
            counts_ref[...] = counts
            vec_ref[...] = jnp.zeros_like(vec_ref)
            for piece in range(7):
                vec_ref[piece : piece + 1, :512] = counts[2 * piece : 2 * piece + 1, :]
                vec_ref[piece : piece + 1, 512:] = counts[2 * piece + 1 : 2 * piece + 2, :]
        if step == attn_at:
            swap(0).wait()
            load_attn.start()
            load_embed.start()
            load_attn.wait()
            for part in range(4):
                at = pl.ds(part * width, width)
                flat_ref[at, :] = attn_v[:, :, :, at].reshape(-1, width).T
            load_embed.wait()
        if attn_at <= step < mlp_at - 1:
            share = -(-row_groups // (mlp_at - 1 - attn_at))
            start, stop = (step - attn_at) * share, min((step - attn_at + 1) * share, row_groups)
            if start < stop:
                lax.fori_loop(start, stop, rows_step, 0)
                if stop == row_groups:
                    exchange(0, part_ref, other_ref).start()
        if step == mlp_at:
            load_mlp.start()
            exchange(0, part_ref, other_ref).wait()
            mlp_first()
            load_mlp.wait()
            lax.fori_loop(0, mlp_v.shape[-1] // 1024, mlp_block, 0)
            last_ref[...] = acc_ref[...].astype(BF16)
            exchange(1, last_ref, far_out_ref).start()
    exchange(1, last_ref, far_out_ref).wait()
    for number in range(1, count):
        if shared[number]:
            swap(number).wait()


def forward_all(masters, shared, pixels, band_ids, kept_index, intersection, table, placed):
    size = lax.axis_size("dp")
    highs = size // 4
    count = len(masters)
    dims_of = []
    for master, split in zip(masters, shared):
        if master.ndim == 3:
            dims_of.append((master.shape[1], master.shape[0] * master.shape[2]))
        else:
            dims_of.append((master.shape[0], master.shape[1] // 2))
    groups = blocks_of([dims[1] for dims in dims_of], 512)
    total = len(groups)
    images, length = kept_index.shape
    rows, wide, local = images * length, D, dims_of[1][1] // 4
    rows_d = pixels.shape[0]
    group = 2 * length
    fulls = []
    for dims, split in zip(dims_of, shared):
        dims = (highs, 4) + dims
        fulls.append(shape((2,) + dims if split else dims, BF16))
    block = (32, 512)
    outs = [shape((rows, wide), F32), shape((3 * local, rows), BF16), shape((local, rows), BF16),
            shape((local // DH, rows), F32), shape((rows, pixels.shape[1]), BF16), shape((rows, wide), F32),
            shape((rows, wide), BF16), shape((rows, wide), BF16), shape(block, F32), shape((4 * local, wide), BF16),
            shape((8, wide), F32), shape((rows_d, 2), F32), shape((rows, 1), jnp.int32)]
    dma = pltpu.SemaphoreType.DMA
    in_vmem = pl.BlockSpec(memory_space=pltpu.VMEM)
    any_space = pl.BlockSpec(memory_space=pl.ANY)
    result = pl.pallas_call(
        functools.partial(forward_kernel, highs, shared, groups, count, length, group, DH),
        out_shape=tuple(fulls + outs),
        in_specs=[in_vmem] * count + [any_space] * 2 + [in_vmem] * 4,
        out_specs=tuple([any_space] * count + [in_vmem] * len(outs)),
        scratch_shapes=[pltpu.VMEM(dims, BF16) for dims in dims_of] + [
            pltpu.VMEM(pixels.shape, BF16), pltpu.VMEM(band_ids.shape, jnp.int32), pltpu.VMEM(fulls[0].shape, BF16),
            pltpu.VMEM(fulls[1].shape, BF16), pltpu.VMEM(fulls[2].shape, BF16), pltpu.VMEM((rows, wide), BF16),
            pltpu.VMEM((rows, wide), BF16), pltpu.VMEM((rows, wide), BF16), pltpu.VMEM((rows, wide), F32),
            pltpu.VMEM(block, F32), pltpu.VMEM((4,) + block, F32), pltpu.VMEM((highs,) + block, F32),
            dma((total,)), dma((total, highs - 1)), dma((total, highs - 1)), dma((total, 2)), dma((total, 2)),
            dma((total,)), dma((total,)), dma((count,)), dma((count,)), dma((5,)), dma((2,)), dma((2,)),
            dma((highs + 2,)), dma((highs + 2,))],
        compiler_params=pltpu.CompilerParams(collective_id=0, has_side_effects=True, vmem_limit_bytes=62 * 2**20),
        cost_estimate=pl.CostEstimate(flops=0, bytes_accessed=2**25, transcendentals=0),
    )(*masters, pixels, band_ids, kept_index, intersection, table, placed)
    weights = [full.reshape(((2,) if split else ()) + (size * dims[0], dims[1]))
               for full, split, dims in zip(result[:count], shared, dims_of)]
    return weights, result[count:]


def gather_all(shards, shared):
    order_a, order_b = orders()
    fulls = []
    for number, shard in enumerate(shards):
        full = gather_dp(shard, 0, (order_a, order_b)[number % 2])
        if shared[number]:
            other, zero = other_core(full), lax.axis_index("mp") == 0
            full = jnp.stack([jnp.where(zero, full, other), jnp.where(zero, other, full)])
        fulls.append(full)
    return fulls


def decoder_kernel(length, head_dim, x1e_ref, mine_ref, other_ref, evec_ref, kept_ref, column_ref, rows_ref,
                   table_ref, totals_ref, target_any, band_any, attn_any, mlp_any, bridge_any, predict_any,
                   gy_out, gattn_ref, gup_ref, gdown_ref, gpred_ref, gbridge_ref, loss_ref, vgrad_ref,
                   gbias_ref, sums_ref, esums_ref, final_ref, glat_ref, x_ref, x1_ref, gy_ref, qkv_ref, mixed_ref, lse_ref, part_ref, from_ref,
                   lowt_ref, gradt_ref, z_ref, gu_ref, flat_ref, mlp_ref, bridge_ref, predict_ref, target_ref,
                   band_ref, gp_ref, gpred_acc, gmix_ref, vec_ref, load_sem, stream_sem, send_sem, receive_sem):
    core, index = lax.axis_index("mp"), lax.axis_index("dp")
    sibling = (index, 1 - core)
    greet([sibling])
    images, side, half = table_ref.shape
    patches = side * side
    width = mixed_ref.shape[0]
    hidden = z_ref.shape[1]
    share = predict_ref.shape[2]
    vec_ref[...] = totals_ref[14:22, :]
    bias = jnp.concatenate([totals_ref[21:22, :], totals_ref[22:23, : 2 * share - totals_ref.shape[1]]], axis=1)
    inverse = [1.0 / jnp.sum(totals_ref[24 + level : 25 + level, :], axis=1, keepdims=True) for level in range(NB)]
    attn_ref = z_ref.at[pl.ds(0, attn_any.shape[0]), pl.ds(0, 4 * width)]

    loads = [pltpu.make_async_copy(source, target, load_sem.at[at]) for at, (source, target) in enumerate(
        ((attn_any, attn_ref), (bridge_any, bridge_ref), (mlp_any, mlp_ref), (predict_any, predict_ref)))]
    for copy in loads:
        copy.start()

    def rows_of(image):
        return pl.ds(pl.multiple_of(image * patches, patches), patches)

    def exchange(phase, image):
        rows = rows_of(image)
        return remote(part_ref.at[phase % 2, rows, :], from_ref.at[phase % 2, rows, :], send_sem.at[phase, image],
                      receive_sem.at[phase, image], sibling)

    def summed(phase, rows):
        return part_ref[phase % 2, rows, :].astype(F32) + from_ref[phase % 2, rows, :].astype(F32)

    def give(phase, image, value):
        part_ref[phase % 2, rows_of(image), :] = value.astype(BF16)
        exchange(phase, image).start()

    def stream(image):
        rows, slot = rows_of(image), lax.rem(image, 2)
        return [pltpu.make_async_copy(target_any.at[rows, :], target_ref.at[slot], stream_sem.at[0, slot]),
                pltpu.make_async_copy(band_any.at[rows, :], band_ref.at[slot], stream_sem.at[1, slot])]

    sums_ref[...] = jnp.zeros_like(sums_ref)
    loss_ref[...] = jnp.zeros_like(loss_ref)
    gbias_ref[...] = jnp.zeros_like(gbias_ref)
    gpred_acc[...] = jnp.zeros_like(gpred_acc)
    for copy in stream(0):
        copy.start()
    loads[0].wait()
    for part in range(4):
        at = pl.ds(part * width, width)
        flat_ref[at, :] = attn_ref[:, at].T
    loads[1].wait()
    ends = bridge_ref.shape[2]
    latent_ref = gy_ref

    def ends_rows(step):
        return pl.ds(pl.multiple_of(step * 128, 128), 128)

    def enc_end(step, carry):
        rows = ends_rows(step)
        out = x1e_ref[rows, :] + both(mine_ref, other_ref, rows)
        gy_out[rows, :] = out
        unit, _ = normalize(out)
        final = (unit * evec_ref[5:6, :] + evec_ref[6:7, :]).astype(BF16)
        final_ref[rows, :] = final
        latent_ref[rows, :ends] = dot_nn(final, bridge_ref[0])
        latent_ref[rows, ends:] = dot_nn(final, bridge_ref[1])
        return carry

    lax.fori_loop(0, x1e_ref.shape[0] // 128, enc_end, 0)

    def phase_a(image, carry):
        rows = rows_of(image)
        hot = lax.broadcasted_iota(jnp.int32, (patches, length), 0) == kept_ref[pl.ds(image, 1), :]
        latent = latent_ref[pl.ds(pl.multiple_of(image * length, length), length), :]
        table = table_ref[image]
        by_row = jnp.broadcast_to(table[:, None, :], (side, side, half)).reshape(patches, half)
        by_col = jnp.broadcast_to(table[None, :, :], (side, side, half)).reshape(patches, half)
        place = jnp.concatenate([by_row, by_col], axis=1)
        rows_x = dot_exact(hot.astype(F32), latent) + rows_ref[rows, 0:1] * vec_ref[0:1, :] + place
        x_ref[rows, :] = rows_x
        unit, _ = normalize(rows_x)
        low = (unit * vec_ref[1:2, :] + vec_ref[2:3, :]).astype(BF16)
        qkv_ref[:, rows] = dot_nt(flat_ref[: 3 * width, :], low).astype(BF16)
        attend(qkv_ref, mixed_ref, lse_ref, rows, width, head_dim, None)
        give(0, image, dot_nn(mixed_ref[:, rows].T, flat_ref[3 * width :, :]))
        return carry

    lax.fori_loop(0, images, phase_a, 0)
    loads[2].wait()
    loads[3].wait()

    def phase_b(image, carry):
        rows = rows_of(image)
        exchange(0, image).wait()
        after = x_ref[rows, :] + summed(0, rows)
        x1_ref[rows, :] = after
        unit, _ = normalize(after)
        low = (unit * vec_ref[3:4, :] + vec_ref[4:5, :]).astype(BF16)
        lowt_ref[:, rows] = low.T
        up = dot_nn(low, mlp_ref[:, :hidden])
        square, bent, rise = gelu_parts(up)
        mid = (up * rise).astype(BF16)
        z_ref[rows, :] = mid
        slope = rise + (0.5 * GELU_C) * up * (1.0 - bent * bent) * (1.0 + (3.0 * 0.044715) * square)
        gu_ref[rows, :] = slope.astype(BF16)
        give(1, image, dot_nt(mid, mlp_ref[:, hidden:]))
        return carry

    lax.fori_loop(0, images, phase_b, 0)

    def phase_c(image, carry):
        rows, slot = rows_of(image), lax.rem(image, 2)

        @pl.when(image + 1 < images)
        def _():
            for copy in stream(image + 1):
                copy.start()

        exchange(1, image).wait()
        unit, rstd = normalize(x1_ref[rows, :] + summed(1, rows))
        gain = vec_ref[5:6, :]
        final = (unit * gain + vec_ref[6:7, :]).astype(BF16)
        for copy in stream(image):
            copy.wait()
        predicted = jnp.concatenate([dot_nn(final, predict_ref[0]), dot_nn(final, predict_ref[1])], axis=1)
        mismatch = predicted + bias - target_ref[slot].astype(F32)
        band = band_ref[slot]
        level = jnp.where(band == 0, inverse[0], jnp.where(band == 1, inverse[1], inverse[2]))
        level = level * rows_ref[rows, 1:2]
        square = mismatch * mismatch + EPS_C
        root = lax.rsqrt(square)
        loss_ref[...] += jnp.sum(level * (square * root), axis=0, keepdims=True)
        grad = level * (mismatch * root)
        gbias_ref[...] += jnp.sum(grad, axis=0, keepdims=True)
        gp_ref[...] = grad.astype(BF16)
        columns = pl.ds(pl.multiple_of(core * share, share), share)
        gpred_acc[...] += dot_tn(final, gp_ref[:, columns])
        grad_final = dot_nt(gp_ref[:, :share], predict_ref[0]) + dot_nt(gp_ref[:, share:], predict_ref[1])
        grad_in, gain_sum, shift_sum = norm_back(grad_final, gain, unit, rstd)
        gy_ref[rows, :] = grad_in
        sums_ref[5:6, :] += gain_sum
        sums_ref[6:7, :] += shift_sum
        low = grad_in.astype(BF16)
        gradt_ref[:, rows] = low.T
        grad_up = (dot_nn(low, mlp_ref[:, hidden:]) * gu_ref[rows, :].astype(F32)).astype(BF16)
        gu_ref[rows, :] = grad_up
        give(2, image, dot_nt(grad_up, mlp_ref[:, :hidden]))
        return carry

    lax.fori_loop(0, images, phase_c, 0)
    gpred_ref[...] = gpred_acc[...].astype(BF16)
    tile = 256
    for start in range(0, hidden, tile):
        at = pl.ds(start, tile)
        gup_ref[:, at] = dot_nn(lowt_ref[...], gu_ref[:, at]).astype(BF16)
        gdown_ref[:, at] = dot_nn(gradt_ref[...], z_ref[:, at]).astype(BF16)

    def phase_d(image, carry):
        rows = rows_of(image)
        exchange(2, image).wait()
        unit, rstd = normalize(x1_ref[rows, :])
        grad_in, gain_sum, shift_sum = norm_back(summed(2, rows), vec_ref[3:4, :], unit, rstd)
        grad_in = grad_in + gy_ref[rows, :]
        gy_ref[rows, :] = grad_in
        sums_ref[3:4, :] += gain_sum
        sums_ref[4:5, :] += shift_sum
        low = grad_in.astype(BF16)
        gradt_ref[:, rows] = low.T
        gmix_ref[...] = dot_nt(flat_ref[3 * width :, :], low).astype(BF16)
        attend_back(qkv_ref, gmix_ref, lse_ref, qkv_ref, rows, width, head_dim, None)
        unit_a, _ = normalize(x_ref[rows, :])
        lowt_ref[:, rows] = (unit_a * vec_ref[1:2, :] + vec_ref[2:3, :]).astype(BF16).T
        give(3, image, dot_nn(qkv_ref[:, rows].T, flat_ref[: 3 * width, :]))
        return carry

    lax.fori_loop(0, images, phase_d, 0)
    for part in range(3):
        at = pl.ds(part * width, width)
        gattn_ref[:, at] = dot_nt(lowt_ref[...], qkv_ref[at, :]).astype(BF16)
    gattn_ref[:, 3 * width :] = dot_nt(gradt_ref[...], mixed_ref[...]).astype(BF16)

    def phase_e(image, carry):
        rows = rows_of(image)
        exchange(3, image).wait()
        unit, rstd = normalize(x_ref[rows, :])
        grad_in, gain_sum, shift_sum = norm_back(summed(3, rows), vec_ref[1:2, :], unit, rstd)
        grad_in = grad_in + gy_ref[rows, :]
        sums_ref[1:2, :] += gain_sum
        sums_ref[2:3, :] += shift_sum
        sums_ref[0:1, :] += jnp.sum(grad_in * rows_ref[rows, 0:1], axis=0, keepdims=True)
        kept_rows = pl.ds(pl.multiple_of(image * length, length), length)
        hot = lax.broadcasted_iota(jnp.int32, (length, patches), 1) == column_ref[kept_rows, :]
        glat_ref[kept_rows, :] = dot_nn(hot.astype(BF16), grad_in.astype(BF16)).astype(BF16)
        return carry

    lax.fori_loop(0, images, phase_e, 0)
    columns = pl.ds(pl.multiple_of(core * ends, ends), ends)
    gbridge_ref[...] = dot_tn(final_ref[...], glat_ref[:, columns]).astype(BF16)
    esums_ref[...] = jnp.zeros_like(esums_ref)

    def enc_start(step, carry):
        rows = ends_rows(step)
        grad_final = dot_nt(glat_ref[rows, :ends], bridge_ref[0]) + dot_nt(glat_ref[rows, ends:], bridge_ref[1])
        unit, rstd = normalize(gy_out[rows, :])
        grad_in, gain_sum, shift_sum = norm_back(grad_final, evec_ref[5:6, :], unit, rstd)
        gy_out[rows, :] = grad_in
        esums_ref[0:1, :] += gain_sum
        esums_ref[1:2, :] += shift_sum
        return carry

    lax.fori_loop(0, x1e_ref.shape[0] // 128, enc_start, 0)
    vgrad_ref[...] = jnp.zeros_like(vgrad_ref)
    vgrad_ref[5:7, :] = esums_ref[0:2, :]
    vgrad_ref[7:14, : sums_ref.shape[1]] = sums_ref[0:7, :]
    vgrad_ref[14:15, : gbias_ref.shape[1]] = gbias_ref[...]


def decoder_all(x1e, mine, other, evec, kept_index, kept_column, row_values, table, totals, target, band,
                attn, mlp, bridge, predict):
    rows_e, wide = x1e.shape
    images, length = kept_index.shape
    rows, pixel_count = target.shape
    patches = rows // images
    low_wide = mlp.shape[0]
    width, hidden, share, ends = attn.shape[1] // 4, mlp.shape[1] // 2, predict.shape[2], bridge.shape[2]
    in_vmem = pl.BlockSpec(memory_space=pltpu.VMEM)
    any_space = pl.BlockSpec(memory_space=pl.ANY)
    dma = pltpu.SemaphoreType.DMA
    vm = pltpu.VMEM
    return pl.pallas_call(
        functools.partial(decoder_kernel, length, DDH),
        out_shape=(
            shape((rows_e, wide), F32), shape((low_wide, 4 * width), BF16), shape((low_wide, hidden), BF16),
            shape((low_wide, hidden), BF16), shape((low_wide, share), BF16), shape((wide, ends), BF16),
            shape((1, pixel_count), F32), shape((16, wide), F32)),
        in_specs=[in_vmem] * 9 + [any_space] * 6,
        out_specs=tuple([in_vmem] * 8),
        scratch_shapes=[
            vm((1, pixel_count), F32), vm((8, low_wide), F32), vm((8, wide), F32),
            vm((rows_e, wide), BF16), vm((rows_e, low_wide), BF16), vm((rows, low_wide), F32),
            vm((rows, low_wide), F32), vm((rows, low_wide), F32), vm((3 * width, rows), BF16), vm((width, rows), BF16),
            vm((width // DDH, rows), F32), vm((2, rows, low_wide), BF16), vm((2, rows, low_wide), BF16),
            vm((low_wide, rows), BF16), vm((low_wide, rows), BF16), vm((rows, hidden), BF16), vm((rows, hidden), BF16),
            vm((4 * width, low_wide), BF16), vm(mlp.shape, BF16), vm(bridge.shape, BF16),
            vm(predict.shape, BF16), vm((2, patches, pixel_count), BF16), vm((2, patches, pixel_count), jnp.int32),
            vm((patches, pixel_count), BF16), vm((low_wide, share), F32), vm((width, patches), BF16),
            vm((8, low_wide), F32),
            dma((4,)), dma((2, 2)), dma((4, images)), dma((4, images))],
        compiler_params=pltpu.CompilerParams(collective_id=3, has_side_effects=True, vmem_limit_bytes=62 * 2**20),
        cost_estimate=pl.CostEstimate(flops=0, bytes_accessed=2**25, transcendentals=0),
    )(x1e, mine, other, evec, kept_index, kept_column, row_values, table, totals, target, band, attn, mlp, bridge, predict)


class Reducer:
    def __init__(self, highs, groups, weights, grads, outs, near, second, far, load_two, load_own, plane, norm, sems):
        self.highs, self.groups, self.weights = highs, groups, weights
        self.grads, self.outs = grads, outs
        self.near, self.second, self.far = near, second, far
        self.load_two, self.load_own, self.plane, self.norm = load_two, load_own, plane, norm
        self.load_sem, self.as_sem, self.ar_sem, self.bs_sem, self.br_sem, self.zs_sem, self.zr_sem = sems
        self.core, self.low, self.high, self.low_x, self.low_y = place_of()
        self.dev_x, self.dev_y = (self.high * 4 + self.low_x, self.core), (self.high * 4 + self.low_y, self.core)
        self.at_high = [(lax.rem(self.high + k, highs) * 4 + self.low, self.core) for k in range(1, highs)]
        self.pairs = (len(groups) + 1) // 2

    def in_pair(self, pair):
        return [at for at in (2 * pair, 2 * pair + 1) if 0 <= at < len(self.groups)] if 0 <= pair < self.pairs else []

    def route(self, at):
        if at % 2 == 0:
            return self.low_y, self.dev_y, self.low_x, self.dev_x
        return self.low_x, self.dev_x, self.low_y, self.dev_y

    def grad(self, at, which):
        number, start, size = self.groups[at]
        return self.grads[number].at[:, which, :, pl.ds(start, size)]

    def slot(self, ref, at, count):
        number, _, size = self.groups[at]
        return ref.at[at % count, :, pl.ds(0, self.outs[number].shape[0]), pl.ds(0, size)]

    def two_ref(self, at):
        return self.slot(self.load_two, at, 6)

    def own_ref(self, at):
        return self.slot(self.load_own, at, 8)

    def loads(self, at):
        return [pltpu.make_async_copy(self.grad(at, self.route(at)[2]), self.two_ref(at), self.load_sem.at[at, 0]),
                pltpu.make_async_copy(self.grad(at, self.low), self.own_ref(at), self.load_sem.at[at, 1])]

    def one(self, at):
        low_one, dev_one, _, _ = self.route(at)
        return [remote(self.grad(at, 3 - self.low), self.near[2 * at], self.as_sem.at[at, 0], self.ar_sem.at[at, 0], dev_one),
                remote(self.grad(at, low_one), self.near[2 * at + 1], self.as_sem.at[at, 1], self.ar_sem.at[at, 1], dev_one)]

    def two(self, at):
        return remote(self.two_ref(at), self.second[at], self.bs_sem.at[at], self.br_sem.at[at], self.route(at)[3])

    def three(self, at):
        return [remote(self.own_ref(at).at[lax.rem(self.high + k, self.highs)], self.far[at].at[k - 1],
                       self.zs_sem.at[at, k - 1], self.zr_sem.at[at, k - 1], self.at_high[k - 1])
                for k in range(1, self.highs)]

    def step(self, step):
        for at in self.in_pair(step):
            for copy in self.one(at) + self.loads(at):
                copy.start()
        for at in self.in_pair(step - 1):
            mine = self.two_ref(at)
            self.loads(at)[0].wait()
            self.one(at)[0].wait()
            mine[...] = (mine[...].astype(F32) + self.near[2 * at][...].astype(F32)).astype(BF16)
            self.two(at).start()
        for at in self.in_pair(step - 2):
            number, start, size = self.groups[at]
            mine = self.own_ref(at)
            self.loads(at)[1].wait()
            self.one(at)[1].wait()
            self.two(at).wait()
            plane = self.slot(self.plane, at, 2)
            plane[...] = (mine[...].astype(F32) + self.near[2 * at + 1][...].astype(F32)
                          + self.second[at][...].astype(F32))
            self.outs[number][:, pl.ds(start, size)] = plane[self.high]
            mine[...] = plane[...].astype(BF16)
            for copy in self.three(at):
                copy.start()
        for at in self.in_pair(step - 3):
            number, start, size = self.groups[at]
            for copy in self.three(at):
                copy.wait()
            cols = pl.ds(start, size)
            done = self.outs[number][:, cols]
            for k in range(self.highs - 1):
                done = done + self.far[at][k].astype(F32)
            self.outs[number][:, cols] = done
            self.norm[0:1, 0:1] += self.weights[number] * jnp.sum(done * done, keepdims=True)


def reducer_scratch(highs, groups, shards):
    piece = lambda lead, group: pltpu.VMEM((lead, shards[group[0]], group[2]), BF16)
    near = [piece(highs, group) for group in groups for _ in range(2)]
    second = [piece(highs, group) for group in groups]
    far = [piece(highs - 1, group) for group in groups]
    slot = (highs, max(shards), max(group[2] for group in groups))
    loads = [pltpu.VMEM((6,) + slot, BF16), pltpu.VMEM((8,) + slot, BF16), pltpu.VMEM((2,) + slot, F32)]
    dma, total = pltpu.SemaphoreType.DMA, len(groups)
    sems = [dma((total, 2)), dma((total, 2)), dma((total, 2)), dma((total,)), dma((total,)),
            dma((total, highs - 1)), dma((total, highs - 1))]
    return near + second + far + loads + sems


def make_reducer(highs, groups, weights, grads, outs, norm, refs):
    total = len(groups)
    near, second, far, refs = refs[: 2 * total], refs[2 * total : 3 * total], refs[3 * total : 4 * total], refs[4 * total :]
    return Reducer(highs, groups, weights, grads, outs, near, second, far, *refs[:3], norm, refs[3:10]), refs[10:]


def backward_kernel(highs, weights, groups, ready, count, shared, length, group, head_dim, *refs):
    given = count - 4
    gy_ref, x1_ref, vec_ref, vgrad_ref, loss_ref, lse_ref = refs[:6]
    x_any, qkv_any, mixed_any, flat_any, pixk_any, mlp_any = refs[6:12]
    refs = refs[12:]
    grads, refs = refs[:given], refs[given:]
    outs, sums_ref, vflat_ref, refs = refs[:count], refs[count], refs[count + 1], refs[count + 2 :]
    made, refs = refs[:4], refs[4:]
    grads = tuple(grads) + tuple(made)
    (x_ref, qkv_ref, mixed_ref, flat_ref, pixk_ref, wmlp_ref, low_ref, lowt_ref, grad_ref, gradt_ref, acc_ref, part_ref,
     other_ref, last_ref, gmix_ref, gqkv_ref, stage_ref, norm_ref, spots_ref, far_ref, vnear_ref, vfar_ref,
     vsum_ref) = refs[:23]
    (load_sem, wload_sem, store_sem, xs_sem, xr_sem, ns_sem, nr_sem, hs_sem, hr_sem, ts_sem, tr_sem, js_sem,
     jr_sem) = refs[23:36]
    core_at = lax.axis_index("mp")
    views = [ref.at[core_at] if split else ref for ref, split in zip(outs, shared)]
    red, _ = make_reducer(highs, groups, weights, grads, views, norm_ref, refs[36:])
    core, low, high = red.core, red.low, red.high
    spot = low * 2 + core
    sibling = (high * 4 + low, 1 - core)
    near = [(high * 4 + lax.rem(spot + k, 8) // 2, lax.rem(lax.rem(spot + k, 8), 2)) for k in range(1, 8)]
    greet(near + red.at_high)
    rows, wide = x_ref.shape
    width = mixed_ref.shape[0]
    hidden = mlp_any.shape[-1] // 2
    size = 512
    tiles = hidden // size
    mask = group_mask(group, length)

    late = [pltpu.make_async_copy(source, target, load_sem.at[at]) for at, (source, target) in enumerate(
        ((x_any, x_ref), (qkv_any, qkv_ref), (mixed_any, mixed_ref), (flat_any, flat_ref), (pixk_any, pixk_ref)))]

    def weight_loads(tile):
        return [pltpu.make_async_copy(mlp_any.at[:, :, :, pl.ds(half * hidden + tile * size, size)],
                                      wmlp_ref.at[tile % 2, half], wload_sem.at[tile % 2, half]) for half in range(2)]

    def store(slot, target, start, columns=512):
        return pltpu.make_async_copy(stage_ref.at[slot, :, :, :, pl.ds(0, columns)],
                                     target.at[:, :, :, pl.ds(start, columns)], store_sem.at[slot])

    def exchange(at, target):
        return remote(part_ref, target, xs_sem.at[at], xr_sem.at[at], sibling)

    def staged(slot, value):
        columns = value.shape[1]
        stage_ref[slot, :, :, :, :columns] = value.astype(BF16).reshape(stage_ref.shape[1:4] + (columns,))

    def mlp_first():
        unit, _ = normalize(x1_ref[...])
        value = (unit * vec_ref[3:4, :] + vec_ref[4:5, :]).astype(BF16)
        low_ref[...] = value
        lowt_ref[...] = value.T
        value = gy_ref[...].astype(BF16)
        grad_ref[...] = value
        gradt_ref[...] = value.T
        acc_ref[...] = jnp.zeros_like(acc_ref)

    def mlp_block(tile):
        for copy in weight_loads(tile):
            copy.wait()
        if tile + 1 < tiles:
            for copy in weight_loads(tile + 1):
                copy.start()
        w_up = wmlp_ref[tile % 2, 0].reshape(wide, size)
        w_down = wmlp_ref[tile % 2, 1].reshape(wide, size)
        up = dot_nn(low_ref[...], w_up)
        square, bent, half = gelu_parts(up)
        mid = (up * half).astype(BF16)
        slope = half + (0.5 * GELU_C) * up * (1.0 - bent * bent) * (1.0 + (3.0 * 0.044715) * square)
        grad_up = (dot_nn(grad_ref[...], w_down) * slope).astype(BF16)
        acc_ref[...] += dot_nt(grad_up, w_up)
        slot = 2 * (tile % 2)
        if tile >= 2:
            store(slot, made[0], (tile - 2) * size).wait()
            store(slot + 1, made[1], (tile - 2) * size).wait()
        staged(slot, dot_nn(lowt_ref[...], grad_up))
        store(slot, made[0], tile * size).start()
        staged(slot + 1, dot_nn(gradt_ref[...], mid))
        store(slot + 1, made[1], tile * size).start()

    def mlp_last():
        part_ref[...] = acc_ref[...].astype(BF16)
        exchange(0, other_ref).start()

    def stores_done(tile):
        slot = 2 * (tile % 2)
        store(slot, made[0], tile * size).wait()
        store(slot + 1, made[1], tile * size).wait()

    def rows_step(number, carry):
        at = pl.ds(pl.multiple_of(number * group, group), group)
        unit, rstd = normalize(x1_ref[at, :])
        grad_in, gain_sum, shift_sum = norm_back(both(part_ref, other_ref, at), vec_ref[3:4, :], unit, rstd)
        grad_in = grad_in + gy_ref[at, :]
        gy_ref[at, :] = grad_in
        vsum_ref[3:4, :] += gain_sum
        vsum_ref[4:5, :] += shift_sum
        low_grad = grad_in.astype(BF16)
        gradt_ref[:, at] = low_grad.T
        gmix_ref[...] = dot_nt(flat_ref[3 * width :, :], low_grad).astype(BF16)
        attend_back(qkv_ref, gmix_ref, lse_ref, gqkv_ref, at, width, head_dim, mask)
        part_ref[at, :] = dot_nn(gqkv_ref[:, at].T, flat_ref[: 3 * width, :]).astype(BF16)
        unit_a, _ = normalize(x_ref[at, :])
        lowt_ref[:, at] = (unit_a * vec_ref[1:2, :] + vec_ref[2:3, :]).astype(BF16).T
        return carry

    def attn_grads():
        for slot in range(4):
            if slot < 3:
                value = dot_nt(lowt_ref[...], gqkv_ref[pl.ds(slot * width, width), :])
            else:
                value = dot_nt(gradt_ref[...], mixed_ref[...])
            staged(slot, value)
            store(slot, made[2], slot * width, width).start()

    def enc_out():
        unit, rstd = normalize(x_ref[...])
        grad_in, gain_sum, shift_sum = norm_back(both(part_ref, last_ref, pl.ds(0, rows)), vec_ref[1:2, :], unit, rstd)
        grad_in = grad_in + gy_ref[...]
        vsum_ref[0:1, :] = jnp.sum(grad_in, axis=0, keepdims=True)
        vsum_ref[1:2, :] = gain_sum
        vsum_ref[2:3, :] = shift_sum
        share = made[3].shape[-1]
        columns = pl.ds(pl.multiple_of(core * share, share), share)
        staged(0, dot_tn(grad_in.astype(BF16), pixk_ref[:, columns]))
        store(0, made[3], 0, share).start()

    stages = functools.partial(total_blocks, vsum_ref, vnear_ref, vfar_ref, (ts_sem, tr_sem), low, high, core, highs)
    mlp_ready, attn_ready, embed_ready = ready
    row_groups = rows // group
    norm_ref[...] = jnp.zeros_like(norm_ref)
    vsum_ref[...] = vgrad_ref[...]
    for copy in weight_loads(0):
        copy.start()
    for step in range(red.pairs + 3):
        if tiles - 2 <= step - mlp_ready < tiles:
            stores_done(step - mlp_ready)
        if step == attn_ready:
            for slot in range(4):
                store(slot, made[2], slot * width, width).wait()
        if step == embed_ready:
            store(0, made[3], 0, made[3].shape[-1]).wait()
        red.step(step)
        if step == 0:
            for copy in late:
                copy.start()
            mlp_first()
        if step < tiles:
            mlp_block(step)
            if step == tiles - 1:
                mlp_last()
        if tiles <= step < attn_ready - 1:
            if step == tiles:
                for copy in late:
                    copy.wait()
                exchange(0, other_ref).wait()
            share = -(-row_groups // (attn_ready - 1 - tiles))
            start, stop = (step - tiles) * share, min((step - tiles + 1) * share, row_groups)
            if start < stop:
                lax.fori_loop(start, stop, rows_step, 0)
                if stop == row_groups:
                    exchange(1, last_ref).start()
        if step == attn_ready - 1:
            attn_grads()
        if step == embed_ready - 1:
            exchange(1, last_ref).wait()
            enc_out()
            vnear_ref[low] = vsum_ref[...]
            for copy in stages(0):
                copy.start()
        if step == embed_ready:
            for copy in stages(0):
                copy.wait()
            vsum_ref[...] = (vnear_ref[0] + vnear_ref[1]) + (vnear_ref[2] + vnear_ref[3])
            vfar_ref[high] = vsum_ref[...]
            for copy in stages(1):
                copy.start()
        if step == embed_ready + 1:
            for copy in stages(1):
                copy.wait()
            every = vfar_ref[0]
            for k in range(1, highs):
                every = every + vfar_ref[k]
            for row in range(7):
                vflat_ref[2 * row : 2 * row + 1, :] = every[row : row + 1, :512]
                vflat_ref[2 * row + 1 : 2 * row + 2, :] = every[row : row + 1, 512:]
            vflat_ref[14:22, :] = every[7:15, :512]
            vflat_ref[22:23, :] = every[14:15, 512:]
            vflat_ref[23:24, :] = jnp.zeros_like(vflat_ref[23:24, :])
            norm_ref[0:1, 0:1] += jnp.sum(every * every, keepdims=True) * (1.0 / (8 * highs))
    joins = [remote(view, view, js_sem.at[at], jr_sem.at[at], sibling)
             for at, (view, split) in enumerate(zip(views, shared)) if split]
    for copy in joins:
        copy.start()
    norm_ref[1:2, 0:1] = jnp.sum(loss_ref[...], keepdims=True)
    spots_ref[spot] = norm_ref[...]
    copies = [remote(norm_ref, spots_ref.at[spot], ns_sem.at[k], nr_sem.at[k], near[k]) for k in range(7)]
    for copy in copies:
        copy.start()
    for copy in copies:
        copy.wait()
    local = spots_ref[0]
    for k in range(1, 8):
        local = local + spots_ref[k]
    norm_ref[...] = local
    far_ref[high] = local
    copies = [remote(norm_ref, far_ref.at[high], hs_sem.at[k], hr_sem.at[k], red.at_high[k]) for k in range(highs - 1)]
    for copy in copies:
        copy.start()
    for copy in copies:
        copy.wait()
    every = far_ref[0]
    for k in range(1, highs):
        every = every + far_ref[k]
    sums_ref[...] = every
    for copy in joins:
        copy.wait()


def backward_all(gy, x1, evec, vec_grads, loss_parts, enc_saved, x0, flat, pixk, mlp, grads, shared, length, head_dim):
    size = lax.axis_size("dp")
    highs = size // 4
    qkv, mixed, lse = enc_saved
    rows, wide = x1.shape
    width = mixed.shape[0]
    hidden = mlp.shape[1] // 2
    group = 2 * length
    shard = wide // size
    lead = (highs, 4, shard)
    fresh = [lead + (hidden,), lead + (hidden,), lead + (4 * width,), lead + (pixk.shape[1] // 2,)]
    widths = [a.shape[1] for a in grads] + [dims[-1] for dims in fresh]
    shards = [a.shape[0] // size for a in grads] + [shard] * 4
    count, given = len(widths), len(grads)
    blocks = blocks_of(widths, 512)
    first = [b for b in blocks if b[0] < given]
    if len(first) % 2:
        raise ValueError("odd blocks")
    middle = [b for at in range(0, hidden, 512) for b in ((given, at, 512), (given + 1, at, 512))]
    attn = [b for b in blocks if b[0] == given + 2]
    groups = first + middle + attn + [b for b in blocks if b[0] == given + 3]
    ready = (len(first) // 2, (len(first) + len(middle)) // 2, (len(first) + len(middle) + len(attn)) // 2)
    dma = pltpu.SemaphoreType.DMA
    small, vec_block = (8, 128), vec_grads.shape
    in_vmem = pl.BlockSpec(memory_space=pltpu.VMEM)
    any_space = pl.BlockSpec(memory_space=pl.ANY)
    result = pl.pallas_call(
        functools.partial(backward_kernel, highs, (1.0,) * count, groups, ready, count, shared, length, group, head_dim),
        out_shape=tuple([shape((2, r, w) if split else (r, w), F32) for r, w, split in zip(shards, widths, shared)]
                        + [shape(small, F32), shape((24, 512), F32)]
                        + [shape(dims, BF16) for dims in fresh]),
        in_specs=[in_vmem] * 6 + [any_space] * (6 + given),
        out_specs=tuple([in_vmem] * (count + 2) + [any_space] * 4),
        scratch_shapes=[
            pltpu.VMEM((rows, wide), F32), pltpu.VMEM(qkv.shape, BF16), pltpu.VMEM(mixed.shape, BF16),
            pltpu.VMEM(flat.shape, BF16), pltpu.VMEM(pixk.shape, BF16), pltpu.VMEM((2, 2) + lead + (512,), BF16),
            pltpu.VMEM((rows, wide), BF16), pltpu.VMEM((wide, rows), BF16), pltpu.VMEM((rows, wide), BF16),
            pltpu.VMEM((wide, rows), BF16), pltpu.VMEM((rows, wide), F32), pltpu.VMEM((rows, wide), BF16),
            pltpu.VMEM((rows, wide), BF16), pltpu.VMEM((rows, wide), BF16), pltpu.VMEM((width, group), BF16),
            pltpu.VMEM((3 * width, rows), BF16), pltpu.VMEM((4,) + lead + (512,), BF16), pltpu.VMEM(small, F32),
            pltpu.VMEM((8,) + small, F32), pltpu.VMEM((highs,) + small, F32), pltpu.VMEM((4,) + vec_block, F32),
            pltpu.VMEM((highs,) + vec_block, F32), pltpu.VMEM(vec_block, F32),
            dma((5,)), dma((2, 2)), dma((4,)), dma((2,)), dma((2,)), dma((7,)), dma((7,)), dma((highs - 1,)),
            dma((highs - 1,)), dma((highs + 2,)), dma((highs + 2,)), dma((count,)), dma((count,))] + reducer_scratch(highs, groups, shards),
        compiler_params=pltpu.CompilerParams(collective_id=1, has_side_effects=True, vmem_limit_bytes=62 * 2**20),
        cost_estimate=pl.CostEstimate(flops=0, bytes_accessed=sum(a.size * 2 for a in grads), transcendentals=0),
    )(gy, x1, evec, vec_grads, loss_parts, lse, x0, qkv, mixed, flat, pixk, mlp.reshape(lead + (2 * hidden,)),
      *[a.reshape(highs, 4, r, a.shape[1]) for r, a in zip(shards, grads)])
    return list(result[:count]), result[count], result[count + 1]


def reduce_plain(grads, loss_parts, vec_grads):
    order_a, order_b = orders()
    outs = [reduce_dp(a, 0, (order_a, order_b)[number % 2], a.dtype) for number, a in enumerate(grads)]
    vec_sums = total_dp(vec_grads)
    sums = jnp.stack([sum(jnp.sum(a * a) for a in outs), jnp.sum(loss_parts)])
    sums = total_dp(sums)
    sums = sums + other_core(sums)
    return outs, sums[0] + jnp.sum(vec_sums * vec_sums), 0.5 * sums[1], vec_sums


def adam_update(master, gradient, first_old, second_old, step_rate, decay_rate):
    first_new = BETA_ONE * first_old + (1.0 - BETA_ONE) * gradient
    second_new = BETA_TWO * second_old + (1.0 - BETA_TWO) * gradient * gradient
    first_hat = first_new / (1.0 - BETA_ONE**STEP)
    second_hat = second_new / (1.0 - BETA_TWO**STEP)
    updated = master - step_rate * (
        first_hat / (jnp.sqrt(second_hat) + ADAM_EPS) + decay_rate * master
    )
    return (updated, first_new, second_new)


def adam_kernel(count, averaged, sums_ref, *refs):
    sources, refs = refs[: count + 2], refs[count + 2 :]
    masters, firsts, seconds, refs = refs[:count], refs[count : 2 * count], refs[2 * count : 3 * count], refs[3 * count :]
    means, refs = refs[:averaged], refs[averaged:]
    news, new_firsts, new_seconds, new_means = (
        refs[:count], refs[count : 2 * count], refs[2 * count : 3 * count], refs[3 * count :])
    factor = CLIP / jnp.maximum(jnp.sqrt(sums_ref[0:1, 0:1]), CLIP)

    def update(number, at, gradient):
        new, first, second = adam_update(masters[number][at], gradient * factor, firsts[number][at], seconds[number][at],
                                         RATE_MAT, DECAY_MAT)
        news[number][at] = new
        new_firsts[number][at] = first
        new_seconds[number][at] = second
        mean = {0: 0, 1: 1, 4: 2}.get(number)
        if mean is not None:
            new_means[mean][at] = EMA_KEEP * means[mean][at] + (1.0 - EMA_KEEP) * new

    enc_attn, enc_up, enc_down, dec_attn, dec_up, dec_down, embed, bridge, predict = sources
    for number, source in ((0, enc_attn), (2, dec_attn)):
        wide = source.shape[1] // 4
        for part in range(4):
            update(number, part, source[:, part * wide : (part + 1) * wide])
    for number, pair in ((1, (enc_up, enc_down)), (3, (dec_up, dec_down))):
        for part, source in enumerate(pair):
            update(number, part, source[...])
    for number, source in ((4, embed), (5, bridge), (6, predict)):
        share = source.shape[2]
        for half in range(2):
            update(number, (slice(None), pl.ds(half * share, share)), source[half])


def adam_all(sums, sources, masters, firsts, seconds, means):
    like = lambda arrays: [shape(a.shape, F32) for a in arrays]
    outs = like(masters) * 3 + like(means)
    count = len(masters)
    result = run(functools.partial(adam_kernel, count, len(means)), outs, [],
                 (sums, *sources, *masters, *firsts, *seconds, *means), 0)
    return (result[:count], result[count : 2 * count], result[2 * count : 3 * count], result[3 * count :])


def plain_step(pixels, target, band_ids, kept_index, intersection, gsd_scale, masters, enc_table, dec_table):
    enc_attn, enc_mlp, dec_attn, dec_mlp, patch_embed, bridge, predict, vectors = masters
    images, keep_count = kept_index.shape
    patch_count = intersection.shape[1]
    patch_index = jnp.arange(patch_count, dtype=jnp.int32)
    kept_flags = jnp.any(kept_index[:, :, None] == patch_index[None, None, :], axis=1).astype(F32)
    patch_weight = ((1.0 - kept_flags) * (1.0 - 0.5 * intersection.astype(F32))).reshape(-1, 1)
    hidden_rows = (1.0 - kept_flags).reshape(-1, 1)
    core = lax.axis_index("mp").astype(jnp.int32).reshape(1)
    size = lax.axis_size("dp")

    def flat(stack):
        return jnp.concatenate([part.astype(BF16) for part in stack], axis=1)

    def core_half(block):
        half = block.shape[1] // 2
        return lax.dynamic_slice_in_dim(block, lax.axis_index("mp") * half, half, 1).astype(BF16)

    vec_shard = vectors.shape[0]
    vec_room = -(-vec_shard // 1024) * 1024
    vec_rows = jnp.pad(lax.reduce_precision(vectors, 8, 7), (0, vec_room - vec_shard)).reshape(-1, 128)
    vec_full = gather_dp(vec_rows, 0, orders()[0])
    pieces = split_vectors(vec_full.reshape(size, vec_room)[:, :vec_shard].reshape(-1), D, E)
    evec = jnp.stack(pieces[:7] + [jnp.zeros_like(pieces[0])])
    dvec = jnp.stack(pieces[7:14] + [jnp.zeros_like(pieces[7])])
    kept_column = kept_index.reshape(-1, 1)
    rows, rows_d = images * keep_count, images * patch_count
    pixel_count = pixels.shape[1]
    group = 2 * keep_count
    shards = [core_half(patch_embed.T), flat(enc_attn), flat(enc_mlp), flat(dec_attn), flat(dec_mlp), core_half(bridge),
              core_half(predict)]
    weights = gather_all(shards, (True, False, False, False, False, True, True))
    embed_w, enc_attn_w, enc_mlp_w, dec_attn_w, dec_mlp_w, bridge_w, predict_w = weights
    local = enc_attn_w.shape[1] // 4
    band_weight = total_dp(jnp.stack([jnp.sum(jnp.where(band_ids == level, patch_weight, 0.0)) for level in range(NB)]))
    inverse = 1.0 / band_weight
    x0, *enc_saved, part, kept_pixels = run(
        functools.partial(enc_in_kernel, keep_count, group, DH),
        [shape((rows, D), F32), shape((3 * local, rows), BF16), shape((local, rows), BF16),
         shape((local // DH, rows), F32), shape((rows, D), BF16), shape((rows, pixel_count), BF16)],
        [pltpu.VMEM((4 * local, D), BF16)],
        (pixels, kept_column, enc_table, embed_w, evec, enc_attn_w),
        rows * D * (2 * pixel_count + 8 * local))
    x1, part = mlp_forward(x0, part, evec, enc_mlp_w)
    other = other_core(part)
    one_d, one_e = shape((1, D), F32), shape((1, E), F32)
    local_d = dec_attn_w.shape[1] // 4
    x2, final_enc, xd, *dec_saved, part = run(
        functools.partial(dec_in_kernel, keep_count, DDH),
        [shape((rows, D), F32), shape((rows, D), BF16), shape((rows_d, E), F32), shape((3 * local_d, rows_d), BF16),
         shape((local_d, rows_d), BF16), shape((local_d // DDH, rows_d), F32), shape((rows_d, E), BF16)],
        [pltpu.VMEM((4 * local_d, E), BF16), pltpu.VMEM((rows, E), F32)],
        (x1, part, other, evec, bridge_w, kept_index, hidden_rows, dec_table, dvec,
         dec_attn_w),
        rows_d * E * 8 * local_d + 2 * rows * D * E)
    xd1, part = mlp_forward(xd, part, dvec, dec_mlp_w)
    gyd, grad_predict, grad_pbias, loss_parts, grad_dec_fg, grad_dec_fb = head(
        core, inverse, xd1, part, dvec, pieces[14].reshape(1, -1), predict_w, target, band_ids, patch_weight, patch_count)
    grad_dec_up, grad_dec_down, part = mlp_backward(gyd, xd1, dvec, dec_mlp_w)
    gxd, grad_dec_attn, grad_dec_gb, grad_dec_bb, part = attn_backward(
        gyd, xd1, part, xd, dec_saved, dvec, dec_attn_w, patch_count, patch_count, DDH)
    grad_dec_ga, grad_dec_ba, grad_mask, grad_bridge, grad_enc_fg, grad_enc_fb, gye = run(
        functools.partial(between_kernel, keep_count),
        [one_e, one_e, one_e, shape((D, E // 2), BF16), one_d, one_d, shape((rows, D), F32)],
        [pltpu.VMEM((rows, E), BF16)],
        (core, gxd, xd, part, other_core(part), dvec, kept_column, hidden_rows, final_enc, x2, evec, bridge_w),
        3 * rows * D * E, 1)
    wide_row = lambda row: jnp.pad(row, ((0, 0), (0, D - row.shape[1])))
    no_row = jnp.zeros((1, D), F32)
    late_rows = [grad_enc_fg, grad_enc_fb] + [wide_row(row) for row in (
        grad_mask, grad_dec_ga, grad_dec_ba, grad_dec_gb, grad_dec_bb, grad_dec_fg, grad_dec_fb, grad_pbias)] + [no_row]
    dec_grads = [grad_predict, grad_dec_up, grad_dec_down, grad_dec_attn, grad_bridge]
    grad_enc_up, grad_enc_down, part = mlp_backward(gye, x1, evec, enc_mlp_w)
    gxe, grad_enc_attn, grad_enc_gb, grad_enc_bb, part = attn_backward(
        gye, x1, part, x0, enc_saved, evec, enc_attn_w, keep_count, group, DH)
    grad_enc_ga, grad_enc_ba, grad_ebias, grad_embed = run(
        enc_out_kernel,
        [one_d, one_d, one_d, shape((D, pixel_count // 2), BF16)],
        [], (core, gxe, x0, part, other_core(part), evec, kept_pixels), rows * D * pixel_count, 1)
    vec_grads = jnp.concatenate([grad_ebias, grad_enc_ga, grad_enc_ba, grad_enc_gb, grad_enc_bb] + late_rows)
    sums, total_squares, loss, vec_sums = reduce_plain(
        dec_grads + [grad_enc_up, grad_enc_down, grad_enc_attn, grad_embed], loss_parts, vec_grads)
    sums = [jnp.stack([jnp.where(core == 0, a, b), jnp.where(core == 0, b, a)]) if at in (0, 4, 8) else a
            for at, a in enumerate(sums) for b in ([other_core(a)] if at in (0, 4, 8) else [a])]
    return sums, total_squares, loss, vec_sums, band_weight


def per_device(
    pixels,
    target,
    band_ids,
    kept_index,
    intersection,
    gsd_scale,
    enc_attn,
    enc_mlp,
    dec_attn,
    dec_mlp,
    patch_embed,
    bridge,
    predict,
    vectors,
    first_enc_attn,
    first_enc_mlp,
    first_dec_attn,
    first_dec_mlp,
    first_patch_embed,
    first_bridge,
    first_predict,
    first_vectors,
    second_enc_attn,
    second_enc_mlp,
    second_dec_attn,
    second_dec_mlp,
    second_patch_embed,
    second_bridge,
    second_predict,
    second_vectors,
    ema_enc_attn,
    ema_enc_mlp,
    ema_patch_embed,
):
    masters = (enc_attn, enc_mlp, dec_attn, dec_mlp, patch_embed, bridge, predict, vectors)
    firsts = (
        first_enc_attn,
        first_enc_mlp,
        first_dec_attn,
        first_dec_mlp,
        first_patch_embed,
        first_bridge,
        first_predict,
        first_vectors,
    )
    seconds = (
        second_enc_attn,
        second_enc_mlp,
        second_dec_attn,
        second_dec_mlp,
        second_patch_embed,
        second_bridge,
        second_predict,
        second_vectors,
    )
    averages = (ema_enc_attn, ema_enc_mlp, ema_patch_embed)
    enc_table, dec_table = sine_table(gsd_scale, D, GRID), sine_table(gsd_scale, E, GRID)
    vec_shard = vectors.shape[0]
    vec_start = lax.axis_index("dp") * vec_shard
    if patch_embed.shape[1] % 16 == 0 and dec_attn.shape[1] % 16 == 0:
        placed = lax.dynamic_update_slice(
            jnp.zeros((24 * 512,), F32), lax.reduce_precision(vectors, 8, 7), (vec_start,)).reshape(24, 512)
        weights, results = forward_all(
            [patch_embed.T, enc_attn, enc_mlp, dec_attn, dec_mlp, bridge, predict],
            (True, False, False, False, False, True, True), pixels, band_ids, kept_index, intersection, enc_table, placed)
        embed_w, enc_attn_w, enc_mlp_w, dec_attn_w, dec_mlp_w, bridge_w, predict_w = weights
        x0, *enc_saved, kept_pixels, x1, part, other, totals, enc_flat, evec, row_values, kept_column = results
        band_weight = jnp.sum(totals[24 : 24 + NB], axis=1)
        gye, grad_dec_attn, grad_dec_up, grad_dec_down, grad_predict, grad_bridge, loss_parts, vec_grads = decoder_all(
            x1, part, other, evec, kept_index, kept_column, row_values, dec_table, totals, target, band_ids, dec_attn_w,
            dec_mlp_w, bridge_w, predict_w)
        sums, norms, vec_grad = backward_all(
            gye, x1, evec, vec_grads, loss_parts, enc_saved, x0, enc_flat, kept_pixels, enc_mlp_w,
            [grad_predict, grad_dec_up, grad_dec_down, grad_dec_attn, grad_bridge],
            (True, False, False, False, True, False, False, False, True), kept_index.shape[1], DH)
        total_squares, loss = norms[0, 0], 0.5 * norms[1, 0]
    else:
        sums, total_squares, loss, vec_sums, band_weight = plain_step(
            pixels, target, band_ids, kept_index, intersection, gsd_scale, masters, enc_table, dec_table)
        norms = jnp.broadcast_to(total_squares, (8, 128))
        vec_grad = jnp.concatenate(
            [vec_sums[:7].reshape(-1), vec_sums[7:14, :E].reshape(-1), vec_sums[14, : pixels.shape[1]]])
    vec_grad = lax.dynamic_slice_in_dim(vec_grad.reshape(-1), vec_start, vec_shard)
    grad_norm = jnp.sqrt(total_squares)
    factor = CLIP / jnp.maximum(grad_norm, CLIP)
    order = (7, 5, 6, 3, 1, 2, 8, 4, 0)
    flip = lambda arrays, at: [a.T if number == at else a for number, a in enumerate(arrays)]
    news, new_firsts, new_seconds, means = adam_all(
        norms, [sums[at] for at in order], flip(masters[:7], 4), flip(firsts[:7], 4), flip(seconds[:7], 4),
        flip(averages, 2))
    news, new_firsts, new_seconds, means = flip(news, 4), flip(new_firsts, 4), flip(new_seconds, 4), flip(means, 2)
    vec_new = adam_update(vectors, vec_grad * factor, firsts[7], seconds[7], RATE_VEC, 0.0)
    news, new_firsts, new_seconds = [
        list(many) + [one] for many, one in zip((news, new_firsts, new_seconds), vec_new)]
    ema_attn, ema_mlp, ema_embed = means
    return (
        loss,
        band_weight,
        grad_norm,
        news[0],
        news[1],
        news[2],
        news[3],
        news[4],
        news[5],
        news[6],
        news[7],
        new_firsts[0],
        new_firsts[1],
        new_firsts[2],
        new_firsts[3],
        new_firsts[4],
        new_firsts[5],
        new_firsts[6],
        new_firsts[7],
        new_seconds[0],
        new_seconds[1],
        new_seconds[2],
        new_seconds[3],
        new_seconds[4],
        new_seconds[5],
        new_seconds[6],
        new_seconds[7],
        ema_attn,
        ema_mlp,
        ema_embed,
    )


def solution(mesh):
    return jax.shard_map(
        per_device,
        mesh=mesh,
        in_specs=(
            P("dp", None),
            P("dp", None),
            P("dp", None),
            P("dp", None),
            P("dp", None),
            P("dp"),
            P(None, "dp", "mp"),
            P(None, "dp", "mp"),
            P(None, "dp", "mp"),
            P(None, "dp", "mp"),
            P(None, "dp"),
            P("dp", None),
            P("dp", None),
            P("dp"),
            P(None, "dp", "mp"),
            P(None, "dp", "mp"),
            P(None, "dp", "mp"),
            P(None, "dp", "mp"),
            P(None, "dp"),
            P("dp", None),
            P("dp", None),
            P("dp"),
            P(None, "dp", "mp"),
            P(None, "dp", "mp"),
            P(None, "dp", "mp"),
            P(None, "dp", "mp"),
            P(None, "dp"),
            P("dp", None),
            P("dp", None),
            P("dp"),
            P(None, "dp", "mp"),
            P(None, "dp", "mp"),
            P(None, "dp"),
        ),
        out_specs=(
            P(),
            P(),
            P(),
            P(None, "dp", "mp"),
            P(None, "dp", "mp"),
            P(None, "dp", "mp"),
            P(None, "dp", "mp"),
            P(None, "dp"),
            P("dp", None),
            P("dp", None),
            P("dp"),
            P(None, "dp", "mp"),
            P(None, "dp", "mp"),
            P(None, "dp", "mp"),
            P(None, "dp", "mp"),
            P(None, "dp"),
            P("dp", None),
            P("dp", None),
            P("dp"),
            P(None, "dp", "mp"),
            P(None, "dp", "mp"),
            P(None, "dp", "mp"),
            P(None, "dp", "mp"),
            P(None, "dp"),
            P("dp", None),
            P("dp", None),
            P("dp"),
            P(None, "dp", "mp"),
            P(None, "dp", "mp"),
            P(None, "dp"),
        ),
        check_vma=False,
    )
```

```python
import functools
import math

import jax
import jax.numpy as jnp
from jax import lax
from jax.experimental import pallas as pl
from jax.experimental.pallas import tpu as pltpu
from jax.sharding import PartitionSpec as P

D = 1024
DH = 64
E = 512
DDH = 32
GRID = 16
NB = 3
STEP = 10


EPS_LN = 1e-06
EPS_C = 0.01
CLIP = 0.0002
BETA_ONE = 0.9
BETA_TWO = 0.999
ADAM_EPS = 1e-12
RATE_MAT = 0.06
RATE_VEC = 0.5
DECAY_MAT = 0.05
EMA_KEEP = 0.9
REF_GSD = 4.0


def split_vectors(flat_vec, enc_width, dec_width):
    lengths = [enc_width] * 7 + [dec_width] * 7
    pieces = []
    offset = 0
    for length in lengths:
        pieces.append(flat_vec[offset : offset + length])
        offset = offset + length
    pieces.append(flat_vec[offset:])
    return pieces


F32 = jnp.float32
BF16 = jnp.bfloat16
VMEM_LIMIT = 58 * 2**20
GELU_C = math.sqrt(2.0 / math.pi)


def dot_nn(left, right):
    return jnp.dot(left, right, preferred_element_type=F32)


def dot_nt(left, right):
    return lax.dot_general(left, right, (((1,), (1,)), ((), ())), preferred_element_type=F32)


def dot_tn(left, right):
    return lax.dot_general(left, right, (((0,), (0,)), ((), ())), preferred_element_type=F32)


def dot_exact(left, right):
    return jnp.dot(left, right, preferred_element_type=F32, precision=lax.Precision.HIGHEST)


def normalize(rows):
    centred = rows - jnp.mean(rows, axis=-1, keepdims=True)
    rstd = lax.rsqrt(jnp.mean(centred * centred, axis=-1, keepdims=True) + EPS_LN)
    return centred * rstd, rstd


def norm_back(grad, gain, unit, rstd):
    scaled = grad * gain
    mean_one = jnp.mean(scaled, axis=-1, keepdims=True)
    mean_two = jnp.mean(scaled * unit, axis=-1, keepdims=True)
    grad_in = rstd * (scaled - mean_one - unit * mean_two)
    return (
        grad_in,
        jnp.sum(grad * unit, axis=0, keepdims=True),
        jnp.sum(grad, axis=0, keepdims=True),
    )


def both(mine_ref, other_ref, rows):
    return mine_ref[rows, :].astype(F32) + other_ref[rows, :].astype(F32)


def gelu_parts(up):
    square = up * up
    bent = jnp.tanh(GELU_C * up * (1.0 + 0.044715 * square))
    half = 0.5 * (1.0 + bent)
    return square, bent, half


def group_mask(group, length):
    if group == length:
        return None
    row_image = lax.broadcasted_iota(jnp.int32, (group, group), 0) // length
    col_image = lax.broadcasted_iota(jnp.int32, (group, group), 1) // length
    return row_image == col_image


def attend(qkv_ref, mixed_ref, lse_ref, cols, width, head_dim, mask):
    scale = head_dim ** (-0.5)
    for head in range(width // head_dim):
        at = pl.ds(head * head_dim, head_dim)
        queries = qkv_ref[at, cols]
        keys = qkv_ref[pl.ds(width + head * head_dim, head_dim), cols]
        values = qkv_ref[pl.ds(2 * width + head * head_dim, head_dim), cols]
        scores = dot_tn(keys, queries) * scale
        if mask is not None:
            scores = jnp.where(mask, scores, -1e30)
        top = jnp.max(scores, axis=0, keepdims=True)
        weights = jnp.exp(scores - top)
        total = jnp.sum(weights, axis=0, keepdims=True)
        lse_ref[pl.ds(head, 1), cols] = top + jnp.log(total)
        soft = (weights * (1.0 / total)).astype(BF16)
        mixed_ref[at, cols] = dot_nn(values, soft).astype(BF16)


def attend_back(qkv_ref, grad_ref, lse_ref, out_ref, cols, width, head_dim, mask):
    scale = head_dim ** (-0.5)
    for head in range(width // head_dim):
        at = pl.ds(head * head_dim, head_dim)
        at_k = pl.ds(width + head * head_dim, head_dim)
        at_v = pl.ds(2 * width + head * head_dim, head_dim)
        queries, keys, values = qkv_ref[at, cols], qkv_ref[at_k, cols], qkv_ref[at_v, cols]
        grad = grad_ref[at, :]
        scores = dot_tn(keys, queries) * scale
        if mask is not None:
            scores = jnp.where(mask, scores, -1e30)
        soft = jnp.exp(scores - lse_ref[pl.ds(head, 1), cols])
        out_ref[at_v, cols] = dot_nt(grad, soft.astype(BF16)).astype(BF16)
        grad_soft = dot_tn(values, grad)
        inner = jnp.sum(soft * grad_soft, axis=0, keepdims=True)
        grad_scores = (soft * (grad_soft - inner)).astype(BF16)
        out_ref[at, cols] = (dot_nn(keys, grad_scores) * scale).astype(BF16)
        out_ref[at_k, cols] = (dot_nt(queries, grad_scores) * scale).astype(BF16)


def transposed_weights(attn_ref, flat_ref):
    width = attn_ref.shape[1] // 4
    for part in range(4):
        at = pl.ds(part * width, width)
        flat_ref[at, :] = attn_ref[:, at].T


def attention_rows(unit, vec_ref, flat_ref, qkv_ref, mixed_ref, lse_ref, part_ref, rows, head_dim, mask, attn_ref):
    width = mixed_ref.shape[0]
    low = (unit * vec_ref[1:2, :] + vec_ref[2:3, :]).astype(BF16)
    qkv_ref[:, rows] = dot_nt(flat_ref[: 3 * width, :], low).astype(BF16)
    attend(qkv_ref, mixed_ref, lse_ref, rows, width, head_dim, mask)
    part_ref[rows, :] = dot_nt(mixed_ref[:, rows].T, attn_ref[:, 3 * width :]).astype(BF16)


def enc_in_kernel(length, group, head_dim, pix_ref, kept_ref, table_ref, embed_ref, vec_ref, attn_ref,
                  x_ref, qkv_ref, mixed_ref, lse_ref, part_ref, pixk_ref, flat_ref):
    images, patches = table_ref.shape[0], pix_ref.shape[0] // table_ref.shape[0]
    side = table_ref.shape[1]
    transposed_weights(attn_ref, flat_ref)

    def pick(image, carry):
        rows = pl.ds(image * length, length)
        index = kept_ref[rows, :]
        hot = lax.broadcasted_iota(jnp.int32, (length, patches), 1) == index
        pixels = pix_ref[pl.ds(image * patches, patches), :]
        pixk_ref[rows, :] = dot_nn(hot.astype(BF16), pixels).astype(BF16)
        grid_at = lax.broadcasted_iota(jnp.int32, (length, side), 1)
        table = table_ref[image]
        half = table.shape[1]
        x_ref[rows, :half] = dot_exact((grid_at == index // side).astype(F32), table)
        x_ref[rows, half:] = dot_exact((grid_at == index % side).astype(F32), table)
        return carry

    lax.fori_loop(0, images, pick, 0)
    mask = group_mask(group, length)

    def step(number, carry):
        rows = pl.ds(pl.multiple_of(number * group, group), group)
        share = embed_ref.shape[2]
        rows_x = dot_nt(pixk_ref[rows, :share], embed_ref[0]) + dot_nt(pixk_ref[rows, share:], embed_ref[1])
        rows_x = rows_x + vec_ref[0:1, :] + x_ref[rows, :]
        x_ref[rows, :] = rows_x
        unit, _ = normalize(rows_x)
        attention_rows(unit, vec_ref, flat_ref, qkv_ref, mixed_ref, lse_ref, part_ref, rows, head_dim, mask, attn_ref)
        return carry

    lax.fori_loop(0, x_ref.shape[0] // group, step, 0)


def dec_in_kernel(length, head_dim, x1_ref, mine_ref, other_ref, evec_ref, bridge_ref, kept_ref, hidden_ref,
                  table_ref, vec_ref, attn_ref,
                  x2_ref, final_ref, x_ref, qkv_ref, mixed_ref, lse_ref, part_ref, flat_ref, latent_ref):
    images, side, half = table_ref.shape
    patches = side * side
    transposed_weights(attn_ref, flat_ref)
    every = pl.ds(0, x1_ref.shape[0])
    out = x1_ref[...] + both(mine_ref, other_ref, every)
    x2_ref[...] = out
    unit, _ = normalize(out)
    final = (unit * evec_ref[5:6, :] + evec_ref[6:7, :]).astype(BF16)
    final_ref[...] = final
    share = bridge_ref.shape[2]
    latent_ref[:, :share] = dot_nn(final, bridge_ref[0])
    latent_ref[:, share:] = dot_nn(final, bridge_ref[1])

    def step(image, carry):
        rows = pl.ds(pl.multiple_of(image * patches, patches), patches)
        hot = lax.broadcasted_iota(jnp.int32, (patches, length), 0) == kept_ref[pl.ds(image, 1), :]
        latent = latent_ref[pl.ds(image * length, length), :]
        table = table_ref[image]
        by_row = jnp.broadcast_to(table[:, None, :], (side, side, half)).reshape(patches, half)
        by_col = jnp.broadcast_to(table[None, :, :], (side, side, half)).reshape(patches, half)
        place = jnp.concatenate([by_row, by_col], axis=1)
        rows_x = dot_exact(hot.astype(F32), latent) + hidden_ref[rows, :] * vec_ref[0:1, :] + place
        x_ref[rows, :] = rows_x
        unit, _ = normalize(rows_x)
        attention_rows(unit, vec_ref, flat_ref, qkv_ref, mixed_ref, lse_ref, part_ref, rows, head_dim, None, attn_ref)
        return carry

    lax.fori_loop(0, images, step, 0)


def mlp_kernel(tile, x_ref, mine_ref, other_ref, vec_ref, up_ref, down_ref, x1_ref, part_ref, low_ref, acc_ref):
    number = pl.program_id(0)
    count = x_ref.shape[0] // tile

    def first(step, carry):
        rows = pl.ds(pl.multiple_of(step * tile, tile), tile)
        after = x_ref[rows, :] + both(mine_ref, other_ref, rows)
        x1_ref[rows, :] = after
        unit, _ = normalize(after)
        low_ref[rows, :] = (unit * vec_ref[3:4, :] + vec_ref[4:5, :]).astype(BF16)
        return carry

    @pl.when(number == 0)
    def _():
        lax.fori_loop(0, count, first, 0)
        acc_ref[...] = jnp.zeros_like(acc_ref)

    def step(piece, carry):
        rows = pl.ds(pl.multiple_of(piece * tile, tile), tile)
        up = dot_nn(low_ref[rows, :], up_ref[...])
        _, _, half = gelu_parts(up)
        acc_ref[rows, :] += dot_nt((up * half).astype(BF16), down_ref[...])
        return carry

    lax.fori_loop(0, count, step, 0)

    @pl.when(number == pl.num_programs(0) - 1)
    def _():
        part_ref[...] = acc_ref[...].astype(BF16)


def head_kernel(core_ref, inverse_ref, x1_ref, mine_ref, other_ref, vec_ref, bias_ref, predict_ref, target_ref,
                band_ref, weight_ref, gy_ref, glow_ref, gbias_ref, loss_ref, gain_ref, shift_ref, low_ref, gpred_ref):
    number = pl.program_id(0)

    @pl.when(number == 0)
    def _():
        for ref in (gpred_ref, gbias_ref, loss_ref, gain_ref, shift_ref):
            ref[...] = jnp.zeros_like(ref)

    every = pl.ds(0, x1_ref.shape[0])
    unit, rstd = normalize(x1_ref[...] + both(mine_ref, other_ref, every))
    gain = vec_ref[5:6, :]
    final = (unit * gain + vec_ref[6:7, :]).astype(BF16)
    share = gpred_ref.shape[1]
    predicted = jnp.concatenate([dot_nn(final, predict_ref[0]), dot_nn(final, predict_ref[1])], axis=1)
    mismatch = predicted + bias_ref[...] - target_ref[...].astype(F32)
    band = band_ref[...]
    level = jnp.where(band == 0, inverse_ref[0], jnp.where(band == 1, inverse_ref[1], inverse_ref[2]))
    level = level * weight_ref[...]
    square = mismatch * mismatch + EPS_C
    root = lax.rsqrt(square)
    loss_ref[...] += jnp.sum(level * (square * root), axis=0, keepdims=True)
    grad = level * (mismatch * root)
    gbias_ref[...] += jnp.sum(grad, axis=0, keepdims=True)
    low_ref[...] = grad.astype(BF16)
    columns = pl.ds(pl.multiple_of(core_ref[0] * share, share), share)
    gpred_ref[...] += dot_tn(final, low_ref[:, columns])
    grad_final = dot_nt(low_ref[:, :share], predict_ref[0]) + dot_nt(low_ref[:, share:], predict_ref[1])
    grad_in, gain_sum, shift_sum = norm_back(grad_final, gain, unit, rstd)
    gy_ref[...] = grad_in
    gain_ref[...] += gain_sum
    shift_ref[...] += shift_sum

    @pl.when(number == pl.num_programs(0) - 1)
    def _():
        glow_ref[...] = gpred_ref[...].astype(BF16)


def mlp_back_kernel(tile, gy_ref, x1_ref, vec_ref, up_ref, down_ref, gup_ref, gdown_ref, part_ref,
                    low_ref, lowt_ref, grad_ref, gradt_ref, gu_ref, z_ref, acc_ref):
    number = pl.program_id(0)
    count = x1_ref.shape[0] // tile

    def first(step, carry):
        rows = pl.ds(pl.multiple_of(step * tile, tile), tile)
        unit, _ = normalize(x1_ref[rows, :])
        low = (unit * vec_ref[3:4, :] + vec_ref[4:5, :]).astype(BF16)
        low_ref[rows, :] = low
        lowt_ref[:, rows] = low.T
        grad = gy_ref[rows, :].astype(BF16)
        grad_ref[rows, :] = grad
        gradt_ref[:, rows] = grad.T
        return carry

    @pl.when(number == 0)
    def _():
        lax.fori_loop(0, count, first, 0)
        acc_ref[...] = jnp.zeros_like(acc_ref)

    def step(piece, carry):
        rows = pl.ds(pl.multiple_of(piece * tile, tile), tile)
        up = dot_nn(low_ref[rows, :], up_ref[...])
        square, bent, half = gelu_parts(up)
        z_ref[rows, :] = (up * half).astype(BF16)
        slope = half + (0.5 * GELU_C) * up * (1.0 - bent * bent) * (1.0 + (3.0 * 0.044715) * square)
        grad_up = (dot_nn(grad_ref[rows, :], down_ref[...]) * slope).astype(BF16)
        gu_ref[rows, :] = grad_up
        acc_ref[rows, :] += dot_nt(grad_up, up_ref[...])
        return carry

    lax.fori_loop(0, count, step, 0)
    gup_ref[...] = dot_nn(lowt_ref[...], gu_ref[...]).astype(BF16)
    gdown_ref[...] = dot_nn(gradt_ref[...], z_ref[...]).astype(BF16)

    @pl.when(number == pl.num_programs(0) - 1)
    def _():
        part_ref[...] = acc_ref[...].astype(BF16)


def attn_back_kernel(length, group, head_dim, gy_ref, x1_ref, mine_ref, other_ref, x_ref, qkv_ref, mixed_ref, lse_ref,
                     vec_ref, attn_ref, gx_ref, grad_ref, gain_ref, shift_ref, part_ref,
                     flat_ref, lowt_ref, gradt_ref, gmix_ref, gqkv_ref):
    width = mixed_ref.shape[0]
    transposed_weights(attn_ref, flat_ref)
    gain_ref[...] = jnp.zeros_like(gain_ref)
    shift_ref[...] = jnp.zeros_like(shift_ref)
    mask = group_mask(group, length)

    def step(number, carry):
        rows = pl.ds(pl.multiple_of(number * group, group), group)
        unit, rstd = normalize(x1_ref[rows, :])
        grad_in, gain_sum, shift_sum = norm_back(both(mine_ref, other_ref, rows), vec_ref[3:4, :], unit, rstd)
        grad_in = grad_in + gy_ref[rows, :]
        gx_ref[rows, :] = grad_in
        gain_ref[...] += gain_sum
        shift_ref[...] += shift_sum
        low_grad = grad_in.astype(BF16)
        gradt_ref[:, rows] = low_grad.T
        gmix_ref[...] = dot_nt(flat_ref[3 * width :, :], low_grad).astype(BF16)
        attend_back(qkv_ref, gmix_ref, lse_ref, gqkv_ref, rows, width, head_dim, mask)
        part_ref[rows, :] = dot_nn(gqkv_ref[:, rows].T, flat_ref[: 3 * width, :]).astype(BF16)
        unit_a, _ = normalize(x_ref[rows, :])
        lowt_ref[:, rows] = (unit_a * vec_ref[1:2, :] + vec_ref[2:3, :]).astype(BF16).T
        return carry

    lax.fori_loop(0, x_ref.shape[0] // group, step, 0)
    grad_ref[:, : 3 * width] = dot_nt(lowt_ref[...], gqkv_ref[...]).astype(BF16)
    grad_ref[:, 3 * width :] = dot_nt(gradt_ref[...], mixed_ref[...]).astype(BF16)


def between_kernel(length, core_ref, gx_ref, x_ref, mine_ref, other_ref, vec_ref, kept_ref, hidden_ref, final_ref, x2_ref,
                   evec_ref, bridge_ref, gain_ref, shift_ref, mask_ref, gbridge_ref, egain_ref, eshift_ref, gy_ref,
                   latent_ref):
    images = kept_ref.shape[0] // length
    patches = x_ref.shape[0] // images
    for ref in (gain_ref, shift_ref, mask_ref):
        ref[...] = jnp.zeros_like(ref)

    def step(image, carry):
        rows = pl.ds(pl.multiple_of(image * patches, patches), patches)
        unit, rstd = normalize(x_ref[rows, :])
        grad_in, gain_sum, shift_sum = norm_back(both(mine_ref, other_ref, rows), vec_ref[1:2, :], unit, rstd)
        grad_in = grad_in + gx_ref[rows, :]
        gain_ref[...] += gain_sum
        shift_ref[...] += shift_sum
        mask_ref[...] += jnp.sum(grad_in * hidden_ref[rows, :], axis=0, keepdims=True)
        kept_rows = pl.ds(pl.multiple_of(image * length, length), length)
        hot = lax.broadcasted_iota(jnp.int32, (length, patches), 1) == kept_ref[kept_rows, :]
        latent_ref[kept_rows, :] = dot_nn(hot.astype(BF16), grad_in.astype(BF16)).astype(BF16)
        return carry

    lax.fori_loop(0, images, step, 0)
    share = gbridge_ref.shape[1]
    columns = pl.ds(pl.multiple_of(core_ref[0] * share, share), share)
    gbridge_ref[...] = dot_tn(final_ref[...], latent_ref[:, columns]).astype(BF16)
    grad_final = dot_nt(latent_ref[:, :share], bridge_ref[0]) + dot_nt(latent_ref[:, share:], bridge_ref[1])
    unit, rstd = normalize(x2_ref[...])
    gy_ref[...], egain_ref[...], eshift_ref[...] = norm_back(grad_final, evec_ref[5:6, :], unit, rstd)


def enc_out_kernel(core_ref, gx_ref, x_ref, mine_ref, other_ref, vec_ref, pixk_ref,
                   gain_ref, shift_ref, ebias_ref, gembed_ref):
    every = pl.ds(0, x_ref.shape[0])
    unit, rstd = normalize(x_ref[...])
    grad_in, gain_ref[...], shift_ref[...] = norm_back(both(mine_ref, other_ref, every), vec_ref[1:2, :], unit, rstd)
    grad_in = grad_in + gx_ref[...]
    ebias_ref[...] = jnp.sum(grad_in, axis=0, keepdims=True)
    share = gembed_ref.shape[1]
    columns = pl.ds(pl.multiple_of(core_ref[0] * share, share), share)
    gembed_ref[...] = dot_tn(grad_in.astype(BF16), pixk_ref[:, columns]).astype(BF16)


def shape(dims, dtype):
    return jax.ShapeDtypeStruct(dims, dtype)


def run(kernel, outs, scratch, args, flops, scalars=0):
    moved = sum(math.prod(a.shape) * a.dtype.itemsize for a in list(args) + list(outs))
    in_vmem = pl.BlockSpec(memory_space=pltpu.VMEM)
    return pl.pallas_call(
        kernel,
        out_shape=tuple(outs),
        in_specs=[pl.BlockSpec(memory_space=pltpu.SMEM)] * scalars + [in_vmem] * (len(args) - scalars),
        out_specs=tuple([in_vmem] * len(outs)),
        scratch_shapes=scratch,
        compiler_params=pltpu.CompilerParams(vmem_limit_bytes=VMEM_LIMIT),
        cost_estimate=pl.CostEstimate(flops=flops, bytes_accessed=moved, transcendentals=0),
    )(*args)


def other_core(block):
    return lax.ppermute(block, "mp", [(0, 1), (1, 0)])


def mlp_forward(x, mine, vec, stack):
    rows, width = x.shape
    hidden = stack.shape[1] // 2
    block = min(hidden, 512)
    tile = min(rows, 512)
    other = other_core(mine)
    whole = pl.BlockSpec((rows, width), lambda i: (0, 0))
    cols = pl.BlockSpec((width, block), lambda i: (0, i))
    later = pl.BlockSpec((width, block), lambda i: (0, i + hidden // block))
    return pl.pallas_call(
        functools.partial(mlp_kernel, tile),
        out_shape=(shape((rows, width), F32), shape((rows, width), BF16)),
        grid=(hidden // block,),
        in_specs=[whole] * 3 + [pl.BlockSpec((8, width), lambda i: (0, 0)), cols, later],
        out_specs=(whole, whole),
        scratch_shapes=[pltpu.VMEM((rows, width), BF16), pltpu.VMEM((rows, width), F32)],
        compiler_params=pltpu.CompilerParams(vmem_limit_bytes=VMEM_LIMIT),
        cost_estimate=pl.CostEstimate(flops=4 * rows * width * hidden, bytes_accessed=rows * width * 14 + width * hidden * 4,
                                      transcendentals=rows * hidden),
    )(x, mine, other, vec, stack, stack)


def mlp_backward(gy, x1, vec, stack):
    rows, width = x1.shape
    hidden = stack.shape[1] // 2
    block = min(hidden, 512)
    tile = min(rows, 256)
    whole = pl.BlockSpec((rows, width), lambda i: (0, 0))
    cols = pl.BlockSpec((width, block), lambda i: (0, i))
    later = pl.BlockSpec((width, block), lambda i: (0, i + hidden // block))
    return pl.pallas_call(
        functools.partial(mlp_back_kernel, tile),
        out_shape=(shape((width, hidden), BF16), shape((width, hidden), BF16), shape((rows, width), BF16)),
        grid=(hidden // block,),
        in_specs=[whole] * 2 + [pl.BlockSpec((8, width), lambda i: (0, 0)), cols, later],
        out_specs=(cols, cols, whole),
        scratch_shapes=[
            pltpu.VMEM((rows, width), BF16), pltpu.VMEM((width, rows), BF16),
            pltpu.VMEM((rows, width), BF16), pltpu.VMEM((width, rows), BF16),
            pltpu.VMEM((rows, block), BF16), pltpu.VMEM((rows, block), BF16),
            pltpu.VMEM((rows, width), F32)],
        compiler_params=pltpu.CompilerParams(vmem_limit_bytes=VMEM_LIMIT),
        cost_estimate=pl.CostEstimate(flops=10 * rows * width * hidden, bytes_accessed=rows * width * 10 + width * hidden * 8,
                                      transcendentals=rows * hidden),
    )(gy, x1, vec, stack, stack)


def head(core, inverse, x1, mine, vec, bias, predict, target, band, weight, patches):
    rows, width = x1.shape
    pixels = target.shape[1]
    share = pixels // 2
    other = other_core(mine)
    smem = pl.BlockSpec(memory_space=pltpu.SMEM)
    row_w = pl.BlockSpec((patches, width), lambda i: (i, 0))
    row_p = pl.BlockSpec((patches, pixels), lambda i: (i, 0))
    fix = lambda a, b: pl.BlockSpec((a, b), lambda i: (0, 0))
    return pl.pallas_call(
        head_kernel,
        out_shape=(shape((rows, width), F32), shape((width, share), BF16), shape((1, pixels), F32),
                   shape((1, pixels), F32), shape((1, width), F32), shape((1, width), F32)),
        grid=(rows // patches,),
        in_specs=[smem, smem, row_w, row_w, row_w, fix(8, width), fix(1, pixels), pl.BlockSpec((2, width, share), lambda i: (0, 0, 0)), row_p, row_p,
                  pl.BlockSpec((patches, 1), lambda i: (i, 0))],
        out_specs=(row_w, fix(width, share), fix(1, pixels), fix(1, pixels), fix(1, width), fix(1, width)),
        scratch_shapes=[pltpu.VMEM((patches, pixels), BF16), pltpu.VMEM((width, share), F32)],
        compiler_params=pltpu.CompilerParams(vmem_limit_bytes=VMEM_LIMIT),
        cost_estimate=pl.CostEstimate(flops=5 * rows * width * pixels, bytes_accessed=rows * (width * 12 + pixels * 6),
                                      transcendentals=rows * pixels),
    )(core, inverse, x1, mine, other, vec, bias, predict, target, band, weight)


def attn_backward(gy, x1, mine, x, saved, vec, attn, length, group, head_dim):
    qkv, mixed, lse = saved
    rows, width = x.shape
    local = mixed.shape[0]
    return run(
        functools.partial(attn_back_kernel, length, group, head_dim),
        [shape((rows, width), F32), shape((width, 4 * local), BF16),
         shape((1, width), F32), shape((1, width), F32), shape((rows, width), BF16)],
        [pltpu.VMEM((4 * local, width), BF16), pltpu.VMEM((width, rows), BF16), pltpu.VMEM((width, rows), BF16),
         pltpu.VMEM((local, group), BF16), pltpu.VMEM((3 * local, rows), BF16)],
        (gy, x1, mine, other_core(mine), x, qkv, mixed, lse, vec, attn),
        18 * rows * width * local)


def sine_table(gsd_values, feature_width, grid_side):
    quarter = feature_width // 4
    frequency = jnp.exp(-jnp.log(10000.0) * jnp.arange(quarter).astype(F32) / quarter)
    gsd_ratio = gsd_values.astype(F32)[:, None, None] / REF_GSD
    line = jnp.arange(grid_side, dtype=jnp.int32).astype(F32)
    arg = line[None, :, None] * gsd_ratio * frequency
    return jnp.concatenate([jnp.sin(arg), jnp.cos(arg)], axis=-1)


def dp_bits():
    return lax.axis_size("dp").bit_length() - 1


def orders():
    bits = dp_bits()
    high = list(range(bits - 1, 1, -1))
    return (high + [0, 1], high + [1, 0])


def swap(block, bit):
    size = lax.axis_size("dp")
    return lax.ppermute(block, "dp", [(i, i ^ (1 << bit)) for i in range(size)])


def my_bit(bit):
    return (lax.axis_index("dp") >> bit) & 1


def gather_dp(block, axis, order):
    lead, rest = (block.shape[:axis], block.shape[axis:])
    done = []
    cur = block
    for bit in order:
        other = swap(cur, bit)
        mine = my_bit(bit) == 1
        place = axis + sum(1 for b in done if b > bit)
        cur = jnp.stack([jnp.where(mine, other, cur), jnp.where(mine, cur, other)], axis=place)
        done.append(bit)
    return cur.reshape(lead + (rest[0] * lax.axis_size("dp"),) + rest[1:])


def reduce_dp(block, axis, order, wire):
    bits = dp_bits()
    lead, rest = (block.shape[:axis], block.shape[axis:])
    shard = rest[0] // lax.axis_size("dp")
    cur = block.reshape(lead + (2,) * bits + (shard,) + rest[1:])
    left = list(range(bits - 1, -1, -1))
    for bit in reversed(order):
        place = axis + left.index(bit)
        mine = my_bit(bit)
        keep = lax.dynamic_index_in_dim(cur, mine, place, keepdims=False)
        give = lax.dynamic_index_in_dim(cur, 1 - mine, place, keepdims=False)
        other = swap(give.astype(wire), bit)
        cur = keep.astype(F32) + other.astype(F32)
        left.remove(bit)
    return cur


def join_cores(mine, core):
    other = other_core(mine)
    return jnp.concatenate([jnp.where(core == 0, mine, other), jnp.where(core == 0, other, mine)], axis=1)


def total_dp(value):
    for bit in range(dp_bits()):
        value = value + swap(value, bit)
    return value


def place_of():
    index = lax.axis_index("dp")
    core = lax.axis_index("mp")
    low, high = lax.rem(index, 4), index // 4
    bit_x, bit_y = lax.rem(low, 2), low // 2
    low_x, low_y = low + 1 - 2 * bit_x, low + 2 - 4 * bit_y
    return core, low, high, low_x, low_y


def greet(partners):
    barrier = pltpu.get_barrier_semaphore()
    for partner in partners:
        pl.semaphore_signal(barrier, inc=1, device_id=partner, device_id_type=pl.DeviceIdType.MESH)
    pl.semaphore_wait(barrier, len(partners))


def blocks_of(widths, limit):
    found = []
    for number, width in enumerate(widths):
        start = 0
        while start < width:
            size = min(limit, width - start)
            found.append((number, start, size))
            start += size
    return found


def remote(source, target, send, receive, device):
    return pltpu.make_async_remote_copy(
        src_ref=source, dst_ref=target, send_sem=send, recv_sem=receive,
        device_id=device, device_id_type=pl.DeviceIdType.MESH)


def total_blocks(block_ref, near_ref, far_ref, sems, low, high, core, highs, stage):
    send, receive = sems
    if stage == 0:
        spots = [(high * 4 + lax.rem(low + k, 4), core) for k in range(1, 4)]
        return [remote(block_ref, near_ref.at[low], send.at[k], receive.at[k], spots[k]) for k in range(3)]
    spots = [(lax.rem(high + k, highs) * 4 + low, core) for k in range(1, highs)]
    return [remote(block_ref, far_ref.at[high], send.at[3 + k], receive.at[3 + k], spots[k]) for k in range(highs - 1)]


def forward_kernel(highs, shared, groups, count, length, group, head_dim, *refs):
    masters, refs = refs[:count], refs[count:]
    pix_any, band_ref, kept_ref, inter_ref, table_ref, placed_ref = refs[:6]
    fulls, refs = refs[6 : 6 + count], refs[6 + count :]
    (x_ref, qkv_ref, mixed_ref, lse_ref, pixk_ref, x1_ref, last_ref, far_out_ref, counts_ref, flat_ref, vec_ref, rows_ref,
     column_ref) = refs[:13]
    refs = refs[13:]
    shards, refs = refs[:count], refs[count:]
    (pix_ref, bands_v, embed_v, attn_v, mlp_v, part_ref, other_ref, low_ref, acc_ref, block_ref, near_ref,
     far_ref) = refs[:12]
    (own_sem, zs_sem, zr_sem, cs_sem, cr_sem, fs_sem, fr_sem, ms_sem, mr_sem, load_sem, xs_sem, xr_sem, ts_sem,
     tr_sem, mload_sem) = refs[12:]
    core, low, high, low_x, low_y = place_of()
    at_x, at_y = (high * 4 + low_x, core), (high * 4 + low_y, core)
    at_high = [(lax.rem(high + k, highs) * 4 + low, core) for k in range(1, highs)]
    sibling = (high * 4 + low, 1 - core)
    near = [(high * 4 + lax.rem(low + k, 4), core) for k in range(1, 4)]
    greet([sibling] + near + at_high)
    for master, shard, split in zip(masters, shards, shared):
        if len(master.shape) == 3:
            wide = master.shape[2]
            for part in range(master.shape[0]):
                shard[:, part * wide : (part + 1) * wide] = master[part].astype(BF16)
        else:
            share = shard.shape[1]
            shard[...] = master[:, pl.ds(pl.multiple_of(core * share, share), share)].astype(BF16)

    def full(at):
        number, start, size = groups[at]
        ref = fulls[number].at[core] if shared[number] else fulls[number]
        return ref, pl.ds(start, size)

    def first(at):
        ref, cols = full(at)
        shard = shards[groups[at][0]].at[:, cols]
        mine = ref.at[high, low, :, cols]
        copies = [pltpu.make_async_copy(shard, mine, own_sem.at[at])]
        for k in range(1, highs):
            copies.append(remote(shard, mine, zs_sem.at[at, k - 1], zr_sem.at[at, k - 1], at_high[k - 1]))
        return copies

    def column(at):
        ref, cols = full(at)
        part = ref.at[:, low, :, cols]
        return [remote(part, part, cs_sem.at[at, 0], cr_sem.at[at, 0], at_x),
                remote(part, part, cs_sem.at[at, 1], cr_sem.at[at, 1], at_y)]

    def forward(at):
        ref, cols = full(at)
        which, device = (low_x, at_y) if at % 2 == 0 else (low_y, at_x)
        part = ref.at[:, which, :, cols]
        return remote(part, part, fs_sem.at[at], fr_sem.at[at], device)

    def swap(number):
        part = fulls[number].at[core]
        return remote(part, part, ms_sem.at[number], mr_sem.at[number], sibling)

    def exchange(at, source, target):
        return remote(source, target, xs_sem.at[at], xr_sem.at[at], sibling)

    total = len(groups)
    pairs = (total + 1) // 2
    in_pair = lambda pair: [at for at in (2 * pair, 2 * pair + 1) if at < total]
    pair_of = lambda number: max(at for at in range(total) if groups[at][0] == number) // 2
    images, side = table_ref.shape[0], table_ref.shape[1]
    patches = side * side
    width = mixed_ref.shape[0]
    mask = group_mask(group, length)

    def lane_of(image, flipped):
        lanes = lax.broadcasted_iota(jnp.int32, flipped.shape, 1)
        return jnp.sum(jnp.where(lanes == image, flipped, 0.0), axis=1, keepdims=True)

    def pick(image, carry):
        rows = pl.ds(pl.multiple_of(image * length, length), length)
        index = lane_of(image, kept_ref[...].astype(F32).T).astype(jnp.int32)
        column_ref[rows, :] = index
        hot = lax.broadcasted_iota(jnp.int32, (length, patches), 1) == index
        pixels = pix_ref[pl.ds(pl.multiple_of(image * patches, patches), patches), :]
        pixk_ref[rows, :] = dot_nn(hot.astype(BF16), pixels).astype(BF16)
        grid_at = lax.broadcasted_iota(jnp.int32, (length, side), 1)
        table = table_ref[image]
        half = table.shape[1]
        x_ref[rows, :half] = dot_exact((grid_at == index // side).astype(F32), table)
        x_ref[rows, half:] = dot_exact((grid_at == index % side).astype(F32), table)
        return carry

    def tally(image, carry):
        rows = pl.ds(pl.multiple_of(image * patches, patches), patches)
        hot = lax.broadcasted_iota(jnp.int32, (patches, length), 0) == kept_ref[pl.ds(image, 1), :]
        hidden = 1.0 - jnp.max(jnp.where(hot, 1.0, 0.0), axis=1, keepdims=True)
        weight = hidden * (1.0 - 0.5 * lane_of(image, inter_ref[...].astype(F32).T))
        rows_ref[rows, 0:1] = hidden
        rows_ref[rows, 1:2] = weight
        band = bands_v[rows, :]
        for level in range(NB):
            row = jnp.sum(jnp.where(band == level, weight, 0.0), axis=0, keepdims=True)
            for start in range(0, row.shape[1], 128):
                block_ref[24 + level : 25 + level, 0:128] += row[:, start : start + 128]
        return carry

    def rows_step(number, carry):
        rows = pl.ds(pl.multiple_of(number * group, group), group)
        share = embed_v.shape[-1]
        embed = lambda half: embed_v[half].reshape(-1, share)
        rows_x = dot_nt(pixk_ref[rows, :share], embed(0)) + dot_nt(pixk_ref[rows, share:], embed(1))
        rows_x = rows_x + vec_ref[0:1, :] + x_ref[rows, :]
        x_ref[rows, :] = rows_x
        unit, _ = normalize(rows_x)
        low_a = (unit * vec_ref[1:2, :] + vec_ref[2:3, :]).astype(BF16)
        qkv_ref[:, rows] = dot_nt(flat_ref[: 3 * width, :], low_a).astype(BF16)
        attend(qkv_ref, mixed_ref, lse_ref, rows, width, head_dim, mask)
        part_ref[rows, :] = dot_nn(mixed_ref[:, rows].T, flat_ref[3 * width :, :]).astype(BF16)
        return carry

    def mlp_first():
        after = x_ref[...] + both(part_ref, other_ref, pl.ds(0, x_ref.shape[0]))
        x1_ref[...] = after
        unit, _ = normalize(after)
        low_ref[...] = (unit * vec_ref[3:4, :] + vec_ref[4:5, :]).astype(BF16)
        acc_ref[...] = jnp.zeros_like(acc_ref)

    def mlp_block(piece, carry):
        size = 512
        hidden = mlp_v.shape[-1] // 2
        start = piece * size
        wide = x_ref.shape[1]
        up = dot_nn(low_ref[...], mlp_v[:, :, :, pl.ds(start, size)].reshape(wide, size))
        _, _, half = gelu_parts(up)
        down = mlp_v[:, :, :, pl.ds(hidden + start, size)].reshape(wide, size)
        acc_ref[...] += dot_nt((up * half).astype(BF16), down)
        return carry

    load_bands = pltpu.make_async_copy(band_ref, bands_v, load_sem.at[0])
    load_pixels = pltpu.make_async_copy(pix_any, pix_ref, load_sem.at[4])
    load_attn = pltpu.make_async_copy(fulls[1], attn_v, load_sem.at[1])
    load_embed = pltpu.make_async_copy(fulls[0], embed_v, load_sem.at[2])

    def load_mlp(at):
        cols = pl.ds(groups[at][1], groups[at][2])
        return pltpu.make_async_copy(fulls[2].at[:, :, :, cols], mlp_v.at[:, :, :, cols], mload_sem.at[groups[at][1] // 512])

    stages = functools.partial(total_blocks, block_ref, near_ref, far_ref, (ts_sem, tr_sem), low, high, core, highs)
    attn_at, blocks_done = pair_of(1) + 3, 0
    row_groups = x_ref.shape[0] // group
    swapped = set()
    for step in range(pairs + 3):
        if step < pairs:
            for at in in_pair(step):
                for copy in first(at):
                    copy.start()
        if 0 <= step - 1 < pairs:
            for at in in_pair(step - 1):
                for copy in first(at):
                    copy.wait()
                for copy in column(at):
                    copy.start()
        if 0 <= step - 2 < pairs:
            for at in in_pair(step - 2):
                column(at)[at % 2].wait()
                forward(at).start()
        if 0 <= step - 3 < pairs:
            for at in in_pair(step - 3):
                column(at)[1 - at % 2].wait()
                forward(at).wait()
                if groups[at][0] == 2:
                    load_mlp(at).start()
        for number in range(count):
            if shared[number] and number not in swapped and pair_of(number) + 3 <= step:
                swap(number).start()
                swapped.add(number)
        if step == 0:
            load_bands.start()
            load_pixels.start()
            block_ref[...] = jnp.zeros_like(block_ref)
            block_ref[:24, :] = placed_ref[...]
            load_bands.wait()
            lax.fori_loop(0, images, tally, 0)
            near_ref[low] = block_ref[...]
            for copy in stages(0):
                copy.start()
        if step == 1:
            for copy in stages(0):
                copy.wait()
            block_ref[...] = (near_ref[0] + near_ref[1]) + (near_ref[2] + near_ref[3])
            far_ref[high] = block_ref[...]
            for copy in stages(1):
                copy.start()
            load_pixels.wait()
            lax.fori_loop(0, images, pick, 0)
        if step == 2:
            for copy in stages(1):
                copy.wait()
            counts = far_ref[0]
            for k in range(1, highs):
                counts = counts + far_ref[k]
            counts_ref[...] = counts
            vec_ref[...] = jnp.zeros_like(vec_ref)
            for piece in range(7):
                vec_ref[piece : piece + 1, :512] = counts[2 * piece : 2 * piece + 1, :]
                vec_ref[piece : piece + 1, 512:] = counts[2 * piece + 1 : 2 * piece + 2, :]
        if step == attn_at:
            swap(0).wait()
            load_attn.start()
            load_embed.start()
            load_attn.wait()
            for part in range(4):
                at = pl.ds(part * width, width)
                flat_ref[at, :] = attn_v[:, :, :, at].reshape(-1, width).T
            load_embed.wait()
        if attn_at <= step < attn_at + 2:
            lax.fori_loop((step - attn_at) * row_groups // 2, (step - attn_at + 1) * row_groups // 2, rows_step, 0)
            if step == attn_at + 1:
                exchange(0, part_ref, other_ref).start()
        if step == attn_at + 2:
            exchange(0, part_ref, other_ref).wait()
            mlp_first()
        if step >= attn_at + 2:
            half = mlp_v.shape[-1] // 2
            for tile in range(blocks_done, half // 512):
                ends = [at for at in range(total) if groups[at][0] == 2 and groups[at][1] in (tile * 512, half + tile * 512)]
                if max(ends) // 2 + 3 > step:
                    break
                for at in ends:
                    load_mlp(at).wait()
                mlp_block(tile, 0)
                blocks_done = tile + 1
                if blocks_done == half // 512:
                    last_ref[...] = acc_ref[...].astype(BF16)
                    exchange(1, last_ref, far_out_ref).start()
    exchange(1, last_ref, far_out_ref).wait()
    for number in range(1, count):
        if shared[number]:
            swap(number).wait()


def forward_all(masters, shared, pixels, band_ids, kept_index, intersection, table, placed):
    size = lax.axis_size("dp")
    highs = size // 4
    count = len(masters)
    dims_of = []
    for master, split in zip(masters, shared):
        if master.ndim == 3:
            dims_of.append((master.shape[1], master.shape[0] * master.shape[2]))
        else:
            dims_of.append((master.shape[0], master.shape[1] // 2))
    groups = blocks_of([dims[1] for dims in dims_of], 512)
    half = dims_of[2][1] // 2
    groups.sort(key=lambda block: (block[0], block[1] % half if block[0] == 2 else 0, block[1]))
    total = len(groups)
    images, length = kept_index.shape
    rows, wide, local = images * length, D, dims_of[1][1] // 4
    rows_d = pixels.shape[0]
    group = 2 * length
    fulls = []
    for dims, split in zip(dims_of, shared):
        dims = (highs, 4) + dims
        fulls.append(shape((2,) + dims if split else dims, BF16))
    block = (32, 512)
    outs = [shape((rows, wide), F32), shape((3 * local, rows), BF16), shape((local, rows), BF16),
            shape((local // DH, rows), F32), shape((rows, pixels.shape[1]), BF16), shape((rows, wide), F32),
            shape((rows, wide), BF16), shape((rows, wide), BF16), shape(block, F32), shape((4 * local, wide), BF16),
            shape((8, wide), F32), shape((rows_d, 2), F32), shape((rows, 1), jnp.int32)]
    dma = pltpu.SemaphoreType.DMA
    in_vmem = pl.BlockSpec(memory_space=pltpu.VMEM)
    any_space = pl.BlockSpec(memory_space=pl.ANY)
    result = pl.pallas_call(
        functools.partial(forward_kernel, highs, shared, groups, count, length, group, DH),
        out_shape=tuple(fulls + outs),
        in_specs=[in_vmem] * count + [any_space] * 2 + [in_vmem] * 4,
        out_specs=tuple([any_space] * count + [in_vmem] * len(outs)),
        scratch_shapes=[pltpu.VMEM(dims, BF16) for dims in dims_of] + [
            pltpu.VMEM(pixels.shape, BF16), pltpu.VMEM(band_ids.shape, jnp.int32), pltpu.VMEM(fulls[0].shape, BF16),
            pltpu.VMEM(fulls[1].shape, BF16), pltpu.VMEM(fulls[2].shape, BF16), pltpu.VMEM((rows, wide), BF16),
            pltpu.VMEM((rows, wide), BF16), pltpu.VMEM((rows, wide), BF16), pltpu.VMEM((rows, wide), F32),
            pltpu.VMEM(block, F32), pltpu.VMEM((4,) + block, F32), pltpu.VMEM((highs,) + block, F32),
            dma((total,)), dma((total, highs - 1)), dma((total, highs - 1)), dma((total, 2)), dma((total, 2)),
            dma((total,)), dma((total,)), dma((count,)), dma((count,)), dma((5,)), dma((2,)), dma((2,)),
            dma((highs + 2,)), dma((highs + 2,)), dma((2 * half // 512,))],
        compiler_params=pltpu.CompilerParams(collective_id=0, has_side_effects=True, vmem_limit_bytes=62 * 2**20),
        cost_estimate=pl.CostEstimate(flops=0, bytes_accessed=2**25, transcendentals=0),
    )(*masters, pixels, band_ids, kept_index, intersection, table, placed)
    weights = [full.reshape(((2,) if split else ()) + (size * dims[0], dims[1]))
               for full, split, dims in zip(result[:count], shared, dims_of)]
    return weights, result[count:]


def gather_all(shards, shared):
    order_a, order_b = orders()
    fulls = []
    for number, shard in enumerate(shards):
        full = gather_dp(shard, 0, (order_a, order_b)[number % 2])
        if shared[number]:
            other, zero = other_core(full), lax.axis_index("mp") == 0
            full = jnp.stack([jnp.where(zero, full, other), jnp.where(zero, other, full)])
        fulls.append(full)
    return fulls


class Gatherer:
    def __init__(self, highs, groups, shards, fulls, sems):
        self.highs, self.groups, self.shards, self.fulls = highs, groups, shards, fulls
        self.own_sem, self.zs_sem, self.zr_sem, self.cs_sem, self.cr_sem, self.fs_sem, self.fr_sem = sems
        self.core, self.low, self.high, self.low_x, self.low_y = place_of()
        self.at_x, self.at_y = (self.high * 4 + self.low_x, self.core), (self.high * 4 + self.low_y, self.core)
        self.at_high = [(lax.rem(self.high + k, highs) * 4 + self.low, self.core) for k in range(1, highs)]
        self.pairs = (len(groups) + 1) // 2

    def in_pair(self, pair):
        return [at for at in (2 * pair, 2 * pair + 1) if 0 <= at < len(self.groups)] if 0 <= pair < self.pairs else []

    def full(self, at):
        number, start, size = self.groups[at]
        return self.fulls[number], pl.ds(start, size)

    def first(self, at):
        ref, cols = self.full(at)
        shard = self.shards[self.groups[at][0]].at[:, cols]
        mine = ref.at[self.high, self.low, :, cols]
        return [pltpu.make_async_copy(shard, mine, self.own_sem.at[at])] + [
            remote(shard, mine, self.zs_sem.at[at, k - 1], self.zr_sem.at[at, k - 1], self.at_high[k - 1])
            for k in range(1, self.highs)]

    def column(self, at, way):
        ref, cols = self.full(at)
        part = ref.at[:, self.low, :, cols]
        return remote(part, part, self.cs_sem.at[at, way], self.cr_sem.at[at, way], (self.at_x, self.at_y)[way])

    def forward(self, at):
        ref, cols = self.full(at)
        which, device = (self.low_x, self.at_y) if at % 2 == 0 else (self.low_y, self.at_x)
        part = ref.at[:, which, :, cols]
        return remote(part, part, self.fs_sem.at[at], self.fr_sem.at[at], device)

    def step(self, step):
        for at in self.in_pair(step):
            for copy in self.first(at):
                copy.start()
        for at in self.in_pair(step - 1):
            for copy in self.first(at):
                copy.wait()
            for way in range(2):
                self.column(at, way).start()
        for at in self.in_pair(step - 2):
            self.column(at, at % 2).wait()
            self.forward(at).start()
        for at in self.in_pair(step - 3):
            self.column(at, 1 - at % 2).wait()
            self.forward(at).wait()


def gatherer_sems(highs, groups):
    dma, total = pltpu.SemaphoreType.DMA, len(groups)
    return [dma((total,)), dma((total, highs - 1)), dma((total, highs - 1)), dma((total, 2)), dma((total, 2)),
            dma((total,)), dma((total,))]


def decoder_kernel(length, head_dim, highs, gathered, reduced, evec_ref, kept_ref, column_ref,
                   rows_ref, table_ref, totals_ref, mlp_in, predict_in, x1e_any, mine_any, other_any, target_any, band_any, attn_any, bridge_any,
                   gy_out, gattn_ref, gbridge_ref, rpred_ref, rup_ref, rdown_ref, norm_ref, loss_ref, vgrad_ref,
                   gup_ref, gdown_ref, gpred_ref, mlp_shard, predict_shard,
                   gbias_ref, sums_ref, esums_ref, final_ref, glat_ref, x_ref, x1_ref, gy_ref, qkv_ref, mixed_ref, lse_ref,
                   part_ref, from_ref, lowt_ref, gradt_ref, z_ref, gu_ref, flat_ref, mlp_ref, bridge_ref, predict_ref,
                   target_ref, band_ref, gp_ref, gpred_acc, gmix_ref, vec_ref, load_sem, stream_sem, send_sem, receive_sem,
                   join_sem, *comm):
    core, index = lax.axis_index("mp"), lax.axis_index("dp")
    sibling = (index, 1 - core)
    gather = Gatherer(highs, gathered, (mlp_shard, predict_shard), (mlp_ref, predict_ref.at[core]), comm[:7])
    pred_view = rpred_ref.at[core]
    red, _ = make_reducer(highs, reduced, (1.0,) * 3, (gpred_ref, gup_ref, gdown_ref), (pred_view, rup_ref, rdown_ref),
                          norm_ref, comm[7:])
    greet([sibling, gather.at_x, gather.at_y] + gather.at_high)
    for part in range(2):
        wide = mlp_in.shape[2]
        mlp_shard[:, part * wide : (part + 1) * wide] = mlp_in[part].astype(BF16)
    predict_shard[...] = predict_in[:, pl.ds(pl.multiple_of(core * predict_shard.shape[1], predict_shard.shape[1]),
                                             predict_shard.shape[1])].astype(BF16)
    gather.step(0)
    images, side, half = table_ref.shape
    patches = side * side
    width = mixed_ref.shape[0]
    hidden = z_ref.shape[1]
    wide = x_ref.shape[1]
    share = predict_ref.shape[-1]
    w_up = lambda: mlp_ref[:, :, :, :hidden].reshape(wide, hidden)
    w_down = lambda: mlp_ref[:, :, :, hidden:].reshape(wide, hidden)
    predict_half = lambda half: predict_ref[half].reshape(wide, share)
    vec_ref[...] = totals_ref[14:22, :]
    bias = jnp.concatenate([totals_ref[21:22, :], totals_ref[22:23, : 2 * share - totals_ref.shape[1]]], axis=1)
    inverse = [1.0 / jnp.sum(totals_ref[24 + level : 25 + level, :], axis=1, keepdims=True) for level in range(NB)]
    mine_ref = final_ref
    other_ref = lowt_ref.at[pl.ds(0, other_any.shape[0]), pl.ds(0, other_any.shape[1])]
    attn_ref = z_ref.at[pl.ds(0, attn_any.shape[0]), pl.ds(0, 4 * width)]

    loads = [pltpu.make_async_copy(source, target, load_sem.at[at]) for at, (source, target) in enumerate(
        ((attn_any, attn_ref), (bridge_any, bridge_ref), (x1e_any, gy_out),
         (mine_any, mine_ref), (other_any, other_ref)))]
    for copy in loads:
        copy.start()

    def rows_of(image):
        return pl.ds(pl.multiple_of(image * patches, patches), patches)

    def exchange(phase, image):
        rows = rows_of(image)
        return remote(part_ref.at[phase % 2, rows, :], from_ref.at[phase % 2, rows, :], send_sem.at[phase, image],
                      receive_sem.at[phase, image], sibling)

    def summed(phase, rows):
        return part_ref[phase % 2, rows, :].astype(F32) + from_ref[phase % 2, rows, :].astype(F32)

    def give(phase, image, value):
        part_ref[phase % 2, rows_of(image), :] = value.astype(BF16)
        exchange(phase, image).start()

    def stream(image):
        rows, slot = rows_of(image), lax.rem(image, 2)
        return [pltpu.make_async_copy(target_any.at[rows, :], target_ref.at[slot], stream_sem.at[0, slot]),
                pltpu.make_async_copy(band_any.at[rows, :], band_ref.at[slot], stream_sem.at[1, slot])]

    sums_ref[...] = jnp.zeros_like(sums_ref)
    loss_ref[...] = jnp.zeros_like(loss_ref)
    gbias_ref[...] = jnp.zeros_like(gbias_ref)
    gpred_acc[...] = jnp.zeros_like(gpred_acc)
    for copy in stream(0):
        copy.start()
    loads[0].wait()
    for part in range(4):
        at = pl.ds(part * width, width)
        flat_ref[at, :] = attn_ref[:, at].T
    loads[1].wait()
    for copy in loads[2:]:
        copy.wait()
    ends = bridge_ref.shape[2]
    latent_ref = gy_ref

    def ends_rows(step):
        return pl.ds(pl.multiple_of(step * 128, 128), 128)

    def enc_end(step, carry):
        rows = ends_rows(step)
        out = gy_out[rows, :] + both(mine_ref, other_ref, rows)
        gy_out[rows, :] = out
        unit, _ = normalize(out)
        final = (unit * evec_ref[5:6, :] + evec_ref[6:7, :]).astype(BF16)
        final_ref[rows, :] = final
        latent_ref[rows, :ends] = dot_nn(final, bridge_ref[0])
        latent_ref[rows, ends:] = dot_nn(final, bridge_ref[1])
        return carry

    lax.fori_loop(0, gy_out.shape[0] // 128, enc_end, 0)

    def phase_a(image, carry):
        rows = rows_of(image)
        hot = lax.broadcasted_iota(jnp.int32, (patches, length), 0) == kept_ref[pl.ds(image, 1), :]
        latent = latent_ref[pl.ds(pl.multiple_of(image * length, length), length), :]
        table = table_ref[image]
        by_row = jnp.broadcast_to(table[:, None, :], (side, side, half)).reshape(patches, half)
        by_col = jnp.broadcast_to(table[None, :, :], (side, side, half)).reshape(patches, half)
        place = jnp.concatenate([by_row, by_col], axis=1)
        rows_x = dot_exact(hot.astype(F32), latent) + rows_ref[rows, 0:1] * vec_ref[0:1, :] + place
        x_ref[rows, :] = rows_x
        unit, _ = normalize(rows_x)
        low = (unit * vec_ref[1:2, :] + vec_ref[2:3, :]).astype(BF16)
        qkv_ref[:, rows] = dot_nt(flat_ref[: 3 * width, :], low).astype(BF16)
        attend(qkv_ref, mixed_ref, lse_ref, rows, width, head_dim, None)
        give(0, image, dot_nn(mixed_ref[:, rows].T, flat_ref[3 * width :, :]))
        return carry

    swap = remote(predict_ref.at[core], predict_ref.at[core], join_sem.at[0], join_sem.at[1], sibling)
    gather.step(1)
    last = gather.pairs + 2
    for step in range(2, last + 1):
        lax.fori_loop((step - 2) * images // (last - 1), (step - 1) * images // (last - 1), phase_a, 0)
        if step < last:
            gather.step(step)

    def phase_b(image, carry):
        rows = rows_of(image)
        exchange(0, image).wait()
        after = x_ref[rows, :] + summed(0, rows)
        x1_ref[rows, :] = after
        unit, _ = normalize(after)
        low = (unit * vec_ref[3:4, :] + vec_ref[4:5, :]).astype(BF16)
        lowt_ref[:, rows] = low.T
        up = dot_nn(low, w_up())
        square, bent, rise = gelu_parts(up)
        mid = (up * rise).astype(BF16)
        z_ref[rows, :] = mid
        slope = rise + (0.5 * GELU_C) * up * (1.0 - bent * bent) * (1.0 + (3.0 * 0.044715) * square)
        gu_ref[rows, :] = slope.astype(BF16)
        give(1, image, dot_nt(mid, w_down()))
        return carry

    lax.fori_loop(0, images, phase_b, 0)
    gather.step(last)
    swap.start()
    swap.wait()

    def phase_c(image, carry):
        rows, slot = rows_of(image), lax.rem(image, 2)

        @pl.when(image + 1 < images)
        def _():
            for copy in stream(image + 1):
                copy.start()

        exchange(1, image).wait()
        unit, rstd = normalize(x1_ref[rows, :] + summed(1, rows))
        gain = vec_ref[5:6, :]
        final = (unit * gain + vec_ref[6:7, :]).astype(BF16)
        for copy in stream(image):
            copy.wait()
        predicted = jnp.concatenate([dot_nn(final, predict_half(0)), dot_nn(final, predict_half(1))], axis=1)
        mismatch = predicted + bias - target_ref[slot].astype(F32)
        band = band_ref[slot]
        level = jnp.where(band == 0, inverse[0], jnp.where(band == 1, inverse[1], inverse[2]))
        level = level * rows_ref[rows, 1:2]
        square = mismatch * mismatch + EPS_C
        root = lax.rsqrt(square)
        loss_ref[...] += jnp.sum(level * (square * root), axis=0, keepdims=True)
        grad = level * (mismatch * root)
        gbias_ref[...] += jnp.sum(grad, axis=0, keepdims=True)
        gp_ref[...] = grad.astype(BF16)
        columns = pl.ds(pl.multiple_of(core * share, share), share)
        gpred_acc[...] += dot_tn(final, gp_ref[:, columns])
        grad_final = dot_nt(gp_ref[:, :share], predict_half(0)) + dot_nt(gp_ref[:, share:], predict_half(1))
        grad_in, gain_sum, shift_sum = norm_back(grad_final, gain, unit, rstd)
        gy_ref[rows, :] = grad_in
        sums_ref[5:6, :] += gain_sum
        sums_ref[6:7, :] += shift_sum
        low = grad_in.astype(BF16)
        gradt_ref[:, rows] = low.T
        grad_up = (dot_nn(low, w_down()) * gu_ref[rows, :].astype(F32)).astype(BF16)
        gu_ref[rows, :] = grad_up
        give(2, image, dot_nt(grad_up, w_up()))
        return carry

    lax.fori_loop(0, images, phase_c, 0)
    lead = gpred_ref.shape[:3]
    norm_ref[...] = jnp.zeros_like(norm_ref)
    gpred_ref[...] = gpred_acc[...].astype(BF16).reshape(gpred_ref.shape)
    tile = 256
    for start in range(0, hidden, tile):
        at = pl.ds(start, tile)
        gup_ref[:, :, :, at] = dot_nn(lowt_ref[...], gu_ref[:, at]).astype(BF16).reshape(lead + (tile,))
        gdown_ref[:, :, :, at] = dot_nn(gradt_ref[...], z_ref[:, at]).astype(BF16).reshape(lead + (tile,))
    red.step(0)

    def phase_d(image, carry):
        rows = rows_of(image)
        exchange(2, image).wait()
        unit, rstd = normalize(x1_ref[rows, :])
        grad_in, gain_sum, shift_sum = norm_back(summed(2, rows), vec_ref[3:4, :], unit, rstd)
        grad_in = grad_in + gy_ref[rows, :]
        gy_ref[rows, :] = grad_in
        sums_ref[3:4, :] += gain_sum
        sums_ref[4:5, :] += shift_sum
        low = grad_in.astype(BF16)
        gradt_ref[:, rows] = low.T
        gmix_ref[...] = dot_nt(flat_ref[3 * width :, :], low).astype(BF16)
        attend_back(qkv_ref, gmix_ref, lse_ref, qkv_ref, rows, width, head_dim, None)
        unit_a, _ = normalize(x_ref[rows, :])
        lowt_ref[:, rows] = (unit_a * vec_ref[1:2, :] + vec_ref[2:3, :]).astype(BF16).T
        give(3, image, dot_nn(qkv_ref[:, rows].T, flat_ref[: 3 * width, :]))
        return carry

    final_step = red.pairs + 2
    for step in range(1, final_step):
        lax.fori_loop((step - 1) * images // (final_step - 1), step * images // (final_step - 1), phase_d, 0)
        red.step(step)
    join = remote(pred_view, pred_view, join_sem.at[2], join_sem.at[3], sibling)
    for part in range(3):
        at = pl.ds(part * width, width)
        gattn_ref[:, at] = dot_nt(lowt_ref[...], qkv_ref[at, :]).astype(BF16)
    gattn_ref[:, 3 * width :] = dot_nt(gradt_ref[...], mixed_ref[...]).astype(BF16)

    def phase_e(image, carry):
        rows = rows_of(image)
        exchange(3, image).wait()
        unit, rstd = normalize(x_ref[rows, :])
        grad_in, gain_sum, shift_sum = norm_back(summed(3, rows), vec_ref[1:2, :], unit, rstd)
        grad_in = grad_in + gy_ref[rows, :]
        sums_ref[1:2, :] += gain_sum
        sums_ref[2:3, :] += shift_sum
        sums_ref[0:1, :] += jnp.sum(grad_in * rows_ref[rows, 0:1], axis=0, keepdims=True)
        kept_rows = pl.ds(pl.multiple_of(image * length, length), length)
        hot = lax.broadcasted_iota(jnp.int32, (length, patches), 1) == column_ref[kept_rows, :]
        glat_ref[kept_rows, :] = dot_nn(hot.astype(BF16), grad_in.astype(BF16)).astype(BF16)
        return carry

    lax.fori_loop(0, images, phase_e, 0)
    red.step(final_step)
    join.start()
    columns = pl.ds(pl.multiple_of(core * ends, ends), ends)
    gbridge_ref[...] = dot_tn(final_ref[...], glat_ref[:, columns]).astype(BF16)
    esums_ref[...] = jnp.zeros_like(esums_ref)

    def enc_start(step, carry):
        rows = ends_rows(step)
        grad_final = dot_nt(glat_ref[rows, :ends], bridge_ref[0]) + dot_nt(glat_ref[rows, ends:], bridge_ref[1])
        unit, rstd = normalize(gy_out[rows, :])
        grad_in, gain_sum, shift_sum = norm_back(grad_final, evec_ref[5:6, :], unit, rstd)
        gy_out[rows, :] = grad_in
        esums_ref[0:1, :] += gain_sum
        esums_ref[1:2, :] += shift_sum
        return carry

    lax.fori_loop(0, gy_out.shape[0] // 128, enc_start, 0)
    join.wait()
    vgrad_ref[...] = jnp.zeros_like(vgrad_ref)
    vgrad_ref[5:7, :] = esums_ref[0:2, :]
    vgrad_ref[7:14, : sums_ref.shape[1]] = sums_ref[0:7, :]
    vgrad_ref[14:15, : gbias_ref.shape[1]] = gbias_ref[...]


def decoder_all(x1e, mine, other, evec, kept_index, kept_column, row_values, table, totals, mlp, predict, target, band,
                attn, bridge):
    size = lax.axis_size("dp")
    highs = size // 4
    rows_e, wide = x1e.shape
    images, length = kept_index.shape
    rows, pixel_count = target.shape
    patches = rows // images
    shard, hidden = mlp.shape[1], mlp.shape[2]
    low_wide = shard * size
    width, share, ends = attn.shape[1] // 4, predict.shape[1] // 2, bridge.shape[2]
    lead = (highs, 4, shard)
    gathered = blocks_of([2 * hidden, share], 512)
    reduced = blocks_of([share, hidden, hidden], 512)
    in_vmem = pl.BlockSpec(memory_space=pltpu.VMEM)
    any_space = pl.BlockSpec(memory_space=pl.ANY)
    dma = pltpu.SemaphoreType.DMA
    vm = pltpu.VMEM
    return pl.pallas_call(
        functools.partial(decoder_kernel, length, DDH, highs, gathered, reduced),
        out_shape=(
            shape((rows_e, wide), F32), shape((low_wide, 4 * width), BF16), shape((wide, ends), BF16),
            shape((2, shard, share), F32), shape((shard, hidden), F32), shape((shard, hidden), F32), shape((8, 128), F32),
            shape((1, pixel_count), F32), shape((16, wide), F32)),
        in_specs=[in_vmem] * 8 + [any_space] * 7,
        out_specs=tuple([in_vmem] * 9),
        scratch_shapes=[
            vm(lead + (hidden,), BF16), vm(lead + (hidden,), BF16), vm(lead + (share,), BF16),
            vm((shard, 2 * hidden), BF16), vm((shard, share), BF16),
            vm((1, pixel_count), F32), vm((8, low_wide), F32), vm((8, wide), F32),
            vm((rows_e, wide), BF16), vm((rows_e, low_wide), BF16), vm((rows, low_wide), F32),
            vm((rows, low_wide), F32), vm((rows, low_wide), F32), vm((3 * width, rows), BF16), vm((width, rows), BF16),
            vm((width // DDH, rows), F32), vm((2, rows, low_wide), BF16), vm((2, rows, low_wide), BF16),
            vm((low_wide, rows), BF16), vm((low_wide, rows), BF16), vm((rows, hidden), BF16), vm((rows, hidden), BF16),
            vm((4 * width, low_wide), BF16), vm(lead + (2 * hidden,), BF16), vm(bridge.shape, BF16),
            vm((2,) + lead + (share,), BF16), vm((2, patches, pixel_count), BF16), vm((2, patches, pixel_count), jnp.int32),
            vm((patches, pixel_count), BF16), vm((low_wide, share), F32), vm((width, patches), BF16),
            vm((8, low_wide), F32),
            dma((5,)), dma((2, 2)), dma((4, images)), dma((4, images)), dma((4,))]
        + gatherer_sems(highs, gathered) + reducer_scratch(highs, reduced, [shard] * 3),
        compiler_params=pltpu.CompilerParams(collective_id=3, has_side_effects=True, vmem_limit_bytes=62 * 2**20),
        cost_estimate=pl.CostEstimate(flops=0, bytes_accessed=2**25, transcendentals=0),
    )(evec, kept_index, kept_column, row_values, table, totals, mlp, predict, x1e, mine, other, target, band, attn, bridge)


class Reducer:
    def __init__(self, highs, groups, weights, grads, outs, near, second, far, load_two, load_own, plane, norm, sems):
        self.highs, self.groups, self.weights = highs, groups, weights
        self.grads, self.outs = grads, outs
        self.near, self.second, self.far = near, second, far
        self.load_two, self.load_own, self.plane, self.norm = load_two, load_own, plane, norm
        self.load_sem, self.as_sem, self.ar_sem, self.bs_sem, self.br_sem, self.zs_sem, self.zr_sem = sems
        self.core, self.low, self.high, self.low_x, self.low_y = place_of()
        self.dev_x, self.dev_y = (self.high * 4 + self.low_x, self.core), (self.high * 4 + self.low_y, self.core)
        self.at_high = [(lax.rem(self.high + k, highs) * 4 + self.low, self.core) for k in range(1, highs)]
        self.pairs = (len(groups) + 1) // 2

    def in_pair(self, pair):
        return [at for at in (2 * pair, 2 * pair + 1) if 0 <= at < len(self.groups)] if 0 <= pair < self.pairs else []

    def route(self, at):
        if at % 2 == 0:
            return self.low_y, self.dev_y, self.low_x, self.dev_x
        return self.low_x, self.dev_x, self.low_y, self.dev_y

    def grad(self, at, which):
        number, start, size = self.groups[at]
        return self.grads[number].at[:, which, :, pl.ds(start, size)]

    def slot(self, ref, at, count):
        number, _, size = self.groups[at]
        return ref.at[at % count, :, pl.ds(0, self.outs[number].shape[0]), pl.ds(0, size)]

    def two_ref(self, at):
        return self.slot(self.load_two, at, 6)

    def own_ref(self, at):
        return self.slot(self.load_own, at, 8)

    def loads(self, at):
        return [pltpu.make_async_copy(self.grad(at, self.route(at)[2]), self.two_ref(at), self.load_sem.at[at, 0]),
                pltpu.make_async_copy(self.grad(at, self.low), self.own_ref(at), self.load_sem.at[at, 1])]

    def one(self, at):
        low_one, dev_one, _, _ = self.route(at)
        return [remote(self.grad(at, 3 - self.low), self.near[2 * at], self.as_sem.at[at, 0], self.ar_sem.at[at, 0], dev_one),
                remote(self.grad(at, low_one), self.near[2 * at + 1], self.as_sem.at[at, 1], self.ar_sem.at[at, 1], dev_one)]

    def two(self, at):
        return remote(self.two_ref(at), self.second[at], self.bs_sem.at[at], self.br_sem.at[at], self.route(at)[3])

    def three(self, at):
        return [remote(self.own_ref(at).at[lax.rem(self.high + k, self.highs)], self.far[at].at[k - 1],
                       self.zs_sem.at[at, k - 1], self.zr_sem.at[at, k - 1], self.at_high[k - 1])
                for k in range(1, self.highs)]

    def step(self, step):
        for at in self.in_pair(step):
            for copy in self.one(at) + self.loads(at):
                copy.start()
        for at in self.in_pair(step - 1):
            mine = self.two_ref(at)
            self.loads(at)[0].wait()
            self.one(at)[0].wait()
            mine[...] = (mine[...].astype(F32) + self.near[2 * at][...].astype(F32)).astype(BF16)
            self.two(at).start()
        for at in self.in_pair(step - 2):
            number, start, size = self.groups[at]
            mine = self.own_ref(at)
            self.loads(at)[1].wait()
            self.one(at)[1].wait()
            self.two(at).wait()
            plane = self.slot(self.plane, at, 2)
            plane[...] = (mine[...].astype(F32) + self.near[2 * at + 1][...].astype(F32)
                          + self.second[at][...].astype(F32))
            self.outs[number][:, pl.ds(start, size)] = plane[self.high]
            mine[...] = plane[...].astype(BF16)
            for copy in self.three(at):
                copy.start()
        for at in self.in_pair(step - 3):
            number, start, size = self.groups[at]
            for copy in self.three(at):
                copy.wait()
            cols = pl.ds(start, size)
            done = self.outs[number][:, cols]
            for k in range(self.highs - 1):
                done = done + self.far[at][k].astype(F32)
            self.outs[number][:, cols] = done
            self.norm[0:1, 0:1] += self.weights[number] * jnp.sum(done * done, keepdims=True)


def reducer_scratch(highs, groups, shards):
    piece = lambda lead, group: pltpu.VMEM((lead, shards[group[0]], group[2]), BF16)
    near = [piece(highs, group) for group in groups for _ in range(2)]
    second = [piece(highs, group) for group in groups]
    far = [piece(highs - 1, group) for group in groups]
    slot = (highs, max(shards), max(group[2] for group in groups))
    loads = [pltpu.VMEM((6,) + slot, BF16), pltpu.VMEM((8,) + slot, BF16), pltpu.VMEM((2,) + slot, F32)]
    dma, total = pltpu.SemaphoreType.DMA, len(groups)
    sems = [dma((total, 2)), dma((total, 2)), dma((total, 2)), dma((total,)), dma((total,)),
            dma((total, highs - 1)), dma((total, highs - 1))]
    return near + second + far + loads + sems


def make_reducer(highs, groups, weights, grads, outs, norm, refs):
    total = len(groups)
    near, second, far, refs = refs[: 2 * total], refs[2 * total : 3 * total], refs[3 * total : 4 * total], refs[4 * total :]
    return Reducer(highs, groups, weights, grads, outs, near, second, far, *refs[:3], norm, refs[3:10]), refs[10:]


def backward_kernel(highs, weights, groups, ready, count, shared, length, group, head_dim, *refs):
    given = count - 4
    gy_ref, x1_ref, vec_ref, vgrad_ref, loss_ref, lse_ref, norm_in = refs[:7]
    x_any, qkv_any, mixed_any, flat_any, pixk_any, mlp_any = refs[7:13]
    refs = refs[13:]
    grads, refs = refs[:given], refs[given:]
    outs, sums_ref, vflat_ref, refs = refs[:count], refs[count], refs[count + 1], refs[count + 2 :]
    made, refs = refs[:4], refs[4:]
    grads = tuple(grads) + tuple(made)
    (x_ref, qkv_ref, mixed_ref, flat_ref, pixk_ref, wmlp_ref, low_ref, lowt_ref, grad_ref, gradt_ref, acc_ref, part_ref,
     other_ref, last_ref, gmix_ref, gqkv_ref, stage_ref, norm_ref, spots_ref, far_ref, vnear_ref, vfar_ref,
     vsum_ref) = refs[:23]
    (load_sem, wload_sem, store_sem, xs_sem, xr_sem, ns_sem, nr_sem, hs_sem, hr_sem, ts_sem, tr_sem, js_sem,
     jr_sem) = refs[23:36]
    core_at = lax.axis_index("mp")
    views = [ref.at[core_at] if split else ref for ref, split in zip(outs, shared)]
    red, _ = make_reducer(highs, groups, weights, grads, views, norm_ref, refs[36:])
    core, low, high = red.core, red.low, red.high
    spot = low * 2 + core
    sibling = (high * 4 + low, 1 - core)
    near = [(high * 4 + lax.rem(spot + k, 8) // 2, lax.rem(lax.rem(spot + k, 8), 2)) for k in range(1, 8)]
    greet(near + red.at_high)
    rows, wide = x_ref.shape
    width = mixed_ref.shape[0]
    hidden = mlp_any.shape[-1] // 2
    size = 512
    tiles = hidden // size
    mask = group_mask(group, length)

    late = [pltpu.make_async_copy(source, target, load_sem.at[at]) for at, (source, target) in enumerate(
        ((x_any, x_ref), (qkv_any, qkv_ref), (mixed_any, mixed_ref), (flat_any, flat_ref), (pixk_any, pixk_ref)))]

    def weight_loads(tile):
        return [pltpu.make_async_copy(mlp_any.at[:, :, :, pl.ds(half * hidden + tile * size, size)],
                                      wmlp_ref.at[tile % 2, half], wload_sem.at[tile % 2, half]) for half in range(2)]

    def store(slot, target, start, columns=512):
        return pltpu.make_async_copy(stage_ref.at[slot, :, :, :, pl.ds(0, columns)],
                                     target.at[:, :, :, pl.ds(start, columns)], store_sem.at[slot])

    def exchange(at, target):
        return remote(part_ref, target, xs_sem.at[at], xr_sem.at[at], sibling)

    def staged(slot, value):
        columns = value.shape[1]
        stage_ref[slot, :, :, :, :columns] = value.astype(BF16).reshape(stage_ref.shape[1:4] + (columns,))

    def mlp_first():
        unit, _ = normalize(x1_ref[...])
        value = (unit * vec_ref[3:4, :] + vec_ref[4:5, :]).astype(BF16)
        low_ref[...] = value
        lowt_ref[...] = value.T
        value = gy_ref[...].astype(BF16)
        grad_ref[...] = value
        gradt_ref[...] = value.T
        acc_ref[...] = jnp.zeros_like(acc_ref)

    def mlp_block(tile):
        for copy in weight_loads(tile):
            copy.wait()
        if tile + 1 < tiles:
            for copy in weight_loads(tile + 1):
                copy.start()
        w_up = wmlp_ref[tile % 2, 0].reshape(wide, size)
        w_down = wmlp_ref[tile % 2, 1].reshape(wide, size)
        up = dot_nn(low_ref[...], w_up)
        square, bent, half = gelu_parts(up)
        mid = (up * half).astype(BF16)
        slope = half + (0.5 * GELU_C) * up * (1.0 - bent * bent) * (1.0 + (3.0 * 0.044715) * square)
        grad_up = (dot_nn(grad_ref[...], w_down) * slope).astype(BF16)
        acc_ref[...] += dot_nt(grad_up, w_up)
        slot = 2 * (tile % 2)
        staged(slot, dot_nn(lowt_ref[...], grad_up))
        store(slot, made[0], tile * size).start()
        staged(slot + 1, dot_nn(gradt_ref[...], mid))
        store(slot + 1, made[1], tile * size).start()

    def mlp_last():
        part_ref[...] = acc_ref[...].astype(BF16)
        exchange(0, other_ref).start()

    def stores_done(tile):
        slot = 2 * (tile % 2)
        store(slot, made[0], tile * size).wait()
        store(slot + 1, made[1], tile * size).wait()

    def rows_step(number, carry):
        at = pl.ds(pl.multiple_of(number * group, group), group)
        unit, rstd = normalize(x1_ref[at, :])
        grad_in, gain_sum, shift_sum = norm_back(both(part_ref, other_ref, at), vec_ref[3:4, :], unit, rstd)
        grad_in = grad_in + gy_ref[at, :]
        gy_ref[at, :] = grad_in
        vsum_ref[3:4, :] += gain_sum
        vsum_ref[4:5, :] += shift_sum
        low_grad = grad_in.astype(BF16)
        gradt_ref[:, at] = low_grad.T
        gmix_ref[...] = dot_nt(flat_ref[3 * width :, :], low_grad).astype(BF16)
        attend_back(qkv_ref, gmix_ref, lse_ref, gqkv_ref, at, width, head_dim, mask)
        part_ref[at, :] = dot_nn(gqkv_ref[:, at].T, flat_ref[: 3 * width, :]).astype(BF16)
        unit_a, _ = normalize(x_ref[at, :])
        lowt_ref[:, at] = (unit_a * vec_ref[1:2, :] + vec_ref[2:3, :]).astype(BF16).T
        return carry

    def attn_grads():
        for slot in range(4):
            if slot < 3:
                value = dot_nt(lowt_ref[...], gqkv_ref[pl.ds(slot * width, width), :])
            else:
                value = dot_nt(gradt_ref[...], mixed_ref[...])
            staged(slot, value)
            store(slot, made[2], slot * width, width).start()

    def enc_out():
        unit, rstd = normalize(x_ref[...])
        grad_in, gain_sum, shift_sum = norm_back(both(part_ref, last_ref, pl.ds(0, rows)), vec_ref[1:2, :], unit, rstd)
        grad_in = grad_in + gy_ref[...]
        vsum_ref[0:1, :] = jnp.sum(grad_in, axis=0, keepdims=True)
        vsum_ref[1:2, :] = gain_sum
        vsum_ref[2:3, :] = shift_sum
        share = made[3].shape[-1]
        columns = pl.ds(pl.multiple_of(core * share, share), share)
        staged(0, dot_tn(grad_in.astype(BF16), pixk_ref[:, columns]))
        store(0, made[3], 0, share).start()

    stages = functools.partial(total_blocks, vsum_ref, vnear_ref, vfar_ref, (ts_sem, tr_sem), low, high, core, highs)
    mlp_ready, attn_ready, embed_ready = ready
    row_groups = rows // group
    norm_ref[...] = norm_in[...]
    vsum_ref[...] = vgrad_ref[...]
    for copy in weight_loads(0):
        copy.start()
    work = {0: range(0, 1), 1: range(1, tiles - 1), 2: range(tiles - 1, tiles)}
    for step in range(red.pairs + 3):
        if 0 <= step - mlp_ready < tiles:
            stores_done(step - mlp_ready)
        if step == attn_ready:
            for slot in range(4):
                store(slot, made[2], slot * width, width).wait()
        if step == embed_ready:
            store(0, made[3], 0, made[3].shape[-1]).wait()
        red.step(step)
        if step == 0:
            for copy in late:
                copy.start()
            mlp_first()
        for tile in work.get(step, ()):
            mlp_block(tile)
            if tile == tiles - 1:
                mlp_last()
        if step == 3:
            for copy in late:
                copy.wait()
            exchange(0, other_ref).wait()
            lax.fori_loop(0, row_groups // 2, rows_step, 0)
        if step == 4:
            lax.fori_loop(row_groups // 2, row_groups, rows_step, 0)
            exchange(1, last_ref).start()
            attn_grads()
        if step == embed_ready - 1:
            exchange(1, last_ref).wait()
            enc_out()
            vnear_ref[low] = vsum_ref[...]
            for copy in stages(0):
                copy.start()
        if step == embed_ready:
            for copy in stages(0):
                copy.wait()
            vsum_ref[...] = (vnear_ref[0] + vnear_ref[1]) + (vnear_ref[2] + vnear_ref[3])
            vfar_ref[high] = vsum_ref[...]
            for copy in stages(1):
                copy.start()
        if step == embed_ready + 1:
            for copy in stages(1):
                copy.wait()
            every = vfar_ref[0]
            for k in range(1, highs):
                every = every + vfar_ref[k]
            for row in range(7):
                vflat_ref[2 * row : 2 * row + 1, :] = every[row : row + 1, :512]
                vflat_ref[2 * row + 1 : 2 * row + 2, :] = every[row : row + 1, 512:]
            vflat_ref[14:22, :] = every[7:15, :512]
            vflat_ref[22:23, :] = every[14:15, 512:]
            vflat_ref[23:24, :] = jnp.zeros_like(vflat_ref[23:24, :])
            norm_ref[0:1, 0:1] += jnp.sum(every * every, keepdims=True) * (1.0 / (8 * highs))
    joins = [remote(view, view, js_sem.at[at], jr_sem.at[at], sibling)
             for at, (view, split) in enumerate(zip(views, shared)) if split]
    for copy in joins:
        copy.start()
    norm_ref[1:2, 0:1] = jnp.sum(loss_ref[...], keepdims=True)
    spots_ref[spot] = norm_ref[...]
    copies = [remote(norm_ref, spots_ref.at[spot], ns_sem.at[k], nr_sem.at[k], near[k]) for k in range(7)]
    for copy in copies:
        copy.start()
    for copy in copies:
        copy.wait()
    local = spots_ref[0]
    for k in range(1, 8):
        local = local + spots_ref[k]
    norm_ref[...] = local
    far_ref[high] = local
    copies = [remote(norm_ref, far_ref.at[high], hs_sem.at[k], hr_sem.at[k], red.at_high[k]) for k in range(highs - 1)]
    for copy in copies:
        copy.start()
    for copy in copies:
        copy.wait()
    every = far_ref[0]
    for k in range(1, highs):
        every = every + far_ref[k]
    sums_ref[...] = every
    for copy in joins:
        copy.wait()


def backward_all(gy, x1, evec, vec_grads, loss_parts, norm, enc_saved, x0, flat, pixk, mlp, grads, shared, length, head_dim):
    size = lax.axis_size("dp")
    highs = size // 4
    qkv, mixed, lse = enc_saved
    rows, wide = x1.shape
    width = mixed.shape[0]
    hidden = mlp.shape[1] // 2
    group = 2 * length
    shard = wide // size
    lead = (highs, 4, shard)
    fresh = [lead + (hidden,), lead + (hidden,), lead + (4 * width,), lead + (pixk.shape[1] // 2,)]
    widths = [a.shape[1] for a in grads] + [dims[-1] for dims in fresh]
    shards = [a.shape[0] // size for a in grads] + [shard] * 4
    count, given = len(widths), len(grads)
    blocks = blocks_of(widths, 512)
    first = [b for b in blocks if b[0] == 0]
    last = [b for b in blocks if b[0] == given + 3] + [b for b in blocks if 0 < b[0] < given]
    middle = [b for at in range(0, hidden, 512) for b in ((given, at, 512), (given + 1, at, 512))]
    attn = [b for b in blocks if b[0] == given + 2]
    groups = first + middle + attn + last
    if len(first) != 2 or hidden // 512 != 4 or len(attn) != 4:
        raise ValueError("blocks")
    ready = (len(first) // 2, (len(first) + len(middle)) // 2, (len(first) + len(middle) + len(attn)) // 2)
    dma = pltpu.SemaphoreType.DMA
    small, vec_block = (8, 128), vec_grads.shape
    in_vmem = pl.BlockSpec(memory_space=pltpu.VMEM)
    any_space = pl.BlockSpec(memory_space=pl.ANY)
    result = pl.pallas_call(
        functools.partial(backward_kernel, highs, (1.0,) * count, groups, ready, count, shared, length, group, head_dim),
        out_shape=tuple([shape((2, r, w) if split else (r, w), F32) for r, w, split in zip(shards, widths, shared)]
                        + [shape(small, F32), shape((24, 512), F32)]
                        + [shape(dims, BF16) for dims in fresh]),
        in_specs=[in_vmem] * 7 + [any_space] * (6 + given),
        out_specs=tuple([in_vmem] * (count + 2) + [any_space] * 4),
        scratch_shapes=[
            pltpu.VMEM((rows, wide), F32), pltpu.VMEM(qkv.shape, BF16), pltpu.VMEM(mixed.shape, BF16),
            pltpu.VMEM(flat.shape, BF16), pltpu.VMEM(pixk.shape, BF16), pltpu.VMEM((2, 2) + lead + (512,), BF16),
            pltpu.VMEM((rows, wide), BF16), pltpu.VMEM((wide, rows), BF16), pltpu.VMEM((rows, wide), BF16),
            pltpu.VMEM((wide, rows), BF16), pltpu.VMEM((rows, wide), F32), pltpu.VMEM((rows, wide), BF16),
            pltpu.VMEM((rows, wide), BF16), pltpu.VMEM((rows, wide), BF16), pltpu.VMEM((width, group), BF16),
            pltpu.VMEM((3 * width, rows), BF16), pltpu.VMEM((4,) + lead + (512,), BF16), pltpu.VMEM(small, F32),
            pltpu.VMEM((8,) + small, F32), pltpu.VMEM((highs,) + small, F32), pltpu.VMEM((4,) + vec_block, F32),
            pltpu.VMEM((highs,) + vec_block, F32), pltpu.VMEM(vec_block, F32),
            dma((5,)), dma((2, 2)), dma((4,)), dma((2,)), dma((2,)), dma((7,)), dma((7,)), dma((highs - 1,)),
            dma((highs - 1,)), dma((highs + 2,)), dma((highs + 2,)), dma((count,)), dma((count,))] + reducer_scratch(highs, groups, shards),
        compiler_params=pltpu.CompilerParams(collective_id=1, has_side_effects=True, vmem_limit_bytes=62 * 2**20),
        cost_estimate=pl.CostEstimate(flops=0, bytes_accessed=sum(a.size * 2 for a in grads), transcendentals=0),
    )(gy, x1, evec, vec_grads, loss_parts, lse, norm, x0, qkv, mixed, flat, pixk, mlp.reshape(lead + (2 * hidden,)),
      *[a.reshape(highs, 4, r, a.shape[1]) for r, a in zip(shards, grads)])
    return list(result[:count]), result[count], result[count + 1]


def reduce_plain(grads, loss_parts, vec_grads):
    order_a, order_b = orders()
    outs = [reduce_dp(a, 0, (order_a, order_b)[number % 2], a.dtype) for number, a in enumerate(grads)]
    vec_sums = total_dp(vec_grads)
    sums = jnp.stack([sum(jnp.sum(a * a) for a in outs), jnp.sum(loss_parts)])
    sums = total_dp(sums)
    sums = sums + other_core(sums)
    return outs, sums[0] + jnp.sum(vec_sums * vec_sums), 0.5 * sums[1], vec_sums


def adam_update(master, gradient, first_old, second_old, step_rate, decay_rate):
    first_new = BETA_ONE * first_old + (1.0 - BETA_ONE) * gradient
    second_new = BETA_TWO * second_old + (1.0 - BETA_TWO) * gradient * gradient
    first_hat = first_new / (1.0 - BETA_ONE**STEP)
    second_hat = second_new / (1.0 - BETA_TWO**STEP)
    updated = master - step_rate * (
        first_hat / (jnp.sqrt(second_hat) + ADAM_EPS) + decay_rate * master
    )
    return (updated, first_new, second_new)


def adam_kernel(count, averaged, sums_ref, *refs):
    sources, refs = refs[: count + 2], refs[count + 2 :]
    masters, firsts, seconds, refs = refs[:count], refs[count : 2 * count], refs[2 * count : 3 * count], refs[3 * count :]
    means, refs = refs[:averaged], refs[averaged:]
    news, new_firsts, new_seconds, new_means = (
        refs[:count], refs[count : 2 * count], refs[2 * count : 3 * count], refs[3 * count :])
    factor = CLIP / jnp.maximum(jnp.sqrt(sums_ref[0:1, 0:1]), CLIP)

    def update(number, at, gradient):
        new, first, second = adam_update(masters[number][at], gradient * factor, firsts[number][at], seconds[number][at],
                                         RATE_MAT, DECAY_MAT)
        news[number][at] = new
        new_firsts[number][at] = first
        new_seconds[number][at] = second
        mean = {0: 0, 1: 1, 4: 2}.get(number)
        if mean is not None:
            new_means[mean][at] = EMA_KEEP * means[mean][at] + (1.0 - EMA_KEEP) * new

    enc_attn, enc_up, enc_down, dec_attn, dec_up, dec_down, embed, bridge, predict = sources
    for number, source in ((0, enc_attn), (2, dec_attn)):
        wide = source.shape[1] // 4
        for part in range(4):
            update(number, part, source[:, part * wide : (part + 1) * wide])
    for number, pair in ((1, (enc_up, enc_down)), (3, (dec_up, dec_down))):
        for part, source in enumerate(pair):
            update(number, part, source[...])
    for number, source in ((4, embed), (5, bridge), (6, predict)):
        share = source.shape[2]
        for half in range(2):
            update(number, (slice(None), pl.ds(half * share, share)), source[half])


def adam_all(sums, sources, masters, firsts, seconds, means):
    like = lambda arrays: [shape(a.shape, F32) for a in arrays]
    outs = like(masters) * 3 + like(means)
    count = len(masters)
    result = run(functools.partial(adam_kernel, count, len(means)), outs, [],
                 (sums, *sources, *masters, *firsts, *seconds, *means), 0)
    return (result[:count], result[count : 2 * count], result[2 * count : 3 * count], result[3 * count :])


def plain_step(pixels, target, band_ids, kept_index, intersection, gsd_scale, masters, enc_table, dec_table):
    enc_attn, enc_mlp, dec_attn, dec_mlp, patch_embed, bridge, predict, vectors = masters
    images, keep_count = kept_index.shape
    patch_count = intersection.shape[1]
    patch_index = jnp.arange(patch_count, dtype=jnp.int32)
    kept_flags = jnp.any(kept_index[:, :, None] == patch_index[None, None, :], axis=1).astype(F32)
    patch_weight = ((1.0 - kept_flags) * (1.0 - 0.5 * intersection.astype(F32))).reshape(-1, 1)
    hidden_rows = (1.0 - kept_flags).reshape(-1, 1)
    core = lax.axis_index("mp").astype(jnp.int32).reshape(1)
    size = lax.axis_size("dp")

    def flat(stack):
        return jnp.concatenate([part.astype(BF16) for part in stack], axis=1)

    def core_half(block):
        half = block.shape[1] // 2
        return lax.dynamic_slice_in_dim(block, lax.axis_index("mp") * half, half, 1).astype(BF16)

    vec_shard = vectors.shape[0]
    vec_room = -(-vec_shard // 1024) * 1024
    vec_rows = jnp.pad(lax.reduce_precision(vectors, 8, 7), (0, vec_room - vec_shard)).reshape(-1, 128)
    vec_full = gather_dp(vec_rows, 0, orders()[0])
    pieces = split_vectors(vec_full.reshape(size, vec_room)[:, :vec_shard].reshape(-1), D, E)
    evec = jnp.stack(pieces[:7] + [jnp.zeros_like(pieces[0])])
    dvec = jnp.stack(pieces[7:14] + [jnp.zeros_like(pieces[7])])
    kept_column = kept_index.reshape(-1, 1)
    rows, rows_d = images * keep_count, images * patch_count
    pixel_count = pixels.shape[1]
    group = 2 * keep_count
    shards = [core_half(patch_embed.T), flat(enc_attn), flat(enc_mlp), flat(dec_attn), flat(dec_mlp), core_half(bridge),
              core_half(predict)]
    weights = gather_all(shards, (True, False, False, False, False, True, True))
    embed_w, enc_attn_w, enc_mlp_w, dec_attn_w, dec_mlp_w, bridge_w, predict_w = weights
    local = enc_attn_w.shape[1] // 4
    band_weight = total_dp(jnp.stack([jnp.sum(jnp.where(band_ids == level, patch_weight, 0.0)) for level in range(NB)]))
    inverse = 1.0 / band_weight
    x0, *enc_saved, part, kept_pixels = run(
        functools.partial(enc_in_kernel, keep_count, group, DH),
        [shape((rows, D), F32), shape((3 * local, rows), BF16), shape((local, rows), BF16),
         shape((local // DH, rows), F32), shape((rows, D), BF16), shape((rows, pixel_count), BF16)],
        [pltpu.VMEM((4 * local, D), BF16)],
        (pixels, kept_column, enc_table, embed_w, evec, enc_attn_w),
        rows * D * (2 * pixel_count + 8 * local))
    x1, part = mlp_forward(x0, part, evec, enc_mlp_w)
    other = other_core(part)
    one_d, one_e = shape((1, D), F32), shape((1, E), F32)
    local_d = dec_attn_w.shape[1] // 4
    x2, final_enc, xd, *dec_saved, part = run(
        functools.partial(dec_in_kernel, keep_count, DDH),
        [shape((rows, D), F32), shape((rows, D), BF16), shape((rows_d, E), F32), shape((3 * local_d, rows_d), BF16),
         shape((local_d, rows_d), BF16), shape((local_d // DDH, rows_d), F32), shape((rows_d, E), BF16)],
        [pltpu.VMEM((4 * local_d, E), BF16), pltpu.VMEM((rows, E), F32)],
        (x1, part, other, evec, bridge_w, kept_index, hidden_rows, dec_table, dvec,
         dec_attn_w),
        rows_d * E * 8 * local_d + 2 * rows * D * E)
    xd1, part = mlp_forward(xd, part, dvec, dec_mlp_w)
    gyd, grad_predict, grad_pbias, loss_parts, grad_dec_fg, grad_dec_fb = head(
        core, inverse, xd1, part, dvec, pieces[14].reshape(1, -1), predict_w, target, band_ids, patch_weight, patch_count)
    grad_dec_up, grad_dec_down, part = mlp_backward(gyd, xd1, dvec, dec_mlp_w)
    gxd, grad_dec_attn, grad_dec_gb, grad_dec_bb, part = attn_backward(
        gyd, xd1, part, xd, dec_saved, dvec, dec_attn_w, patch_count, patch_count, DDH)
    grad_dec_ga, grad_dec_ba, grad_mask, grad_bridge, grad_enc_fg, grad_enc_fb, gye = run(
        functools.partial(between_kernel, keep_count),
        [one_e, one_e, one_e, shape((D, E // 2), BF16), one_d, one_d, shape((rows, D), F32)],
        [pltpu.VMEM((rows, E), BF16)],
        (core, gxd, xd, part, other_core(part), dvec, kept_column, hidden_rows, final_enc, x2, evec, bridge_w),
        3 * rows * D * E, 1)
    wide_row = lambda row: jnp.pad(row, ((0, 0), (0, D - row.shape[1])))
    no_row = jnp.zeros((1, D), F32)
    late_rows = [grad_enc_fg, grad_enc_fb] + [wide_row(row) for row in (
        grad_mask, grad_dec_ga, grad_dec_ba, grad_dec_gb, grad_dec_bb, grad_dec_fg, grad_dec_fb, grad_pbias)] + [no_row]
    dec_grads = [grad_predict, grad_dec_up, grad_dec_down, grad_dec_attn, grad_bridge]
    grad_enc_up, grad_enc_down, part = mlp_backward(gye, x1, evec, enc_mlp_w)
    gxe, grad_enc_attn, grad_enc_gb, grad_enc_bb, part = attn_backward(
        gye, x1, part, x0, enc_saved, evec, enc_attn_w, keep_count, group, DH)
    grad_enc_ga, grad_enc_ba, grad_ebias, grad_embed = run(
        enc_out_kernel,
        [one_d, one_d, one_d, shape((D, pixel_count // 2), BF16)],
        [], (core, gxe, x0, part, other_core(part), evec, kept_pixels), rows * D * pixel_count, 1)
    vec_grads = jnp.concatenate([grad_ebias, grad_enc_ga, grad_enc_ba, grad_enc_gb, grad_enc_bb] + late_rows)
    sums, total_squares, loss, vec_sums = reduce_plain(
        dec_grads + [grad_enc_up, grad_enc_down, grad_enc_attn, grad_embed], loss_parts, vec_grads)
    sums = [jnp.stack([jnp.where(core == 0, a, b), jnp.where(core == 0, b, a)]) if at in (0, 4, 8) else a
            for at, a in enumerate(sums) for b in ([other_core(a)] if at in (0, 4, 8) else [a])]
    return sums, total_squares, loss, vec_sums, band_weight


def per_device(
    pixels,
    target,
    band_ids,
    kept_index,
    intersection,
    gsd_scale,
    enc_attn,
    enc_mlp,
    dec_attn,
    dec_mlp,
    patch_embed,
    bridge,
    predict,
    vectors,
    first_enc_attn,
    first_enc_mlp,
    first_dec_attn,
    first_dec_mlp,
    first_patch_embed,
    first_bridge,
    first_predict,
    first_vectors,
    second_enc_attn,
    second_enc_mlp,
    second_dec_attn,
    second_dec_mlp,
    second_patch_embed,
    second_bridge,
    second_predict,
    second_vectors,
    ema_enc_attn,
    ema_enc_mlp,
    ema_patch_embed,
):
    masters = (enc_attn, enc_mlp, dec_attn, dec_mlp, patch_embed, bridge, predict, vectors)
    firsts = (
        first_enc_attn,
        first_enc_mlp,
        first_dec_attn,
        first_dec_mlp,
        first_patch_embed,
        first_bridge,
        first_predict,
        first_vectors,
    )
    seconds = (
        second_enc_attn,
        second_enc_mlp,
        second_dec_attn,
        second_dec_mlp,
        second_patch_embed,
        second_bridge,
        second_predict,
        second_vectors,
    )
    averages = (ema_enc_attn, ema_enc_mlp, ema_patch_embed)
    enc_table, dec_table = sine_table(gsd_scale, D, GRID), sine_table(gsd_scale, E, GRID)
    vec_shard = vectors.shape[0]
    vec_start = lax.axis_index("dp") * vec_shard
    if patch_embed.shape[1] % 16 == 0 and dec_attn.shape[1] % 16 == 0:
        placed = lax.dynamic_update_slice(
            jnp.zeros((24 * 512,), F32), lax.reduce_precision(vectors, 8, 7), (vec_start,)).reshape(24, 512)
        weights, results = forward_all(
            [patch_embed.T, enc_attn, enc_mlp, dec_attn, bridge], (True, False, False, False, True), pixels, band_ids,
            kept_index, intersection, enc_table, placed)
        embed_w, enc_attn_w, enc_mlp_w, dec_attn_w, bridge_w = weights
        x0, *enc_saved, kept_pixels, x1, part, other, totals, enc_flat, evec, row_values, kept_column = results
        band_weight = jnp.sum(totals[24 : 24 + NB], axis=1)
        gye, grad_dec_attn, grad_bridge, sum_predict, sum_up, sum_down, norm, loss_parts, vec_grads = decoder_all(
            x1, part, other, evec, kept_index, kept_column, row_values, dec_table, totals, dec_mlp, predict, target,
            band_ids, dec_attn_w, bridge_w)
        sums, norms, vec_grad = backward_all(
            gye, x1, evec, vec_grads, loss_parts, norm, enc_saved, x0, enc_flat, kept_pixels, enc_mlp_w,
            [grad_dec_attn, grad_bridge], (False, True, False, False, False, True), kept_index.shape[1], DH)
        sums = [sum_predict, sum_up, sum_down] + sums
        total_squares, loss = norms[0, 0], 0.5 * norms[1, 0]
    else:
        sums, total_squares, loss, vec_sums, band_weight = plain_step(
            pixels, target, band_ids, kept_index, intersection, gsd_scale, masters, enc_table, dec_table)
        norms = jnp.broadcast_to(total_squares, (8, 128))
        vec_grad = jnp.concatenate(
            [vec_sums[:7].reshape(-1), vec_sums[7:14, :E].reshape(-1), vec_sums[14, : pixels.shape[1]]])
    vec_grad = lax.dynamic_slice_in_dim(vec_grad.reshape(-1), vec_start, vec_shard)
    grad_norm = jnp.sqrt(total_squares)
    factor = CLIP / jnp.maximum(grad_norm, CLIP)
    order = (7, 5, 6, 3, 1, 2, 8, 4, 0)
    flip = lambda arrays, at: [a.T if number == at else a for number, a in enumerate(arrays)]
    news, new_firsts, new_seconds, means = adam_all(
        norms, [sums[at] for at in order], flip(masters[:7], 4), flip(firsts[:7], 4), flip(seconds[:7], 4),
        flip(averages, 2))
    news, new_firsts, new_seconds, means = flip(news, 4), flip(new_firsts, 4), flip(new_seconds, 4), flip(means, 2)
    vec_new = adam_update(vectors, vec_grad * factor, firsts[7], seconds[7], RATE_VEC, 0.0)
    news, new_firsts, new_seconds = [
        list(many) + [one] for many, one in zip((news, new_firsts, new_seconds), vec_new)]
    ema_attn, ema_mlp, ema_embed = means
    return (
        loss,
        band_weight,
        grad_norm,
        news[0],
        news[1],
        news[2],
        news[3],
        news[4],
        news[5],
        news[6],
        news[7],
        new_firsts[0],
        new_firsts[1],
        new_firsts[2],
        new_firsts[3],
        new_firsts[4],
        new_firsts[5],
        new_firsts[6],
        new_firsts[7],
        new_seconds[0],
        new_seconds[1],
        new_seconds[2],
        new_seconds[3],
        new_seconds[4],
        new_seconds[5],
        new_seconds[6],
        new_seconds[7],
        ema_attn,
        ema_mlp,
        ema_embed,
    )


def solution(mesh):
    return jax.shard_map(
        per_device,
        mesh=mesh,
        in_specs=(
            P("dp", None),
            P("dp", None),
            P("dp", None),
            P("dp", None),
            P("dp", None),
            P("dp"),
            P(None, "dp", "mp"),
            P(None, "dp", "mp"),
            P(None, "dp", "mp"),
            P(None, "dp", "mp"),
            P(None, "dp"),
            P("dp", None),
            P("dp", None),
            P("dp"),
            P(None, "dp", "mp"),
            P(None, "dp", "mp"),
            P(None, "dp", "mp"),
            P(None, "dp", "mp"),
            P(None, "dp"),
            P("dp", None),
            P("dp", None),
            P("dp"),
            P(None, "dp", "mp"),
            P(None, "dp", "mp"),
            P(None, "dp", "mp"),
            P(None, "dp", "mp"),
            P(None, "dp"),
            P("dp", None),
            P("dp", None),
            P("dp"),
            P(None, "dp", "mp"),
            P(None, "dp", "mp"),
            P(None, "dp"),
        ),
        out_specs=(
            P(),
            P(),
            P(),
            P(None, "dp", "mp"),
            P(None, "dp", "mp"),
            P(None, "dp", "mp"),
            P(None, "dp", "mp"),
            P(None, "dp"),
            P("dp", None),
            P("dp", None),
            P("dp"),
            P(None, "dp", "mp"),
            P(None, "dp", "mp"),
            P(None, "dp", "mp"),
            P(None, "dp", "mp"),
            P(None, "dp"),
            P("dp", None),
            P("dp", None),
            P("dp"),
            P(None, "dp", "mp"),
            P(None, "dp", "mp"),
            P(None, "dp", "mp"),
            P(None, "dp", "mp"),
            P(None, "dp"),
            P("dp", None),
            P("dp", None),
            P("dp"),
            P(None, "dp", "mp"),
            P(None, "dp", "mp"),
            P(None, "dp"),
        ),
        check_vma=False,
    )
```

```python
import functools
import math

import jax
import jax.numpy as jnp
from jax import lax
from jax.experimental import pallas as pl
from jax.experimental.pallas import tpu as pltpu
from jax.sharding import PartitionSpec as P

D = 1024
DH = 64
E = 512
DDH = 32
GRID = 16
NB = 3
STEP = 10


EPS_LN = 1e-06
EPS_C = 0.01
CLIP = 0.0002
BETA_ONE = 0.9
BETA_TWO = 0.999
ADAM_EPS = 1e-12
RATE_MAT = 0.06
RATE_VEC = 0.5
DECAY_MAT = 0.05
EMA_KEEP = 0.9
REF_GSD = 4.0


def split_vectors(flat_vec, enc_width, dec_width):
    lengths = [enc_width] * 7 + [dec_width] * 7
    pieces = []
    offset = 0
    for length in lengths:
        pieces.append(flat_vec[offset : offset + length])
        offset = offset + length
    pieces.append(flat_vec[offset:])
    return pieces


F32 = jnp.float32
BF16 = jnp.bfloat16
VMEM_LIMIT = 58 * 2**20
GELU_C = math.sqrt(2.0 / math.pi)


def dot_nn(left, right):
    return jnp.dot(left, right, preferred_element_type=F32)


def dot_nt(left, right):
    return lax.dot_general(left, right, (((1,), (1,)), ((), ())), preferred_element_type=F32)


def dot_tn(left, right):
    return lax.dot_general(left, right, (((0,), (0,)), ((), ())), preferred_element_type=F32)


def dot_exact(left, right):
    return jnp.dot(left, right, preferred_element_type=F32, precision=lax.Precision.HIGHEST)


def normalize(rows):
    centred = rows - jnp.mean(rows, axis=-1, keepdims=True)
    rstd = lax.rsqrt(jnp.mean(centred * centred, axis=-1, keepdims=True) + EPS_LN)
    return centred * rstd, rstd


def norm_back(grad, gain, unit, rstd):
    scaled = grad * gain
    mean_one = jnp.mean(scaled, axis=-1, keepdims=True)
    mean_two = jnp.mean(scaled * unit, axis=-1, keepdims=True)
    grad_in = rstd * (scaled - mean_one - unit * mean_two)
    return (
        grad_in,
        jnp.sum(grad * unit, axis=0, keepdims=True),
        jnp.sum(grad, axis=0, keepdims=True),
    )


def both(mine_ref, other_ref, rows):
    return mine_ref[rows, :].astype(F32) + other_ref[rows, :].astype(F32)


def gelu_parts(up):
    square = up * up
    bent = jnp.tanh(GELU_C * up * (1.0 + 0.044715 * square))
    half = 0.5 * (1.0 + bent)
    return square, bent, half


def group_mask(group, length):
    if group == length:
        return None
    row_image = lax.broadcasted_iota(jnp.int32, (group, group), 0) // length
    col_image = lax.broadcasted_iota(jnp.int32, (group, group), 1) // length
    return row_image == col_image


LOG2E = math.log2(math.e)


def attend(qkv_ref, mixed_ref, lse_ref, cols, width, head_dim, mask):
    scale = head_dim ** (-0.5) * LOG2E
    for head in range(width // head_dim):
        at = pl.ds(head * head_dim, head_dim)
        queries = qkv_ref[at, cols]
        keys = qkv_ref[pl.ds(width + head * head_dim, head_dim), cols]
        values = qkv_ref[pl.ds(2 * width + head * head_dim, head_dim), cols]
        scores = dot_tn(keys, queries)
        if mask is not None:
            scores = jnp.where(mask, scores, -1e30)
        top = jnp.max(scores, axis=0, keepdims=True)
        weights = jnp.exp2((scores - top) * scale)
        total = jnp.sum(weights, axis=0, keepdims=True)
        lse_ref[pl.ds(head, 1), cols] = top * scale + jnp.log2(total)
        mixed_ref[at, cols] = (dot_nn(values, weights.astype(BF16)) * (1.0 / total)).astype(BF16)


def attend_back(qkv_ref, grad_ref, lse_ref, out_ref, cols, out_cols, width, head_dim, mask):
    scale = head_dim ** (-0.5)
    for head in range(width // head_dim):
        at = pl.ds(head * head_dim, head_dim)
        at_k = pl.ds(width + head * head_dim, head_dim)
        at_v = pl.ds(2 * width + head * head_dim, head_dim)
        queries, keys, values = qkv_ref[at, cols], qkv_ref[at_k, cols], qkv_ref[at_v, cols]
        grad = grad_ref[at, :]
        scores = dot_tn(keys, queries)
        if mask is not None:
            scores = jnp.where(mask, scores, -1e30)
        soft = jnp.exp2(scores * (scale * LOG2E) - lse_ref[pl.ds(head, 1), cols])
        out_ref[at_v, out_cols] = dot_nt(grad, soft.astype(BF16)).astype(BF16)
        grad_soft = dot_tn(values, grad)
        inner = jnp.sum(soft * grad_soft, axis=0, keepdims=True)
        grad_scores = (soft * (grad_soft - inner)).astype(BF16)
        out_ref[at, out_cols] = (dot_nn(keys, grad_scores) * scale).astype(BF16)
        out_ref[at_k, out_cols] = (dot_nt(queries, grad_scores) * scale).astype(BF16)


def transposed_weights(attn_ref, flat_ref):
    width = attn_ref.shape[1] // 4
    for part in range(4):
        at = pl.ds(part * width, width)
        flat_ref[at, :] = attn_ref[:, at].T


def attention_rows(unit, vec_ref, flat_ref, qkv_ref, mixed_ref, lse_ref, part_ref, rows, head_dim, mask, attn_ref):
    width = mixed_ref.shape[0]
    low = (unit * vec_ref[1:2, :] + vec_ref[2:3, :]).astype(BF16)
    qkv_ref[:, rows] = dot_nt(flat_ref[: 3 * width, :], low).astype(BF16)
    attend(qkv_ref, mixed_ref, lse_ref, rows, width, head_dim, mask)
    part_ref[rows, :] = dot_nt(mixed_ref[:, rows].T, attn_ref[:, 3 * width :]).astype(BF16)


def enc_in_kernel(length, group, head_dim, pix_ref, kept_ref, table_ref, embed_ref, vec_ref, attn_ref,
                  x_ref, qkv_ref, mixed_ref, lse_ref, part_ref, pixk_ref, flat_ref):
    images, patches = table_ref.shape[0], pix_ref.shape[0] // table_ref.shape[0]
    side = table_ref.shape[1]
    transposed_weights(attn_ref, flat_ref)

    def pick(image, carry):
        rows = pl.ds(image * length, length)
        index = kept_ref[rows, :]
        hot = lax.broadcasted_iota(jnp.int32, (length, patches), 1) == index
        pixels = pix_ref[pl.ds(image * patches, patches), :]
        pixk_ref[rows, :] = dot_nn(hot.astype(BF16), pixels).astype(BF16)
        grid_at = lax.broadcasted_iota(jnp.int32, (length, side), 1)
        table = table_ref[image]
        half = table.shape[1]
        x_ref[rows, :half] = dot_exact((grid_at == index // side).astype(F32), table)
        x_ref[rows, half:] = dot_exact((grid_at == index % side).astype(F32), table)
        return carry

    lax.fori_loop(0, images, pick, 0)
    mask = group_mask(group, length)

    def step(number, carry):
        rows = pl.ds(pl.multiple_of(number * group, group), group)
        share = embed_ref.shape[2]
        rows_x = dot_nt(pixk_ref[rows, :share], embed_ref[0]) + dot_nt(pixk_ref[rows, share:], embed_ref[1])
        rows_x = rows_x + vec_ref[0:1, :] + x_ref[rows, :]
        x_ref[rows, :] = rows_x
        unit, _ = normalize(rows_x)
        attention_rows(unit, vec_ref, flat_ref, qkv_ref, mixed_ref, lse_ref, part_ref, rows, head_dim, mask, attn_ref)
        return carry

    lax.fori_loop(0, x_ref.shape[0] // group, step, 0)


def dec_in_kernel(length, head_dim, x1_ref, mine_ref, other_ref, evec_ref, bridge_ref, kept_ref, hidden_ref,
                  table_ref, vec_ref, attn_ref,
                  x2_ref, final_ref, x_ref, qkv_ref, mixed_ref, lse_ref, part_ref, flat_ref, latent_ref):
    images, side, half = table_ref.shape
    patches = side * side
    transposed_weights(attn_ref, flat_ref)
    every = pl.ds(0, x1_ref.shape[0])
    out = x1_ref[...] + both(mine_ref, other_ref, every)
    x2_ref[...] = out
    unit, _ = normalize(out)
    final = (unit * evec_ref[5:6, :] + evec_ref[6:7, :]).astype(BF16)
    final_ref[...] = final
    share = bridge_ref.shape[2]
    latent_ref[:, :share] = dot_nn(final, bridge_ref[0])
    latent_ref[:, share:] = dot_nn(final, bridge_ref[1])

    def step(image, carry):
        rows = pl.ds(pl.multiple_of(image * patches, patches), patches)
        hot = lax.broadcasted_iota(jnp.int32, (patches, length), 0) == kept_ref[pl.ds(image, 1), :]
        latent = latent_ref[pl.ds(image * length, length), :]
        table = table_ref[image]
        by_row = jnp.broadcast_to(table[:, None, :], (side, side, half)).reshape(patches, half)
        by_col = jnp.broadcast_to(table[None, :, :], (side, side, half)).reshape(patches, half)
        place = jnp.concatenate([by_row, by_col], axis=1)
        rows_x = dot_exact(hot.astype(F32), latent) + hidden_ref[rows, :] * vec_ref[0:1, :] + place
        x_ref[rows, :] = rows_x
        unit, _ = normalize(rows_x)
        attention_rows(unit, vec_ref, flat_ref, qkv_ref, mixed_ref, lse_ref, part_ref, rows, head_dim, None, attn_ref)
        return carry

    lax.fori_loop(0, images, step, 0)


def mlp_kernel(tile, x_ref, mine_ref, other_ref, vec_ref, up_ref, down_ref, x1_ref, part_ref, low_ref, acc_ref):
    number = pl.program_id(0)
    count = x_ref.shape[0] // tile

    def first(step, carry):
        rows = pl.ds(pl.multiple_of(step * tile, tile), tile)
        after = x_ref[rows, :] + both(mine_ref, other_ref, rows)
        x1_ref[rows, :] = after
        unit, _ = normalize(after)
        low_ref[rows, :] = (unit * vec_ref[3:4, :] + vec_ref[4:5, :]).astype(BF16)
        return carry

    @pl.when(number == 0)
    def _():
        lax.fori_loop(0, count, first, 0)
        acc_ref[...] = jnp.zeros_like(acc_ref)

    def step(piece, carry):
        rows = pl.ds(pl.multiple_of(piece * tile, tile), tile)
        up = dot_nn(low_ref[rows, :], up_ref[...])
        _, _, half = gelu_parts(up)
        acc_ref[rows, :] += dot_nt((up * half).astype(BF16), down_ref[...])
        return carry

    lax.fori_loop(0, count, step, 0)

    @pl.when(number == pl.num_programs(0) - 1)
    def _():
        part_ref[...] = acc_ref[...].astype(BF16)


def head_kernel(core_ref, inverse_ref, x1_ref, mine_ref, other_ref, vec_ref, bias_ref, predict_ref, target_ref,
                band_ref, weight_ref, gy_ref, glow_ref, gbias_ref, loss_ref, gain_ref, shift_ref, low_ref, gpred_ref):
    number = pl.program_id(0)

    @pl.when(number == 0)
    def _():
        for ref in (gpred_ref, gbias_ref, loss_ref, gain_ref, shift_ref):
            ref[...] = jnp.zeros_like(ref)

    every = pl.ds(0, x1_ref.shape[0])
    unit, rstd = normalize(x1_ref[...] + both(mine_ref, other_ref, every))
    gain = vec_ref[5:6, :]
    final = (unit * gain + vec_ref[6:7, :]).astype(BF16)
    share = gpred_ref.shape[1]
    predicted = jnp.concatenate([dot_nn(final, predict_ref[0]), dot_nn(final, predict_ref[1])], axis=1)
    mismatch = predicted + bias_ref[...] - target_ref[...].astype(F32)
    band = band_ref[...]
    level = jnp.where(band == 0, inverse_ref[0], jnp.where(band == 1, inverse_ref[1], inverse_ref[2]))
    level = level * weight_ref[...]
    square = mismatch * mismatch + EPS_C
    root = lax.rsqrt(square)
    loss_ref[...] += jnp.sum(level * (square * root), axis=0, keepdims=True)
    grad = level * (mismatch * root)
    gbias_ref[...] += jnp.sum(grad, axis=0, keepdims=True)
    low_ref[...] = grad.astype(BF16)
    columns = pl.ds(pl.multiple_of(core_ref[0] * share, share), share)
    gpred_ref[...] += dot_tn(final, low_ref[:, columns])
    grad_final = dot_nt(low_ref[:, :share], predict_ref[0]) + dot_nt(low_ref[:, share:], predict_ref[1])
    grad_in, gain_sum, shift_sum = norm_back(grad_final, gain, unit, rstd)
    gy_ref[...] = grad_in
    gain_ref[...] += gain_sum
    shift_ref[...] += shift_sum

    @pl.when(number == pl.num_programs(0) - 1)
    def _():
        glow_ref[...] = gpred_ref[...].astype(BF16)


def mlp_back_kernel(tile, gy_ref, x1_ref, vec_ref, up_ref, down_ref, gup_ref, gdown_ref, part_ref,
                    low_ref, lowt_ref, grad_ref, gradt_ref, gu_ref, z_ref, acc_ref):
    number = pl.program_id(0)
    count = x1_ref.shape[0] // tile

    def first(step, carry):
        rows = pl.ds(pl.multiple_of(step * tile, tile), tile)
        unit, _ = normalize(x1_ref[rows, :])
        low = (unit * vec_ref[3:4, :] + vec_ref[4:5, :]).astype(BF16)
        low_ref[rows, :] = low
        lowt_ref[:, rows] = low.T
        grad = gy_ref[rows, :].astype(BF16)
        grad_ref[rows, :] = grad
        gradt_ref[:, rows] = grad.T
        return carry

    @pl.when(number == 0)
    def _():
        lax.fori_loop(0, count, first, 0)
        acc_ref[...] = jnp.zeros_like(acc_ref)

    def step(piece, carry):
        rows = pl.ds(pl.multiple_of(piece * tile, tile), tile)
        up = dot_nn(low_ref[rows, :], up_ref[...])
        square, bent, half = gelu_parts(up)
        z_ref[rows, :] = (up * half).astype(BF16)
        slope = half + (0.5 * GELU_C) * up * (1.0 - bent * bent) * (1.0 + (3.0 * 0.044715) * square)
        grad_up = (dot_nn(grad_ref[rows, :], down_ref[...]) * slope).astype(BF16)
        gu_ref[rows, :] = grad_up
        acc_ref[rows, :] += dot_nt(grad_up, up_ref[...])
        return carry

    lax.fori_loop(0, count, step, 0)
    gup_ref[...] = dot_nn(lowt_ref[...], gu_ref[...]).astype(BF16)
    gdown_ref[...] = dot_nn(gradt_ref[...], z_ref[...]).astype(BF16)

    @pl.when(number == pl.num_programs(0) - 1)
    def _():
        part_ref[...] = acc_ref[...].astype(BF16)


def attn_back_kernel(length, group, head_dim, gy_ref, x1_ref, mine_ref, other_ref, x_ref, qkv_ref, mixed_ref, lse_ref,
                     vec_ref, attn_ref, gx_ref, grad_ref, gain_ref, shift_ref, part_ref,
                     flat_ref, lowt_ref, gradt_ref, gmix_ref, gqkv_ref):
    width = mixed_ref.shape[0]
    transposed_weights(attn_ref, flat_ref)
    gain_ref[...] = jnp.zeros_like(gain_ref)
    shift_ref[...] = jnp.zeros_like(shift_ref)
    mask = group_mask(group, length)

    def step(number, carry):
        rows = pl.ds(pl.multiple_of(number * group, group), group)
        unit, rstd = normalize(x1_ref[rows, :])
        grad_in, gain_sum, shift_sum = norm_back(both(mine_ref, other_ref, rows), vec_ref[3:4, :], unit, rstd)
        grad_in = grad_in + gy_ref[rows, :]
        gx_ref[rows, :] = grad_in
        gain_ref[...] += gain_sum
        shift_ref[...] += shift_sum
        low_grad = grad_in.astype(BF16)
        gradt_ref[:, rows] = low_grad.T
        gmix_ref[...] = dot_nt(flat_ref[3 * width :, :], low_grad).astype(BF16)
        attend_back(qkv_ref, gmix_ref, lse_ref, gqkv_ref, rows, rows, width, head_dim, mask)
        part_ref[rows, :] = dot_nn(gqkv_ref[:, rows].T, flat_ref[: 3 * width, :]).astype(BF16)
        unit_a, _ = normalize(x_ref[rows, :])
        lowt_ref[:, rows] = (unit_a * vec_ref[1:2, :] + vec_ref[2:3, :]).astype(BF16).T
        return carry

    lax.fori_loop(0, x_ref.shape[0] // group, step, 0)
    grad_ref[:, : 3 * width] = dot_nt(lowt_ref[...], gqkv_ref[...]).astype(BF16)
    grad_ref[:, 3 * width :] = dot_nt(gradt_ref[...], mixed_ref[...]).astype(BF16)


def between_kernel(length, core_ref, gx_ref, x_ref, mine_ref, other_ref, vec_ref, kept_ref, hidden_ref, final_ref, x2_ref,
                   evec_ref, bridge_ref, gain_ref, shift_ref, mask_ref, gbridge_ref, egain_ref, eshift_ref, gy_ref,
                   latent_ref):
    images = kept_ref.shape[0] // length
    patches = x_ref.shape[0] // images
    for ref in (gain_ref, shift_ref, mask_ref):
        ref[...] = jnp.zeros_like(ref)

    def step(image, carry):
        rows = pl.ds(pl.multiple_of(image * patches, patches), patches)
        unit, rstd = normalize(x_ref[rows, :])
        grad_in, gain_sum, shift_sum = norm_back(both(mine_ref, other_ref, rows), vec_ref[1:2, :], unit, rstd)
        grad_in = grad_in + gx_ref[rows, :]
        gain_ref[...] += gain_sum
        shift_ref[...] += shift_sum
        mask_ref[...] += jnp.sum(grad_in * hidden_ref[rows, :], axis=0, keepdims=True)
        kept_rows = pl.ds(pl.multiple_of(image * length, length), length)
        hot = lax.broadcasted_iota(jnp.int32, (length, patches), 1) == kept_ref[kept_rows, :]
        latent_ref[kept_rows, :] = dot_nn(hot.astype(BF16), grad_in.astype(BF16)).astype(BF16)
        return carry

    lax.fori_loop(0, images, step, 0)
    share = gbridge_ref.shape[1]
    columns = pl.ds(pl.multiple_of(core_ref[0] * share, share), share)
    gbridge_ref[...] = dot_tn(final_ref[...], latent_ref[:, columns]).astype(BF16)
    grad_final = dot_nt(latent_ref[:, :share], bridge_ref[0]) + dot_nt(latent_ref[:, share:], bridge_ref[1])
    unit, rstd = normalize(x2_ref[...])
    gy_ref[...], egain_ref[...], eshift_ref[...] = norm_back(grad_final, evec_ref[5:6, :], unit, rstd)


def enc_out_kernel(core_ref, gx_ref, x_ref, mine_ref, other_ref, vec_ref, pixk_ref,
                   gain_ref, shift_ref, ebias_ref, gembed_ref):
    every = pl.ds(0, x_ref.shape[0])
    unit, rstd = normalize(x_ref[...])
    grad_in, gain_ref[...], shift_ref[...] = norm_back(both(mine_ref, other_ref, every), vec_ref[1:2, :], unit, rstd)
    grad_in = grad_in + gx_ref[...]
    ebias_ref[...] = jnp.sum(grad_in, axis=0, keepdims=True)
    share = gembed_ref.shape[1]
    columns = pl.ds(pl.multiple_of(core_ref[0] * share, share), share)
    gembed_ref[...] = dot_tn(grad_in.astype(BF16), pixk_ref[:, columns]).astype(BF16)


def shape(dims, dtype):
    return jax.ShapeDtypeStruct(dims, dtype)


def run(kernel, outs, scratch, args, flops, scalars=0):
    moved = sum(math.prod(a.shape) * a.dtype.itemsize for a in list(args) + list(outs))
    in_vmem = pl.BlockSpec(memory_space=pltpu.VMEM)
    return pl.pallas_call(
        kernel,
        out_shape=tuple(outs),
        in_specs=[pl.BlockSpec(memory_space=pltpu.SMEM)] * scalars + [in_vmem] * (len(args) - scalars),
        out_specs=tuple([in_vmem] * len(outs)),
        scratch_shapes=scratch,
        compiler_params=pltpu.CompilerParams(vmem_limit_bytes=VMEM_LIMIT),
        cost_estimate=pl.CostEstimate(flops=flops, bytes_accessed=moved, transcendentals=0),
    )(*args)


def other_core(block):
    return lax.ppermute(block, "mp", [(0, 1), (1, 0)])


def mlp_forward(x, mine, vec, stack):
    rows, width = x.shape
    hidden = stack.shape[1] // 2
    block = min(hidden, 512)
    tile = min(rows, 512)
    other = other_core(mine)
    whole = pl.BlockSpec((rows, width), lambda i: (0, 0))
    cols = pl.BlockSpec((width, block), lambda i: (0, i))
    later = pl.BlockSpec((width, block), lambda i: (0, i + hidden // block))
    return pl.pallas_call(
        functools.partial(mlp_kernel, tile),
        out_shape=(shape((rows, width), F32), shape((rows, width), BF16)),
        grid=(hidden // block,),
        in_specs=[whole] * 3 + [pl.BlockSpec((8, width), lambda i: (0, 0)), cols, later],
        out_specs=(whole, whole),
        scratch_shapes=[pltpu.VMEM((rows, width), BF16), pltpu.VMEM((rows, width), F32)],
        compiler_params=pltpu.CompilerParams(vmem_limit_bytes=VMEM_LIMIT),
        cost_estimate=pl.CostEstimate(flops=4 * rows * width * hidden, bytes_accessed=rows * width * 14 + width * hidden * 4,
                                      transcendentals=rows * hidden),
    )(x, mine, other, vec, stack, stack)


def mlp_backward(gy, x1, vec, stack):
    rows, width = x1.shape
    hidden = stack.shape[1] // 2
    block = min(hidden, 512)
    tile = min(rows, 256)
    whole = pl.BlockSpec((rows, width), lambda i: (0, 0))
    cols = pl.BlockSpec((width, block), lambda i: (0, i))
    later = pl.BlockSpec((width, block), lambda i: (0, i + hidden // block))
    return pl.pallas_call(
        functools.partial(mlp_back_kernel, tile),
        out_shape=(shape((width, hidden), BF16), shape((width, hidden), BF16), shape((rows, width), BF16)),
        grid=(hidden // block,),
        in_specs=[whole] * 2 + [pl.BlockSpec((8, width), lambda i: (0, 0)), cols, later],
        out_specs=(cols, cols, whole),
        scratch_shapes=[
            pltpu.VMEM((rows, width), BF16), pltpu.VMEM((width, rows), BF16),
            pltpu.VMEM((rows, width), BF16), pltpu.VMEM((width, rows), BF16),
            pltpu.VMEM((rows, block), BF16), pltpu.VMEM((rows, block), BF16),
            pltpu.VMEM((rows, width), F32)],
        compiler_params=pltpu.CompilerParams(vmem_limit_bytes=VMEM_LIMIT),
        cost_estimate=pl.CostEstimate(flops=10 * rows * width * hidden, bytes_accessed=rows * width * 10 + width * hidden * 8,
                                      transcendentals=rows * hidden),
    )(gy, x1, vec, stack, stack)


def head(core, inverse, x1, mine, vec, bias, predict, target, band, weight, patches):
    rows, width = x1.shape
    pixels = target.shape[1]
    share = pixels // 2
    other = other_core(mine)
    smem = pl.BlockSpec(memory_space=pltpu.SMEM)
    row_w = pl.BlockSpec((patches, width), lambda i: (i, 0))
    row_p = pl.BlockSpec((patches, pixels), lambda i: (i, 0))
    fix = lambda a, b: pl.BlockSpec((a, b), lambda i: (0, 0))
    return pl.pallas_call(
        head_kernel,
        out_shape=(shape((rows, width), F32), shape((width, share), BF16), shape((1, pixels), F32),
                   shape((1, pixels), F32), shape((1, width), F32), shape((1, width), F32)),
        grid=(rows // patches,),
        in_specs=[smem, smem, row_w, row_w, row_w, fix(8, width), fix(1, pixels), pl.BlockSpec((2, width, share), lambda i: (0, 0, 0)), row_p, row_p,
                  pl.BlockSpec((patches, 1), lambda i: (i, 0))],
        out_specs=(row_w, fix(width, share), fix(1, pixels), fix(1, pixels), fix(1, width), fix(1, width)),
        scratch_shapes=[pltpu.VMEM((patches, pixels), BF16), pltpu.VMEM((width, share), F32)],
        compiler_params=pltpu.CompilerParams(vmem_limit_bytes=VMEM_LIMIT),
        cost_estimate=pl.CostEstimate(flops=5 * rows * width * pixels, bytes_accessed=rows * (width * 12 + pixels * 6),
                                      transcendentals=rows * pixels),
    )(core, inverse, x1, mine, other, vec, bias, predict, target, band, weight)


def attn_backward(gy, x1, mine, x, saved, vec, attn, length, group, head_dim):
    qkv, mixed, lse = saved
    rows, width = x.shape
    local = mixed.shape[0]
    return run(
        functools.partial(attn_back_kernel, length, group, head_dim),
        [shape((rows, width), F32), shape((width, 4 * local), BF16),
         shape((1, width), F32), shape((1, width), F32), shape((rows, width), BF16)],
        [pltpu.VMEM((4 * local, width), BF16), pltpu.VMEM((width, rows), BF16), pltpu.VMEM((width, rows), BF16),
         pltpu.VMEM((local, group), BF16), pltpu.VMEM((3 * local, rows), BF16)],
        (gy, x1, mine, other_core(mine), x, qkv, mixed, lse, vec, attn),
        18 * rows * width * local)


def sine_table(gsd_values, feature_width, grid_side):
    quarter = feature_width // 4
    frequency = jnp.exp(-jnp.log(10000.0) * jnp.arange(quarter).astype(F32) / quarter)
    gsd_ratio = gsd_values.astype(F32)[:, None, None] / REF_GSD
    line = jnp.arange(grid_side, dtype=jnp.int32).astype(F32)
    arg = line[None, :, None] * gsd_ratio * frequency
    return jnp.concatenate([jnp.sin(arg), jnp.cos(arg)], axis=-1)


def dp_bits():
    return lax.axis_size("dp").bit_length() - 1


def orders():
    bits = dp_bits()
    high = list(range(bits - 1, 1, -1))
    return (high + [0, 1], high + [1, 0])


def swap(block, bit):
    size = lax.axis_size("dp")
    return lax.ppermute(block, "dp", [(i, i ^ (1 << bit)) for i in range(size)])


def my_bit(bit):
    return (lax.axis_index("dp") >> bit) & 1


def gather_dp(block, axis, order):
    lead, rest = (block.shape[:axis], block.shape[axis:])
    done = []
    cur = block
    for bit in order:
        other = swap(cur, bit)
        mine = my_bit(bit) == 1
        place = axis + sum(1 for b in done if b > bit)
        cur = jnp.stack([jnp.where(mine, other, cur), jnp.where(mine, cur, other)], axis=place)
        done.append(bit)
    return cur.reshape(lead + (rest[0] * lax.axis_size("dp"),) + rest[1:])


def reduce_dp(block, axis, order, wire):
    bits = dp_bits()
    lead, rest = (block.shape[:axis], block.shape[axis:])
    shard = rest[0] // lax.axis_size("dp")
    cur = block.reshape(lead + (2,) * bits + (shard,) + rest[1:])
    left = list(range(bits - 1, -1, -1))
    for bit in reversed(order):
        place = axis + left.index(bit)
        mine = my_bit(bit)
        keep = lax.dynamic_index_in_dim(cur, mine, place, keepdims=False)
        give = lax.dynamic_index_in_dim(cur, 1 - mine, place, keepdims=False)
        other = swap(give.astype(wire), bit)
        cur = keep.astype(F32) + other.astype(F32)
        left.remove(bit)
    return cur


def join_cores(mine, core):
    other = other_core(mine)
    return jnp.concatenate([jnp.where(core == 0, mine, other), jnp.where(core == 0, other, mine)], axis=1)


def total_dp(value):
    for bit in range(dp_bits()):
        value = value + swap(value, bit)
    return value


def place_of():
    index = lax.axis_index("dp")
    core = lax.axis_index("mp")
    low, high = lax.rem(index, 4), index // 4
    bit_x, bit_y = lax.rem(low, 2), low // 2
    low_x, low_y = low + 1 - 2 * bit_x, low + 2 - 4 * bit_y
    return core, low, high, low_x, low_y


def greet(partners):
    barrier = pltpu.get_barrier_semaphore()
    for partner in partners:
        pl.semaphore_signal(barrier, inc=1, device_id=partner, device_id_type=pl.DeviceIdType.MESH)
    pl.semaphore_wait(barrier, len(partners))


def blocks_of(widths, limit, fine=()):
    found = []
    for number, width in enumerate(widths):
        start = 0
        while start < width:
            size = min(limit // 2 if number in fine else limit, width - start)
            found.append((number, start, size))
            start += size
    return found


def remote(source, target, send, receive, device):
    return pltpu.make_async_remote_copy(
        src_ref=source, dst_ref=target, send_sem=send, recv_sem=receive,
        device_id=device, device_id_type=pl.DeviceIdType.MESH)


def total_blocks(block_ref, near_ref, far_ref, sems, low, high, core, highs, stage):
    send, receive = sems
    if stage == 0:
        spots = [(high * 4 + lax.rem(low + k, 4), core) for k in range(1, 4)]
        return [remote(block_ref, near_ref.at[low], send.at[k], receive.at[k], spots[k]) for k in range(3)]
    spots = [(lax.rem(high + k, highs) * 4 + low, core) for k in range(1, highs)]
    return [remote(block_ref, far_ref.at[high], send.at[3 + k], receive.at[3 + k], spots[k]) for k in range(highs - 1)]


def forward_kernel(highs, shared, groups, count, length, group, head_dim, *refs):
    masters, refs = refs[:count], refs[count:]
    pix_any, band_ref, kept_ref, inter_ref, table_ref, placed_ref = refs[:6]
    fulls, refs = refs[6 : 6 + count], refs[6 + count :]
    (x_ref, qkv_ref, mixed_ref, lse_ref, pixk_ref, x1_ref, last_ref, far_out_ref, counts_ref, flat_ref, vec_ref, rows_ref,
     column_ref) = refs[:13]
    refs = refs[13:]
    shards, refs = refs[:count], refs[count:]
    (pix_ref, bands_v, embed_v, attn_v, mlp_v, part_ref, other_ref, low_ref, acc_ref, block_ref, near_ref,
     far_ref) = refs[:12]
    (own_sem, zs_sem, zr_sem, cs_sem, cr_sem, fs_sem, fr_sem, ms_sem, mr_sem, load_sem, xs_sem, xr_sem, ts_sem,
     tr_sem, mload_sem) = refs[12:]
    core, low, high, low_x, low_y = place_of()
    at_x, at_y = (high * 4 + low_x, core), (high * 4 + low_y, core)
    at_high = [(lax.rem(high + k, highs) * 4 + low, core) for k in range(1, highs)]
    sibling = (high * 4 + low, 1 - core)
    near = [(high * 4 + lax.rem(low + k, 4), core) for k in range(1, 4)]
    greet([sibling] + near + at_high)
    for master, shard, split in zip(masters, shards, shared):
        if len(master.shape) == 3:
            wide = master.shape[2]
            for part in range(master.shape[0]):
                shard[:, part * wide : (part + 1) * wide] = master[part].astype(BF16)
        else:
            share = shard.shape[1]
            shard[...] = master[:, pl.ds(pl.multiple_of(core * share, share), share)].astype(BF16)

    def full(at):
        number, start, size = groups[at]
        ref = fulls[number].at[core] if shared[number] else fulls[number]
        return ref, pl.ds(start, size)

    def first(at):
        ref, cols = full(at)
        shard = shards[groups[at][0]].at[:, cols]
        mine = ref.at[high, low, :, cols]
        copies = [pltpu.make_async_copy(shard, mine, own_sem.at[at])]
        for k in range(1, highs):
            copies.append(remote(shard, mine, zs_sem.at[at, k - 1], zr_sem.at[at, k - 1], at_high[k - 1]))
        return copies

    def column(at):
        ref, cols = full(at)
        part = ref.at[:, low, :, cols]
        return [remote(part, part, cs_sem.at[at, 0], cr_sem.at[at, 0], at_x),
                remote(part, part, cs_sem.at[at, 1], cr_sem.at[at, 1], at_y)]

    def forward(at):
        ref, cols = full(at)
        which, device = (low_x, at_y) if at % 2 == 0 else (low_y, at_x)
        part = ref.at[:, which, :, cols]
        return remote(part, part, fs_sem.at[at], fr_sem.at[at], device)

    def swap(number):
        part = fulls[number].at[core]
        return remote(part, part, ms_sem.at[number], mr_sem.at[number], sibling)

    def exchange(at, source, target):
        return remote(source, target, xs_sem.at[at], xr_sem.at[at], sibling)

    total = len(groups)
    pairs = (total + 1) // 2
    in_pair = lambda pair: [at for at in (2 * pair, 2 * pair + 1) if at < total]
    pair_of = lambda number: max(at for at in range(total) if groups[at][0] == number) // 2
    images, side = table_ref.shape[0], table_ref.shape[1]
    patches = side * side
    width = mixed_ref.shape[0]
    mask = group_mask(group, length)

    def lane_of(image, flipped):
        lanes = lax.broadcasted_iota(jnp.int32, flipped.shape, 1)
        return jnp.sum(jnp.where(lanes == image, flipped, 0.0), axis=1, keepdims=True)

    def pick(image, carry):
        rows = pl.ds(pl.multiple_of(image * length, length), length)
        index = lane_of(image, kept_ref[...].astype(F32).T).astype(jnp.int32)
        column_ref[rows, :] = index
        hot = lax.broadcasted_iota(jnp.int32, (length, patches), 1) == index
        pixels = pix_ref[pl.ds(pl.multiple_of(image * patches, patches), patches), :]
        pixk_ref[rows, :] = dot_nn(hot.astype(BF16), pixels).astype(BF16)
        grid_at = lax.broadcasted_iota(jnp.int32, (length, side), 1)
        table = table_ref[image]
        half = table.shape[1]
        x_ref[rows, :half] = dot_exact((grid_at == index // side).astype(F32), table)
        x_ref[rows, half:] = dot_exact((grid_at == index % side).astype(F32), table)
        return carry

    def tally(image, carry):
        rows = pl.ds(pl.multiple_of(image * patches, patches), patches)
        hot = lax.broadcasted_iota(jnp.int32, (patches, length), 0) == kept_ref[pl.ds(image, 1), :]
        hidden = 1.0 - jnp.max(jnp.where(hot, 1.0, 0.0), axis=1, keepdims=True)
        weight = hidden * (1.0 - 0.5 * lane_of(image, inter_ref[...].astype(F32).T))
        rows_ref[rows, 0:1] = hidden
        rows_ref[rows, 1:2] = weight
        band = bands_v[rows, :]
        for level in range(NB):
            row = jnp.sum(jnp.where(band == level, weight, 0.0), axis=0, keepdims=True)
            for start in range(0, row.shape[1], 128):
                block_ref[24 + level : 25 + level, 0:128] += row[:, start : start + 128]
        return carry

    def rows_step(number, carry):
        rows = pl.ds(pl.multiple_of(number * group, group), group)
        share = embed_v.shape[-1]
        embed = lambda half: embed_v[half].reshape(-1, share)
        rows_x = dot_nt(pixk_ref[rows, :share], embed(0)) + dot_nt(pixk_ref[rows, share:], embed(1))
        rows_x = rows_x + vec_ref[0:1, :] + x_ref[rows, :]
        x_ref[rows, :] = rows_x
        unit, _ = normalize(rows_x)
        low_a = (unit * vec_ref[1:2, :] + vec_ref[2:3, :]).astype(BF16)
        qkv_ref[:, rows] = dot_nt(flat_ref[: 3 * width, :], low_a).astype(BF16)
        attend(qkv_ref, mixed_ref, lse_ref, rows, width, head_dim, mask)
        part_ref[rows, :] = dot_nn(mixed_ref[:, rows].T, flat_ref[3 * width :, :]).astype(BF16)
        return carry

    def mlp_first():
        after = x_ref[...] + both(part_ref, other_ref, pl.ds(0, x_ref.shape[0]))
        x1_ref[...] = after
        unit, _ = normalize(after)
        low_ref[...] = (unit * vec_ref[3:4, :] + vec_ref[4:5, :]).astype(BF16)
        acc_ref[...] = jnp.zeros_like(acc_ref)

    def mlp_block(piece, carry):
        size = 512
        hidden = mlp_v.shape[-1] // 2
        start = piece * size
        wide = x_ref.shape[1]
        up = dot_nn(low_ref[...], mlp_v[:, :, :, pl.ds(start, size)].reshape(wide, size))
        _, _, half = gelu_parts(up)
        down = mlp_v[:, :, :, pl.ds(hidden + start, size)].reshape(wide, size)
        acc_ref[...] += dot_nt((up * half).astype(BF16), down)
        return carry

    load_bands = pltpu.make_async_copy(band_ref, bands_v, load_sem.at[0])
    load_pixels = pltpu.make_async_copy(pix_any, pix_ref, load_sem.at[4])
    load_attn = pltpu.make_async_copy(fulls[1], attn_v, load_sem.at[1])
    load_embed = pltpu.make_async_copy(fulls[0], embed_v, load_sem.at[2])

    def load_mlp(at):
        cols = pl.ds(groups[at][1], groups[at][2])
        return pltpu.make_async_copy(fulls[2].at[:, :, :, cols], mlp_v.at[:, :, :, cols], mload_sem.at[groups[at][1] // 512])

    stages = functools.partial(total_blocks, block_ref, near_ref, far_ref, (ts_sem, tr_sem), low, high, core, highs)
    attn_at, blocks_done = pair_of(1) + 3, 0
    row_groups = x_ref.shape[0] // group
    swapped = set()
    for step in range(pairs + 3):
        if step < pairs:
            for at in in_pair(step):
                for copy in first(at):
                    copy.start()
        if 0 <= step - 1 < pairs:
            for at in in_pair(step - 1):
                for copy in first(at):
                    copy.wait()
                for copy in column(at):
                    copy.start()
        if 0 <= step - 2 < pairs:
            for at in in_pair(step - 2):
                column(at)[at % 2].wait()
                forward(at).start()
        if 0 <= step - 3 < pairs:
            for at in in_pair(step - 3):
                column(at)[1 - at % 2].wait()
                forward(at).wait()
                if groups[at][0] == 2:
                    load_mlp(at).start()
        for number in range(count):
            if shared[number] and number not in swapped and pair_of(number) + 3 <= step:
                swap(number).start()
                swapped.add(number)
        if step == 0:
            load_bands.start()
            load_pixels.start()
            block_ref[...] = jnp.zeros_like(block_ref)
            block_ref[:24, :] = placed_ref[...]
            load_bands.wait()
            lax.fori_loop(0, images, tally, 0)
            near_ref[low] = block_ref[...]
            for copy in stages(0):
                copy.start()
        if step == 1:
            for copy in stages(0):
                copy.wait()
            block_ref[...] = (near_ref[0] + near_ref[1]) + (near_ref[2] + near_ref[3])
            far_ref[high] = block_ref[...]
            for copy in stages(1):
                copy.start()
            load_pixels.wait()
            lax.fori_loop(0, images, pick, 0)
        if step == 2:
            for copy in stages(1):
                copy.wait()
            counts = far_ref[0]
            for k in range(1, highs):
                counts = counts + far_ref[k]
            counts_ref[...] = counts
            vec_ref[...] = jnp.zeros_like(vec_ref)
            for piece in range(7):
                vec_ref[piece : piece + 1, :512] = counts[2 * piece : 2 * piece + 1, :]
                vec_ref[piece : piece + 1, 512:] = counts[2 * piece + 1 : 2 * piece + 2, :]
        if step == attn_at:
            swap(0).wait()
            load_attn.start()
            load_embed.start()
            load_attn.wait()
            for part in range(4):
                at = pl.ds(part * width, width)
                flat_ref[at, :] = attn_v[:, :, :, at].reshape(-1, width).T
            load_embed.wait()
        if attn_at <= step < attn_at + 2:
            lax.fori_loop((step - attn_at) * row_groups // 2, (step - attn_at + 1) * row_groups // 2, rows_step, 0)
            if step == attn_at + 1:
                exchange(0, part_ref, other_ref).start()
        if step == attn_at + 2:
            exchange(0, part_ref, other_ref).wait()
            mlp_first()
        if step >= attn_at + 2:
            half = mlp_v.shape[-1] // 2
            for tile in range(blocks_done, half // 512):
                ends = [at for at in range(total) if groups[at][0] == 2 and groups[at][1] in (tile * 512, half + tile * 512)]
                if max(ends) // 2 + 3 > step:
                    break
                for at in ends:
                    load_mlp(at).wait()
                mlp_block(tile, 0)
                blocks_done = tile + 1
                if blocks_done == half // 512:
                    last_ref[...] = acc_ref[...].astype(BF16)
                    exchange(1, last_ref, far_out_ref).start()
    exchange(1, last_ref, far_out_ref).wait()
    for number in range(1, count):
        if shared[number]:
            swap(number).wait()


def forward_all(masters, shared, pixels, band_ids, kept_index, intersection, table, placed):
    size = lax.axis_size("dp")
    highs = size // 4
    count = len(masters)
    dims_of = []
    for master, split in zip(masters, shared):
        if master.ndim == 3:
            dims_of.append((master.shape[1], master.shape[0] * master.shape[2]))
        else:
            dims_of.append((master.shape[0], master.shape[1] // 2))
    groups = blocks_of([dims[1] for dims in dims_of], 512, (0, 1))
    half = dims_of[2][1] // 2
    groups.sort(key=lambda block: (block[0], block[1] % half if block[0] == 2 else 0, block[1]))
    total = len(groups)
    images, length = kept_index.shape
    rows, wide, local = images * length, D, dims_of[1][1] // 4
    rows_d = pixels.shape[0]
    group = 2 * length
    fulls = []
    for dims, split in zip(dims_of, shared):
        dims = (highs, 4) + dims
        fulls.append(shape((2,) + dims if split else dims, BF16))
    block = (32, 512)
    outs = [shape((rows, wide), F32), shape((3 * local, rows), BF16), shape((local, rows), BF16),
            shape((local // DH, rows), F32), shape((rows, pixels.shape[1]), BF16), shape((rows, wide), F32),
            shape((rows, wide), BF16), shape((rows, wide), BF16), shape(block, F32), shape((4 * local, wide), BF16),
            shape((8, wide), F32), shape((rows_d, 2), F32), shape((rows, 1), jnp.int32)]
    dma = pltpu.SemaphoreType.DMA
    in_vmem = pl.BlockSpec(memory_space=pltpu.VMEM)
    any_space = pl.BlockSpec(memory_space=pl.ANY)
    result = pl.pallas_call(
        functools.partial(forward_kernel, highs, shared, groups, count, length, group, DH),
        out_shape=tuple(fulls + outs),
        in_specs=[in_vmem] * count + [any_space] * 2 + [in_vmem] * 4,
        out_specs=tuple([any_space] * count + [in_vmem] * len(outs)),
        scratch_shapes=[pltpu.VMEM(dims, BF16) for dims in dims_of] + [
            pltpu.VMEM(pixels.shape, BF16), pltpu.VMEM(band_ids.shape, jnp.int32), pltpu.VMEM(fulls[0].shape, BF16),
            pltpu.VMEM(fulls[1].shape, BF16), pltpu.VMEM(fulls[2].shape, BF16), pltpu.VMEM((rows, wide), BF16),
            pltpu.VMEM((rows, wide), BF16), pltpu.VMEM((rows, wide), BF16), pltpu.VMEM((rows, wide), F32),
            pltpu.VMEM(block, F32), pltpu.VMEM((4,) + block, F32), pltpu.VMEM((highs,) + block, F32),
            dma((total,)), dma((total, highs - 1)), dma((total, highs - 1)), dma((total, 2)), dma((total, 2)),
            dma((total,)), dma((total,)), dma((count,)), dma((count,)), dma((5,)), dma((2,)), dma((2,)),
            dma((highs + 2,)), dma((highs + 2,)), dma((2 * half // 512,))],
        compiler_params=pltpu.CompilerParams(collective_id=0, has_side_effects=True, vmem_limit_bytes=62 * 2**20),
        cost_estimate=pl.CostEstimate(flops=0, bytes_accessed=2**25, transcendentals=0),
    )(*masters, pixels, band_ids, kept_index, intersection, table, placed)
    weights = [full.reshape(((2,) if split else ()) + (size * dims[0], dims[1]))
               for full, split, dims in zip(result[:count], shared, dims_of)]
    return weights, result[count:]


def gather_all(shards, shared):
    order_a, order_b = orders()
    fulls = []
    for number, shard in enumerate(shards):
        full = gather_dp(shard, 0, (order_a, order_b)[number % 2])
        if shared[number]:
            other, zero = other_core(full), lax.axis_index("mp") == 0
            full = jnp.stack([jnp.where(zero, full, other), jnp.where(zero, other, full)])
        fulls.append(full)
    return fulls


class Gatherer:
    def __init__(self, highs, groups, shards, fulls, sems):
        self.highs, self.groups, self.shards, self.fulls = highs, groups, shards, fulls
        self.own_sem, self.zs_sem, self.zr_sem, self.cs_sem, self.cr_sem, self.fs_sem, self.fr_sem = sems
        self.core, self.low, self.high, self.low_x, self.low_y = place_of()
        self.at_x, self.at_y = (self.high * 4 + self.low_x, self.core), (self.high * 4 + self.low_y, self.core)
        self.at_high = [(lax.rem(self.high + k, highs) * 4 + self.low, self.core) for k in range(1, highs)]
        self.pairs = (len(groups) + 1) // 2

    def in_pair(self, pair):
        return [at for at in (2 * pair, 2 * pair + 1) if 0 <= at < len(self.groups)] if 0 <= pair < self.pairs else []

    def full(self, at):
        number, start, size = self.groups[at]
        return self.fulls[number], pl.ds(start, size)

    def first(self, at):
        ref, cols = self.full(at)
        shard = self.shards[self.groups[at][0]].at[:, cols]
        mine = ref.at[self.high, self.low, :, cols]
        return [pltpu.make_async_copy(shard, mine, self.own_sem.at[at])] + [
            remote(shard, mine, self.zs_sem.at[at, k - 1], self.zr_sem.at[at, k - 1], self.at_high[k - 1])
            for k in range(1, self.highs)]

    def column(self, at, way):
        ref, cols = self.full(at)
        part = ref.at[:, self.low, :, cols]
        return remote(part, part, self.cs_sem.at[at, way], self.cr_sem.at[at, way], (self.at_x, self.at_y)[way])

    def forward(self, at):
        ref, cols = self.full(at)
        which, device = (self.low_x, self.at_y) if at % 2 == 0 else (self.low_y, self.at_x)
        part = ref.at[:, which, :, cols]
        return remote(part, part, self.fs_sem.at[at], self.fr_sem.at[at], device)

    def step(self, step):
        for at in self.in_pair(step):
            for copy in self.first(at):
                copy.start()
        for at in self.in_pair(step - 1):
            for copy in self.first(at):
                copy.wait()
            for way in range(2):
                self.column(at, way).start()
        for at in self.in_pair(step - 2):
            self.column(at, at % 2).wait()
            self.forward(at).start()
        for at in self.in_pair(step - 3):
            self.column(at, 1 - at % 2).wait()
            self.forward(at).wait()


def gatherer_sems(highs, groups):
    dma, total = pltpu.SemaphoreType.DMA, len(groups)
    return [dma((total,)), dma((total, highs - 1)), dma((total, highs - 1)), dma((total, 2)), dma((total, 2)),
            dma((total,)), dma((total,))]


def decoder_kernel(length, head_dim, highs, gathered, reduced, evec_ref, kept_ref, column_ref,
                   rows_ref, table_ref, totals_ref, mlp_in, predict_in, x1e_any, mine_any, other_any, target_any, band_any, attn_any, bridge_any,
                   gy_out, gattn_ref, gbridge_ref, rpred_ref, rup_ref, rdown_ref, norm_ref, loss_ref, vgrad_ref,
                   gup_ref, gdown_ref, gpred_ref, mlp_shard, predict_shard,
                   gbias_ref, sums_ref, esums_ref, final_ref, glat_ref, x_ref, x1_ref, gy_ref, qkv_ref, mixed_ref, lse_ref,
                   part_ref, from_ref, lowt_ref, gradt_ref, z_ref, gu_ref, flat_ref, mlp_ref, bridge_ref, predict_ref,
                   target_ref, band_ref, gp_ref, gpred_acc, gmix_ref, gq_ref, vec_ref, load_sem, stream_sem, send_sem, receive_sem,
                   join_sem, *comm):
    core, index = lax.axis_index("mp"), lax.axis_index("dp")
    sibling = (index, 1 - core)
    gather = Gatherer(highs, gathered, (mlp_shard, predict_shard), (mlp_ref, predict_ref.at[core]), comm[:7])
    pred_view = rpred_ref.at[core]
    red, _ = make_reducer(highs, reduced, (1.0,) * 3, (gpred_ref, gup_ref, gdown_ref), (pred_view, rup_ref, rdown_ref),
                          norm_ref, comm[7:])
    greet([sibling, gather.at_x, gather.at_y] + gather.at_high)
    for part in range(2):
        wide = mlp_in.shape[2]
        mlp_shard[:, part * wide : (part + 1) * wide] = mlp_in[part].astype(BF16)
    predict_shard[...] = predict_in[:, pl.ds(pl.multiple_of(core * predict_shard.shape[1], predict_shard.shape[1]),
                                             predict_shard.shape[1])].astype(BF16)
    gather.step(0)
    images, side, half = table_ref.shape
    patches = side * side
    width = mixed_ref.shape[0]
    hidden = z_ref.shape[1]
    wide = x_ref.shape[1]
    share = predict_ref.shape[-1]
    w_up = lambda: mlp_ref[:, :, :, :hidden].reshape(wide, hidden)
    w_down = lambda: mlp_ref[:, :, :, hidden:].reshape(wide, hidden)
    predict_half = lambda half: predict_ref[half].reshape(wide, share)
    vec_ref[...] = totals_ref[14:22, :]
    bias = jnp.concatenate([totals_ref[21:22, :], totals_ref[22:23, : 2 * share - totals_ref.shape[1]]], axis=1)
    inverse = [1.0 / jnp.sum(totals_ref[24 + level : 25 + level, :], axis=1, keepdims=True) for level in range(NB)]
    mine_ref = final_ref
    other_ref = lowt_ref.at[pl.ds(0, other_any.shape[0]), pl.ds(0, other_any.shape[1])]
    attn_ref = z_ref.at[pl.ds(0, attn_any.shape[0]), pl.ds(0, 4 * width)]

    loads = [pltpu.make_async_copy(source, target, load_sem.at[at]) for at, (source, target) in enumerate(
        ((attn_any, attn_ref), (bridge_any, bridge_ref), (x1e_any, gy_out),
         (mine_any, mine_ref), (other_any, other_ref)))]
    for copy in loads:
        copy.start()

    def rows_of(image):
        return pl.ds(pl.multiple_of(image * patches, patches), patches)

    def exchange(phase, image):
        rows = rows_of(image)
        return remote(part_ref.at[phase % 2, rows, :], from_ref.at[phase % 2, rows, :], send_sem.at[phase, image],
                      receive_sem.at[phase, image], sibling)

    def summed(phase, rows):
        return part_ref[phase % 2, rows, :].astype(F32) + from_ref[phase % 2, rows, :].astype(F32)

    def give(phase, image, value):
        part_ref[phase % 2, rows_of(image), :] = value.astype(BF16)
        exchange(phase, image).start()

    def stream(image):
        rows, slot = rows_of(image), lax.rem(image, 2)
        return [pltpu.make_async_copy(target_any.at[rows, :], target_ref.at[slot], stream_sem.at[0, slot]),
                pltpu.make_async_copy(band_any.at[rows, :], band_ref.at[slot], stream_sem.at[1, slot])]

    sums_ref[...] = jnp.zeros_like(sums_ref)
    loss_ref[...] = jnp.zeros_like(loss_ref)
    gbias_ref[...] = jnp.zeros_like(gbias_ref)
    gpred_acc[...] = jnp.zeros_like(gpred_acc)
    for copy in stream(0):
        copy.start()
    loads[0].wait()
    for part in range(4):
        at = pl.ds(part * width, width)
        flat_ref[at, :] = attn_ref[:, at].T
    loads[1].wait()
    for copy in loads[2:]:
        copy.wait()
    ends = bridge_ref.shape[2]
    parts = 3
    latent_start = attn_any.shape[0]

    def ends_rows(step):
        return pl.ds(pl.multiple_of(step * 128, 128), 128)

    def enc_end(image, carry):
        rows = pl.ds(pl.multiple_of(image * length, length), length)
        out = gy_out[rows, :] + both(mine_ref, other_ref, rows)
        gy_out[rows, :] = out
        unit, _ = normalize(out)
        final = (unit * evec_ref[5:6, :] + evec_ref[6:7, :]).astype(BF16)
        final_ref[rows, :] = final
        for half in range(2):
            rest = dot_nn(final, bridge_ref[half])
            for part in range(parts):
                value = rest.astype(BF16)
                at = pl.multiple_of(latent_start + (image * parts + part) * length, length)
                z_ref[pl.ds(at, length), half * ends : (half + 1) * ends] = value
                rest = rest - value.astype(F32)
        return carry

    lax.fori_loop(0, images, enc_end, 0)

    def phase_a(image, carry):
        rows = rows_of(image)
        hot = lax.broadcasted_iota(jnp.int32, (patches, length), 0) == kept_ref[pl.ds(image, 1), :]
        hot = jnp.where(hot, 1.0, 0.0).astype(BF16)
        at = pl.multiple_of(latent_start + image * parts * length, length)
        latent = z_ref[pl.ds(at, parts * length), : 2 * ends]
        spread = dot_nn(jnp.concatenate([hot] * parts, axis=1), latent)
        table = table_ref[image]
        by_row = jnp.broadcast_to(table[:, None, :], (side, side, half)).reshape(patches, half)
        by_col = jnp.broadcast_to(table[None, :, :], (side, side, half)).reshape(patches, half)
        place = jnp.concatenate([by_row, by_col], axis=1)
        rows_x = spread + rows_ref[rows, 0:1] * vec_ref[0:1, :] + place
        x_ref[rows, :] = rows_x
        unit, _ = normalize(rows_x)
        low = (unit * vec_ref[1:2, :] + vec_ref[2:3, :]).astype(BF16)
        qkv_ref[:, rows] = dot_nt(flat_ref[: 3 * width, :], low).astype(BF16)
        attend(qkv_ref, mixed_ref, lse_ref, rows, width, head_dim, None)
        give(0, image, dot_nn(mixed_ref[:, rows].T, flat_ref[3 * width :, :]))
        return carry

    swap = remote(predict_ref.at[core], predict_ref.at[core], join_sem.at[0], join_sem.at[1], sibling)
    gather.step(1)
    last = gather.pairs + 2
    for step in range(2, last + 1):
        lax.fori_loop((step - 2) * images // (last - 1), (step - 1) * images // (last - 1), phase_a, 0)
        if step < last:
            gather.step(step)

    def phase_b(image, carry):
        rows = rows_of(image)
        exchange(0, image).wait()
        after = x_ref[rows, :] + summed(0, rows)
        x1_ref[rows, :] = after
        unit, _ = normalize(after)
        low = (unit * vec_ref[3:4, :] + vec_ref[4:5, :]).astype(BF16)
        lowt_ref[:, rows] = low.T
        up = dot_nn(low, w_up())
        square, bent, rise = gelu_parts(up)
        mid = (up * rise).astype(BF16)
        z_ref[rows, :] = mid
        slope = rise + (0.5 * GELU_C) * up * (1.0 - bent * bent) * (1.0 + (3.0 * 0.044715) * square)
        gu_ref[rows, :] = slope.astype(BF16)
        give(1, image, dot_nt(mid, w_down()))
        return carry

    lax.fori_loop(0, images, phase_b, 0)
    gather.step(last)
    swap.start()
    swap.wait()

    def phase_c(image, carry):
        rows, slot = rows_of(image), lax.rem(image, 2)

        @pl.when(image + 1 < images)
        def _():
            for copy in stream(image + 1):
                copy.start()

        exchange(1, image).wait()
        unit, rstd = normalize(x1_ref[rows, :] + summed(1, rows))
        gain = vec_ref[5:6, :]
        final = (unit * gain + vec_ref[6:7, :]).astype(BF16)
        for copy in stream(image):
            copy.wait()
        predicted = jnp.concatenate([dot_nn(final, predict_half(0)), dot_nn(final, predict_half(1))], axis=1)
        mismatch = predicted + bias - target_ref[slot].astype(F32)
        band = band_ref[slot]
        level = jnp.where(band == 0, inverse[0], jnp.where(band == 1, inverse[1], inverse[2]))
        level = level * rows_ref[rows, 1:2]
        square = mismatch * mismatch + EPS_C
        root = lax.rsqrt(square)
        loss_ref[...] += jnp.sum(level * (square * root), axis=0, keepdims=True)
        grad = level * (mismatch * root)
        gbias_ref[...] += jnp.sum(grad, axis=0, keepdims=True)
        gp_ref[...] = grad.astype(BF16)
        columns = pl.ds(pl.multiple_of(core * share, share), share)
        gpred_acc[...] += dot_tn(final, gp_ref[:, columns])
        grad_final = dot_nt(gp_ref[:, :share], predict_half(0)) + dot_nt(gp_ref[:, share:], predict_half(1))
        grad_in, gain_sum, shift_sum = norm_back(grad_final, gain, unit, rstd)
        gy_ref[rows, :] = grad_in
        sums_ref[5:6, :] += gain_sum
        sums_ref[6:7, :] += shift_sum
        low = grad_in.astype(BF16)
        gradt_ref[:, rows] = low.T
        grad_up = (dot_nn(low, w_down()) * gu_ref[rows, :].astype(F32)).astype(BF16)
        gu_ref[rows, :] = grad_up
        give(2, image, dot_nt(grad_up, w_up()))
        return carry

    lax.fori_loop(0, images, phase_c, 0)
    lead = gpred_ref.shape[:3]
    norm_ref[...] = jnp.zeros_like(norm_ref)
    gpred_ref[...] = gpred_acc[...].astype(BF16).reshape(gpred_ref.shape)
    tile = 256
    for start in range(0, hidden, tile):
        at = pl.ds(start, tile)
        gup_ref[:, :, :, at] = dot_nn(lowt_ref[...], gu_ref[:, at]).astype(BF16).reshape(lead + (tile,))
        gdown_ref[:, :, :, at] = dot_nn(gradt_ref[...], z_ref[:, at]).astype(BF16).reshape(lead + (tile,))
    red.step(0)

    def phase_d(image, carry):
        rows = rows_of(image)
        exchange(2, image).wait()
        unit, rstd = normalize(x1_ref[rows, :])
        grad_in, gain_sum, shift_sum = norm_back(summed(2, rows), vec_ref[3:4, :], unit, rstd)
        grad_in = grad_in + gy_ref[rows, :]
        gy_ref[rows, :] = grad_in
        sums_ref[3:4, :] += gain_sum
        sums_ref[4:5, :] += shift_sum
        low = grad_in.astype(BF16)
        gradt_ref[:, rows] = low.T
        gmix_ref[...] = dot_nt(flat_ref[3 * width :, :], low).astype(BF16)
        attend_back(qkv_ref, gmix_ref, lse_ref, gq_ref, rows, pl.ds(0, patches), width, head_dim, None)
        qkv_ref[:, rows] = gq_ref[...]
        unit_a, _ = normalize(x_ref[rows, :])
        lowt_ref[:, rows] = (unit_a * vec_ref[1:2, :] + vec_ref[2:3, :]).astype(BF16).T
        give(3, image, dot_nn(gq_ref[...].T, flat_ref[: 3 * width, :]))
        return carry

    final_step = red.pairs + 2
    for step in range(1, final_step):
        lax.fori_loop((step - 1) * images // (final_step - 1), step * images // (final_step - 1), phase_d, 0)
        red.step(step)
    join = remote(pred_view, pred_view, join_sem.at[2], join_sem.at[3], sibling)
    for part in range(3):
        at = pl.ds(part * width, width)
        gattn_ref[:, at] = dot_nt(lowt_ref[...], qkv_ref[at, :]).astype(BF16)
    gattn_ref[:, 3 * width :] = dot_nt(gradt_ref[...], mixed_ref[...]).astype(BF16)

    def phase_e(image, carry):
        rows = rows_of(image)
        exchange(3, image).wait()
        unit, rstd = normalize(x_ref[rows, :])
        grad_in, gain_sum, shift_sum = norm_back(summed(3, rows), vec_ref[1:2, :], unit, rstd)
        grad_in = grad_in + gy_ref[rows, :]
        sums_ref[1:2, :] += gain_sum
        sums_ref[2:3, :] += shift_sum
        sums_ref[0:1, :] += jnp.sum(grad_in * rows_ref[rows, 0:1], axis=0, keepdims=True)
        kept_rows = pl.ds(pl.multiple_of(image * length, length), length)
        hot = lax.broadcasted_iota(jnp.int32, (length, patches), 1) == column_ref[kept_rows, :]
        glat_ref[kept_rows, :] = dot_nn(hot.astype(BF16), grad_in.astype(BF16)).astype(BF16)
        return carry

    lax.fori_loop(0, images, phase_e, 0)
    red.step(final_step)
    join.start()
    columns = pl.ds(pl.multiple_of(core * ends, ends), ends)
    gbridge_ref[...] = dot_tn(final_ref[...], glat_ref[:, columns]).astype(BF16)
    esums_ref[...] = jnp.zeros_like(esums_ref)

    def enc_start(step, carry):
        rows = ends_rows(step)
        grad_final = dot_nt(glat_ref[rows, :ends], bridge_ref[0]) + dot_nt(glat_ref[rows, ends:], bridge_ref[1])
        unit, rstd = normalize(gy_out[rows, :])
        grad_in, gain_sum, shift_sum = norm_back(grad_final, evec_ref[5:6, :], unit, rstd)
        gy_out[rows, :] = grad_in
        esums_ref[0:1, :] += gain_sum
        esums_ref[1:2, :] += shift_sum
        return carry

    lax.fori_loop(0, gy_out.shape[0] // 128, enc_start, 0)
    join.wait()
    vgrad_ref[...] = jnp.zeros_like(vgrad_ref)
    vgrad_ref[5:7, :] = esums_ref[0:2, :]
    vgrad_ref[7:14, : sums_ref.shape[1]] = sums_ref[0:7, :]
    vgrad_ref[14:15, : gbias_ref.shape[1]] = gbias_ref[...]


def decoder_all(x1e, mine, other, evec, kept_index, kept_column, row_values, table, totals, mlp, predict, target, band,
                attn, bridge):
    size = lax.axis_size("dp")
    highs = size // 4
    rows_e, wide = x1e.shape
    images, length = kept_index.shape
    rows, pixel_count = target.shape
    patches = rows // images
    shard, hidden = mlp.shape[1], mlp.shape[2]
    low_wide = shard * size
    width, share, ends = attn.shape[1] // 4, predict.shape[1] // 2, bridge.shape[2]
    lead = (highs, 4, shard)
    gathered = blocks_of([2 * hidden, share], 512)
    reduced = blocks_of([share, hidden, hidden], 512)
    in_vmem = pl.BlockSpec(memory_space=pltpu.VMEM)
    any_space = pl.BlockSpec(memory_space=pl.ANY)
    dma = pltpu.SemaphoreType.DMA
    vm = pltpu.VMEM
    return pl.pallas_call(
        functools.partial(decoder_kernel, length, DDH, highs, gathered, reduced),
        out_shape=(
            shape((rows_e, wide), F32), shape((low_wide, 4 * width), BF16), shape((wide, ends), BF16),
            shape((2, shard, share), F32), shape((shard, hidden), F32), shape((shard, hidden), F32), shape((8, 128), F32),
            shape((1, pixel_count), F32), shape((16, wide), F32)),
        in_specs=[in_vmem] * 8 + [any_space] * 7,
        out_specs=tuple([in_vmem] * 9),
        scratch_shapes=[
            vm(lead + (hidden,), BF16), vm(lead + (hidden,), BF16), vm(lead + (share,), BF16),
            vm((shard, 2 * hidden), BF16), vm((shard, share), BF16),
            vm((1, pixel_count), F32), vm((8, low_wide), F32), vm((8, wide), F32),
            vm((rows_e, wide), BF16), vm((rows_e, low_wide), BF16), vm((rows, low_wide), F32),
            vm((rows, low_wide), F32), vm((rows, low_wide), F32), vm((3 * width, rows), BF16), vm((width, rows), BF16),
            vm((width // DDH, rows), F32), vm((2, rows, low_wide), BF16), vm((2, rows, low_wide), BF16),
            vm((low_wide, rows), BF16), vm((low_wide, rows), BF16), vm((rows, hidden), BF16), vm((rows, hidden), BF16),
            vm((4 * width, low_wide), BF16), vm(lead + (2 * hidden,), BF16), vm(bridge.shape, BF16),
            vm((2,) + lead + (share,), BF16), vm((2, patches, pixel_count), BF16), vm((2, patches, pixel_count), jnp.int32),
            vm((patches, pixel_count), BF16), vm((low_wide, share), F32), vm((width, patches), BF16),
            vm((3 * width, patches), BF16), vm((8, low_wide), F32),
            dma((5,)), dma((2, 2)), dma((4, images)), dma((4, images)), dma((4,))]
        + gatherer_sems(highs, gathered) + reducer_scratch(highs, reduced, [shard] * 3),
        compiler_params=pltpu.CompilerParams(collective_id=3, has_side_effects=True, vmem_limit_bytes=62 * 2**20),
        cost_estimate=pl.CostEstimate(flops=0, bytes_accessed=2**25, transcendentals=0),
    )(evec, kept_index, kept_column, row_values, table, totals, mlp, predict, x1e, mine, other, target, band, attn, bridge)


class Reducer:
    def __init__(self, highs, groups, weights, grads, outs, near, second, far, load_two, load_own, plane, norm, sems):
        self.highs, self.groups, self.weights = highs, groups, weights
        self.grads, self.outs = grads, outs
        self.near, self.second, self.far = near, second, far
        self.load_two, self.load_own, self.plane, self.norm = load_two, load_own, plane, norm
        self.load_sem, self.as_sem, self.ar_sem, self.bs_sem, self.br_sem, self.zs_sem, self.zr_sem = sems
        self.core, self.low, self.high, self.low_x, self.low_y = place_of()
        self.dev_x, self.dev_y = (self.high * 4 + self.low_x, self.core), (self.high * 4 + self.low_y, self.core)
        self.at_high = [(lax.rem(self.high + k, highs) * 4 + self.low, self.core) for k in range(1, highs)]
        self.pairs = (len(groups) + 1) // 2

    def in_pair(self, pair):
        return [at for at in (2 * pair, 2 * pair + 1) if 0 <= at < len(self.groups)] if 0 <= pair < self.pairs else []

    def route(self, at):
        if at % 2 == 0:
            return self.low_y, self.dev_y, self.low_x, self.dev_x
        return self.low_x, self.dev_x, self.low_y, self.dev_y

    def grad(self, at, which):
        number, start, size = self.groups[at]
        return self.grads[number].at[:, which, :, pl.ds(start, size)]

    def slot(self, ref, at, count):
        number, _, size = self.groups[at]
        return ref.at[at % count, :, pl.ds(0, self.outs[number].shape[0]), pl.ds(0, size)]

    def two_ref(self, at):
        return self.slot(self.load_two, at, 6)

    def own_ref(self, at):
        return self.slot(self.load_own, at, 8)

    def loads(self, at):
        return [pltpu.make_async_copy(self.grad(at, self.route(at)[2]), self.two_ref(at), self.load_sem.at[at, 0]),
                pltpu.make_async_copy(self.grad(at, self.low), self.own_ref(at), self.load_sem.at[at, 1])]

    def one(self, at):
        low_one, dev_one, _, _ = self.route(at)
        return [remote(self.grad(at, 3 - self.low), self.near[2 * at], self.as_sem.at[at, 0], self.ar_sem.at[at, 0], dev_one),
                remote(self.grad(at, low_one), self.near[2 * at + 1], self.as_sem.at[at, 1], self.ar_sem.at[at, 1], dev_one)]

    def two(self, at):
        return remote(self.two_ref(at), self.second[at], self.bs_sem.at[at], self.br_sem.at[at], self.route(at)[3])

    def three(self, at):
        return [remote(self.own_ref(at).at[lax.rem(self.high + k, self.highs)], self.far[at].at[k - 1],
                       self.zs_sem.at[at, k - 1], self.zr_sem.at[at, k - 1], self.at_high[k - 1])
                for k in range(1, self.highs)]

    def step(self, step):
        for at in self.in_pair(step):
            for copy in self.one(at) + self.loads(at):
                copy.start()
        for at in self.in_pair(step - 1):
            mine = self.two_ref(at)
            self.loads(at)[0].wait()
            self.one(at)[0].wait()
            mine[...] = (mine[...].astype(F32) + self.near[2 * at][...].astype(F32)).astype(BF16)
            self.two(at).start()
        for at in self.in_pair(step - 2):
            number, start, size = self.groups[at]
            mine = self.own_ref(at)
            self.loads(at)[1].wait()
            self.one(at)[1].wait()
            self.two(at).wait()
            plane = self.slot(self.plane, at, 2)
            plane[...] = (mine[...].astype(F32) + self.near[2 * at + 1][...].astype(F32)
                          + self.second[at][...].astype(F32))
            self.outs[number][:, pl.ds(start, size)] = plane[self.high]
            mine[...] = plane[...].astype(BF16)
            for copy in self.three(at):
                copy.start()
        for at in self.in_pair(step - 3):
            number, start, size = self.groups[at]
            for copy in self.three(at):
                copy.wait()
            cols = pl.ds(start, size)
            done = self.outs[number][:, cols]
            for k in range(self.highs - 1):
                done = done + self.far[at][k].astype(F32)
            self.outs[number][:, cols] = done
            self.norm[0:1, 0:1] += self.weights[number] * jnp.sum(done * done, keepdims=True)


def reducer_scratch(highs, groups, shards):
    piece = lambda lead, group: pltpu.VMEM((lead, shards[group[0]], group[2]), BF16)
    near = [piece(highs, group) for group in groups for _ in range(2)]
    second = [piece(highs, group) for group in groups]
    far = [piece(highs - 1, group) for group in groups]
    slot = (highs, max(shards), max(group[2] for group in groups))
    loads = [pltpu.VMEM((6,) + slot, BF16), pltpu.VMEM((8,) + slot, BF16), pltpu.VMEM((2,) + slot, F32)]
    dma, total = pltpu.SemaphoreType.DMA, len(groups)
    sems = [dma((total, 2)), dma((total, 2)), dma((total, 2)), dma((total,)), dma((total,)),
            dma((total, highs - 1)), dma((total, highs - 1))]
    return near + second + far + loads + sems


def make_reducer(highs, groups, weights, grads, outs, norm, refs):
    total = len(groups)
    near, second, far, refs = refs[: 2 * total], refs[2 * total : 3 * total], refs[3 * total : 4 * total], refs[4 * total :]
    return Reducer(highs, groups, weights, grads, outs, near, second, far, *refs[:3], norm, refs[3:10]), refs[10:]


def backward_kernel(highs, weights, groups, ready, count, shared, length, group, head_dim, *refs):
    given = count - 4
    gy_ref, x1_ref, vec_ref, vgrad_ref, loss_ref, lse_ref, norm_in = refs[:7]
    x_any, qkv_any, mixed_any, flat_any, pixk_any, mlp_any = refs[7:13]
    refs = refs[13:]
    grads, refs = refs[:given], refs[given:]
    outs, sums_ref, vflat_ref, refs = refs[:count], refs[count], refs[count + 1], refs[count + 2 :]
    made, refs = refs[:4], refs[4:]
    grads = tuple(grads) + tuple(made)
    (x_ref, qkv_ref, mixed_ref, flat_ref, pixk_ref, wmlp_ref, low_ref, lowt_ref, grad_ref, gradt_ref, acc_ref, part_ref,
     other_ref, last_ref, gmix_ref, gqkv_ref, stage_ref, norm_ref, spots_ref, far_ref, vnear_ref, vfar_ref,
     vsum_ref) = refs[:23]
    (load_sem, wload_sem, store_sem, xs_sem, xr_sem, ns_sem, nr_sem, hs_sem, hr_sem, ts_sem, tr_sem, js_sem,
     jr_sem) = refs[23:36]
    core_at = lax.axis_index("mp")
    views = [ref.at[core_at] if split else ref for ref, split in zip(outs, shared)]
    red, _ = make_reducer(highs, groups, weights, grads, views, norm_ref, refs[36:])
    core, low, high = red.core, red.low, red.high
    spot = low * 2 + core
    sibling = (high * 4 + low, 1 - core)
    near = [(high * 4 + lax.rem(spot + k, 8) // 2, lax.rem(lax.rem(spot + k, 8), 2)) for k in range(1, 8)]
    greet(near + red.at_high)
    rows, wide = x_ref.shape
    width = mixed_ref.shape[0]
    hidden = mlp_any.shape[-1] // 2
    size = 512
    tiles = hidden // size
    mask = group_mask(group, length)

    late = [pltpu.make_async_copy(source, target, load_sem.at[at]) for at, (source, target) in enumerate(
        ((x_any, x_ref), (qkv_any, qkv_ref), (mixed_any, mixed_ref), (flat_any, flat_ref), (pixk_any, pixk_ref)))]

    def weight_loads(tile):
        return [pltpu.make_async_copy(mlp_any.at[:, :, :, pl.ds(half * hidden + tile * size, size)],
                                      wmlp_ref.at[tile % 2, half], wload_sem.at[tile % 2, half]) for half in range(2)]

    def store(slot, target, start, columns=512):
        return pltpu.make_async_copy(stage_ref.at[slot, :, :, :, pl.ds(0, columns)],
                                     target.at[:, :, :, pl.ds(start, columns)], store_sem.at[slot])

    def exchange(at, target):
        return remote(part_ref, target, xs_sem.at[at], xr_sem.at[at], sibling)

    def staged(slot, value):
        columns = value.shape[1]
        stage_ref[slot, :, :, :, :columns] = value.astype(BF16).reshape(stage_ref.shape[1:4] + (columns,))

    def mlp_first():
        unit, _ = normalize(x1_ref[...])
        value = (unit * vec_ref[3:4, :] + vec_ref[4:5, :]).astype(BF16)
        low_ref[...] = value
        lowt_ref[...] = value.T
        value = gy_ref[...].astype(BF16)
        grad_ref[...] = value
        gradt_ref[...] = value.T
        acc_ref[...] = jnp.zeros_like(acc_ref)

    def mlp_block(tile):
        for copy in weight_loads(tile):
            copy.wait()
        if tile + 1 < tiles:
            for copy in weight_loads(tile + 1):
                copy.start()
        w_up = wmlp_ref[tile % 2, 0].reshape(wide, size)
        w_down = wmlp_ref[tile % 2, 1].reshape(wide, size)
        up = dot_nn(low_ref[...], w_up)
        square, bent, half = gelu_parts(up)
        mid = (up * half).astype(BF16)
        slope = half + (0.5 * GELU_C) * up * (1.0 - bent * bent) * (1.0 + (3.0 * 0.044715) * square)
        grad_up = (dot_nn(grad_ref[...], w_down) * slope).astype(BF16)
        acc_ref[...] += dot_nt(grad_up, w_up)
        slot = 2 * (tile % 2)
        staged(slot, dot_nn(lowt_ref[...], grad_up))
        store(slot, made[0], tile * size).start()
        staged(slot + 1, dot_nn(gradt_ref[...], mid))
        store(slot + 1, made[1], tile * size).start()

    def mlp_last():
        part_ref[...] = acc_ref[...].astype(BF16)
        exchange(0, other_ref).start()

    def stores_done(tile):
        slot = 2 * (tile % 2)
        store(slot, made[0], tile * size).wait()
        store(slot + 1, made[1], tile * size).wait()

    def rows_step(number, carry):
        at = pl.ds(pl.multiple_of(number * group, group), group)
        unit, rstd = normalize(x1_ref[at, :])
        grad_in, gain_sum, shift_sum = norm_back(both(part_ref, other_ref, at), vec_ref[3:4, :], unit, rstd)
        grad_in = grad_in + gy_ref[at, :]
        gy_ref[at, :] = grad_in
        vsum_ref[3:4, :] += gain_sum
        vsum_ref[4:5, :] += shift_sum
        low_grad = grad_in.astype(BF16)
        gradt_ref[:, at] = low_grad.T
        gmix_ref[...] = dot_nt(flat_ref[3 * width :, :], low_grad).astype(BF16)
        attend_back(qkv_ref, gmix_ref, lse_ref, gqkv_ref, at, at, width, head_dim, mask)
        part_ref[at, :] = dot_nn(gqkv_ref[:, at].T, flat_ref[: 3 * width, :]).astype(BF16)
        unit_a, _ = normalize(x_ref[at, :])
        lowt_ref[:, at] = (unit_a * vec_ref[1:2, :] + vec_ref[2:3, :]).astype(BF16).T
        return carry

    def attn_grads():
        for slot in range(4):
            if slot < 3:
                value = dot_nt(lowt_ref[...], gqkv_ref[pl.ds(slot * width, width), :])
            else:
                value = dot_nt(gradt_ref[...], mixed_ref[...])
            staged(slot, value)
            store(slot, made[2], slot * width, width).start()

    def enc_out():
        unit, rstd = normalize(x_ref[...])
        grad_in, gain_sum, shift_sum = norm_back(both(part_ref, last_ref, pl.ds(0, rows)), vec_ref[1:2, :], unit, rstd)
        grad_in = grad_in + gy_ref[...]
        vsum_ref[0:1, :] = jnp.sum(grad_in, axis=0, keepdims=True)
        vsum_ref[1:2, :] = gain_sum
        vsum_ref[2:3, :] = shift_sum
        share = made[3].shape[-1]
        columns = pl.ds(pl.multiple_of(core * share, share), share)
        staged(0, dot_tn(grad_in.astype(BF16), pixk_ref[:, columns]))
        store(0, made[3], 0, share).start()

    stages = functools.partial(total_blocks, vsum_ref, vnear_ref, vfar_ref, (ts_sem, tr_sem), low, high, core, highs)
    mlp_ready, attn_ready, embed_ready = ready
    row_groups = rows // group
    norm_ref[...] = norm_in[...]
    vsum_ref[...] = vgrad_ref[...]
    for copy in weight_loads(0):
        copy.start()
    work = {0: range(0, 1), 1: range(1, tiles - 1), 2: range(tiles - 1, tiles)}
    for step in range(red.pairs + 3):
        if 0 <= step - mlp_ready < tiles:
            stores_done(step - mlp_ready)
        if step == attn_ready:
            for slot in range(4):
                store(slot, made[2], slot * width, width).wait()
        if step == embed_ready:
            store(0, made[3], 0, made[3].shape[-1]).wait()
        red.step(step)
        if step == 0:
            for copy in late:
                copy.start()
            mlp_first()
        for tile in work.get(step, ()):
            mlp_block(tile)
            if tile == tiles - 1:
                mlp_last()
        if step == 3:
            for copy in late:
                copy.wait()
            exchange(0, other_ref).wait()
            lax.fori_loop(0, row_groups // 2, rows_step, 0)
        if step == 4:
            lax.fori_loop(row_groups // 2, row_groups, rows_step, 0)
            exchange(1, last_ref).start()
            attn_grads()
        if step == embed_ready - 1:
            exchange(1, last_ref).wait()
            enc_out()
            vnear_ref[low] = vsum_ref[...]
            for copy in stages(0):
                copy.start()
        if step == embed_ready:
            for copy in stages(0):
                copy.wait()
            vsum_ref[...] = (vnear_ref[0] + vnear_ref[1]) + (vnear_ref[2] + vnear_ref[3])
            vfar_ref[high] = vsum_ref[...]
            for copy in stages(1):
                copy.start()
        if step == embed_ready + 1:
            for copy in stages(1):
                copy.wait()
            every = vfar_ref[0]
            for k in range(1, highs):
                every = every + vfar_ref[k]
            for row in range(7):
                vflat_ref[2 * row : 2 * row + 1, :] = every[row : row + 1, :512]
                vflat_ref[2 * row + 1 : 2 * row + 2, :] = every[row : row + 1, 512:]
            vflat_ref[14:22, :] = every[7:15, :512]
            vflat_ref[22:23, :] = every[14:15, 512:]
            vflat_ref[23:24, :] = jnp.zeros_like(vflat_ref[23:24, :])
            norm_ref[0:1, 0:1] += jnp.sum(every * every, keepdims=True) * (1.0 / (8 * highs))
    joins = [remote(view, view, js_sem.at[at], jr_sem.at[at], sibling)
             for at, (view, split) in enumerate(zip(views, shared)) if split]
    for copy in joins:
        copy.start()
    norm_ref[1:2, 0:1] = jnp.sum(loss_ref[...], keepdims=True)
    spots_ref[spot] = norm_ref[...]
    copies = [remote(norm_ref, spots_ref.at[spot], ns_sem.at[k], nr_sem.at[k], near[k]) for k in range(7)]
    for copy in copies:
        copy.start()
    for copy in copies:
        copy.wait()
    local = spots_ref[0]
    for k in range(1, 8):
        local = local + spots_ref[k]
    norm_ref[...] = local
    far_ref[high] = local
    copies = [remote(norm_ref, far_ref.at[high], hs_sem.at[k], hr_sem.at[k], red.at_high[k]) for k in range(highs - 1)]
    for copy in copies:
        copy.start()
    for copy in copies:
        copy.wait()
    every = far_ref[0]
    for k in range(1, highs):
        every = every + far_ref[k]
    sums_ref[...] = every
    for copy in joins:
        copy.wait()


def backward_all(gy, x1, evec, vec_grads, loss_parts, norm, enc_saved, x0, flat, pixk, mlp, grads, shared, length, head_dim):
    size = lax.axis_size("dp")
    highs = size // 4
    qkv, mixed, lse = enc_saved
    rows, wide = x1.shape
    width = mixed.shape[0]
    hidden = mlp.shape[1] // 2
    group = 2 * length
    shard = wide // size
    lead = (highs, 4, shard)
    fresh = [lead + (hidden,), lead + (hidden,), lead + (4 * width,), lead + (pixk.shape[1] // 2,)]
    widths = [a.shape[1] for a in grads] + [dims[-1] for dims in fresh]
    shards = [a.shape[0] // size for a in grads] + [shard] * 4
    count, given = len(widths), len(grads)
    blocks = blocks_of(widths, 512, (given + 2,))
    first = [b for b in blocks if b[0] == 0]
    last = [b for b in blocks if b[0] == given + 3] + [b for b in blocks if 0 < b[0] < given]
    middle = [b for at in range(0, hidden, 512) for b in ((given, at, 512), (given + 1, at, 512))]
    attn = [b for b in blocks if b[0] == given + 2]
    groups = first + middle + attn + last
    if len(first) != 2 or hidden // 512 != 4 or len(attn) != 8:
        raise ValueError("blocks")
    ready = (len(first) // 2, (len(first) + len(middle)) // 2, (len(first) + len(middle) + len(attn)) // 2)
    dma = pltpu.SemaphoreType.DMA
    small, vec_block = (8, 128), vec_grads.shape
    in_vmem = pl.BlockSpec(memory_space=pltpu.VMEM)
    any_space = pl.BlockSpec(memory_space=pl.ANY)
    result = pl.pallas_call(
        functools.partial(backward_kernel, highs, (1.0,) * count, groups, ready, count, shared, length, group, head_dim),
        out_shape=tuple([shape((2, r, w) if split else (r, w), F32) for r, w, split in zip(shards, widths, shared)]
                        + [shape(small, F32), shape((24, 512), F32)]
                        + [shape(dims, BF16) for dims in fresh]),
        in_specs=[in_vmem] * 7 + [any_space] * (6 + given),
        out_specs=tuple([in_vmem] * (count + 2) + [any_space] * 4),
        scratch_shapes=[
            pltpu.VMEM((rows, wide), F32), pltpu.VMEM(qkv.shape, BF16), pltpu.VMEM(mixed.shape, BF16),
            pltpu.VMEM(flat.shape, BF16), pltpu.VMEM(pixk.shape, BF16), pltpu.VMEM((2, 2) + lead + (512,), BF16),
            pltpu.VMEM((rows, wide), BF16), pltpu.VMEM((wide, rows), BF16), pltpu.VMEM((rows, wide), BF16),
            pltpu.VMEM((wide, rows), BF16), pltpu.VMEM((rows, wide), F32), pltpu.VMEM((rows, wide), BF16),
            pltpu.VMEM((rows, wide), BF16), pltpu.VMEM((rows, wide), BF16), pltpu.VMEM((width, group), BF16),
            pltpu.VMEM((3 * width, rows), BF16), pltpu.VMEM((4,) + lead + (512,), BF16), pltpu.VMEM(small, F32),
            pltpu.VMEM((8,) + small, F32), pltpu.VMEM((highs,) + small, F32), pltpu.VMEM((4,) + vec_block, F32),
            pltpu.VMEM((highs,) + vec_block, F32), pltpu.VMEM(vec_block, F32),
            dma((5,)), dma((2, 2)), dma((4,)), dma((2,)), dma((2,)), dma((7,)), dma((7,)), dma((highs - 1,)),
            dma((highs - 1,)), dma((highs + 2,)), dma((highs + 2,)), dma((count,)), dma((count,))] + reducer_scratch(highs, groups, shards),
        compiler_params=pltpu.CompilerParams(collective_id=1, has_side_effects=True, vmem_limit_bytes=62 * 2**20),
        cost_estimate=pl.CostEstimate(flops=0, bytes_accessed=sum(a.size * 2 for a in grads), transcendentals=0),
    )(gy, x1, evec, vec_grads, loss_parts, lse, norm, x0, qkv, mixed, flat, pixk, mlp.reshape(lead + (2 * hidden,)),
      *[a.reshape(highs, 4, r, a.shape[1]) for r, a in zip(shards, grads)])
    return list(result[:count]), result[count], result[count + 1]


def reduce_plain(grads, loss_parts, vec_grads):
    order_a, order_b = orders()
    outs = [reduce_dp(a, 0, (order_a, order_b)[number % 2], a.dtype) for number, a in enumerate(grads)]
    vec_sums = total_dp(vec_grads)
    sums = jnp.stack([sum(jnp.sum(a * a) for a in outs), jnp.sum(loss_parts)])
    sums = total_dp(sums)
    sums = sums + other_core(sums)
    return outs, sums[0] + jnp.sum(vec_sums * vec_sums), 0.5 * sums[1], vec_sums


def adam_update(master, gradient, first_old, second_old, step_rate, decay_rate):
    first_new = BETA_ONE * first_old + (1.0 - BETA_ONE) * gradient
    second_new = BETA_TWO * second_old + (1.0 - BETA_TWO) * gradient * gradient
    first_hat = first_new / (1.0 - BETA_ONE**STEP)
    second_hat = second_new / (1.0 - BETA_TWO**STEP)
    updated = master - step_rate * (
        first_hat / (jnp.sqrt(second_hat) + ADAM_EPS) + decay_rate * master
    )
    return (updated, first_new, second_new)


def adam_kernel(count, averaged, sums_ref, *refs):
    sources, refs = refs[: count + 2], refs[count + 2 :]
    masters, firsts, seconds, refs = refs[:count], refs[count : 2 * count], refs[2 * count : 3 * count], refs[3 * count :]
    means, refs = refs[:averaged], refs[averaged:]
    news, new_firsts, new_seconds, new_means = (
        refs[:count], refs[count : 2 * count], refs[2 * count : 3 * count], refs[3 * count :])
    factor = CLIP / jnp.maximum(jnp.sqrt(sums_ref[0:1, 0:1]), CLIP)

    def update(number, at, gradient):
        new, first, second = adam_update(masters[number][at], gradient * factor, firsts[number][at], seconds[number][at],
                                         RATE_MAT, DECAY_MAT)
        news[number][at] = new
        new_firsts[number][at] = first
        new_seconds[number][at] = second
        mean = {0: 0, 1: 1, 4: 2}.get(number)
        if mean is not None:
            new_means[mean][at] = EMA_KEEP * means[mean][at] + (1.0 - EMA_KEEP) * new

    enc_attn, enc_up, enc_down, dec_attn, dec_up, dec_down, embed, bridge, predict = sources
    for number, source in ((0, enc_attn), (2, dec_attn)):
        wide = source.shape[1] // 4
        for part in range(4):
            update(number, part, source[:, part * wide : (part + 1) * wide])
    for number, pair in ((1, (enc_up, enc_down)), (3, (dec_up, dec_down))):
        for part, source in enumerate(pair):
            update(number, part, source[...])
    for number, source in ((4, embed), (5, bridge), (6, predict)):
        share = source.shape[2]
        for half in range(2):
            update(number, (slice(None), pl.ds(half * share, share)), source[half])


def adam_all(sums, sources, masters, firsts, seconds, means):
    like = lambda arrays: [shape(a.shape, F32) for a in arrays]
    outs = like(masters) * 3 + like(means)
    count = len(masters)
    result = run(functools.partial(adam_kernel, count, len(means)), outs, [],
                 (sums, *sources, *masters, *firsts, *seconds, *means), 0)
    return (result[:count], result[count : 2 * count], result[2 * count : 3 * count], result[3 * count :])


def plain_step(pixels, target, band_ids, kept_index, intersection, gsd_scale, masters, enc_table, dec_table):
    enc_attn, enc_mlp, dec_attn, dec_mlp, patch_embed, bridge, predict, vectors = masters
    images, keep_count = kept_index.shape
    patch_count = intersection.shape[1]
    patch_index = jnp.arange(patch_count, dtype=jnp.int32)
    kept_flags = jnp.any(kept_index[:, :, None] == patch_index[None, None, :], axis=1).astype(F32)
    patch_weight = ((1.0 - kept_flags) * (1.0 - 0.5 * intersection.astype(F32))).reshape(-1, 1)
    hidden_rows = (1.0 - kept_flags).reshape(-1, 1)
    core = lax.axis_index("mp").astype(jnp.int32).reshape(1)
    size = lax.axis_size("dp")

    def flat(stack):
        return jnp.concatenate([part.astype(BF16) for part in stack], axis=1)

    def core_half(block):
        half = block.shape[1] // 2
        return lax.dynamic_slice_in_dim(block, lax.axis_index("mp") * half, half, 1).astype(BF16)

    vec_shard = vectors.shape[0]
    vec_room = -(-vec_shard // 1024) * 1024
    vec_rows = jnp.pad(lax.reduce_precision(vectors, 8, 7), (0, vec_room - vec_shard)).reshape(-1, 128)
    vec_full = gather_dp(vec_rows, 0, orders()[0])
    pieces = split_vectors(vec_full.reshape(size, vec_room)[:, :vec_shard].reshape(-1), D, E)
    evec = jnp.stack(pieces[:7] + [jnp.zeros_like(pieces[0])])
    dvec = jnp.stack(pieces[7:14] + [jnp.zeros_like(pieces[7])])
    kept_column = kept_index.reshape(-1, 1)
    rows, rows_d = images * keep_count, images * patch_count
    pixel_count = pixels.shape[1]
    group = 2 * keep_count
    shards = [core_half(patch_embed.T), flat(enc_attn), flat(enc_mlp), flat(dec_attn), flat(dec_mlp), core_half(bridge),
              core_half(predict)]
    weights = gather_all(shards, (True, False, False, False, False, True, True))
    embed_w, enc_attn_w, enc_mlp_w, dec_attn_w, dec_mlp_w, bridge_w, predict_w = weights
    local = enc_attn_w.shape[1] // 4
    band_weight = total_dp(jnp.stack([jnp.sum(jnp.where(band_ids == level, patch_weight, 0.0)) for level in range(NB)]))
    inverse = 1.0 / band_weight
    x0, *enc_saved, part, kept_pixels = run(
        functools.partial(enc_in_kernel, keep_count, group, DH),
        [shape((rows, D), F32), shape((3 * local, rows), BF16), shape((local, rows), BF16),
         shape((local // DH, rows), F32), shape((rows, D), BF16), shape((rows, pixel_count), BF16)],
        [pltpu.VMEM((4 * local, D), BF16)],
        (pixels, kept_column, enc_table, embed_w, evec, enc_attn_w),
        rows * D * (2 * pixel_count + 8 * local))
    x1, part = mlp_forward(x0, part, evec, enc_mlp_w)
    other = other_core(part)
    one_d, one_e = shape((1, D), F32), shape((1, E), F32)
    local_d = dec_attn_w.shape[1] // 4
    x2, final_enc, xd, *dec_saved, part = run(
        functools.partial(dec_in_kernel, keep_count, DDH),
        [shape((rows, D), F32), shape((rows, D), BF16), shape((rows_d, E), F32), shape((3 * local_d, rows_d), BF16),
         shape((local_d, rows_d), BF16), shape((local_d // DDH, rows_d), F32), shape((rows_d, E), BF16)],
        [pltpu.VMEM((4 * local_d, E), BF16), pltpu.VMEM((rows, E), F32)],
        (x1, part, other, evec, bridge_w, kept_index, hidden_rows, dec_table, dvec,
         dec_attn_w),
        rows_d * E * 8 * local_d + 2 * rows * D * E)
    xd1, part = mlp_forward(xd, part, dvec, dec_mlp_w)
    gyd, grad_predict, grad_pbias, loss_parts, grad_dec_fg, grad_dec_fb = head(
        core, inverse, xd1, part, dvec, pieces[14].reshape(1, -1), predict_w, target, band_ids, patch_weight, patch_count)
    grad_dec_up, grad_dec_down, part = mlp_backward(gyd, xd1, dvec, dec_mlp_w)
    gxd, grad_dec_attn, grad_dec_gb, grad_dec_bb, part = attn_backward(
        gyd, xd1, part, xd, dec_saved, dvec, dec_attn_w, patch_count, patch_count, DDH)
    grad_dec_ga, grad_dec_ba, grad_mask, grad_bridge, grad_enc_fg, grad_enc_fb, gye = run(
        functools.partial(between_kernel, keep_count),
        [one_e, one_e, one_e, shape((D, E // 2), BF16), one_d, one_d, shape((rows, D), F32)],
        [pltpu.VMEM((rows, E), BF16)],
        (core, gxd, xd, part, other_core(part), dvec, kept_column, hidden_rows, final_enc, x2, evec, bridge_w),
        3 * rows * D * E, 1)
    wide_row = lambda row: jnp.pad(row, ((0, 0), (0, D - row.shape[1])))
    no_row = jnp.zeros((1, D), F32)
    late_rows = [grad_enc_fg, grad_enc_fb] + [wide_row(row) for row in (
        grad_mask, grad_dec_ga, grad_dec_ba, grad_dec_gb, grad_dec_bb, grad_dec_fg, grad_dec_fb, grad_pbias)] + [no_row]
    dec_grads = [grad_predict, grad_dec_up, grad_dec_down, grad_dec_attn, grad_bridge]
    grad_enc_up, grad_enc_down, part = mlp_backward(gye, x1, evec, enc_mlp_w)
    gxe, grad_enc_attn, grad_enc_gb, grad_enc_bb, part = attn_backward(
        gye, x1, part, x0, enc_saved, evec, enc_attn_w, keep_count, group, DH)
    grad_enc_ga, grad_enc_ba, grad_ebias, grad_embed = run(
        enc_out_kernel,
        [one_d, one_d, one_d, shape((D, pixel_count // 2), BF16)],
        [], (core, gxe, x0, part, other_core(part), evec, kept_pixels), rows * D * pixel_count, 1)
    vec_grads = jnp.concatenate([grad_ebias, grad_enc_ga, grad_enc_ba, grad_enc_gb, grad_enc_bb] + late_rows)
    sums, total_squares, loss, vec_sums = reduce_plain(
        dec_grads + [grad_enc_up, grad_enc_down, grad_enc_attn, grad_embed], loss_parts, vec_grads)
    sums = [jnp.stack([jnp.where(core == 0, a, b), jnp.where(core == 0, b, a)]) if at in (0, 4, 8) else a
            for at, a in enumerate(sums) for b in ([other_core(a)] if at in (0, 4, 8) else [a])]
    return sums, total_squares, loss, vec_sums, band_weight


def per_device(
    pixels,
    target,
    band_ids,
    kept_index,
    intersection,
    gsd_scale,
    enc_attn,
    enc_mlp,
    dec_attn,
    dec_mlp,
    patch_embed,
    bridge,
    predict,
    vectors,
    first_enc_attn,
    first_enc_mlp,
    first_dec_attn,
    first_dec_mlp,
    first_patch_embed,
    first_bridge,
    first_predict,
    first_vectors,
    second_enc_attn,
    second_enc_mlp,
    second_dec_attn,
    second_dec_mlp,
    second_patch_embed,
    second_bridge,
    second_predict,
    second_vectors,
    ema_enc_attn,
    ema_enc_mlp,
    ema_patch_embed,
):
    masters = (enc_attn, enc_mlp, dec_attn, dec_mlp, patch_embed, bridge, predict, vectors)
    firsts = (
        first_enc_attn,
        first_enc_mlp,
        first_dec_attn,
        first_dec_mlp,
        first_patch_embed,
        first_bridge,
        first_predict,
        first_vectors,
    )
    seconds = (
        second_enc_attn,
        second_enc_mlp,
        second_dec_attn,
        second_dec_mlp,
        second_patch_embed,
        second_bridge,
        second_predict,
        second_vectors,
    )
    averages = (ema_enc_attn, ema_enc_mlp, ema_patch_embed)
    enc_table, dec_table = sine_table(gsd_scale, D, GRID), sine_table(gsd_scale, E, GRID)
    vec_shard = vectors.shape[0]
    vec_start = lax.axis_index("dp") * vec_shard
    if patch_embed.shape[1] % 16 == 0 and dec_attn.shape[1] % 16 == 0:
        placed = lax.dynamic_update_slice(
            jnp.zeros((24 * 512,), F32), lax.reduce_precision(vectors, 8, 7), (vec_start,)).reshape(24, 512)
        weights, results = forward_all(
            [patch_embed.T, enc_attn, enc_mlp, dec_attn, bridge], (True, False, False, False, True), pixels, band_ids,
            kept_index, intersection, enc_table, placed)
        embed_w, enc_attn_w, enc_mlp_w, dec_attn_w, bridge_w = weights
        x0, *enc_saved, kept_pixels, x1, part, other, totals, enc_flat, evec, row_values, kept_column = results
        band_weight = jnp.sum(totals[24 : 24 + NB], axis=1)
        gye, grad_dec_attn, grad_bridge, sum_predict, sum_up, sum_down, norm, loss_parts, vec_grads = decoder_all(
            x1, part, other, evec, kept_index, kept_column, row_values, dec_table, totals, dec_mlp, predict, target,
            band_ids, dec_attn_w, bridge_w)
        sums, norms, vec_grad = backward_all(
            gye, x1, evec, vec_grads, loss_parts, norm, enc_saved, x0, enc_flat, kept_pixels, enc_mlp_w,
            [grad_dec_attn, grad_bridge], (False, True, False, False, False, True), kept_index.shape[1], DH)
        sums = [sum_predict, sum_up, sum_down] + sums
        total_squares, loss = norms[0, 0], 0.5 * norms[1, 0]
    else:
        sums, total_squares, loss, vec_sums, band_weight = plain_step(
            pixels, target, band_ids, kept_index, intersection, gsd_scale, masters, enc_table, dec_table)
        norms = jnp.broadcast_to(total_squares, (8, 128))
        vec_grad = jnp.concatenate(
            [vec_sums[:7].reshape(-1), vec_sums[7:14, :E].reshape(-1), vec_sums[14, : pixels.shape[1]]])
    vec_grad = lax.dynamic_slice_in_dim(vec_grad.reshape(-1), vec_start, vec_shard)
    grad_norm = jnp.sqrt(total_squares)
    factor = CLIP / jnp.maximum(grad_norm, CLIP)
    order = (7, 5, 6, 3, 1, 2, 8, 4, 0)
    flip = lambda arrays, at: [a.T if number == at else a for number, a in enumerate(arrays)]
    news, new_firsts, new_seconds, means = adam_all(
        norms, [sums[at] for at in order], flip(masters[:7], 4), flip(firsts[:7], 4), flip(seconds[:7], 4),
        flip(averages, 2))
    news, new_firsts, new_seconds, means = flip(news, 4), flip(new_firsts, 4), flip(new_seconds, 4), flip(means, 2)
    vec_new = adam_update(vectors, vec_grad * factor, firsts[7], seconds[7], RATE_VEC, 0.0)
    news, new_firsts, new_seconds = [
        list(many) + [one] for many, one in zip((news, new_firsts, new_seconds), vec_new)]
    ema_attn, ema_mlp, ema_embed = means
    return (
        loss,
        band_weight,
        grad_norm,
        news[0],
        news[1],
        news[2],
        news[3],
        news[4],
        news[5],
        news[6],
        news[7],
        new_firsts[0],
        new_firsts[1],
        new_firsts[2],
        new_firsts[3],
        new_firsts[4],
        new_firsts[5],
        new_firsts[6],
        new_firsts[7],
        new_seconds[0],
        new_seconds[1],
        new_seconds[2],
        new_seconds[3],
        new_seconds[4],
        new_seconds[5],
        new_seconds[6],
        new_seconds[7],
        ema_attn,
        ema_mlp,
        ema_embed,
    )


def solution(mesh):
    return jax.shard_map(
        per_device,
        mesh=mesh,
        in_specs=(
            P("dp", None),
            P("dp", None),
            P("dp", None),
            P("dp", None),
            P("dp", None),
            P("dp"),
            P(None, "dp", "mp"),
            P(None, "dp", "mp"),
            P(None, "dp", "mp"),
            P(None, "dp", "mp"),
            P(None, "dp"),
            P("dp", None),
            P("dp", None),
            P("dp"),
            P(None, "dp", "mp"),
            P(None, "dp", "mp"),
            P(None, "dp", "mp"),
            P(None, "dp", "mp"),
            P(None, "dp"),
            P("dp", None),
            P("dp", None),
            P("dp"),
            P(None, "dp", "mp"),
            P(None, "dp", "mp"),
            P(None, "dp", "mp"),
            P(None, "dp", "mp"),
            P(None, "dp"),
            P("dp", None),
            P("dp", None),
            P("dp"),
            P(None, "dp", "mp"),
            P(None, "dp", "mp"),
            P(None, "dp"),
        ),
        out_specs=(
            P(),
            P(),
            P(),
            P(None, "dp", "mp"),
            P(None, "dp", "mp"),
            P(None, "dp", "mp"),
            P(None, "dp", "mp"),
            P(None, "dp"),
            P("dp", None),
            P("dp", None),
            P("dp"),
            P(None, "dp", "mp"),
            P(None, "dp", "mp"),
            P(None, "dp", "mp"),
            P(None, "dp", "mp"),
            P(None, "dp"),
            P("dp", None),
            P("dp", None),
            P("dp"),
            P(None, "dp", "mp"),
            P(None, "dp", "mp"),
            P(None, "dp", "mp"),
            P(None, "dp", "mp"),
            P(None, "dp"),
            P("dp", None),
            P("dp", None),
            P("dp"),
            P(None, "dp", "mp"),
            P(None, "dp", "mp"),
            P(None, "dp"),
        ),
        check_vma=False,
    )
```

```python
import functools
import math

import jax
import jax.numpy as jnp
from jax import lax
from jax.experimental import pallas as pl
from jax.experimental.pallas import tpu as pltpu
from jax.sharding import PartitionSpec as P

D = 1024
DH = 64
E = 512
DDH = 32
GRID = 16
NB = 3
STEP = 10


EPS_LN = 1e-06
EPS_C = 0.01
CLIP = 0.0002
BETA_ONE = 0.9
BETA_TWO = 0.999
ADAM_EPS = 1e-12
RATE_MAT = 0.06
RATE_VEC = 0.5
DECAY_MAT = 0.05
EMA_KEEP = 0.9
REF_GSD = 4.0


def split_vectors(flat_vec, enc_width, dec_width):
    lengths = [enc_width] * 7 + [dec_width] * 7
    pieces = []
    offset = 0
    for length in lengths:
        pieces.append(flat_vec[offset : offset + length])
        offset = offset + length
    pieces.append(flat_vec[offset:])
    return pieces


F32 = jnp.float32
BF16 = jnp.bfloat16
VMEM_LIMIT = 58 * 2**20
GELU_C = math.sqrt(2.0 / math.pi)


def dot_nn(left, right):
    return jnp.dot(left, right, preferred_element_type=F32)


def dot_nt(left, right):
    return lax.dot_general(left, right, (((1,), (1,)), ((), ())), preferred_element_type=F32)


def dot_tn(left, right):
    return lax.dot_general(left, right, (((0,), (0,)), ((), ())), preferred_element_type=F32)


def dot_exact(left, right):
    return jnp.dot(left, right, preferred_element_type=F32, precision=lax.Precision.HIGHEST)


def normalize(rows):
    centred = rows - jnp.mean(rows, axis=-1, keepdims=True)
    rstd = lax.rsqrt(jnp.mean(centred * centred, axis=-1, keepdims=True) + EPS_LN)
    return centred * rstd, rstd


def norm_back(grad, gain, unit, rstd):
    scaled = grad * gain
    mean_one = jnp.mean(scaled, axis=-1, keepdims=True)
    mean_two = jnp.mean(scaled * unit, axis=-1, keepdims=True)
    grad_in = rstd * (scaled - mean_one - unit * mean_two)
    return (
        grad_in,
        jnp.sum(grad * unit, axis=0, keepdims=True),
        jnp.sum(grad, axis=0, keepdims=True),
    )


def both(mine_ref, other_ref, rows):
    return mine_ref[rows, :].astype(F32) + other_ref[rows, :].astype(F32)


def gelu_parts(up):
    square = up * up
    bent = jnp.tanh(GELU_C * up * (1.0 + 0.044715 * square))
    half = 0.5 * (1.0 + bent)
    return square, bent, half


def group_mask(group, length):
    if group == length:
        return None
    row_image = lax.broadcasted_iota(jnp.int32, (group, group), 0) // length
    col_image = lax.broadcasted_iota(jnp.int32, (group, group), 1) // length
    return row_image == col_image


LOG2E = math.log2(math.e)


def attend(qkv_ref, mixed_ref, lse_ref, cols, width, head_dim, mask):
    scale = head_dim ** (-0.5) * LOG2E
    for head in range(width // head_dim):
        at = pl.ds(head * head_dim, head_dim)
        queries = qkv_ref[at, cols]
        keys = qkv_ref[pl.ds(width + head * head_dim, head_dim), cols]
        values = qkv_ref[pl.ds(2 * width + head * head_dim, head_dim), cols]
        scores = dot_tn(keys, queries)
        if mask is not None:
            scores = jnp.where(mask, scores, -1e30)
        top = jnp.max(scores, axis=0, keepdims=True)
        weights = jnp.exp2((scores - top) * scale)
        total = jnp.sum(weights, axis=0, keepdims=True)
        lse_ref[pl.ds(head, 1), cols] = top * scale + jnp.log2(total)
        mixed_ref[at, cols] = (dot_nn(values, weights.astype(BF16)) * (1.0 / total)).astype(BF16)


def attend_back(qkv_ref, mixed_ref, grad_ref, lse_ref, out_ref, cols, out_cols, width, head_dim, mask):
    scale = head_dim ** (-0.5)
    for head in range(width // head_dim):
        at = pl.ds(head * head_dim, head_dim)
        at_k = pl.ds(width + head * head_dim, head_dim)
        at_v = pl.ds(2 * width + head * head_dim, head_dim)
        queries, keys, values = qkv_ref[at, cols], qkv_ref[at_k, cols], qkv_ref[at_v, cols]
        grad = grad_ref[at, :]
        scores = dot_tn(keys, queries)
        if mask is not None:
            scores = jnp.where(mask, scores, -1e30)
        soft = jnp.exp2(scores * (scale * LOG2E) - lse_ref[pl.ds(head, 1), cols])
        out_ref[at_v, out_cols] = dot_nt(grad, soft.astype(BF16)).astype(BF16)
        grad_soft = dot_tn(values, grad)
        inner = jnp.sum(grad.astype(F32) * mixed_ref[at, cols].astype(F32), axis=0, keepdims=True)
        grad_scores = (soft * (grad_soft - inner)).astype(BF16)
        out_ref[at, out_cols] = (dot_nn(keys, grad_scores) * scale).astype(BF16)
        out_ref[at_k, out_cols] = (dot_nt(queries, grad_scores) * scale).astype(BF16)


def transposed_weights(attn_ref, flat_ref):
    width = attn_ref.shape[1] // 4
    for part in range(4):
        at = pl.ds(part * width, width)
        flat_ref[at, :] = attn_ref[:, at].T


def attention_rows(unit, vec_ref, flat_ref, qkv_ref, mixed_ref, lse_ref, part_ref, rows, head_dim, mask, attn_ref):
    width = mixed_ref.shape[0]
    low = (unit * vec_ref[1:2, :] + vec_ref[2:3, :]).astype(BF16)
    qkv_ref[:, rows] = dot_nt(flat_ref[: 3 * width, :], low).astype(BF16)
    attend(qkv_ref, mixed_ref, lse_ref, rows, width, head_dim, mask)
    part_ref[rows, :] = dot_nt(mixed_ref[:, rows].T, attn_ref[:, 3 * width :]).astype(BF16)


def enc_in_kernel(length, group, head_dim, pix_ref, kept_ref, table_ref, embed_ref, vec_ref, attn_ref,
                  x_ref, qkv_ref, mixed_ref, lse_ref, part_ref, pixk_ref, flat_ref):
    images, patches = table_ref.shape[0], pix_ref.shape[0] // table_ref.shape[0]
    side = table_ref.shape[1]
    transposed_weights(attn_ref, flat_ref)

    def pick(image, carry):
        rows = pl.ds(image * length, length)
        index = kept_ref[rows, :]
        hot = lax.broadcasted_iota(jnp.int32, (length, patches), 1) == index
        pixels = pix_ref[pl.ds(image * patches, patches), :]
        pixk_ref[rows, :] = dot_nn(hot.astype(BF16), pixels).astype(BF16)
        grid_at = lax.broadcasted_iota(jnp.int32, (length, side), 1)
        table = table_ref[image]
        half = table.shape[1]
        x_ref[rows, :half] = dot_exact((grid_at == index // side).astype(F32), table)
        x_ref[rows, half:] = dot_exact((grid_at == index % side).astype(F32), table)
        return carry

    lax.fori_loop(0, images, pick, 0)
    mask = group_mask(group, length)

    def step(number, carry):
        rows = pl.ds(pl.multiple_of(number * group, group), group)
        share = embed_ref.shape[2]
        rows_x = dot_nt(pixk_ref[rows, :share], embed_ref[0]) + dot_nt(pixk_ref[rows, share:], embed_ref[1])
        rows_x = rows_x + vec_ref[0:1, :] + x_ref[rows, :]
        x_ref[rows, :] = rows_x
        unit, _ = normalize(rows_x)
        attention_rows(unit, vec_ref, flat_ref, qkv_ref, mixed_ref, lse_ref, part_ref, rows, head_dim, mask, attn_ref)
        return carry

    lax.fori_loop(0, x_ref.shape[0] // group, step, 0)


def dec_in_kernel(length, head_dim, x1_ref, mine_ref, other_ref, evec_ref, bridge_ref, kept_ref, hidden_ref,
                  table_ref, vec_ref, attn_ref,
                  x2_ref, final_ref, x_ref, qkv_ref, mixed_ref, lse_ref, part_ref, flat_ref, latent_ref):
    images, side, half = table_ref.shape
    patches = side * side
    transposed_weights(attn_ref, flat_ref)
    every = pl.ds(0, x1_ref.shape[0])
    out = x1_ref[...] + both(mine_ref, other_ref, every)
    x2_ref[...] = out
    unit, _ = normalize(out)
    final = (unit * evec_ref[5:6, :] + evec_ref[6:7, :]).astype(BF16)
    final_ref[...] = final
    share = bridge_ref.shape[2]
    latent_ref[:, :share] = dot_nn(final, bridge_ref[0])
    latent_ref[:, share:] = dot_nn(final, bridge_ref[1])

    def step(image, carry):
        rows = pl.ds(pl.multiple_of(image * patches, patches), patches)
        hot = lax.broadcasted_iota(jnp.int32, (patches, length), 0) == kept_ref[pl.ds(image, 1), :]
        latent = latent_ref[pl.ds(image * length, length), :]
        table = table_ref[image]
        by_row = jnp.broadcast_to(table[:, None, :], (side, side, half)).reshape(patches, half)
        by_col = jnp.broadcast_to(table[None, :, :], (side, side, half)).reshape(patches, half)
        place = jnp.concatenate([by_row, by_col], axis=1)
        rows_x = dot_exact(hot.astype(F32), latent) + hidden_ref[rows, :] * vec_ref[0:1, :] + place
        x_ref[rows, :] = rows_x
        unit, _ = normalize(rows_x)
        attention_rows(unit, vec_ref, flat_ref, qkv_ref, mixed_ref, lse_ref, part_ref, rows, head_dim, None, attn_ref)
        return carry

    lax.fori_loop(0, images, step, 0)


def mlp_kernel(tile, x_ref, mine_ref, other_ref, vec_ref, up_ref, down_ref, x1_ref, part_ref, low_ref, acc_ref):
    number = pl.program_id(0)
    count = x_ref.shape[0] // tile

    def first(step, carry):
        rows = pl.ds(pl.multiple_of(step * tile, tile), tile)
        after = x_ref[rows, :] + both(mine_ref, other_ref, rows)
        x1_ref[rows, :] = after
        unit, _ = normalize(after)
        low_ref[rows, :] = (unit * vec_ref[3:4, :] + vec_ref[4:5, :]).astype(BF16)
        return carry

    @pl.when(number == 0)
    def _():
        lax.fori_loop(0, count, first, 0)
        acc_ref[...] = jnp.zeros_like(acc_ref)

    def step(piece, carry):
        rows = pl.ds(pl.multiple_of(piece * tile, tile), tile)
        up = dot_nn(low_ref[rows, :], up_ref[...])
        _, _, half = gelu_parts(up)
        acc_ref[rows, :] += dot_nt((up * half).astype(BF16), down_ref[...])
        return carry

    lax.fori_loop(0, count, step, 0)

    @pl.when(number == pl.num_programs(0) - 1)
    def _():
        part_ref[...] = acc_ref[...].astype(BF16)


def head_kernel(core_ref, inverse_ref, x1_ref, mine_ref, other_ref, vec_ref, bias_ref, predict_ref, target_ref,
                band_ref, weight_ref, gy_ref, glow_ref, gbias_ref, loss_ref, gain_ref, shift_ref, low_ref, gpred_ref):
    number = pl.program_id(0)

    @pl.when(number == 0)
    def _():
        for ref in (gpred_ref, gbias_ref, loss_ref, gain_ref, shift_ref):
            ref[...] = jnp.zeros_like(ref)

    every = pl.ds(0, x1_ref.shape[0])
    unit, rstd = normalize(x1_ref[...] + both(mine_ref, other_ref, every))
    gain = vec_ref[5:6, :]
    final = (unit * gain + vec_ref[6:7, :]).astype(BF16)
    share = gpred_ref.shape[1]
    predicted = jnp.concatenate([dot_nn(final, predict_ref[0]), dot_nn(final, predict_ref[1])], axis=1)
    mismatch = predicted + bias_ref[...] - target_ref[...].astype(F32)
    band = band_ref[...]
    level = jnp.where(band == 0, inverse_ref[0], jnp.where(band == 1, inverse_ref[1], inverse_ref[2]))
    level = level * weight_ref[...]
    square = mismatch * mismatch + EPS_C
    root = lax.rsqrt(square)
    loss_ref[...] += jnp.sum(level * (square * root), axis=0, keepdims=True)
    grad = level * (mismatch * root)
    gbias_ref[...] += jnp.sum(grad, axis=0, keepdims=True)
    low_ref[...] = grad.astype(BF16)
    columns = pl.ds(pl.multiple_of(core_ref[0] * share, share), share)
    gpred_ref[...] += dot_tn(final, low_ref[:, columns])
    grad_final = dot_nt(low_ref[:, :share], predict_ref[0]) + dot_nt(low_ref[:, share:], predict_ref[1])
    grad_in, gain_sum, shift_sum = norm_back(grad_final, gain, unit, rstd)
    gy_ref[...] = grad_in
    gain_ref[...] += gain_sum
    shift_ref[...] += shift_sum

    @pl.when(number == pl.num_programs(0) - 1)
    def _():
        glow_ref[...] = gpred_ref[...].astype(BF16)


def mlp_back_kernel(tile, gy_ref, x1_ref, vec_ref, up_ref, down_ref, gup_ref, gdown_ref, part_ref,
                    low_ref, lowt_ref, grad_ref, gradt_ref, gu_ref, z_ref, acc_ref):
    number = pl.program_id(0)
    count = x1_ref.shape[0] // tile

    def first(step, carry):
        rows = pl.ds(pl.multiple_of(step * tile, tile), tile)
        unit, _ = normalize(x1_ref[rows, :])
        low = (unit * vec_ref[3:4, :] + vec_ref[4:5, :]).astype(BF16)
        low_ref[rows, :] = low
        lowt_ref[:, rows] = low.T
        grad = gy_ref[rows, :].astype(BF16)
        grad_ref[rows, :] = grad
        gradt_ref[:, rows] = grad.T
        return carry

    @pl.when(number == 0)
    def _():
        lax.fori_loop(0, count, first, 0)
        acc_ref[...] = jnp.zeros_like(acc_ref)

    def step(piece, carry):
        rows = pl.ds(pl.multiple_of(piece * tile, tile), tile)
        up = dot_nn(low_ref[rows, :], up_ref[...])
        square, bent, half = gelu_parts(up)
        z_ref[rows, :] = (up * half).astype(BF16)
        slope = half + (0.5 * GELU_C) * up * (1.0 - bent * bent) * (1.0 + (3.0 * 0.044715) * square)
        grad_up = (dot_nn(grad_ref[rows, :], down_ref[...]) * slope).astype(BF16)
        gu_ref[rows, :] = grad_up
        acc_ref[rows, :] += dot_nt(grad_up, up_ref[...])
        return carry

    lax.fori_loop(0, count, step, 0)
    gup_ref[...] = dot_nn(lowt_ref[...], gu_ref[...]).astype(BF16)
    gdown_ref[...] = dot_nn(gradt_ref[...], z_ref[...]).astype(BF16)

    @pl.when(number == pl.num_programs(0) - 1)
    def _():
        part_ref[...] = acc_ref[...].astype(BF16)


def attn_back_kernel(length, group, head_dim, gy_ref, x1_ref, mine_ref, other_ref, x_ref, qkv_ref, mixed_ref, lse_ref,
                     vec_ref, attn_ref, gx_ref, grad_ref, gain_ref, shift_ref, part_ref,
                     flat_ref, lowt_ref, gradt_ref, gmix_ref, gqkv_ref):
    width = mixed_ref.shape[0]
    transposed_weights(attn_ref, flat_ref)
    gain_ref[...] = jnp.zeros_like(gain_ref)
    shift_ref[...] = jnp.zeros_like(shift_ref)
    mask = group_mask(group, length)

    def step(number, carry):
        rows = pl.ds(pl.multiple_of(number * group, group), group)
        unit, rstd = normalize(x1_ref[rows, :])
        grad_in, gain_sum, shift_sum = norm_back(both(mine_ref, other_ref, rows), vec_ref[3:4, :], unit, rstd)
        grad_in = grad_in + gy_ref[rows, :]
        gx_ref[rows, :] = grad_in
        gain_ref[...] += gain_sum
        shift_ref[...] += shift_sum
        low_grad = grad_in.astype(BF16)
        gradt_ref[:, rows] = low_grad.T
        gmix_ref[...] = dot_nt(flat_ref[3 * width :, :], low_grad).astype(BF16)
        attend_back(qkv_ref, mixed_ref, gmix_ref, lse_ref, gqkv_ref, rows, rows, width, head_dim, mask)
        part_ref[rows, :] = dot_nn(gqkv_ref[:, rows].T, flat_ref[: 3 * width, :]).astype(BF16)
        unit_a, _ = normalize(x_ref[rows, :])
        lowt_ref[:, rows] = (unit_a * vec_ref[1:2, :] + vec_ref[2:3, :]).astype(BF16).T
        return carry

    lax.fori_loop(0, x_ref.shape[0] // group, step, 0)
    grad_ref[:, : 3 * width] = dot_nt(lowt_ref[...], gqkv_ref[...]).astype(BF16)
    grad_ref[:, 3 * width :] = dot_nt(gradt_ref[...], mixed_ref[...]).astype(BF16)


def between_kernel(length, core_ref, gx_ref, x_ref, mine_ref, other_ref, vec_ref, kept_ref, hidden_ref, final_ref, x2_ref,
                   evec_ref, bridge_ref, gain_ref, shift_ref, mask_ref, gbridge_ref, egain_ref, eshift_ref, gy_ref,
                   latent_ref):
    images = kept_ref.shape[0] // length
    patches = x_ref.shape[0] // images
    for ref in (gain_ref, shift_ref, mask_ref):
        ref[...] = jnp.zeros_like(ref)

    def step(image, carry):
        rows = pl.ds(pl.multiple_of(image * patches, patches), patches)
        unit, rstd = normalize(x_ref[rows, :])
        grad_in, gain_sum, shift_sum = norm_back(both(mine_ref, other_ref, rows), vec_ref[1:2, :], unit, rstd)
        grad_in = grad_in + gx_ref[rows, :]
        gain_ref[...] += gain_sum
        shift_ref[...] += shift_sum
        mask_ref[...] += jnp.sum(grad_in * hidden_ref[rows, :], axis=0, keepdims=True)
        kept_rows = pl.ds(pl.multiple_of(image * length, length), length)
        hot = lax.broadcasted_iota(jnp.int32, (length, patches), 1) == kept_ref[kept_rows, :]
        latent_ref[kept_rows, :] = dot_nn(hot.astype(BF16), grad_in.astype(BF16)).astype(BF16)
        return carry

    lax.fori_loop(0, images, step, 0)
    share = gbridge_ref.shape[1]
    columns = pl.ds(pl.multiple_of(core_ref[0] * share, share), share)
    gbridge_ref[...] = dot_tn(final_ref[...], latent_ref[:, columns]).astype(BF16)
    grad_final = dot_nt(latent_ref[:, :share], bridge_ref[0]) + dot_nt(latent_ref[:, share:], bridge_ref[1])
    unit, rstd = normalize(x2_ref[...])
    gy_ref[...], egain_ref[...], eshift_ref[...] = norm_back(grad_final, evec_ref[5:6, :], unit, rstd)


def enc_out_kernel(core_ref, gx_ref, x_ref, mine_ref, other_ref, vec_ref, pixk_ref,
                   gain_ref, shift_ref, ebias_ref, gembed_ref):
    every = pl.ds(0, x_ref.shape[0])
    unit, rstd = normalize(x_ref[...])
    grad_in, gain_ref[...], shift_ref[...] = norm_back(both(mine_ref, other_ref, every), vec_ref[1:2, :], unit, rstd)
    grad_in = grad_in + gx_ref[...]
    ebias_ref[...] = jnp.sum(grad_in, axis=0, keepdims=True)
    share = gembed_ref.shape[1]
    columns = pl.ds(pl.multiple_of(core_ref[0] * share, share), share)
    gembed_ref[...] = dot_tn(grad_in.astype(BF16), pixk_ref[:, columns]).astype(BF16)


def shape(dims, dtype):
    return jax.ShapeDtypeStruct(dims, dtype)


def run(kernel, outs, scratch, args, flops, scalars=0):
    moved = sum(math.prod(a.shape) * a.dtype.itemsize for a in list(args) + list(outs))
    in_vmem = pl.BlockSpec(memory_space=pltpu.VMEM)
    return pl.pallas_call(
        kernel,
        out_shape=tuple(outs),
        in_specs=[pl.BlockSpec(memory_space=pltpu.SMEM)] * scalars + [in_vmem] * (len(args) - scalars),
        out_specs=tuple([in_vmem] * len(outs)),
        scratch_shapes=scratch,
        compiler_params=pltpu.CompilerParams(vmem_limit_bytes=VMEM_LIMIT),
        cost_estimate=pl.CostEstimate(flops=flops, bytes_accessed=moved, transcendentals=0),
    )(*args)


def other_core(block):
    return lax.ppermute(block, "mp", [(0, 1), (1, 0)])


def mlp_forward(x, mine, vec, stack):
    rows, width = x.shape
    hidden = stack.shape[1] // 2
    block = min(hidden, 512)
    tile = min(rows, 512)
    other = other_core(mine)
    whole = pl.BlockSpec((rows, width), lambda i: (0, 0))
    cols = pl.BlockSpec((width, block), lambda i: (0, i))
    later = pl.BlockSpec((width, block), lambda i: (0, i + hidden // block))
    return pl.pallas_call(
        functools.partial(mlp_kernel, tile),
        out_shape=(shape((rows, width), F32), shape((rows, width), BF16)),
        grid=(hidden // block,),
        in_specs=[whole] * 3 + [pl.BlockSpec((8, width), lambda i: (0, 0)), cols, later],
        out_specs=(whole, whole),
        scratch_shapes=[pltpu.VMEM((rows, width), BF16), pltpu.VMEM((rows, width), F32)],
        compiler_params=pltpu.CompilerParams(vmem_limit_bytes=VMEM_LIMIT),
        cost_estimate=pl.CostEstimate(flops=4 * rows * width * hidden, bytes_accessed=rows * width * 14 + width * hidden * 4,
                                      transcendentals=rows * hidden),
    )(x, mine, other, vec, stack, stack)


def mlp_backward(gy, x1, vec, stack):
    rows, width = x1.shape
    hidden = stack.shape[1] // 2
    block = min(hidden, 512)
    tile = min(rows, 256)
    whole = pl.BlockSpec((rows, width), lambda i: (0, 0))
    cols = pl.BlockSpec((width, block), lambda i: (0, i))
    later = pl.BlockSpec((width, block), lambda i: (0, i + hidden // block))
    return pl.pallas_call(
        functools.partial(mlp_back_kernel, tile),
        out_shape=(shape((width, hidden), BF16), shape((width, hidden), BF16), shape((rows, width), BF16)),
        grid=(hidden // block,),
        in_specs=[whole] * 2 + [pl.BlockSpec((8, width), lambda i: (0, 0)), cols, later],
        out_specs=(cols, cols, whole),
        scratch_shapes=[
            pltpu.VMEM((rows, width), BF16), pltpu.VMEM((width, rows), BF16),
            pltpu.VMEM((rows, width), BF16), pltpu.VMEM((width, rows), BF16),
            pltpu.VMEM((rows, block), BF16), pltpu.VMEM((rows, block), BF16),
            pltpu.VMEM((rows, width), F32)],
        compiler_params=pltpu.CompilerParams(vmem_limit_bytes=VMEM_LIMIT),
        cost_estimate=pl.CostEstimate(flops=10 * rows * width * hidden, bytes_accessed=rows * width * 10 + width * hidden * 8,
                                      transcendentals=rows * hidden),
    )(gy, x1, vec, stack, stack)


def head(core, inverse, x1, mine, vec, bias, predict, target, band, weight, patches):
    rows, width = x1.shape
    pixels = target.shape[1]
    share = pixels // 2
    other = other_core(mine)
    smem = pl.BlockSpec(memory_space=pltpu.SMEM)
    row_w = pl.BlockSpec((patches, width), lambda i: (i, 0))
    row_p = pl.BlockSpec((patches, pixels), lambda i: (i, 0))
    fix = lambda a, b: pl.BlockSpec((a, b), lambda i: (0, 0))
    return pl.pallas_call(
        head_kernel,
        out_shape=(shape((rows, width), F32), shape((width, share), BF16), shape((1, pixels), F32),
                   shape((1, pixels), F32), shape((1, width), F32), shape((1, width), F32)),
        grid=(rows // patches,),
        in_specs=[smem, smem, row_w, row_w, row_w, fix(8, width), fix(1, pixels), pl.BlockSpec((2, width, share), lambda i: (0, 0, 0)), row_p, row_p,
                  pl.BlockSpec((patches, 1), lambda i: (i, 0))],
        out_specs=(row_w, fix(width, share), fix(1, pixels), fix(1, pixels), fix(1, width), fix(1, width)),
        scratch_shapes=[pltpu.VMEM((patches, pixels), BF16), pltpu.VMEM((width, share), F32)],
        compiler_params=pltpu.CompilerParams(vmem_limit_bytes=VMEM_LIMIT),
        cost_estimate=pl.CostEstimate(flops=5 * rows * width * pixels, bytes_accessed=rows * (width * 12 + pixels * 6),
                                      transcendentals=rows * pixels),
    )(core, inverse, x1, mine, other, vec, bias, predict, target, band, weight)


def attn_backward(gy, x1, mine, x, saved, vec, attn, length, group, head_dim):
    qkv, mixed, lse = saved
    rows, width = x.shape
    local = mixed.shape[0]
    return run(
        functools.partial(attn_back_kernel, length, group, head_dim),
        [shape((rows, width), F32), shape((width, 4 * local), BF16),
         shape((1, width), F32), shape((1, width), F32), shape((rows, width), BF16)],
        [pltpu.VMEM((4 * local, width), BF16), pltpu.VMEM((width, rows), BF16), pltpu.VMEM((width, rows), BF16),
         pltpu.VMEM((local, group), BF16), pltpu.VMEM((3 * local, rows), BF16)],
        (gy, x1, mine, other_core(mine), x, qkv, mixed, lse, vec, attn),
        18 * rows * width * local)


def sine_table(gsd_values, feature_width, grid_side):
    quarter = feature_width // 4
    frequency = jnp.exp(-jnp.log(10000.0) * jnp.arange(quarter).astype(F32) / quarter)
    gsd_ratio = gsd_values.astype(F32)[:, None, None] / REF_GSD
    line = jnp.arange(grid_side, dtype=jnp.int32).astype(F32)
    arg = line[None, :, None] * gsd_ratio * frequency
    return jnp.concatenate([jnp.sin(arg), jnp.cos(arg)], axis=-1)


def dp_bits():
    return lax.axis_size("dp").bit_length() - 1


def orders():
    bits = dp_bits()
    high = list(range(bits - 1, 1, -1))
    return (high + [0, 1], high + [1, 0])


def swap(block, bit):
    size = lax.axis_size("dp")
    return lax.ppermute(block, "dp", [(i, i ^ (1 << bit)) for i in range(size)])


def my_bit(bit):
    return (lax.axis_index("dp") >> bit) & 1


def gather_dp(block, axis, order):
    lead, rest = (block.shape[:axis], block.shape[axis:])
    done = []
    cur = block
    for bit in order:
        other = swap(cur, bit)
        mine = my_bit(bit) == 1
        place = axis + sum(1 for b in done if b > bit)
        cur = jnp.stack([jnp.where(mine, other, cur), jnp.where(mine, cur, other)], axis=place)
        done.append(bit)
    return cur.reshape(lead + (rest[0] * lax.axis_size("dp"),) + rest[1:])


def reduce_dp(block, axis, order, wire):
    bits = dp_bits()
    lead, rest = (block.shape[:axis], block.shape[axis:])
    shard = rest[0] // lax.axis_size("dp")
    cur = block.reshape(lead + (2,) * bits + (shard,) + rest[1:])
    left = list(range(bits - 1, -1, -1))
    for bit in reversed(order):
        place = axis + left.index(bit)
        mine = my_bit(bit)
        keep = lax.dynamic_index_in_dim(cur, mine, place, keepdims=False)
        give = lax.dynamic_index_in_dim(cur, 1 - mine, place, keepdims=False)
        other = swap(give.astype(wire), bit)
        cur = keep.astype(F32) + other.astype(F32)
        left.remove(bit)
    return cur


def join_cores(mine, core):
    other = other_core(mine)
    return jnp.concatenate([jnp.where(core == 0, mine, other), jnp.where(core == 0, other, mine)], axis=1)


def total_dp(value):
    for bit in range(dp_bits()):
        value = value + swap(value, bit)
    return value


def place_of():
    index = lax.axis_index("dp")
    core = lax.axis_index("mp")
    low, high = lax.rem(index, 4), index // 4
    bit_x, bit_y = lax.rem(low, 2), low // 2
    low_x, low_y = low + 1 - 2 * bit_x, low + 2 - 4 * bit_y
    return core, low, high, low_x, low_y


def greet(partners):
    barrier = pltpu.get_barrier_semaphore()
    for partner in partners:
        pl.semaphore_signal(barrier, inc=1, device_id=partner, device_id_type=pl.DeviceIdType.MESH)
    pl.semaphore_wait(barrier, len(partners))


def blocks_of(widths, limit, fine=()):
    found = []
    for number, width in enumerate(widths):
        start = 0
        while start < width:
            size = min(limit // 2 if number in fine else limit, width - start)
            found.append((number, start, size))
            start += size
    return found


def remote(source, target, send, receive, device):
    return pltpu.make_async_remote_copy(
        src_ref=source, dst_ref=target, send_sem=send, recv_sem=receive,
        device_id=device, device_id_type=pl.DeviceIdType.MESH)


def total_blocks(block_ref, near_ref, far_ref, sems, low, high, core, highs, stage):
    send, receive = sems
    if stage == 0:
        spots = [(high * 4 + lax.rem(low + k, 4), core) for k in range(1, 4)]
        return [remote(block_ref, near_ref.at[low], send.at[k], receive.at[k], spots[k]) for k in range(3)]
    spots = [(lax.rem(high + k, highs) * 4 + low, core) for k in range(1, highs)]
    return [remote(block_ref, far_ref.at[high], send.at[3 + k], receive.at[3 + k], spots[k]) for k in range(highs - 1)]


def forward_kernel(highs, shared, groups, count, length, group, head_dim, *refs):
    masters, refs = refs[:count], refs[count:]
    pix_any, band_ref, kept_ref, inter_ref, table_ref, placed_ref = refs[:6]
    fulls, refs = refs[6 : 6 + count], refs[6 + count :]
    (x_ref, qkv_ref, mixed_ref, lse_ref, pixk_ref, x1_ref, last_ref, far_out_ref, counts_ref, flat_ref, vec_ref, rows_ref,
     column_ref) = refs[:13]
    refs = refs[13:]
    shards, refs = refs[:count], refs[count:]
    (pix_ref, bands_v, embed_v, attn_v, mlp_v, part_ref, other_ref, low_ref, acc_ref, block_ref, near_ref,
     far_ref) = refs[:12]
    (own_sem, zs_sem, zr_sem, cs_sem, cr_sem, fs_sem, fr_sem, ms_sem, mr_sem, load_sem, xs_sem, xr_sem, ts_sem,
     tr_sem, mload_sem) = refs[12:]
    core, low, high, low_x, low_y = place_of()
    at_x, at_y = (high * 4 + low_x, core), (high * 4 + low_y, core)
    at_high = [(lax.rem(high + k, highs) * 4 + low, core) for k in range(1, highs)]
    sibling = (high * 4 + low, 1 - core)
    near = [(high * 4 + lax.rem(low + k, 4), core) for k in range(1, 4)]
    greet([sibling] + near + at_high)
    for master, shard, split in zip(masters, shards, shared):
        if len(master.shape) == 3:
            wide = master.shape[2]
            for part in range(master.shape[0]):
                shard[:, part * wide : (part + 1) * wide] = master[part].astype(BF16)
        else:
            share = shard.shape[1]
            shard[...] = master[:, pl.ds(pl.multiple_of(core * share, share), share)].astype(BF16)

    def full(at):
        number, start, size = groups[at]
        ref = fulls[number].at[core] if shared[number] else fulls[number]
        return ref, pl.ds(start, size)

    def first(at):
        ref, cols = full(at)
        shard = shards[groups[at][0]].at[:, cols]
        mine = ref.at[high, low, :, cols]
        copies = [pltpu.make_async_copy(shard, mine, own_sem.at[at])]
        for k in range(1, highs):
            copies.append(remote(shard, mine, zs_sem.at[at, k - 1], zr_sem.at[at, k - 1], at_high[k - 1]))
        return copies

    def column(at):
        ref, cols = full(at)
        part = ref.at[:, low, :, cols]
        return [remote(part, part, cs_sem.at[at, 0], cr_sem.at[at, 0], at_x),
                remote(part, part, cs_sem.at[at, 1], cr_sem.at[at, 1], at_y)]

    def forward(at):
        ref, cols = full(at)
        which, device = (low_x, at_y) if at % 2 == 0 else (low_y, at_x)
        part = ref.at[:, which, :, cols]
        return remote(part, part, fs_sem.at[at], fr_sem.at[at], device)

    def swap(number):
        part = fulls[number].at[core]
        return remote(part, part, ms_sem.at[number], mr_sem.at[number], sibling)

    def exchange(at, source, target):
        return remote(source, target, xs_sem.at[at], xr_sem.at[at], sibling)

    total = len(groups)
    pairs = (total + 1) // 2
    in_pair = lambda pair: [at for at in (2 * pair, 2 * pair + 1) if at < total]
    pair_of = lambda number: max(at for at in range(total) if groups[at][0] == number) // 2
    images, side = table_ref.shape[0], table_ref.shape[1]
    patches = side * side
    width = mixed_ref.shape[0]
    mask = group_mask(group, length)

    def lane_of(image, flipped):
        lanes = lax.broadcasted_iota(jnp.int32, flipped.shape, 1)
        return jnp.sum(jnp.where(lanes == image, flipped, 0.0), axis=1, keepdims=True)

    def pick(image, carry):
        rows = pl.ds(pl.multiple_of(image * length, length), length)
        index = lane_of(image, kept_ref[...].astype(F32).T).astype(jnp.int32)
        column_ref[rows, :] = index
        hot = lax.broadcasted_iota(jnp.int32, (length, patches), 1) == index
        pixels = pix_ref[pl.ds(pl.multiple_of(image * patches, patches), patches), :]
        pixk_ref[rows, :] = dot_nn(hot.astype(BF16), pixels).astype(BF16)
        grid_at = lax.broadcasted_iota(jnp.int32, (length, side), 1)
        table = table_ref[image]
        half = table.shape[1]
        x_ref[rows, :half] = dot_exact((grid_at == index // side).astype(F32), table)
        x_ref[rows, half:] = dot_exact((grid_at == index % side).astype(F32), table)
        return carry

    def tally(image, carry):
        rows = pl.ds(pl.multiple_of(image * patches, patches), patches)
        hot = lax.broadcasted_iota(jnp.int32, (patches, length), 0) == kept_ref[pl.ds(image, 1), :]
        hidden = 1.0 - jnp.max(jnp.where(hot, 1.0, 0.0), axis=1, keepdims=True)
        weight = hidden * (1.0 - 0.5 * lane_of(image, inter_ref[...].astype(F32).T))
        rows_ref[rows, 0:1] = hidden
        rows_ref[rows, 1:2] = weight
        band = bands_v[rows, :]
        for level in range(NB):
            row = jnp.sum(jnp.where(band == level, weight, 0.0), axis=0, keepdims=True)
            for start in range(0, row.shape[1], 128):
                block_ref[24 + level : 25 + level, 0:128] += row[:, start : start + 128]
        return carry

    def rows_step(number, carry):
        rows = pl.ds(pl.multiple_of(number * group, group), group)
        share = embed_v.shape[-1]
        embed = lambda half: embed_v[half].reshape(-1, share)
        rows_x = dot_nt(pixk_ref[rows, :share], embed(0)) + dot_nt(pixk_ref[rows, share:], embed(1))
        rows_x = rows_x + vec_ref[0:1, :] + x_ref[rows, :]
        x_ref[rows, :] = rows_x
        unit, _ = normalize(rows_x)
        low_a = (unit * vec_ref[1:2, :] + vec_ref[2:3, :]).astype(BF16)
        qkv_ref[:, rows] = dot_nt(flat_ref[: 3 * width, :], low_a).astype(BF16)
        attend(qkv_ref, mixed_ref, lse_ref, rows, width, head_dim, mask)
        part_ref[rows, :] = dot_nn(mixed_ref[:, rows].T, flat_ref[3 * width :, :]).astype(BF16)
        return carry

    def mlp_first():
        after = x_ref[...] + both(part_ref, other_ref, pl.ds(0, x_ref.shape[0]))
        x1_ref[...] = after
        unit, _ = normalize(after)
        low_ref[...] = (unit * vec_ref[3:4, :] + vec_ref[4:5, :]).astype(BF16)
        acc_ref[...] = jnp.zeros_like(acc_ref)

    def mlp_block(piece, carry):
        size = 512
        hidden = mlp_v.shape[-1] // 2
        start = piece * size
        wide = x_ref.shape[1]
        up = dot_nn(low_ref[...], mlp_v[:, :, :, pl.ds(start, size)].reshape(wide, size))
        _, _, half = gelu_parts(up)
        down = mlp_v[:, :, :, pl.ds(hidden + start, size)].reshape(wide, size)
        acc_ref[...] += dot_nt((up * half).astype(BF16), down)
        return carry

    load_bands = pltpu.make_async_copy(band_ref, bands_v, load_sem.at[0])
    load_pixels = pltpu.make_async_copy(pix_any, pix_ref, load_sem.at[4])
    load_attn = pltpu.make_async_copy(fulls[1], attn_v, load_sem.at[1])
    load_embed = pltpu.make_async_copy(fulls[0], embed_v, load_sem.at[2])

    def load_mlp(at):
        cols = pl.ds(groups[at][1], groups[at][2])
        return pltpu.make_async_copy(fulls[2].at[:, :, :, cols], mlp_v.at[:, :, :, cols], mload_sem.at[groups[at][1] // 512])

    stages = functools.partial(total_blocks, block_ref, near_ref, far_ref, (ts_sem, tr_sem), low, high, core, highs)
    attn_at, blocks_done = pair_of(1) + 3, 0
    row_groups = x_ref.shape[0] // group
    swapped = set()
    for step in range(pairs + 3):
        if step < pairs:
            for at in in_pair(step):
                for copy in first(at):
                    copy.start()
        if 0 <= step - 1 < pairs:
            for at in in_pair(step - 1):
                for copy in first(at):
                    copy.wait()
                for copy in column(at):
                    copy.start()
        if 0 <= step - 2 < pairs:
            for at in in_pair(step - 2):
                column(at)[at % 2].wait()
                forward(at).start()
        if 0 <= step - 3 < pairs:
            for at in in_pair(step - 3):
                column(at)[1 - at % 2].wait()
                forward(at).wait()
                if groups[at][0] == 2:
                    load_mlp(at).start()
        for number in range(count):
            if shared[number] and number not in swapped and pair_of(number) + 3 <= step:
                swap(number).start()
                swapped.add(number)
        if step == 0:
            load_bands.start()
            load_pixels.start()
            block_ref[...] = jnp.zeros_like(block_ref)
            block_ref[:24, :] = placed_ref[...]
            load_bands.wait()
            lax.fori_loop(0, images, tally, 0)
            near_ref[low] = block_ref[...]
            for copy in stages(0):
                copy.start()
        if step == 1:
            for copy in stages(0):
                copy.wait()
            block_ref[...] = (near_ref[0] + near_ref[1]) + (near_ref[2] + near_ref[3])
            far_ref[high] = block_ref[...]
            for copy in stages(1):
                copy.start()
            load_pixels.wait()
            lax.fori_loop(0, images, pick, 0)
        if step == 2:
            for copy in stages(1):
                copy.wait()
            counts = far_ref[0]
            for k in range(1, highs):
                counts = counts + far_ref[k]
            counts_ref[...] = counts
            vec_ref[...] = jnp.zeros_like(vec_ref)
            for piece in range(7):
                vec_ref[piece : piece + 1, :512] = counts[2 * piece : 2 * piece + 1, :]
                vec_ref[piece : piece + 1, 512:] = counts[2 * piece + 1 : 2 * piece + 2, :]
        if step == attn_at:
            swap(0).wait()
            load_attn.start()
            load_embed.start()
            load_attn.wait()
            for part in range(4):
                at = pl.ds(part * width, width)
                flat_ref[at, :] = attn_v[:, :, :, at].reshape(-1, width).T
            load_embed.wait()
        if attn_at <= step < attn_at + 2:
            lax.fori_loop((step - attn_at) * row_groups // 2, (step - attn_at + 1) * row_groups // 2, rows_step, 0)
            if step == attn_at + 1:
                exchange(0, part_ref, other_ref).start()
        if step == attn_at + 2:
            exchange(0, part_ref, other_ref).wait()
            mlp_first()
        if step >= attn_at + 2:
            half = mlp_v.shape[-1] // 2
            for tile in range(blocks_done, half // 512):
                ends = [at for at in range(total) if groups[at][0] == 2 and groups[at][1] in (tile * 512, half + tile * 512)]
                if max(ends) // 2 + 3 > step:
                    break
                for at in ends:
                    load_mlp(at).wait()
                mlp_block(tile, 0)
                blocks_done = tile + 1
                if blocks_done == half // 512:
                    last_ref[...] = acc_ref[...].astype(BF16)
                    exchange(1, last_ref, far_out_ref).start()
    exchange(1, last_ref, far_out_ref).wait()
    for number in range(1, count):
        if shared[number]:
            swap(number).wait()


def forward_all(masters, shared, pixels, band_ids, kept_index, intersection, table, placed):
    size = lax.axis_size("dp")
    highs = size // 4
    count = len(masters)
    dims_of = []
    for master, split in zip(masters, shared):
        if master.ndim == 3:
            dims_of.append((master.shape[1], master.shape[0] * master.shape[2]))
        else:
            dims_of.append((master.shape[0], master.shape[1] // 2))
    groups = blocks_of([dims[1] for dims in dims_of], 512, (0, 1))
    half = dims_of[2][1] // 2
    groups.sort(key=lambda block: (block[0], block[1] % half if block[0] == 2 else 0, block[1]))
    total = len(groups)
    images, length = kept_index.shape
    rows, wide, local = images * length, D, dims_of[1][1] // 4
    rows_d = pixels.shape[0]
    group = 2 * length
    fulls = []
    for dims, split in zip(dims_of, shared):
        dims = (highs, 4) + dims
        fulls.append(shape((2,) + dims if split else dims, BF16))
    block = (32, 512)
    outs = [shape((rows, wide), F32), shape((3 * local, rows), BF16), shape((local, rows), BF16),
            shape((local // DH, rows), F32), shape((rows, pixels.shape[1]), BF16), shape((rows, wide), F32),
            shape((rows, wide), BF16), shape((rows, wide), BF16), shape(block, F32), shape((4 * local, wide), BF16),
            shape((8, wide), F32), shape((rows_d, 2), F32), shape((rows, 1), jnp.int32)]
    dma = pltpu.SemaphoreType.DMA
    in_vmem = pl.BlockSpec(memory_space=pltpu.VMEM)
    any_space = pl.BlockSpec(memory_space=pl.ANY)
    result = pl.pallas_call(
        functools.partial(forward_kernel, highs, shared, groups, count, length, group, DH),
        out_shape=tuple(fulls + outs),
        in_specs=[in_vmem] * count + [any_space] * 2 + [in_vmem] * 4,
        out_specs=tuple([any_space] * count + [in_vmem] * len(outs)),
        scratch_shapes=[pltpu.VMEM(dims, BF16) for dims in dims_of] + [
            pltpu.VMEM(pixels.shape, BF16), pltpu.VMEM(band_ids.shape, jnp.int32), pltpu.VMEM(fulls[0].shape, BF16),
            pltpu.VMEM(fulls[1].shape, BF16), pltpu.VMEM(fulls[2].shape, BF16), pltpu.VMEM((rows, wide), BF16),
            pltpu.VMEM((rows, wide), BF16), pltpu.VMEM((rows, wide), BF16), pltpu.VMEM((rows, wide), F32),
            pltpu.VMEM(block, F32), pltpu.VMEM((4,) + block, F32), pltpu.VMEM((highs,) + block, F32),
            dma((total,)), dma((total, highs - 1)), dma((total, highs - 1)), dma((total, 2)), dma((total, 2)),
            dma((total,)), dma((total,)), dma((count,)), dma((count,)), dma((5,)), dma((2,)), dma((2,)),
            dma((highs + 2,)), dma((highs + 2,)), dma((2 * half // 512,))],
        compiler_params=pltpu.CompilerParams(collective_id=0, has_side_effects=True, vmem_limit_bytes=62 * 2**20),
        cost_estimate=pl.CostEstimate(flops=0, bytes_accessed=2**25, transcendentals=0),
    )(*masters, pixels, band_ids, kept_index, intersection, table, placed)
    weights = [full.reshape(((2,) if split else ()) + (size * dims[0], dims[1]))
               for full, split, dims in zip(result[:count], shared, dims_of)]
    return weights, result[count:]


def gather_all(shards, shared):
    order_a, order_b = orders()
    fulls = []
    for number, shard in enumerate(shards):
        full = gather_dp(shard, 0, (order_a, order_b)[number % 2])
        if shared[number]:
            other, zero = other_core(full), lax.axis_index("mp") == 0
            full = jnp.stack([jnp.where(zero, full, other), jnp.where(zero, other, full)])
        fulls.append(full)
    return fulls


class Gatherer:
    def __init__(self, highs, groups, shards, fulls, sems):
        self.highs, self.groups, self.shards, self.fulls = highs, groups, shards, fulls
        self.own_sem, self.zs_sem, self.zr_sem, self.cs_sem, self.cr_sem, self.fs_sem, self.fr_sem = sems
        self.core, self.low, self.high, self.low_x, self.low_y = place_of()
        self.at_x, self.at_y = (self.high * 4 + self.low_x, self.core), (self.high * 4 + self.low_y, self.core)
        self.at_high = [(lax.rem(self.high + k, highs) * 4 + self.low, self.core) for k in range(1, highs)]
        self.pairs = (len(groups) + 1) // 2

    def in_pair(self, pair):
        return [at for at in (2 * pair, 2 * pair + 1) if 0 <= at < len(self.groups)] if 0 <= pair < self.pairs else []

    def full(self, at):
        number, start, size = self.groups[at]
        return self.fulls[number], pl.ds(start, size)

    def first(self, at):
        ref, cols = self.full(at)
        shard = self.shards[self.groups[at][0]].at[:, cols]
        mine = ref.at[self.high, self.low, :, cols]
        return [pltpu.make_async_copy(shard, mine, self.own_sem.at[at])] + [
            remote(shard, mine, self.zs_sem.at[at, k - 1], self.zr_sem.at[at, k - 1], self.at_high[k - 1])
            for k in range(1, self.highs)]

    def column(self, at, way):
        ref, cols = self.full(at)
        part = ref.at[:, self.low, :, cols]
        return remote(part, part, self.cs_sem.at[at, way], self.cr_sem.at[at, way], (self.at_x, self.at_y)[way])

    def forward(self, at):
        ref, cols = self.full(at)
        which, device = (self.low_x, self.at_y) if at % 2 == 0 else (self.low_y, self.at_x)
        part = ref.at[:, which, :, cols]
        return remote(part, part, self.fs_sem.at[at], self.fr_sem.at[at], device)

    def step(self, step):
        for at in self.in_pair(step):
            for copy in self.first(at):
                copy.start()
        for at in self.in_pair(step - 1):
            for copy in self.first(at):
                copy.wait()
            for way in range(2):
                self.column(at, way).start()
        for at in self.in_pair(step - 2):
            self.column(at, at % 2).wait()
            self.forward(at).start()
        for at in self.in_pair(step - 3):
            self.column(at, 1 - at % 2).wait()
            self.forward(at).wait()


def gatherer_sems(highs, groups):
    dma, total = pltpu.SemaphoreType.DMA, len(groups)
    return [dma((total,)), dma((total, highs - 1)), dma((total, highs - 1)), dma((total, 2)), dma((total, 2)),
            dma((total,)), dma((total,))]


def decoder_kernel(length, head_dim, highs, gathered, reduced, evec_ref, kept_ref, column_ref,
                   rows_ref, table_ref, totals_ref, mlp_in, predict_in, x1e_any, mine_any, other_any, target_any, band_any, attn_any, bridge_any,
                   gy_out, gattn_ref, gbridge_ref, rpred_ref, rup_ref, rdown_ref, norm_ref, loss_ref, vgrad_ref,
                   gup_ref, gdown_ref, gpred_ref, mlp_shard, predict_shard,
                   gbias_ref, sums_ref, esums_ref, final_ref, glat_ref, x_ref, x1_ref, gy_ref, qkv_ref, mixed_ref, lse_ref,
                   part_ref, from_ref, lowt_ref, gradt_ref, z_ref, gu_ref, flat_ref, mlp_ref, bridge_ref, predict_ref,
                   target_ref, band_ref, gp_ref, gpred_acc, gmix_ref, gq_ref, vec_ref, load_sem, stream_sem, send_sem, receive_sem,
                   join_sem, *comm):
    core, index = lax.axis_index("mp"), lax.axis_index("dp")
    sibling = (index, 1 - core)
    gather = Gatherer(highs, gathered, (mlp_shard, predict_shard), (mlp_ref, predict_ref.at[core]), comm[:7])
    pred_view = rpred_ref.at[core]
    red, _ = make_reducer(highs, reduced, (1.0,) * 3, (gpred_ref, gup_ref, gdown_ref), (pred_view, rup_ref, rdown_ref),
                          norm_ref, comm[7:])
    greet([sibling, gather.at_x, gather.at_y] + gather.at_high)
    for part in range(2):
        wide = mlp_in.shape[2]
        mlp_shard[:, part * wide : (part + 1) * wide] = mlp_in[part].astype(BF16)
    predict_shard[...] = predict_in[:, pl.ds(pl.multiple_of(core * predict_shard.shape[1], predict_shard.shape[1]),
                                             predict_shard.shape[1])].astype(BF16)
    gather.step(0)
    images, side, half = table_ref.shape
    patches = side * side
    width = mixed_ref.shape[0]
    hidden = z_ref.shape[1]
    wide = x_ref.shape[1]
    share = predict_ref.shape[-1]
    w_up = lambda: mlp_ref[:, :, :, :hidden].reshape(wide, hidden)
    w_down = lambda: mlp_ref[:, :, :, hidden:].reshape(wide, hidden)
    predict_half = lambda half: predict_ref[half].reshape(wide, share)
    vec_ref[...] = totals_ref[14:22, :]
    bias = jnp.concatenate([totals_ref[21:22, :], totals_ref[22:23, : 2 * share - totals_ref.shape[1]]], axis=1)
    inverse = [1.0 / jnp.sum(totals_ref[24 + level : 25 + level, :], axis=1, keepdims=True) for level in range(NB)]
    mine_ref = final_ref
    other_ref = lowt_ref.at[pl.ds(0, other_any.shape[0]), pl.ds(0, other_any.shape[1])]
    attn_ref = z_ref.at[pl.ds(0, attn_any.shape[0]), pl.ds(0, 4 * width)]

    loads = [pltpu.make_async_copy(source, target, load_sem.at[at]) for at, (source, target) in enumerate(
        ((attn_any, attn_ref), (bridge_any, bridge_ref), (x1e_any, gy_out),
         (mine_any, mine_ref), (other_any, other_ref)))]
    for copy in loads:
        copy.start()

    def rows_of(image):
        return pl.ds(pl.multiple_of(image * patches, patches), patches)

    def exchange(phase, image):
        rows = rows_of(image)
        return remote(part_ref.at[phase % 2, rows, :], from_ref.at[phase % 2, rows, :], send_sem.at[phase, image],
                      receive_sem.at[phase, image], sibling)

    def summed(phase, rows):
        return part_ref[phase % 2, rows, :].astype(F32) + from_ref[phase % 2, rows, :].astype(F32)

    def give(phase, image, value):
        part_ref[phase % 2, rows_of(image), :] = value.astype(BF16)
        exchange(phase, image).start()

    def stream(image):
        rows, slot = rows_of(image), lax.rem(image, 2)
        return [pltpu.make_async_copy(target_any.at[rows, :], target_ref.at[slot], stream_sem.at[0, slot]),
                pltpu.make_async_copy(band_any.at[rows, :], band_ref.at[slot], stream_sem.at[1, slot])]

    sums_ref[...] = jnp.zeros_like(sums_ref)
    loss_ref[...] = jnp.zeros_like(loss_ref)
    gbias_ref[...] = jnp.zeros_like(gbias_ref)
    gpred_acc[...] = jnp.zeros_like(gpred_acc)
    for copy in stream(0):
        copy.start()
    loads[0].wait()
    for part in range(4):
        at = pl.ds(part * width, width)
        flat_ref[at, :] = attn_ref[:, at].T
    loads[1].wait()
    for copy in loads[2:]:
        copy.wait()
    ends = bridge_ref.shape[2]
    parts = 3
    latent_start = attn_any.shape[0]

    def ends_rows(step):
        return pl.ds(pl.multiple_of(step * 128, 128), 128)

    def enc_end(image, carry):
        rows = pl.ds(pl.multiple_of(image * length, length), length)
        out = gy_out[rows, :] + both(mine_ref, other_ref, rows)
        gy_out[rows, :] = out
        unit, _ = normalize(out)
        final = (unit * evec_ref[5:6, :] + evec_ref[6:7, :]).astype(BF16)
        final_ref[rows, :] = final
        for half in range(2):
            rest = dot_nn(final, bridge_ref[half])
            for part in range(parts):
                value = rest.astype(BF16)
                at = pl.multiple_of(latent_start + (image * parts + part) * length, length)
                z_ref[pl.ds(at, length), half * ends : (half + 1) * ends] = value
                rest = rest - value.astype(F32)
        return carry

    lax.fori_loop(0, images, enc_end, 0)

    def phase_a(image, carry):
        rows = rows_of(image)
        hot = lax.broadcasted_iota(jnp.int32, (patches, length), 0) == kept_ref[pl.ds(image, 1), :]
        hot = jnp.where(hot, 1.0, 0.0).astype(BF16)
        at = pl.multiple_of(latent_start + image * parts * length, length)
        latent = z_ref[pl.ds(at, parts * length), : 2 * ends]
        spread = dot_nn(jnp.concatenate([hot] * parts, axis=1), latent)
        table = table_ref[image]
        by_row = jnp.broadcast_to(table[:, None, :], (side, side, half)).reshape(patches, half)
        by_col = jnp.broadcast_to(table[None, :, :], (side, side, half)).reshape(patches, half)
        place = jnp.concatenate([by_row, by_col], axis=1)
        rows_x = spread + rows_ref[rows, 0:1] * vec_ref[0:1, :] + place
        x_ref[rows, :] = rows_x
        unit, _ = normalize(rows_x)
        low = (unit * vec_ref[1:2, :] + vec_ref[2:3, :]).astype(BF16)
        qkv_ref[:, rows] = dot_nt(flat_ref[: 3 * width, :], low).astype(BF16)
        attend(qkv_ref, mixed_ref, lse_ref, rows, width, head_dim, None)
        give(0, image, dot_nn(mixed_ref[:, rows].T, flat_ref[3 * width :, :]))
        return carry

    swap = remote(predict_ref.at[core], predict_ref.at[core], join_sem.at[0], join_sem.at[1], sibling)
    gather.step(1)
    lax.fori_loop(0, images // 2, phase_a, 0)
    gather.step(2)
    lax.fori_loop(images // 2, images, phase_a, 0)
    gather.step(3)

    def phase_b(image, carry):
        rows = rows_of(image)
        exchange(0, image).wait()
        after = x_ref[rows, :] + summed(0, rows)
        x1_ref[rows, :] = after
        unit, _ = normalize(after)
        low = (unit * vec_ref[3:4, :] + vec_ref[4:5, :]).astype(BF16)
        lowt_ref[:, rows] = low.T
        up = dot_nn(low, w_up())
        square, bent, rise = gelu_parts(up)
        mid = (up * rise).astype(BF16)
        z_ref[rows, :] = mid
        slope = rise + (0.5 * GELU_C) * up * (1.0 - bent * bent) * (1.0 + (3.0 * 0.044715) * square)
        gu_ref[rows, :] = slope.astype(BF16)
        return carry

    def phase_down(image, carry):
        give(1, image, dot_nt(z_ref[rows_of(image), :], w_down()))
        return carry

    lax.fori_loop(0, images, phase_b, 0)
    gather.step(4)
    lax.fori_loop(0, images, phase_down, 0)
    for step in range(5, gather.pairs + 3):
        gather.step(step)
    swap.start()
    swap.wait()

    def phase_c(image, carry):
        rows, slot = rows_of(image), lax.rem(image, 2)

        @pl.when(image + 1 < images)
        def _():
            for copy in stream(image + 1):
                copy.start()

        exchange(1, image).wait()
        unit, rstd = normalize(x1_ref[rows, :] + summed(1, rows))
        gain = vec_ref[5:6, :]
        final = (unit * gain + vec_ref[6:7, :]).astype(BF16)
        for copy in stream(image):
            copy.wait()
        predicted = jnp.concatenate([dot_nn(final, predict_half(0)), dot_nn(final, predict_half(1))], axis=1)
        mismatch = predicted + bias - target_ref[slot].astype(F32)
        band = band_ref[slot]
        level = jnp.where(band == 0, inverse[0], jnp.where(band == 1, inverse[1], inverse[2]))
        level = level * rows_ref[rows, 1:2]
        square = mismatch * mismatch + EPS_C
        root = lax.rsqrt(square)
        loss_ref[...] += jnp.sum(level * (square * root), axis=0, keepdims=True)
        grad = level * (mismatch * root)
        gbias_ref[...] += jnp.sum(grad, axis=0, keepdims=True)
        gp_ref[...] = grad.astype(BF16)
        columns = pl.ds(pl.multiple_of(core * share, share), share)
        gpred_acc[...] += dot_tn(final, gp_ref[:, columns])
        grad_final = dot_nt(gp_ref[:, :share], predict_half(0)) + dot_nt(gp_ref[:, share:], predict_half(1))
        grad_in, gain_sum, shift_sum = norm_back(grad_final, gain, unit, rstd)
        gy_ref[rows, :] = grad_in
        sums_ref[5:6, :] += gain_sum
        sums_ref[6:7, :] += shift_sum
        low = grad_in.astype(BF16)
        gradt_ref[:, rows] = low.T
        grad_up = (dot_nn(low, w_down()) * gu_ref[rows, :].astype(F32)).astype(BF16)
        gu_ref[rows, :] = grad_up
        give(2, image, dot_nt(grad_up, w_up()))
        return carry

    lax.fori_loop(0, images, phase_c, 0)
    lead = gpred_ref.shape[:3]
    norm_ref[...] = jnp.zeros_like(norm_ref)
    gpred_ref[...] = gpred_acc[...].astype(BF16).reshape(gpred_ref.shape)
    tile = 256
    for start in range(0, hidden, tile):
        at = pl.ds(start, tile)
        gup_ref[:, :, :, at] = dot_nn(lowt_ref[...], gu_ref[:, at]).astype(BF16).reshape(lead + (tile,))
        gdown_ref[:, :, :, at] = dot_nn(gradt_ref[...], z_ref[:, at]).astype(BF16).reshape(lead + (tile,))
    red.step(0)

    def phase_d(image, carry):
        rows = rows_of(image)
        exchange(2, image).wait()
        unit, rstd = normalize(x1_ref[rows, :])
        grad_in, gain_sum, shift_sum = norm_back(summed(2, rows), vec_ref[3:4, :], unit, rstd)
        grad_in = grad_in + gy_ref[rows, :]
        gy_ref[rows, :] = grad_in
        sums_ref[3:4, :] += gain_sum
        sums_ref[4:5, :] += shift_sum
        low = grad_in.astype(BF16)
        gradt_ref[:, rows] = low.T
        gmix_ref[...] = dot_nt(flat_ref[3 * width :, :], low).astype(BF16)
        attend_back(qkv_ref, mixed_ref, gmix_ref, lse_ref, gq_ref, rows, pl.ds(0, patches), width, head_dim, None)
        qkv_ref[:, rows] = gq_ref[...]
        unit_a, _ = normalize(x_ref[rows, :])
        lowt_ref[:, rows] = (unit_a * vec_ref[1:2, :] + vec_ref[2:3, :]).astype(BF16).T
        give(3, image, dot_nn(gq_ref[...].T, flat_ref[: 3 * width, :]))
        return carry

    for step in range(1, 4):
        lax.fori_loop((step - 1) * images // 3, step * images // 3, phase_d, 0)
        red.step(step)
    join = remote(pred_view, pred_view, join_sem.at[2], join_sem.at[3], sibling)
    for part in range(3):
        at = pl.ds(part * width, width)
        gattn_ref[:, at] = dot_nt(lowt_ref[...], qkv_ref[at, :]).astype(BF16)
    gattn_ref[:, 3 * width :] = dot_nt(gradt_ref[...], mixed_ref[...]).astype(BF16)
    red.step(4)

    def phase_e(image, carry):
        rows = rows_of(image)
        exchange(3, image).wait()
        unit, rstd = normalize(x_ref[rows, :])
        grad_in, gain_sum, shift_sum = norm_back(summed(3, rows), vec_ref[1:2, :], unit, rstd)
        grad_in = grad_in + gy_ref[rows, :]
        sums_ref[1:2, :] += gain_sum
        sums_ref[2:3, :] += shift_sum
        sums_ref[0:1, :] += jnp.sum(grad_in * rows_ref[rows, 0:1], axis=0, keepdims=True)
        kept_rows = pl.ds(pl.multiple_of(image * length, length), length)
        hot = lax.broadcasted_iota(jnp.int32, (length, patches), 1) == column_ref[kept_rows, :]
        glat_ref[kept_rows, :] = dot_nn(hot.astype(BF16), grad_in.astype(BF16)).astype(BF16)
        return carry

    lax.fori_loop(0, images, phase_e, 0)
    for step in range(5, red.pairs + 3):
        red.step(step)
    join.start()
    columns = pl.ds(pl.multiple_of(core * ends, ends), ends)
    gbridge_ref[...] = dot_tn(final_ref[...], glat_ref[:, columns]).astype(BF16)
    esums_ref[...] = jnp.zeros_like(esums_ref)

    def enc_start(step, carry):
        rows = ends_rows(step)
        grad_final = dot_nt(glat_ref[rows, :ends], bridge_ref[0]) + dot_nt(glat_ref[rows, ends:], bridge_ref[1])
        unit, rstd = normalize(gy_out[rows, :])
        grad_in, gain_sum, shift_sum = norm_back(grad_final, evec_ref[5:6, :], unit, rstd)
        gy_out[rows, :] = grad_in
        esums_ref[0:1, :] += gain_sum
        esums_ref[1:2, :] += shift_sum
        return carry

    lax.fori_loop(0, gy_out.shape[0] // 128, enc_start, 0)
    join.wait()
    vgrad_ref[...] = jnp.zeros_like(vgrad_ref)
    vgrad_ref[5:7, :] = esums_ref[0:2, :]
    vgrad_ref[7:14, : sums_ref.shape[1]] = sums_ref[0:7, :]
    vgrad_ref[14:15, : gbias_ref.shape[1]] = gbias_ref[...]


def decoder_all(x1e, mine, other, evec, kept_index, kept_column, row_values, table, totals, mlp, predict, target, band,
                attn, bridge):
    size = lax.axis_size("dp")
    highs = size // 4
    rows_e, wide = x1e.shape
    images, length = kept_index.shape
    rows, pixel_count = target.shape
    patches = rows // images
    shard, hidden = mlp.shape[1], mlp.shape[2]
    low_wide = shard * size
    width, share, ends = attn.shape[1] // 4, predict.shape[1] // 2, bridge.shape[2]
    lead = (highs, 4, shard)
    gathered = blocks_of([2 * hidden, share], 512)
    reduced = blocks_of([share, hidden, hidden], 512)
    in_vmem = pl.BlockSpec(memory_space=pltpu.VMEM)
    any_space = pl.BlockSpec(memory_space=pl.ANY)
    dma = pltpu.SemaphoreType.DMA
    vm = pltpu.VMEM
    return pl.pallas_call(
        functools.partial(decoder_kernel, length, DDH, highs, gathered, reduced),
        out_shape=(
            shape((rows_e, wide), F32), shape((low_wide, 4 * width), BF16), shape((wide, ends), BF16),
            shape((2, shard, share), F32), shape((shard, hidden), F32), shape((shard, hidden), F32), shape((8, 128), F32),
            shape((1, pixel_count), F32), shape((16, wide), F32)),
        in_specs=[in_vmem] * 8 + [any_space] * 7,
        out_specs=tuple([in_vmem] * 9),
        scratch_shapes=[
            vm(lead + (hidden,), BF16), vm(lead + (hidden,), BF16), vm(lead + (share,), BF16),
            vm((shard, 2 * hidden), BF16), vm((shard, share), BF16),
            vm((1, pixel_count), F32), vm((8, low_wide), F32), vm((8, wide), F32),
            vm((rows_e, wide), BF16), vm((rows_e, low_wide), BF16), vm((rows, low_wide), F32),
            vm((rows, low_wide), F32), vm((rows, low_wide), F32), vm((3 * width, rows), BF16), vm((width, rows), BF16),
            vm((width // DDH, rows), F32), vm((2, rows, low_wide), BF16), vm((2, rows, low_wide), BF16),
            vm((low_wide, rows), BF16), vm((low_wide, rows), BF16), vm((rows, hidden), BF16), vm((rows, hidden), BF16),
            vm((4 * width, low_wide), BF16), vm(lead + (2 * hidden,), BF16), vm(bridge.shape, BF16),
            vm((2,) + lead + (share,), BF16), vm((2, patches, pixel_count), BF16), vm((2, patches, pixel_count), jnp.int32),
            vm((patches, pixel_count), BF16), vm((low_wide, share), F32), vm((width, patches), BF16),
            vm((3 * width, patches), BF16), vm((8, low_wide), F32),
            dma((5,)), dma((2, 2)), dma((4, images)), dma((4, images)), dma((4,))]
        + gatherer_sems(highs, gathered) + reducer_scratch(highs, reduced, [shard] * 3),
        compiler_params=pltpu.CompilerParams(collective_id=3, has_side_effects=True, vmem_limit_bytes=62 * 2**20),
        cost_estimate=pl.CostEstimate(flops=0, bytes_accessed=2**25, transcendentals=0),
    )(evec, kept_index, kept_column, row_values, table, totals, mlp, predict, x1e, mine, other, target, band, attn, bridge)


class Reducer:
    def __init__(self, highs, groups, weights, grads, outs, near, second, far, load_two, load_own, plane, norm, sems):
        self.highs, self.groups, self.weights = highs, groups, weights
        self.grads, self.outs = grads, outs
        self.near, self.second, self.far = near, second, far
        self.load_two, self.load_own, self.plane, self.norm = load_two, load_own, plane, norm
        self.load_sem, self.as_sem, self.ar_sem, self.bs_sem, self.br_sem, self.zs_sem, self.zr_sem = sems
        self.core, self.low, self.high, self.low_x, self.low_y = place_of()
        self.dev_x, self.dev_y = (self.high * 4 + self.low_x, self.core), (self.high * 4 + self.low_y, self.core)
        self.at_high = [(lax.rem(self.high + k, highs) * 4 + self.low, self.core) for k in range(1, highs)]
        self.pairs = (len(groups) + 1) // 2

    def in_pair(self, pair):
        return [at for at in (2 * pair, 2 * pair + 1) if 0 <= at < len(self.groups)] if 0 <= pair < self.pairs else []

    def route(self, at):
        if at % 2 == 0:
            return self.low_y, self.dev_y, self.low_x, self.dev_x
        return self.low_x, self.dev_x, self.low_y, self.dev_y

    def grad(self, at, which):
        number, start, size = self.groups[at]
        return self.grads[number].at[:, which, :, pl.ds(start, size)]

    def slot(self, ref, at, count):
        number, _, size = self.groups[at]
        return ref.at[at % count, :, pl.ds(0, self.outs[number].shape[0]), pl.ds(0, size)]

    def two_ref(self, at):
        return self.slot(self.load_two, at, 6)

    def own_ref(self, at):
        return self.slot(self.load_own, at, 8)

    def loads(self, at):
        return [pltpu.make_async_copy(self.grad(at, self.route(at)[2]), self.two_ref(at), self.load_sem.at[at, 0]),
                pltpu.make_async_copy(self.grad(at, self.low), self.own_ref(at), self.load_sem.at[at, 1])]

    def one(self, at):
        low_one, dev_one, _, _ = self.route(at)
        return [remote(self.grad(at, 3 - self.low), self.near[2 * at], self.as_sem.at[at, 0], self.ar_sem.at[at, 0], dev_one),
                remote(self.grad(at, low_one), self.near[2 * at + 1], self.as_sem.at[at, 1], self.ar_sem.at[at, 1], dev_one)]

    def two(self, at):
        return remote(self.two_ref(at), self.second[at], self.bs_sem.at[at], self.br_sem.at[at], self.route(at)[3])

    def three(self, at):
        return [remote(self.own_ref(at).at[lax.rem(self.high + k, self.highs)], self.far[at].at[k - 1],
                       self.zs_sem.at[at, k - 1], self.zr_sem.at[at, k - 1], self.at_high[k - 1])
                for k in range(1, self.highs)]

    def step(self, step):
        for at in self.in_pair(step):
            for copy in self.one(at) + self.loads(at):
                copy.start()
        for at in self.in_pair(step - 1):
            mine = self.two_ref(at)
            self.loads(at)[0].wait()
            self.one(at)[0].wait()
            mine[...] = (mine[...].astype(F32) + self.near[2 * at][...].astype(F32)).astype(BF16)
            self.two(at).start()
        for at in self.in_pair(step - 2):
            number, start, size = self.groups[at]
            mine = self.own_ref(at)
            self.loads(at)[1].wait()
            self.one(at)[1].wait()
            self.two(at).wait()
            plane = self.slot(self.plane, at, 2)
            plane[...] = (mine[...].astype(F32) + self.near[2 * at + 1][...].astype(F32)
                          + self.second[at][...].astype(F32))
            self.outs[number][:, pl.ds(start, size)] = plane[self.high]
            mine[...] = plane[...].astype(BF16)
            for copy in self.three(at):
                copy.start()
        for at in self.in_pair(step - 3):
            number, start, size = self.groups[at]
            for copy in self.three(at):
                copy.wait()
            cols = pl.ds(start, size)
            done = self.outs[number][:, cols]
            for k in range(self.highs - 1):
                done = done + self.far[at][k].astype(F32)
            self.outs[number][:, cols] = done
            self.norm[0:1, 0:1] += self.weights[number] * jnp.sum(done * done, keepdims=True)


def reducer_scratch(highs, groups, shards):
    piece = lambda lead, group: pltpu.VMEM((lead, shards[group[0]], group[2]), BF16)
    near = [piece(highs, group) for group in groups for _ in range(2)]
    second = [piece(highs, group) for group in groups]
    far = [piece(highs - 1, group) for group in groups]
    slot = (highs, max(shards), max(group[2] for group in groups))
    loads = [pltpu.VMEM((6,) + slot, BF16), pltpu.VMEM((8,) + slot, BF16), pltpu.VMEM((2,) + slot, F32)]
    dma, total = pltpu.SemaphoreType.DMA, len(groups)
    sems = [dma((total, 2)), dma((total, 2)), dma((total, 2)), dma((total,)), dma((total,)),
            dma((total, highs - 1)), dma((total, highs - 1))]
    return near + second + far + loads + sems


def make_reducer(highs, groups, weights, grads, outs, norm, refs):
    total = len(groups)
    near, second, far, refs = refs[: 2 * total], refs[2 * total : 3 * total], refs[3 * total : 4 * total], refs[4 * total :]
    return Reducer(highs, groups, weights, grads, outs, near, second, far, *refs[:3], norm, refs[3:10]), refs[10:]


def backward_kernel(highs, weights, groups, ready, count, shared, length, group, head_dim, *refs):
    given = count - 4
    gy_ref, x1_ref, vec_ref, vgrad_ref, loss_ref, lse_ref, norm_in = refs[:7]
    x_any, qkv_any, mixed_any, flat_any, pixk_any, mlp_any = refs[7:13]
    refs = refs[13:]
    grads, refs = refs[:given], refs[given:]
    outs, sums_ref, vflat_ref, refs = refs[:count], refs[count], refs[count + 1], refs[count + 2 :]
    made, refs = refs[:4], refs[4:]
    grads = tuple(grads) + tuple(made)
    (x_ref, qkv_ref, mixed_ref, flat_ref, pixk_ref, wmlp_ref, low_ref, lowt_ref, grad_ref, gradt_ref, acc_ref, part_ref,
     other_ref, last_ref, gmix_ref, gqkv_ref, stage_ref, norm_ref, spots_ref, far_ref, vnear_ref, vfar_ref,
     vsum_ref) = refs[:23]
    (load_sem, wload_sem, store_sem, xs_sem, xr_sem, ns_sem, nr_sem, hs_sem, hr_sem, ts_sem, tr_sem, js_sem,
     jr_sem) = refs[23:36]
    core_at = lax.axis_index("mp")
    views = [ref.at[core_at] if split else ref for ref, split in zip(outs, shared)]
    red, _ = make_reducer(highs, groups, weights, grads, views, norm_ref, refs[36:])
    core, low, high = red.core, red.low, red.high
    spot = low * 2 + core
    sibling = (high * 4 + low, 1 - core)
    near = [(high * 4 + lax.rem(spot + k, 8) // 2, lax.rem(lax.rem(spot + k, 8), 2)) for k in range(1, 8)]
    greet(near + red.at_high)
    rows, wide = x_ref.shape
    width = mixed_ref.shape[0]
    hidden = mlp_any.shape[-1] // 2
    size = 512
    tiles = hidden // size
    mask = group_mask(group, length)

    late = [pltpu.make_async_copy(source, target, load_sem.at[at]) for at, (source, target) in enumerate(
        ((x_any, x_ref), (qkv_any, qkv_ref), (mixed_any, mixed_ref), (flat_any, flat_ref), (pixk_any, pixk_ref)))]

    def weight_loads(tile):
        return [pltpu.make_async_copy(mlp_any.at[:, :, :, pl.ds(half * hidden + tile * size, size)],
                                      wmlp_ref.at[tile % 2, half], wload_sem.at[tile % 2, half]) for half in range(2)]

    def store(slot, target, start, columns=512):
        return pltpu.make_async_copy(stage_ref.at[slot, :, :, :, pl.ds(0, columns)],
                                     target.at[:, :, :, pl.ds(start, columns)], store_sem.at[slot])

    def exchange(at, target):
        return remote(part_ref, target, xs_sem.at[at], xr_sem.at[at], sibling)

    def staged(slot, value):
        columns = value.shape[1]
        stage_ref[slot, :, :, :, :columns] = value.astype(BF16).reshape(stage_ref.shape[1:4] + (columns,))

    def mlp_first():
        unit, _ = normalize(x1_ref[...])
        value = (unit * vec_ref[3:4, :] + vec_ref[4:5, :]).astype(BF16)
        low_ref[...] = value
        lowt_ref[...] = value.T
        value = gy_ref[...].astype(BF16)
        grad_ref[...] = value
        gradt_ref[...] = value.T
        acc_ref[...] = jnp.zeros_like(acc_ref)

    def mlp_block(tile):
        for copy in weight_loads(tile):
            copy.wait()
        if tile + 1 < tiles:
            for copy in weight_loads(tile + 1):
                copy.start()
        w_up = wmlp_ref[tile % 2, 0].reshape(wide, size)
        w_down = wmlp_ref[tile % 2, 1].reshape(wide, size)
        up = dot_nn(low_ref[...], w_up)
        square, bent, half = gelu_parts(up)
        mid = (up * half).astype(BF16)
        slope = half + (0.5 * GELU_C) * up * (1.0 - bent * bent) * (1.0 + (3.0 * 0.044715) * square)
        grad_up = (dot_nn(grad_ref[...], w_down) * slope).astype(BF16)
        acc_ref[...] += dot_nt(grad_up, w_up)
        slot = 2 * (tile % 2)
        staged(slot, dot_nn(lowt_ref[...], grad_up))
        store(slot, made[0], tile * size).start()
        staged(slot + 1, dot_nn(gradt_ref[...], mid))
        store(slot + 1, made[1], tile * size).start()

    def mlp_last():
        part_ref[...] = acc_ref[...].astype(BF16)
        exchange(0, other_ref).start()

    def stores_done(tile):
        slot = 2 * (tile % 2)
        store(slot, made[0], tile * size).wait()
        store(slot + 1, made[1], tile * size).wait()

    def rows_step(number, carry):
        at = pl.ds(pl.multiple_of(number * group, group), group)
        unit, rstd = normalize(x1_ref[at, :])
        grad_in, gain_sum, shift_sum = norm_back(both(part_ref, other_ref, at), vec_ref[3:4, :], unit, rstd)
        grad_in = grad_in + gy_ref[at, :]
        gy_ref[at, :] = grad_in
        vsum_ref[3:4, :] += gain_sum
        vsum_ref[4:5, :] += shift_sum
        low_grad = grad_in.astype(BF16)
        gradt_ref[:, at] = low_grad.T
        gmix_ref[...] = dot_nt(flat_ref[3 * width :, :], low_grad).astype(BF16)
        attend_back(qkv_ref, mixed_ref, gmix_ref, lse_ref, gqkv_ref, at, at, width, head_dim, mask)
        part_ref[at, :] = dot_nn(gqkv_ref[:, at].T, flat_ref[: 3 * width, :]).astype(BF16)
        unit_a, _ = normalize(x_ref[at, :])
        lowt_ref[:, at] = (unit_a * vec_ref[1:2, :] + vec_ref[2:3, :]).astype(BF16).T
        return carry

    def attn_grads():
        for slot in range(4):
            if slot < 3:
                value = dot_nt(lowt_ref[...], gqkv_ref[pl.ds(slot * width, width), :])
            else:
                value = dot_nt(gradt_ref[...], mixed_ref[...])
            staged(slot, value)
            store(slot, made[2], slot * width, width).start()

    def enc_out():
        unit, rstd = normalize(x_ref[...])
        grad_in, gain_sum, shift_sum = norm_back(both(part_ref, last_ref, pl.ds(0, rows)), vec_ref[1:2, :], unit, rstd)
        grad_in = grad_in + gy_ref[...]
        vsum_ref[0:1, :] = jnp.sum(grad_in, axis=0, keepdims=True)
        vsum_ref[1:2, :] = gain_sum
        vsum_ref[2:3, :] = shift_sum
        share = made[3].shape[-1]
        columns = pl.ds(pl.multiple_of(core * share, share), share)
        staged(0, dot_tn(grad_in.astype(BF16), pixk_ref[:, columns]))
        store(0, made[3], 0, share).start()

    stages = functools.partial(total_blocks, vsum_ref, vnear_ref, vfar_ref, (ts_sem, tr_sem), low, high, core, highs)
    mlp_ready, attn_ready, embed_ready = ready
    row_groups = rows // group
    norm_ref[...] = norm_in[...]
    vsum_ref[...] = vgrad_ref[...]
    for copy in weight_loads(0):
        copy.start()
    work = {0: range(0, 1), 1: range(1, tiles - 1), 2: range(tiles - 1, tiles)}
    for step in range(red.pairs + 3):
        if 0 <= step - mlp_ready < tiles:
            stores_done(step - mlp_ready)
        if step == attn_ready:
            for slot in range(4):
                store(slot, made[2], slot * width, width).wait()
        if step == embed_ready:
            store(0, made[3], 0, made[3].shape[-1]).wait()
        red.step(step)
        if step == 0:
            for copy in late:
                copy.start()
            mlp_first()
        for tile in work.get(step, ()):
            mlp_block(tile)
            if tile == tiles - 1:
                mlp_last()
        if step == 3:
            for copy in late:
                copy.wait()
            exchange(0, other_ref).wait()
            lax.fori_loop(0, row_groups // 2, rows_step, 0)
        if step == 4:
            lax.fori_loop(row_groups // 2, row_groups, rows_step, 0)
            exchange(1, last_ref).start()
            attn_grads()
        if step == embed_ready - 1:
            exchange(1, last_ref).wait()
            enc_out()
            vnear_ref[low] = vsum_ref[...]
            for copy in stages(0):
                copy.start()
        if step == embed_ready:
            for copy in stages(0):
                copy.wait()
            vsum_ref[...] = (vnear_ref[0] + vnear_ref[1]) + (vnear_ref[2] + vnear_ref[3])
            vfar_ref[high] = vsum_ref[...]
            for copy in stages(1):
                copy.start()
        if step == embed_ready + 1:
            for copy in stages(1):
                copy.wait()
            every = vfar_ref[0]
            for k in range(1, highs):
                every = every + vfar_ref[k]
            for row in range(7):
                vflat_ref[2 * row : 2 * row + 1, :] = every[row : row + 1, :512]
                vflat_ref[2 * row + 1 : 2 * row + 2, :] = every[row : row + 1, 512:]
            vflat_ref[14:22, :] = every[7:15, :512]
            vflat_ref[22:23, :] = every[14:15, 512:]
            vflat_ref[23:24, :] = jnp.zeros_like(vflat_ref[23:24, :])
            norm_ref[0:1, 0:1] += jnp.sum(every * every, keepdims=True) * (1.0 / (8 * highs))
    joins = [remote(view, view, js_sem.at[at], jr_sem.at[at], sibling)
             for at, (view, split) in enumerate(zip(views, shared)) if split]
    for copy in joins:
        copy.start()
    norm_ref[1:2, 0:1] = jnp.sum(loss_ref[...], keepdims=True)
    spots_ref[spot] = norm_ref[...]
    copies = [remote(norm_ref, spots_ref.at[spot], ns_sem.at[k], nr_sem.at[k], near[k]) for k in range(7)]
    for copy in copies:
        copy.start()
    for copy in copies:
        copy.wait()
    local = spots_ref[0]
    for k in range(1, 8):
        local = local + spots_ref[k]
    norm_ref[...] = local
    far_ref[high] = local
    copies = [remote(norm_ref, far_ref.at[high], hs_sem.at[k], hr_sem.at[k], red.at_high[k]) for k in range(highs - 1)]
    for copy in copies:
        copy.start()
    for copy in copies:
        copy.wait()
    every = far_ref[0]
    for k in range(1, highs):
        every = every + far_ref[k]
    sums_ref[...] = every
    for copy in joins:
        copy.wait()


def backward_all(gy, x1, evec, vec_grads, loss_parts, norm, enc_saved, x0, flat, pixk, mlp, grads, shared, length, head_dim):
    size = lax.axis_size("dp")
    highs = size // 4
    qkv, mixed, lse = enc_saved
    rows, wide = x1.shape
    width = mixed.shape[0]
    hidden = mlp.shape[1] // 2
    group = 2 * length
    shard = wide // size
    lead = (highs, 4, shard)
    fresh = [lead + (hidden,), lead + (hidden,), lead + (4 * width,), lead + (pixk.shape[1] // 2,)]
    widths = [a.shape[1] for a in grads] + [dims[-1] for dims in fresh]
    shards = [a.shape[0] // size for a in grads] + [shard] * 4
    count, given = len(widths), len(grads)
    blocks = blocks_of(widths, 512, (given + 2,))
    first = [b for b in blocks if b[0] == 0]
    last = [b for b in blocks if b[0] == given + 3] + [b for b in blocks if 0 < b[0] < given]
    middle = [b for at in range(0, hidden, 512) for b in ((given, at, 512), (given + 1, at, 512))]
    attn = [b for b in blocks if b[0] == given + 2]
    groups = first + middle + attn + last
    if len(first) != 2 or hidden // 512 != 4 or len(attn) != 8:
        raise ValueError("blocks")
    ready = (len(first) // 2, (len(first) + len(middle)) // 2, (len(first) + len(middle) + len(attn)) // 2)
    dma = pltpu.SemaphoreType.DMA
    small, vec_block = (8, 128), vec_grads.shape
    in_vmem = pl.BlockSpec(memory_space=pltpu.VMEM)
    any_space = pl.BlockSpec(memory_space=pl.ANY)
    result = pl.pallas_call(
        functools.partial(backward_kernel, highs, (1.0,) * count, groups, ready, count, shared, length, group, head_dim),
        out_shape=tuple([shape((2, r, w) if split else (r, w), F32) for r, w, split in zip(shards, widths, shared)]
                        + [shape(small, F32), shape((24, 512), F32)]
                        + [shape(dims, BF16) for dims in fresh]),
        in_specs=[in_vmem] * 7 + [any_space] * (6 + given),
        out_specs=tuple([in_vmem] * (count + 2) + [any_space] * 4),
        scratch_shapes=[
            pltpu.VMEM((rows, wide), F32), pltpu.VMEM(qkv.shape, BF16), pltpu.VMEM(mixed.shape, BF16),
            pltpu.VMEM(flat.shape, BF16), pltpu.VMEM(pixk.shape, BF16), pltpu.VMEM((2, 2) + lead + (512,), BF16),
            pltpu.VMEM((rows, wide), BF16), pltpu.VMEM((wide, rows), BF16), pltpu.VMEM((rows, wide), BF16),
            pltpu.VMEM((wide, rows), BF16), pltpu.VMEM((rows, wide), F32), pltpu.VMEM((rows, wide), BF16),
            pltpu.VMEM((rows, wide), BF16), pltpu.VMEM((rows, wide), BF16), pltpu.VMEM((width, group), BF16),
            pltpu.VMEM((3 * width, rows), BF16), pltpu.VMEM((4,) + lead + (512,), BF16), pltpu.VMEM(small, F32),
            pltpu.VMEM((8,) + small, F32), pltpu.VMEM((highs,) + small, F32), pltpu.VMEM((4,) + vec_block, F32),
            pltpu.VMEM((highs,) + vec_block, F32), pltpu.VMEM(vec_block, F32),
            dma((5,)), dma((2, 2)), dma((4,)), dma((2,)), dma((2,)), dma((7,)), dma((7,)), dma((highs - 1,)),
            dma((highs - 1,)), dma((highs + 2,)), dma((highs + 2,)), dma((count,)), dma((count,))] + reducer_scratch(highs, groups, shards),
        compiler_params=pltpu.CompilerParams(collective_id=1, has_side_effects=True, vmem_limit_bytes=62 * 2**20),
        cost_estimate=pl.CostEstimate(flops=0, bytes_accessed=sum(a.size * 2 for a in grads), transcendentals=0),
    )(gy, x1, evec, vec_grads, loss_parts, lse, norm, x0, qkv, mixed, flat, pixk, mlp.reshape(lead + (2 * hidden,)),
      *[a.reshape(highs, 4, r, a.shape[1]) for r, a in zip(shards, grads)])
    return list(result[:count]), result[count], result[count + 1]


def reduce_plain(grads, loss_parts, vec_grads):
    order_a, order_b = orders()
    outs = [reduce_dp(a, 0, (order_a, order_b)[number % 2], a.dtype) for number, a in enumerate(grads)]
    vec_sums = total_dp(vec_grads)
    sums = jnp.stack([sum(jnp.sum(a * a) for a in outs), jnp.sum(loss_parts)])
    sums = total_dp(sums)
    sums = sums + other_core(sums)
    return outs, sums[0] + jnp.sum(vec_sums * vec_sums), 0.5 * sums[1], vec_sums


def adam_update(master, gradient, first_old, second_old, step_rate, decay_rate):
    first_new = BETA_ONE * first_old + (1.0 - BETA_ONE) * gradient
    second_new = BETA_TWO * second_old + (1.0 - BETA_TWO) * gradient * gradient
    first_hat = first_new / (1.0 - BETA_ONE**STEP)
    second_hat = second_new / (1.0 - BETA_TWO**STEP)
    updated = master - step_rate * (
        first_hat / (jnp.sqrt(second_hat) + ADAM_EPS) + decay_rate * master
    )
    return (updated, first_new, second_new)


def adam_kernel(count, averaged, sums_ref, *refs):
    sources, refs = refs[: count + 2], refs[count + 2 :]
    masters, firsts, seconds, refs = refs[:count], refs[count : 2 * count], refs[2 * count : 3 * count], refs[3 * count :]
    means, refs = refs[:averaged], refs[averaged:]
    news, new_firsts, new_seconds, new_means = (
        refs[:count], refs[count : 2 * count], refs[2 * count : 3 * count], refs[3 * count :])
    factor = CLIP / jnp.maximum(jnp.sqrt(sums_ref[0:1, 0:1]), CLIP)

    def update(number, at, gradient):
        new, first, second = adam_update(masters[number][at], gradient * factor, firsts[number][at], seconds[number][at],
                                         RATE_MAT, DECAY_MAT)
        news[number][at] = new
        new_firsts[number][at] = first
        new_seconds[number][at] = second
        mean = {0: 0, 1: 1, 4: 2}.get(number)
        if mean is not None:
            new_means[mean][at] = EMA_KEEP * means[mean][at] + (1.0 - EMA_KEEP) * new

    enc_attn, enc_up, enc_down, dec_attn, dec_up, dec_down, embed, bridge, predict = sources
    for number, source in ((0, enc_attn), (2, dec_attn)):
        wide = source.shape[1] // 4
        for part in range(4):
            update(number, part, source[:, part * wide : (part + 1) * wide])
    for number, pair in ((1, (enc_up, enc_down)), (3, (dec_up, dec_down))):
        for part, source in enumerate(pair):
            update(number, part, source[...])
    for number, source in ((4, embed), (5, bridge), (6, predict)):
        share = source.shape[2]
        for half in range(2):
            update(number, (slice(None), pl.ds(half * share, share)), source[half])


def adam_all(sums, sources, masters, firsts, seconds, means):
    like = lambda arrays: [shape(a.shape, F32) for a in arrays]
    outs = like(masters) * 3 + like(means)
    count = len(masters)
    args = (*sources, *masters, *firsts, *seconds, *means)
    rows = [a.shape[-2] for a in args]
    cuts = 4 if all(r % 32 == 0 for r in rows) else 1

    def tiled(a):
        lead = a.shape[:-2]
        return pl.BlockSpec(lead + (a.shape[-2] // cuts, a.shape[-1]), lambda i: (0,) * len(lead) + (i, 0))

    result = pl.pallas_call(
        functools.partial(adam_kernel, count, len(means)),
        out_shape=tuple(outs),
        grid=(cuts,),
        in_specs=[pl.BlockSpec(sums.shape, lambda i: (0, 0))] + [tiled(a) for a in args],
        out_specs=tuple(tiled(a) for a in outs),
        compiler_params=pltpu.CompilerParams(vmem_limit_bytes=VMEM_LIMIT),
        cost_estimate=pl.CostEstimate(flops=0, bytes_accessed=2 * sum(4 * a.size for a in args), transcendentals=0),
    )(sums, *args)
    return (result[:count], result[count : 2 * count], result[2 * count : 3 * count], result[3 * count :])


def plain_step(pixels, target, band_ids, kept_index, intersection, gsd_scale, masters, enc_table, dec_table):
    enc_attn, enc_mlp, dec_attn, dec_mlp, patch_embed, bridge, predict, vectors = masters
    images, keep_count = kept_index.shape
    patch_count = intersection.shape[1]
    patch_index = jnp.arange(patch_count, dtype=jnp.int32)
    kept_flags = jnp.any(kept_index[:, :, None] == patch_index[None, None, :], axis=1).astype(F32)
    patch_weight = ((1.0 - kept_flags) * (1.0 - 0.5 * intersection.astype(F32))).reshape(-1, 1)
    hidden_rows = (1.0 - kept_flags).reshape(-1, 1)
    core = lax.axis_index("mp").astype(jnp.int32).reshape(1)
    size = lax.axis_size("dp")

    def flat(stack):
        return jnp.concatenate([part.astype(BF16) for part in stack], axis=1)

    def core_half(block):
        half = block.shape[1] // 2
        return lax.dynamic_slice_in_dim(block, lax.axis_index("mp") * half, half, 1).astype(BF16)

    vec_shard = vectors.shape[0]
    vec_room = -(-vec_shard // 1024) * 1024
    vec_rows = jnp.pad(lax.reduce_precision(vectors, 8, 7), (0, vec_room - vec_shard)).reshape(-1, 128)
    vec_full = gather_dp(vec_rows, 0, orders()[0])
    pieces = split_vectors(vec_full.reshape(size, vec_room)[:, :vec_shard].reshape(-1), D, E)
    evec = jnp.stack(pieces[:7] + [jnp.zeros_like(pieces[0])])
    dvec = jnp.stack(pieces[7:14] + [jnp.zeros_like(pieces[7])])
    kept_column = kept_index.reshape(-1, 1)
    rows, rows_d = images * keep_count, images * patch_count
    pixel_count = pixels.shape[1]
    group = 2 * keep_count
    shards = [core_half(patch_embed.T), flat(enc_attn), flat(enc_mlp), flat(dec_attn), flat(dec_mlp), core_half(bridge),
              core_half(predict)]
    weights = gather_all(shards, (True, False, False, False, False, True, True))
    embed_w, enc_attn_w, enc_mlp_w, dec_attn_w, dec_mlp_w, bridge_w, predict_w = weights
    local = enc_attn_w.shape[1] // 4
    band_weight = total_dp(jnp.stack([jnp.sum(jnp.where(band_ids == level, patch_weight, 0.0)) for level in range(NB)]))
    inverse = 1.0 / band_weight
    x0, *enc_saved, part, kept_pixels = run(
        functools.partial(enc_in_kernel, keep_count, group, DH),
        [shape((rows, D), F32), shape((3 * local, rows), BF16), shape((local, rows), BF16),
         shape((local // DH, rows), F32), shape((rows, D), BF16), shape((rows, pixel_count), BF16)],
        [pltpu.VMEM((4 * local, D), BF16)],
        (pixels, kept_column, enc_table, embed_w, evec, enc_attn_w),
        rows * D * (2 * pixel_count + 8 * local))
    x1, part = mlp_forward(x0, part, evec, enc_mlp_w)
    other = other_core(part)
    one_d, one_e = shape((1, D), F32), shape((1, E), F32)
    local_d = dec_attn_w.shape[1] // 4
    x2, final_enc, xd, *dec_saved, part = run(
        functools.partial(dec_in_kernel, keep_count, DDH),
        [shape((rows, D), F32), shape((rows, D), BF16), shape((rows_d, E), F32), shape((3 * local_d, rows_d), BF16),
         shape((local_d, rows_d), BF16), shape((local_d // DDH, rows_d), F32), shape((rows_d, E), BF16)],
        [pltpu.VMEM((4 * local_d, E), BF16), pltpu.VMEM((rows, E), F32)],
        (x1, part, other, evec, bridge_w, kept_index, hidden_rows, dec_table, dvec,
         dec_attn_w),
        rows_d * E * 8 * local_d + 2 * rows * D * E)
    xd1, part = mlp_forward(xd, part, dvec, dec_mlp_w)
    gyd, grad_predict, grad_pbias, loss_parts, grad_dec_fg, grad_dec_fb = head(
        core, inverse, xd1, part, dvec, pieces[14].reshape(1, -1), predict_w, target, band_ids, patch_weight, patch_count)
    grad_dec_up, grad_dec_down, part = mlp_backward(gyd, xd1, dvec, dec_mlp_w)
    gxd, grad_dec_attn, grad_dec_gb, grad_dec_bb, part = attn_backward(
        gyd, xd1, part, xd, dec_saved, dvec, dec_attn_w, patch_count, patch_count, DDH)
    grad_dec_ga, grad_dec_ba, grad_mask, grad_bridge, grad_enc_fg, grad_enc_fb, gye = run(
        functools.partial(between_kernel, keep_count),
        [one_e, one_e, one_e, shape((D, E // 2), BF16), one_d, one_d, shape((rows, D), F32)],
        [pltpu.VMEM((rows, E), BF16)],
        (core, gxd, xd, part, other_core(part), dvec, kept_column, hidden_rows, final_enc, x2, evec, bridge_w),
        3 * rows * D * E, 1)
    wide_row = lambda row: jnp.pad(row, ((0, 0), (0, D - row.shape[1])))
    no_row = jnp.zeros((1, D), F32)
    late_rows = [grad_enc_fg, grad_enc_fb] + [wide_row(row) for row in (
        grad_mask, grad_dec_ga, grad_dec_ba, grad_dec_gb, grad_dec_bb, grad_dec_fg, grad_dec_fb, grad_pbias)] + [no_row]
    dec_grads = [grad_predict, grad_dec_up, grad_dec_down, grad_dec_attn, grad_bridge]
    grad_enc_up, grad_enc_down, part = mlp_backward(gye, x1, evec, enc_mlp_w)
    gxe, grad_enc_attn, grad_enc_gb, grad_enc_bb, part = attn_backward(
        gye, x1, part, x0, enc_saved, evec, enc_attn_w, keep_count, group, DH)
    grad_enc_ga, grad_enc_ba, grad_ebias, grad_embed = run(
        enc_out_kernel,
        [one_d, one_d, one_d, shape((D, pixel_count // 2), BF16)],
        [], (core, gxe, x0, part, other_core(part), evec, kept_pixels), rows * D * pixel_count, 1)
    vec_grads = jnp.concatenate([grad_ebias, grad_enc_ga, grad_enc_ba, grad_enc_gb, grad_enc_bb] + late_rows)
    sums, total_squares, loss, vec_sums = reduce_plain(
        dec_grads + [grad_enc_up, grad_enc_down, grad_enc_attn, grad_embed], loss_parts, vec_grads)
    sums = [jnp.stack([jnp.where(core == 0, a, b), jnp.where(core == 0, b, a)]) if at in (0, 4, 8) else a
            for at, a in enumerate(sums) for b in ([other_core(a)] if at in (0, 4, 8) else [a])]
    return sums, total_squares, loss, vec_sums, band_weight


def per_device(
    pixels,
    target,
    band_ids,
    kept_index,
    intersection,
    gsd_scale,
    enc_attn,
    enc_mlp,
    dec_attn,
    dec_mlp,
    patch_embed,
    bridge,
    predict,
    vectors,
    first_enc_attn,
    first_enc_mlp,
    first_dec_attn,
    first_dec_mlp,
    first_patch_embed,
    first_bridge,
    first_predict,
    first_vectors,
    second_enc_attn,
    second_enc_mlp,
    second_dec_attn,
    second_dec_mlp,
    second_patch_embed,
    second_bridge,
    second_predict,
    second_vectors,
    ema_enc_attn,
    ema_enc_mlp,
    ema_patch_embed,
):
    masters = (enc_attn, enc_mlp, dec_attn, dec_mlp, patch_embed, bridge, predict, vectors)
    firsts = (
        first_enc_attn,
        first_enc_mlp,
        first_dec_attn,
        first_dec_mlp,
        first_patch_embed,
        first_bridge,
        first_predict,
        first_vectors,
    )
    seconds = (
        second_enc_attn,
        second_enc_mlp,
        second_dec_attn,
        second_dec_mlp,
        second_patch_embed,
        second_bridge,
        second_predict,
        second_vectors,
    )
    averages = (ema_enc_attn, ema_enc_mlp, ema_patch_embed)
    enc_table, dec_table = sine_table(gsd_scale, D, GRID), sine_table(gsd_scale, E, GRID)
    vec_shard = vectors.shape[0]
    vec_start = lax.axis_index("dp") * vec_shard
    if patch_embed.shape[1] % 16 == 0 and dec_attn.shape[1] % 16 == 0:
        placed = lax.dynamic_update_slice(
            jnp.zeros((24 * 512,), F32), lax.reduce_precision(vectors, 8, 7), (vec_start,)).reshape(24, 512)
        weights, results = forward_all(
            [patch_embed.T, enc_attn, enc_mlp, dec_attn, bridge], (True, False, False, False, True), pixels, band_ids,
            kept_index, intersection, enc_table, placed)
        embed_w, enc_attn_w, enc_mlp_w, dec_attn_w, bridge_w = weights
        x0, *enc_saved, kept_pixels, x1, part, other, totals, enc_flat, evec, row_values, kept_column = results
        band_weight = jnp.sum(totals[24 : 24 + NB], axis=1)
        gye, grad_dec_attn, grad_bridge, sum_predict, sum_up, sum_down, norm, loss_parts, vec_grads = decoder_all(
            x1, part, other, evec, kept_index, kept_column, row_values, dec_table, totals, dec_mlp, predict, target,
            band_ids, dec_attn_w, bridge_w)
        sums, norms, vec_grad = backward_all(
            gye, x1, evec, vec_grads, loss_parts, norm, enc_saved, x0, enc_flat, kept_pixels, enc_mlp_w,
            [grad_dec_attn, grad_bridge], (False, True, False, False, False, True), kept_index.shape[1], DH)
        sums = [sum_predict, sum_up, sum_down] + sums
        total_squares, loss = norms[0, 0], 0.5 * norms[1, 0]
    else:
        sums, total_squares, loss, vec_sums, band_weight = plain_step(
            pixels, target, band_ids, kept_index, intersection, gsd_scale, masters, enc_table, dec_table)
        norms = jnp.broadcast_to(total_squares, (8, 128))
        vec_grad = jnp.concatenate(
            [vec_sums[:7].reshape(-1), vec_sums[7:14, :E].reshape(-1), vec_sums[14, : pixels.shape[1]]])
    vec_grad = lax.dynamic_slice_in_dim(vec_grad.reshape(-1), vec_start, vec_shard)
    grad_norm = jnp.sqrt(total_squares)
    factor = CLIP / jnp.maximum(grad_norm, CLIP)
    order = (7, 5, 6, 3, 1, 2, 8, 4, 0)
    flip = lambda arrays, at: [a.T if number == at else a for number, a in enumerate(arrays)]
    news, new_firsts, new_seconds, means = adam_all(
        norms, [sums[at] for at in order], flip(masters[:7], 4), flip(firsts[:7], 4), flip(seconds[:7], 4),
        flip(averages, 2))
    news, new_firsts, new_seconds, means = flip(news, 4), flip(new_firsts, 4), flip(new_seconds, 4), flip(means, 2)
    vec_new = adam_update(vectors, vec_grad * factor, firsts[7], seconds[7], RATE_VEC, 0.0)
    news, new_firsts, new_seconds = [
        list(many) + [one] for many, one in zip((news, new_firsts, new_seconds), vec_new)]
    ema_attn, ema_mlp, ema_embed = means
    return (
        loss,
        band_weight,
        grad_norm,
        news[0],
        news[1],
        news[2],
        news[3],
        news[4],
        news[5],
        news[6],
        news[7],
        new_firsts[0],
        new_firsts[1],
        new_firsts[2],
        new_firsts[3],
        new_firsts[4],
        new_firsts[5],
        new_firsts[6],
        new_firsts[7],
        new_seconds[0],
        new_seconds[1],
        new_seconds[2],
        new_seconds[3],
        new_seconds[4],
        new_seconds[5],
        new_seconds[6],
        new_seconds[7],
        ema_attn,
        ema_mlp,
        ema_embed,
    )


def solution(mesh):
    return jax.shard_map(
        per_device,
        mesh=mesh,
        in_specs=(
            P("dp", None),
            P("dp", None),
            P("dp", None),
            P("dp", None),
            P("dp", None),
            P("dp"),
            P(None, "dp", "mp"),
            P(None, "dp", "mp"),
            P(None, "dp", "mp"),
            P(None, "dp", "mp"),
            P(None, "dp"),
            P("dp", None),
            P("dp", None),
            P("dp"),
            P(None, "dp", "mp"),
            P(None, "dp", "mp"),
            P(None, "dp", "mp"),
            P(None, "dp", "mp"),
            P(None, "dp"),
            P("dp", None),
            P("dp", None),
            P("dp"),
            P(None, "dp", "mp"),
            P(None, "dp", "mp"),
            P(None, "dp", "mp"),
            P(None, "dp", "mp"),
            P(None, "dp"),
            P("dp", None),
            P("dp", None),
            P("dp"),
            P(None, "dp", "mp"),
            P(None, "dp", "mp"),
            P(None, "dp"),
        ),
        out_specs=(
            P(),
            P(),
            P(),
            P(None, "dp", "mp"),
            P(None, "dp", "mp"),
            P(None, "dp", "mp"),
            P(None, "dp", "mp"),
            P(None, "dp"),
            P("dp", None),
            P("dp", None),
            P("dp"),
            P(None, "dp", "mp"),
            P(None, "dp", "mp"),
            P(None, "dp", "mp"),
            P(None, "dp", "mp"),
            P(None, "dp"),
            P("dp", None),
            P("dp", None),
            P("dp"),
            P(None, "dp", "mp"),
            P(None, "dp", "mp"),
            P(None, "dp", "mp"),
            P(None, "dp", "mp"),
            P(None, "dp"),
            P("dp", None),
            P("dp", None),
            P("dp"),
            P(None, "dp", "mp"),
            P(None, "dp", "mp"),
            P(None, "dp"),
        ),
        check_vma=False,
    )
```
